32 devices in a mesh: dp: 2 (over y), expert: 8 (over z, x), shard: 2 (over core).
Axes of the slice: x: 2, y: 2, z: 4, core: 2. Of those that a mesh axis runs over, the one named last changes fastest.
Arguments:
- hidden_in: bfloat16 [12288, 1536], P(('dp', 'expert', 'shard')), may hold values from -6 to 6
- cotangent: bfloat16 [12288, 1536], P(('dp', 'expert', 'shard')), may hold values from -6 to 6
- deal_order: int32 [32, 384], P(('dp', 'expert', 'shard')), may hold values from 0 to 383, each once within a row
- lengths: int32 [32, 3], P(('dp', 'expert', 'shard')), may hold values from 1 to 288, 384 in all within a row
- routes: int32 [12288, 4], P(('dp', 'expert', 'shard')), may hold values from 0 to 7, all different within a row; in each aligned block of 384 rows (0 to 383, 384 to 767, ...) at most 288 rows name the same one
- attention_gain: bfloat16 [1536], P('shard'), may hold values from 0.5 to 1.5
- expert_gain: bfloat16 [1536], P('shard'), may hold values from 0.5 to 1.5
- qkv_weight: bfloat16 [1536, 2048], P('shard'), may hold values from -0.15625 to 0.15625
- out_weight: bfloat16 [1536, 1536], P('shard'), may hold values from -0.75 to 0.75
- router_weight: bfloat16 [1536, 8], P('shard'), may hold values from -0.078125 to 0.078125
- gate_up_weight: bfloat16 [8, 1536, 1536], P('expert'), may hold values from -0.15625 to 0.15625
- down_weight: bfloat16 [8, 768, 1536], P('expert'), may hold values from -0.4375 to 0.4375
Outputs:
- layer_out: bfloat16 [12288, 1536], P(('dp', 'expert', 'shard'))
- input_gradient: bfloat16 [12288, 1536], P(('dp', 'expert', 'shard'))
- attention_gain_gradient: float32 [1536], P('shard')
- expert_gain_gradient: float32 [1536], P('shard')
- qkv_gradient: float32 [1536, 2048], P('shard')
- out_gradient: float32 [1536, 1536], P('shard')
- router_gradient: float32 [1536, 8], P('shard')
- gate_up_gradient: float32 [8, 1536, 1536], P('expert', ('dp', 'shard'))
- down_gradient: float32 [8, 768, 1536], P('expert', ('dp', 'shard'))
The draws below stay inside these ranges and needn't reach their ends.
Inputs may be any that keep to these rules, and one draw needn't show every extreme that they name: `deal_order`: each device's row is a permutation of 0 to 383. Each device's 3 lengths sum to 384, and the largest is 288. `routes`: each token names 4 different experts; among the rows of one device no expert is named more than 288 times, a bound that some block reaches.
All inputs are finite; a program needn't handle non-finite values.
Results may differ from the reference program's by a relative error of at most 0.017.
Values may be sent and summed in bfloat16 or wider, within the bound.
No kernel may reach another device: no remote copies, remote signals or barrier semaphores. Data moves between devices by JAX's collectives and lax.ppermute only.
A program may use at most 256 MiB of HBM per device.

```python
import math
import jax
import jax.numpy as jnp
import numpy as np
from jax import lax

D = 1536
QUERY_HEADS = 12
KEY_VALUE_HEADS = 2
HEAD_SIZE = 128
EXPERT_FF = 768
TOP = 4
SEQS = 3
TOKENS_PER_CHIP = 384
EXPERTS = 8
QKV = 2048
LONGEST = 288
CAP = 288
TOKENS = 12288
N_DP = 2
N_EXPERT = 8
N_SHARD = 2
DEVICES = 32


def shard_levels(own_key, shape, cuts, smallest, largest):
    loudness, own = 1.0, jax.random.fold_in(own_key, 6)
    for position, blocks in cuts:
        draws = jnp.exp(jax.random.uniform(jax.random.fold_in(own, position), (blocks,), jnp.float32, smallest / len(cuts), largest / len(cuts)))
        loudness = loudness * jnp.repeat(draws, shape[position] // blocks).reshape([-1 if axis == position else 1 for axis in range(len(shape))])
    return loudness


def split_up(number_of, total, limit, slope):
    loads = [(1 << 20) // math.isqrt(standing ** slope) + 1 for standing in range(2, number_of + 1)]
    rest, holding = total - limit - (number_of - 1), [1] * (number_of - 1)
    while rest > 0:
        free = [i for i in range(number_of - 1) if holding[i] < limit]
        mass, left = sum([loads[i] for i in free]), rest
        for i in free:
            addition = min(limit - holding[i], max(1, left * loads[i] // mass), rest)
            holding[i] = holding[i] + addition
            rest = rest - addition
    return np.array([limit] + holding)


def ragged_sizes(stream_key, amount, total, limit, slope):
    if amount == 2:
        one = jax.random.randint(stream_key, (), max(1, total - limit), min(limit, total - 1) + 1)
        return jnp.stack([one, total - one])
    sizes = jnp.asarray(split_up(amount, total, limit, slope), jnp.int32)
    twos = (amount - 1) // 2
    donor, taker = sizes[1:1 + 2 * twos:2], sizes[2:2 + 2 * twos:2]
    margin = jnp.minimum(donor - 1, limit - taker)
    moved = jax.random.randint(jax.random.fold_in(stream_key, 1), (twos,), 0, 1 << 20) % (margin + 1)
    sizes = sizes.at[1:1 + 2 * twos:2].set(donor - moved).at[2:2 + 2 * twos:2].set(taker + moved)
    return sizes[jax.random.permutation(jax.random.fold_in(stream_key, 2), amount)]


def routed_block(stream_key, own, number, rows, count, top, most, lean):
    ranking = jax.random.permutation(stream_key, count)
    heavy_load, ordinary = portions_of(count, rows * top, most, lean, True), portions_of(count, rows * top, most, lean, False)
    places = jnp.arange(count)

    def named(sizes, offset_by):
        used = int((sizes > 0).sum())
        fixed = max(1, used // 4)
        passed = fixed + (places - fixed + offset_by * (used - fixed)) % max(1, count - fixed)
        return jnp.zeros((count,), jnp.int32).at[ranking[jnp.where(places < fixed, places, passed)]].set(jnp.asarray(sizes, jnp.int32))

    sizes = jnp.where(number % 4 == 0, named(heavy_load, number // 4), named(ordinary, number - number // 4 - 1))
    mixed = jax.random.permutation(jax.random.fold_in(own, 3), count)
    donor, sink = mixed[0:count // 2 * 2:2], mixed[1:count // 2 * 2:2]
    margin = jnp.minimum(sizes[donor] - 1, most - sizes[sink]) // 2
    margin = jnp.where((donor == ranking[0]) | (sink == ranking[0]) | (sizes[sink] == 0), 0, jnp.maximum(margin, 0))
    passed = jax.random.randint(jax.random.fold_in(own, 4), (count // 2,), 0, 1 << 20) % (margin + 1)
    sizes = sizes.at[donor].add(-passed).at[sink].add(passed)
    labels = jnp.searchsorted(jnp.cumsum(sizes), jnp.arange(rows * top), side="right").astype(jnp.int32)
    grid = labels.reshape(top, rows).T
    grid = grid[jax.random.permutation(jax.random.fold_in(own, 1), rows)]
    offset_by = jax.random.randint(jax.random.fold_in(own, 2), (rows, 1), 0, top)
    return jnp.take_along_axis(grid, (jnp.arange(top)[None, :] + offset_by) % top, axis=1)


def portions_of(amount, total, bound, skew, full):
    portions = [(1 << 20) // math.isqrt(standing ** skew) + 1 for standing in range(1, amount + 1)]
    largest = bound if full else min(bound, max(-(-total // amount), total * portions[0] // sum(portions)))
    least = 1 if total - largest >= amount - 1 else 0
    holding, rest = [largest] + [least] * (amount - 1), total - largest - least * (amount - 1)
    while rest > 0:
        free = [i for i in range(1, amount) if holding[i] < largest] or [i for i in range(1, amount) if holding[i] < bound]
        mass, remaining = sum([portions[i] for i in free]), rest
        for i in free:
            addition = min(bound - holding[i], max(1, remaining * portions[i] // mass), rest)
            holding[i] = holding[i] + addition
            rest = rest - addition
    return np.array(holding)


def normal_values(key, shape, scale, bound, shards=(), held_as=jnp.bfloat16):
    factor_of = shard_levels(key, shape, shards, -0.22, 0.18) if shards else 1.0
    array = jax.random.normal(key, shape, jnp.float32) * scale * factor_of
    return jnp.minimum(jnp.maximum(array, -bound), bound).astype(held_as)


def setup_inputs(seed: int = 0) -> dict:
    streams_of = jax.random.split(jax.random.key(seed), 13)
    hidden_in = normal_values(streams_of[0], (TOKENS, D), 1.0, 6.0, ((0, 32),))
    cotangent = normal_values(streams_of[1], (TOKENS, D), 1.0, 6.0, ((0, 32),))
    deal_order = jax.vmap(lambda own: jax.random.permutation(own, TOKENS_PER_CHIP))(jax.random.split(streams_of[2], DEVICES)).reshape((DEVICES, TOKENS_PER_CHIP)).astype(jnp.int32)
    lengths = jax.vmap(lambda own: ragged_sizes(own, SEQS, TOKENS_PER_CHIP, LONGEST, 1))(jax.random.split(streams_of[3], DEVICES)).reshape((DEVICES, SEQS)).astype(jnp.int32)
    routes_keys = jax.random.split(jax.random.fold_in(streams_of[4], 1), TOKENS // TOKENS_PER_CHIP)
    routes_turns = jax.random.permutation(jax.random.fold_in(streams_of[4], 3), TOKENS // TOKENS_PER_CHIP)
    routes = jax.vmap(lambda own, number: routed_block(jax.random.fold_in(streams_of[4], 2), own, number, TOKENS_PER_CHIP, EXPERTS, TOP, CAP, 1))(routes_keys, routes_turns).reshape((TOKENS, TOP))
    attention_gain = jnp.clip(1.0 + 0.1 * jax.random.normal(streams_of[5], (D,), jnp.float32), 0.5, 1.5).astype(jnp.bfloat16)
    expert_gain = jnp.clip(1.0 + 0.1 * jax.random.normal(streams_of[6], (D,), jnp.float32), 0.5, 1.5).astype(jnp.bfloat16)
    qkv_weight = normal_values(streams_of[7], (D, QKV), D ** -0.5, 0.15625, ((0, 2),))
    out_weight = normal_values(streams_of[8], (QUERY_HEADS * HEAD_SIZE, D), (QUERY_HEADS * HEAD_SIZE * 16 // TOKENS_PER_CHIP) ** -0.5, 0.75, ((0, 2),))
    router_weight = normal_values(streams_of[9], (D, EXPERTS), (4 * D) ** -0.5, 0.078125, ((0, 2),))
    gate_up_weight = normal_values(streams_of[10], (EXPERTS, D, 2 * EXPERT_FF), D ** -0.5, 0.15625, ((0, 8),))
    down_weight = normal_values(streams_of[11], (EXPERTS, EXPERT_FF, D), (EXPERT_FF // 4) ** -0.5, 0.4375, ((0, 8),))
    return dict(hidden_in=hidden_in, cotangent=cotangent, deal_order=deal_order, lengths=lengths, routes=routes, attention_gain=attention_gain, expert_gain=expert_gain, qkv_weight=qkv_weight, out_weight=out_weight, router_weight=router_weight, gate_up_weight=gate_up_weight, down_weight=down_weight)


EPS = 1e-06
THETA = 1000000.0
HIGH = lax.Precision.HIGHEST

@jax.custom_vjp
def lower_half(v):
    return lax.optimization_barrier(v.astype(jnp.bfloat16)).astype(jnp.float32)

@jax.custom_vjp
def low_back(v):
    return v

def low_keep(v):
    return (lower_half(v), None)

def low_pass(kept, grad):
    return (grad,)

def back_keep(v):
    return (v, None)

def back_low(kept, grad):
    return (lower_half(grad),)
lower_half.defvjp(low_keep, low_pass)
low_back.defvjp(back_keep, back_low)

def norm_rows(field, gain_vec):
    inv_scale = lax.rsqrt(lax.optimization_barrier(jnp.mean(field * field, axis=-1, keepdims=True)) + EPS)
    return field * inv_scale * gain_vec

def positions_of(lengths_dev, count_of_rows):
    seq_ends = jnp.cumsum(lengths_dev).astype(jnp.int32)
    starts = (seq_ends - lengths_dev).astype(jnp.int32)
    places = jnp.arange(count_of_rows, dtype=jnp.int32)
    segment = lax.optimization_barrier(jnp.sum((places[:, None] >= seq_ends[None, :]).astype(jnp.int32), axis=1)).astype(jnp.int32)
    member = segment[:, None] == jnp.arange(lengths_dev.shape[0], dtype=jnp.int32)[None, :]
    start_of = lax.optimization_barrier(jnp.sum(jnp.where(member, starts[None, :], 0), axis=1)).astype(jnp.int32)
    return (segment, (places - start_of).astype(jnp.int32))

def apply_rotation(field, token_position, direction):
    half_dim = field.shape[-1] // 2
    frequency = THETA ** (-jnp.arange(half_dim, dtype=jnp.float32) / half_dim)
    angles = token_position.astype(jnp.float32)[:, None] * frequency[None, :]
    cosine = jnp.cos(angles)[:, None, :]
    sine_term = direction * jnp.sin(angles)[:, None, :]
    lead_part = field[..., :half_dim]
    tail_part = field[..., half_dim:]
    return jnp.concatenate([lead_part * cosine - tail_part * sine_term, tail_part * cosine + lead_part * sine_term], axis=-1)

def attend(query_matrix_rows, key_matrix_rows, value_matrix_rows, segment):
    count_of_rows = query_matrix_rows.shape[0]
    scores = jnp.einsum('ihgd,jhd->hgij', query_matrix_rows, key_matrix_rows, precision=HIGH) * HEAD_SIZE ** (-0.5)
    places = jnp.arange(count_of_rows, dtype=jnp.int32)
    allowed = (segment[:, None] == segment[None, :]) & (places[None, :] <= places[:, None])
    scores = low_back(jnp.where(allowed, scores, -1e+30))
    soft_probs = jax.nn.softmax(scores, axis=-1)
    return jnp.einsum('hgij,jhd->ihgd', lower_half(soft_probs), value_matrix_rows, precision=HIGH)

def to_sequence(field, deal_order):
    blocks = field.reshape(N_DP, N_EXPERT, N_SHARD, N_DP, TOKENS_PER_CHIP // N_DP, field.shape[-1])
    arrived = blocks.transpose(3, 1, 2, 0, 4, 5).reshape(DEVICES, TOKENS_PER_CHIP, field.shape[-1])
    return jnp.take_along_axis(arrived, deal_order[:, :, None].astype(jnp.int32), axis=1)

def to_dealt(field, deal_order):
    device_rows = jnp.arange(DEVICES, dtype=jnp.int32)[:, None]
    place_rows = jnp.broadcast_to(jnp.arange(TOKENS_PER_CHIP, dtype=jnp.int32)[None, :], deal_order.shape)
    inverse = jnp.zeros(deal_order.shape, jnp.int32).at[device_rows, deal_order].set(place_rows)
    arrived = jnp.take_along_axis(field, inverse[:, :, None], axis=1)
    blocks = arrived.reshape(N_DP, N_EXPERT, N_SHARD, N_DP, TOKENS_PER_CHIP // N_DP, field.shape[-1])
    return blocks.transpose(3, 1, 2, 0, 4, 5).reshape(TOKENS, field.shape[-1])

def reference(hidden_in, cotangent, deal_order, lengths, routes, attention_gain, expert_gain, qkv_weight, out_weight, router_weight, gate_up_weight, down_weight):
    head_groups = QUERY_HEADS // KEY_VALUE_HEADS

    def forward(tokens, gain_first, gain_second, proj_qkv, proj_out, proj_router, expert_up, expert_down):
        sequence = to_sequence(tokens, deal_order)

        def attention_part(inputs):
            residual, lengths_dev = inputs
            segment, token_position = positions_of(lengths_dev, TOKENS_PER_CHIP)
            normed = lower_half(norm_rows(residual, gain_first))
            projected_rows = low_back(jnp.dot(normed, proj_qkv, precision=HIGH))
            query_matrix_rows = lower_half(apply_rotation(projected_rows[:, :QUERY_HEADS * HEAD_SIZE].reshape(TOKENS_PER_CHIP, QUERY_HEADS, HEAD_SIZE), token_position, 1.0)).reshape(TOKENS_PER_CHIP, KEY_VALUE_HEADS, head_groups, HEAD_SIZE)
            key_matrix_rows = lower_half(apply_rotation(projected_rows[:, QUERY_HEADS * HEAD_SIZE:(QUERY_HEADS + KEY_VALUE_HEADS) * HEAD_SIZE].reshape(TOKENS_PER_CHIP, KEY_VALUE_HEADS, HEAD_SIZE), token_position, 1.0))
            value_matrix_rows = lower_half(projected_rows[:, (QUERY_HEADS + KEY_VALUE_HEADS) * HEAD_SIZE:].reshape(TOKENS_PER_CHIP, KEY_VALUE_HEADS, HEAD_SIZE))
            mix_rows = attend(query_matrix_rows, key_matrix_rows, value_matrix_rows, segment).reshape(TOKENS_PER_CHIP, QUERY_HEADS * HEAD_SIZE)
            mix_rows = lower_half(low_back(mix_rows))
            return residual + low_back(jnp.dot(mix_rows, proj_out, precision=HIGH))
        middle = lax.map(jax.checkpoint(attention_part), (sequence, lengths)).reshape(TOKENS, D)
        normed_moe = lower_half(norm_rows(middle, gain_second))
        logits = low_back(jnp.dot(normed_moe, proj_router, precision=HIGH))
        gate_probs = jax.nn.softmax(jnp.take_along_axis(logits, routes.astype(jnp.int32), axis=1), axis=-1)

        def expert_step(running, inputs):
            up_matrix, down_matrix, expert_id = inputs
            weighting = lax.optimization_barrier(jnp.sum(jnp.where(routes == expert_id, gate_probs, 0.0), axis=1))
            rows_in = low_back(normed_moe)
            gate_up = low_back(jnp.dot(rows_in, up_matrix, precision=HIGH))
            hidden_rows = lower_half(jax.nn.gelu(gate_up[:, :EXPERT_FF], approximate=True) * gate_up[:, EXPERT_FF:])
            out_rows = lower_half(low_back(jnp.dot(hidden_rows, down_matrix, precision=HIGH)))
            return (running + weighting[:, None] * out_rows, None)
        expert_sum, unused = lax.scan(jax.checkpoint(expert_step), jnp.zeros((TOKENS, D), jnp.float32), (expert_up, expert_down, jnp.arange(EXPERTS, dtype=jnp.int32)))
        return to_dealt((middle + expert_sum).reshape(DEVICES, TOKENS_PER_CHIP, D), deal_order)
    floats = [item.astype(jnp.float32) for item in (hidden_in, attention_gain, expert_gain, qkv_weight, out_weight, router_weight, gate_up_weight, down_weight)]
    layer_out, pull = jax.vjp(forward, *floats)
    grads = pull(cotangent.astype(jnp.float32))
    return (layer_out.astype(jnp.bfloat16), grads[0].astype(jnp.bfloat16), grads[1], grads[2], grads[3], grads[4], grads[5], grads[6], grads[7])
```

```python
import jax
import jax.numpy as jnp
from jax import lax
from jax.sharding import PartitionSpec as P

QUERY_HEADS = 12
KEY_VALUE_HEADS = 2
HEAD_SIZE = 128
TOP = 4


EPS = 1e-06
THETA = 1000000.0


def positions_of(lengths_dev, count_of_rows):
    seq_ends = jnp.cumsum(lengths_dev)
    starts = seq_ends - lengths_dev
    places = jnp.arange(count_of_rows, dtype=jnp.int32)
    segment = jnp.sum((places[:, None] >= seq_ends[None, :]).astype(jnp.int32), axis=1)
    member = segment[:, None] == jnp.arange(lengths_dev.shape[0], dtype=jnp.int32)[None, :]
    start_of = jnp.sum(jnp.where(member, starts[None, :], 0), axis=1)
    return (segment, places - start_of)


def apply_rotation(field, token_position, direction):
    half_dim = field.shape[-1] // 2
    frequency = THETA ** (-jnp.arange(half_dim, dtype=jnp.float32) / half_dim)
    angles = token_position.astype(jnp.float32)[:, None] * frequency[None, :]
    cosine = jnp.cos(angles)[:, None, :]
    sine_term = direction * jnp.sin(angles)[:, None, :]
    lead_part = field[..., :half_dim]
    tail_part = field[..., half_dim:]
    return jnp.concatenate(
        [lead_part * cosine - tail_part * sine_term, tail_part * cosine + lead_part * sine_term],
        axis=-1,
    )


def masked_scores(query_block, key_matrix_rows, segment_block, segment, row_start):
    raw_scores = jnp.einsum(
        "ihgd,jhd->hgij", query_block, key_matrix_rows, preferred_element_type=jnp.float32
    ) * HEAD_SIZE ** (-0.5)
    query_at = row_start + jnp.arange(query_block.shape[0], dtype=jnp.int32)
    key_at = jnp.arange(key_matrix_rows.shape[0], dtype=jnp.int32)
    allowed = (segment_block[:, None] == segment[None, :]) & (key_at[None, :] <= query_at[:, None])
    return jnp.where(allowed, raw_scores, -1e30)


def norm_back(field, inv_scale, gain_vec, grad_normed):
    scaled = grad_normed * gain_vec
    grad_field = inv_scale * scaled - field * inv_scale**3 * jnp.mean(
        scaled * field, axis=1, keepdims=True
    )
    grad_gain = jnp.sum(field * inv_scale * grad_normed, axis=0)
    return (grad_field, grad_gain)


def activate(gate_up):
    hidden_width = gate_up.shape[1] // 2
    return jax.nn.gelu(gate_up[:, :hidden_width], approximate=True) * gate_up[:, hidden_width:]


def routed_shards(
    hidden_in,
    cotangent,
    deal_order,
    lengths,
    routes,
    attention_gain,
    expert_gain,
    qkv_weight,
    out_weight,
    router_weight,
    gate_up_weight,
    down_weight,
):
    count_of_rows = hidden_in.shape[0]
    model_width = hidden_in.shape[1]
    head_groups = QUERY_HEADS // KEY_VALUE_HEADS
    arrived_in, arrived_ct = (
        lax.all_to_all(hidden_in, "dp", split_axis=0, concat_axis=0, tiled=True),
        lax.all_to_all(cotangent, "dp", split_axis=0, concat_axis=0, tiled=True),
    )
    deal_rows = deal_order[0]
    tokens = arrived_in[deal_rows]
    upstream = arrived_ct[deal_rows].astype(jnp.float32)
    gain_first, gain_second, full_qkv, full_out, full_router = (
        lax.all_gather(attention_gain, "shard", axis=0, tiled=True),
        lax.all_gather(expert_gain, "shard", axis=0, tiled=True),
        lax.all_gather(qkv_weight, "shard", axis=0, tiled=True),
        lax.all_gather(out_weight, "shard", axis=0, tiled=True),
        lax.all_gather(router_weight, "shard", axis=0, tiled=True),
    )
    gain_first = gain_first.astype(jnp.float32)
    gain_second = gain_second.astype(jnp.float32)
    residual = tokens.astype(jnp.float32)
    inv_first = lax.rsqrt(jnp.mean(residual * residual, axis=1, keepdims=True) + EPS)
    normed_attn = (residual * inv_first * gain_first).astype(jnp.bfloat16)
    projected_rows = jnp.dot(normed_attn, full_qkv, preferred_element_type=jnp.float32)
    segment, token_position = positions_of(lengths[0], count_of_rows)
    query_matrix_rows = (
        apply_rotation(
            projected_rows[:, : QUERY_HEADS * HEAD_SIZE].reshape(
                count_of_rows, QUERY_HEADS, HEAD_SIZE
            ),
            token_position,
            1.0,
        )
        .astype(jnp.bfloat16)
        .reshape(count_of_rows, KEY_VALUE_HEADS, head_groups, HEAD_SIZE)
    )
    key_matrix_rows = apply_rotation(
        projected_rows[
            :, QUERY_HEADS * HEAD_SIZE : (QUERY_HEADS + KEY_VALUE_HEADS) * HEAD_SIZE
        ].reshape(count_of_rows, KEY_VALUE_HEADS, HEAD_SIZE),
        token_position,
        1.0,
    ).astype(jnp.bfloat16)
    value_matrix_rows = (
        projected_rows[:, (QUERY_HEADS + KEY_VALUE_HEADS) * HEAD_SIZE :]
        .reshape(count_of_rows, KEY_VALUE_HEADS, HEAD_SIZE)
        .astype(jnp.bfloat16)
    )
    block_rows = min(count_of_rows, 512)
    block_starts = jnp.arange(count_of_rows // block_rows, dtype=jnp.int32) * block_rows

    def forward_block(row_start):
        scores = masked_scores(query_matrix_rows, key_matrix_rows, segment, segment, row_start)
        row_max = jnp.max(scores, axis=-1, keepdims=True)
        exp_scores = jnp.exp(scores - row_max)
        exp_total = jnp.sum(exp_scores, axis=-1, keepdims=True)
        soft_probs = (exp_scores / exp_total).astype(jnp.bfloat16)
        mix_block = jnp.einsum(
            "hgij,jhd->ihgd", soft_probs, value_matrix_rows, preferred_element_type=jnp.float32
        )
        return (mix_block, (row_max + jnp.log(exp_total))[..., 0])

    mix_blocks, logsum = lax.map(forward_block, block_starts)
    attn_mix = mix_blocks.reshape(count_of_rows, QUERY_HEADS * HEAD_SIZE).astype(jnp.bfloat16)
    middle = residual + jnp.dot(attn_mix, full_out, preferred_element_type=jnp.float32)
    inv_second = lax.rsqrt(jnp.mean(middle * middle, axis=1, keepdims=True) + EPS)
    normed_moe = (middle * inv_second * gain_second).astype(jnp.bfloat16)
    logits = jnp.dot(normed_moe, full_router, preferred_element_type=jnp.float32)
    gate_probs = jax.nn.softmax(jnp.take_along_axis(logits, routes, axis=1), axis=-1)
    expert_count = full_router.shape[1]
    peer_count = lax.axis_size("expert")
    capacity = min(count_of_rows, max(2, 3 * count_of_rows * TOP // (2 * expert_count)))
    flat_routes = routes.reshape(-1)
    expert_ids = jnp.arange(expert_count, dtype=jnp.int32)
    onehot = (flat_routes[:, None] == expert_ids[None, :]).astype(jnp.int32)
    slot_rank = jnp.sum(jnp.cumsum(onehot, axis=0) * onehot, axis=1) - 1
    target = flat_routes * capacity + slot_rank
    pair_count = count_of_rows * TOP
    slot_pair = (
        jnp.full((expert_count * capacity,), pair_count, jnp.int32)
        .at[target]
        .set(jnp.arange(pair_count, dtype=jnp.int32))
    )
    padded = jnp.concatenate([normed_moe, jnp.zeros((1, model_width), jnp.bfloat16)], axis=0)
    sending = padded[slot_pair // TOP].reshape(peer_count, capacity, model_width)
    received = lax.all_to_all(sending, "expert", split_axis=0, concat_axis=0, tiled=True)
    rows_in = received.reshape(peer_count * capacity, model_width)
    gate_up = jnp.dot(rows_in, gate_up_weight[0], preferred_element_type=jnp.float32)
    hidden_rows = activate(gate_up).astype(jnp.bfloat16)
    expert_out = jnp.dot(hidden_rows, down_weight[0], preferred_element_type=jnp.float32).astype(
        jnp.bfloat16
    )
    returned = lax.all_to_all(
        expert_out.reshape(peer_count, capacity, model_width),
        "expert",
        split_axis=0,
        concat_axis=0,
        tiled=True,
    )
    per_pair = returned.reshape(peer_count * capacity, model_width)[target].reshape(
        count_of_rows, TOP, model_width
    )
    expert_sum = jnp.zeros((count_of_rows, model_width), jnp.float32)
    for choice_slot in range(TOP):
        expert_sum = expert_sum + gate_probs[:, choice_slot : choice_slot + 1] * per_pair[
            :, choice_slot
        ].astype(jnp.float32)
    final_rows = middle + expert_sum
    grad_pairs = (gate_probs[:, :, None] * upstream[:, None, :]).astype(jnp.bfloat16)
    grad_gates = jnp.stack(
        [
            jnp.sum(per_pair[:, choice_slot].astype(jnp.float32) * upstream, axis=1)
            for choice_slot in range(TOP)
        ],
        axis=1,
    )
    padded_grad = jnp.concatenate(
        [grad_pairs.reshape(pair_count, model_width), jnp.zeros((1, model_width), jnp.bfloat16)],
        axis=0,
    )
    sending_back = padded_grad[slot_pair].reshape(peer_count, capacity, model_width)
    grad_rows = lax.all_to_all(
        sending_back, "expert", split_axis=0, concat_axis=0, tiled=True
    ).reshape(peer_count * capacity, model_width)
    grad_hidden = jnp.dot(grad_rows, down_weight[0].T, preferred_element_type=jnp.float32)
    grad_gate_up = jax.vjp(activate, gate_up)[1](grad_hidden)[0].astype(jnp.bfloat16)
    term_down = jnp.dot(hidden_rows.T, grad_rows, preferred_element_type=jnp.float32)
    term_gate_up = jnp.dot(rows_in.T, grad_gate_up, preferred_element_type=jnp.float32)
    grad_rows_in = jnp.dot(
        grad_gate_up, gate_up_weight[0].T, preferred_element_type=jnp.float32
    ).astype(jnp.bfloat16)
    back_rows = lax.all_to_all(
        grad_rows_in.reshape(peer_count, capacity, model_width),
        "expert",
        split_axis=0,
        concat_axis=0,
        tiled=True,
    )
    back_pairs = back_rows.reshape(peer_count * capacity, model_width)[target].reshape(
        count_of_rows, TOP, model_width
    )
    grad_normed = jnp.zeros((count_of_rows, model_width), jnp.float32)
    for choice_slot in range(TOP):
        grad_normed = grad_normed + back_pairs[:, choice_slot].astype(jnp.float32)
    mean_term = jnp.sum(gate_probs * grad_gates, axis=1, keepdims=True)
    grad_chosen = gate_probs * (grad_gates - mean_term)
    grad_logits = jnp.sum(
        jnp.where(routes[:, :, None] == expert_ids[None, None, :], grad_chosen[:, :, None], 0.0),
        axis=1,
    ).astype(jnp.bfloat16)
    term_router = jnp.dot(normed_moe.T, grad_logits, preferred_element_type=jnp.float32)
    grad_normed = grad_normed + jnp.dot(
        grad_logits, full_router.T, preferred_element_type=jnp.float32
    )
    grad_middle_norm, term_gain_second = norm_back(middle, inv_second, gain_second, grad_normed)
    grad_middle = upstream + grad_middle_norm
    grad_attn_out = grad_middle.astype(jnp.bfloat16)
    term_out = jnp.dot(attn_mix.T, grad_attn_out, preferred_element_type=jnp.float32)
    grad_mix = (
        jnp.dot(grad_attn_out, full_out.T, preferred_element_type=jnp.float32)
        .astype(jnp.bfloat16)
        .reshape(count_of_rows, KEY_VALUE_HEADS, head_groups, HEAD_SIZE)
    )

    def backward_block(accums, inputs):
        acc_key, value_accumulator = accums
        row_start, logsum_block = inputs
        scores = masked_scores(query_matrix_rows, key_matrix_rows, segment, segment, row_start)
        soft_probs = jnp.exp(scores - logsum_block[..., None])
        grad_probs = jnp.einsum(
            "ihgd,jhd->hgij", grad_mix, value_matrix_rows, preferred_element_type=jnp.float32
        )
        value_accumulator = value_accumulator + jnp.einsum(
            "hgij,ihgd->jhd",
            soft_probs.astype(jnp.bfloat16),
            grad_mix,
            preferred_element_type=jnp.float32,
        )
        grad_scores = (
            soft_probs * (grad_probs - jnp.sum(soft_probs * grad_probs, axis=-1, keepdims=True))
        ).astype(jnp.bfloat16)
        grad_query = HEAD_SIZE ** (-0.5) * jnp.einsum(
            "hgij,jhd->ihgd", grad_scores, key_matrix_rows, preferred_element_type=jnp.float32
        )
        acc_key = acc_key + HEAD_SIZE ** (-0.5) * jnp.einsum(
            "hgij,ihgd->jhd", grad_scores, query_matrix_rows, preferred_element_type=jnp.float32
        )
        return ((acc_key, value_accumulator), grad_query)

    zero_key_value = jnp.zeros((count_of_rows, KEY_VALUE_HEADS, HEAD_SIZE), jnp.float32)
    (acc_key, value_accumulator), grad_query = lax.scan(
        backward_block, (zero_key_value, zero_key_value), (block_starts, logsum)
    )
    grad_query = apply_rotation(
        grad_query.reshape(count_of_rows, QUERY_HEADS, HEAD_SIZE), token_position, -1.0
    )
    key_gradient = apply_rotation(acc_key, token_position, -1.0)
    grad_projected = jnp.concatenate(
        [
            grad_query.reshape(count_of_rows, QUERY_HEADS * HEAD_SIZE),
            key_gradient.reshape(count_of_rows, KEY_VALUE_HEADS * HEAD_SIZE),
            value_accumulator.reshape(count_of_rows, KEY_VALUE_HEADS * HEAD_SIZE),
        ],
        axis=1,
    ).astype(jnp.bfloat16)
    term_qkv = jnp.dot(normed_attn.T, grad_projected, preferred_element_type=jnp.float32)
    grad_normed_attn = jnp.dot(grad_projected, full_qkv.T, preferred_element_type=jnp.float32)
    grad_resid_norm, term_gain_first = norm_back(residual, inv_first, gain_first, grad_normed_attn)
    grad_tokens = (grad_middle + grad_resid_norm).astype(jnp.bfloat16)
    inverse = (
        jnp.zeros((count_of_rows,), jnp.int32)
        .at[deal_rows]
        .set(jnp.arange(count_of_rows, dtype=jnp.int32))
    )
    layer_out, input_gradient = (
        lax.all_to_all(
            final_rows.astype(jnp.bfloat16)[inverse], "dp", split_axis=0, concat_axis=0, tiled=True
        ),
        lax.all_to_all(grad_tokens[inverse], "dp", split_axis=0, concat_axis=0, tiled=True),
    )
    shard_terms = (
        lax.psum_scatter(
            term_gain_first.astype(jnp.bfloat16), "shard", scatter_dimension=0, tiled=True
        ).astype(jnp.float32),
        lax.psum_scatter(
            term_gain_second.astype(jnp.bfloat16), "shard", scatter_dimension=0, tiled=True
        ).astype(jnp.float32),
        lax.psum_scatter(
            term_qkv.astype(jnp.bfloat16), "shard", scatter_dimension=0, tiled=True
        ).astype(jnp.float32),
        lax.psum_scatter(
            term_out.astype(jnp.bfloat16), "shard", scatter_dimension=0, tiled=True
        ).astype(jnp.float32),
        lax.psum_scatter(
            term_router.astype(jnp.bfloat16), "shard", scatter_dimension=0, tiled=True
        ).astype(jnp.float32),
    )
    gain_first_grad, gain_second_grad, qkv_grad, out_grad, router_grad = lax.psum(
        (shard_terms[0], shard_terms[1], shard_terms[2], shard_terms[3], shard_terms[4]),
        ("dp", "expert"),
    )
    gate_up_grad, down_grad = (
        lax.psum_scatter(
            term_gate_up[None].astype(jnp.bfloat16),
            ("dp", "shard"),
            scatter_dimension=1,
            tiled=True,
        ).astype(jnp.float32),
        lax.psum_scatter(
            term_down[None].astype(jnp.bfloat16), ("dp", "shard"), scatter_dimension=1, tiled=True
        ).astype(jnp.float32),
    )
    return (
        layer_out,
        input_gradient,
        gain_first_grad,
        gain_second_grad,
        qkv_grad,
        out_grad,
        router_grad,
        gate_up_grad,
        down_grad,
    )


RING_NEXT = (1, 3, 0, 2)


def other_core(field):
    return lax.ppermute(field, "shard", [(0, 1), (1, 0)])


def other_dp(field):
    return lax.ppermute(field, "dp", [(0, 1), (1, 0)])


def across_x(field):
    return lax.ppermute(field, "expert", [(i, i ^ 1) for i in range(8)])


def across_dp_x(field):
    pairs = [(d * 8 + e, (1 - d) * 8 + (e ^ 1)) for d in range(2) for e in range(8)]
    return lax.ppermute(field, ("dp", "expert"), pairs)


def across_z(field, distance):
    return lax.ppermute(field, "expert", [(i, i ^ (2 * distance)) for i in range(8)])


def ring_z(field):
    pairs = [(2 * z + x, 2 * RING_NEXT[z] + x) for z in range(4) for x in range(2)]
    return lax.ppermute(field, "expert", pairs)


def to_owner(field):
    pairs = [(e * 2 + c, (e ^ 1) * 2 + c) for e in range(8) for c in range(2) if e % 2 != c]
    return lax.ppermute(field, ("expert", "shard"), pairs)


def from_owner(field):
    pairs = [(e * 2 + c, (e ^ 1) * 2 + c) for e in range(8) for c in range(2) if e % 2 == c]
    return lax.ppermute(field, ("expert", "shard"), pairs)


def in_order(first, own, received):
    return jnp.where(
        first, jnp.concatenate([own, received], axis=0), jnp.concatenate([received, own], axis=0)
    )


def block(field, index, count):
    rows = field.shape[0] // count
    return lax.dynamic_slice_in_dim(field, index * rows, rows, axis=0)


def sum_blocks(*fields):
    total = fields[0].astype(jnp.float32)
    for field in fields[1:]:
        total = total + field.astype(jnp.float32)
    return total


def reduce_weight(term, place):
    dp, x, z, core = place
    mine, theirs = block(term, core, 2), block(term, 1 - core, 2)
    part = sum_blocks(mine, other_core(theirs)).astype(jnp.bfloat16)
    own = 2 * dp + x
    part = sum_blocks(
        block(part, own, 4),
        other_dp(block(part, own ^ 2, 4)),
        across_x(block(part, own ^ 1, 4)),
        across_dp_x(block(part, own ^ 3, 4)),
    ).astype(jnp.bfloat16)
    part = sum_blocks(
        block(part, z, 4), *[across_z(block(part, z ^ k, 4), k) for k in (1, 2, 3)]
    ).astype(jnp.bfloat16)
    pieces = jnp.stack([part] + [across_z(part, k) for k in (1, 2, 3)])
    part = jnp.concatenate([lax.dynamic_index_in_dim(pieces, z ^ b, 0, False) for b in range(4)])
    pieces = jnp.stack([part, across_x(part), other_dp(part), across_dp_x(part)])
    whole = jnp.concatenate(
        [lax.dynamic_index_in_dim(pieces, own ^ b, 0, False) for b in range(4)]
    )
    return whole.astype(jnp.float32)


def reduce_small(term):
    part = term + other_core(term)
    part = part + other_dp(part) + across_x(part) + across_dp_x(part)
    return part + across_z(part, 1) + across_z(part, 2) + across_z(part, 3)


def reduce_expert(term, place):
    dp, x, _, core = place
    half = term.shape[1] // 2
    first, second = term[:, :half].astype(jnp.bfloat16), term[:, half:].astype(jnp.bfloat16)
    first = sum_blocks(first, to_owner(first)).astype(jnp.bfloat16)
    first = sum_blocks(block(first, dp, 2), other_dp(block(first, 1 - dp, 2)))
    second = sum_blocks(block(second, dp, 2), other_dp(block(second, 1 - dp, 2)))
    second = second.astype(jnp.bfloat16)
    second = sum_blocks(second, to_owner(second))
    both = jnp.concatenate([first, second], axis=1).astype(jnp.bfloat16)
    mine, theirs = block(both, core, 2), block(both, 1 - core, 2)
    return jnp.where(core == x, mine, other_core(theirs)).astype(jnp.float32)


def expert_block(rows, upstream, weighting, up_matrix, down_matrix):
    gate_up = jnp.dot(rows, up_matrix, preferred_element_type=jnp.float32)
    hidden = activate(gate_up).astype(jnp.bfloat16)
    out = jnp.dot(hidden, down_matrix, preferred_element_type=jnp.float32).astype(jnp.bfloat16)
    out = out.astype(jnp.float32)
    ct = upstream.astype(jnp.float32)
    weighted = (weighting * out).astype(jnp.bfloat16)
    grad_out = (weighting * ct).astype(jnp.bfloat16)
    grad_gate = jnp.sum(ct * out, axis=1)
    grad_hidden = jnp.dot(grad_out, down_matrix.T, preferred_element_type=jnp.float32)
    grad_gate_up = jax.vjp(activate, gate_up)[1](grad_hidden)[0].astype(jnp.bfloat16)
    grad_rows = jnp.dot(grad_gate_up, up_matrix.T, preferred_element_type=jnp.float32)
    return hidden, weighted, grad_out, grad_gate, grad_gate_up, grad_rows.astype(jnp.bfloat16)


def ring_shards(
    hidden_in,
    cotangent,
    deal_order,
    lengths,
    routes,
    attention_gain,
    expert_gain,
    qkv_weight,
    out_weight,
    router_weight,
    gate_up_weight,
    down_weight,
):
    count_of_rows = hidden_in.shape[0]
    model_width = hidden_in.shape[1]
    half_rows = count_of_rows // 2
    head_groups = QUERY_HEADS // KEY_VALUE_HEADS
    expert_count = router_weight.shape[1]
    dp, core, at = lax.axis_index("dp"), lax.axis_index("shard"), lax.axis_index("expert")
    x, z = at % 2, at // 2
    place = (dp, x, z, core)
    expert_ids = jnp.arange(expert_count, dtype=jnp.int32)

    def from_dealt(field):
        return jnp.concatenate([block(field, dp, 2), other_dp(block(field, 1 - dp, 2))], axis=0)

    def to_dealt(field):
        return in_order(dp == 0, field[:half_rows], other_dp(field[half_rows:]))

    deal_rows = deal_order[0]
    held_at = jnp.where(deal_rows // half_rows == dp, 0, half_rows) + deal_rows % half_rows
    deal = (held_at[:, None] == jnp.arange(count_of_rows, dtype=jnp.int32)[None, :]).astype(
        jnp.bfloat16
    )

    def permute(matrix, field):
        return jnp.dot(matrix, field, preferred_element_type=jnp.float32).astype(jnp.bfloat16)

    tokens = permute(deal, from_dealt(hidden_in))
    upstream_low = permute(deal, from_dealt(cotangent))
    small = jnp.concatenate([attention_gain[None], expert_gain[None], router_weight.T], axis=0)
    small_other = other_core(small)
    small = jnp.where(
        core == 0,
        jnp.concatenate([small, small_other], axis=1),
        jnp.concatenate([small_other, small], axis=1),
    )
    gain_first, gain_second = small[0].astype(jnp.float32), small[1].astype(jnp.float32)
    full_router = small[2:].T
    full_qkv = in_order(core == 0, qkv_weight, other_core(qkv_weight))
    full_out = in_order(core == 0, out_weight, other_core(out_weight))
    up_matrix = jnp.where(core == x, gate_up_weight[0], from_owner(gate_up_weight[0]))
    down_matrix = jnp.where(core == x, down_weight[0], from_owner(down_weight[0]))
    upstream_ring = [upstream_low]
    for _ in range(3):
        upstream_ring.append(ring_z(upstream_ring[-1]))
    upstream_units = [jnp.concatenate([unit, other_core(unit)]) for unit in upstream_ring]

    upstream = upstream_low.astype(jnp.float32)
    residual = tokens.astype(jnp.float32)
    inv_first = lax.rsqrt(jnp.mean(residual * residual, axis=1, keepdims=True) + EPS)
    normed_attn = (residual * inv_first * gain_first).astype(jnp.bfloat16)
    projected_rows = jnp.dot(normed_attn, full_qkv, preferred_element_type=jnp.float32)
    segment, token_position = positions_of(lengths[0], count_of_rows)
    query_matrix_rows = (
        apply_rotation(
            projected_rows[:, : QUERY_HEADS * HEAD_SIZE].reshape(
                count_of_rows, QUERY_HEADS, HEAD_SIZE
            ),
            token_position,
            1.0,
        )
        .astype(jnp.bfloat16)
        .reshape(count_of_rows, KEY_VALUE_HEADS, head_groups, HEAD_SIZE)
    )
    key_matrix_rows = apply_rotation(
        projected_rows[
            :, QUERY_HEADS * HEAD_SIZE : (QUERY_HEADS + KEY_VALUE_HEADS) * HEAD_SIZE
        ].reshape(count_of_rows, KEY_VALUE_HEADS, HEAD_SIZE),
        token_position,
        1.0,
    ).astype(jnp.bfloat16)
    value_matrix_rows = (
        projected_rows[:, (QUERY_HEADS + KEY_VALUE_HEADS) * HEAD_SIZE :]
        .reshape(count_of_rows, KEY_VALUE_HEADS, HEAD_SIZE)
        .astype(jnp.bfloat16)
    )
    scores = masked_scores(query_matrix_rows, key_matrix_rows, segment, segment, 0)
    row_max = jnp.max(scores, axis=-1, keepdims=True)
    exp_scores = jnp.exp(scores - row_max)
    exp_total = jnp.sum(exp_scores, axis=-1, keepdims=True)
    soft_probs = (exp_scores / exp_total).astype(jnp.bfloat16)
    attn_mix = (
        jnp.einsum(
            "hgij,jhd->ihgd", soft_probs, value_matrix_rows, preferred_element_type=jnp.float32
        )
        .reshape(count_of_rows, QUERY_HEADS * HEAD_SIZE)
        .astype(jnp.bfloat16)
    )
    logsum = (row_max + jnp.log(exp_total))[..., 0]
    middle = residual + jnp.dot(attn_mix, full_out, preferred_element_type=jnp.float32)
    inv_second = lax.rsqrt(jnp.mean(middle * middle, axis=1, keepdims=True) + EPS)
    normed_moe = (middle * inv_second * gain_second).astype(jnp.bfloat16)
    logits = jnp.dot(normed_moe, full_router, preferred_element_type=jnp.float32)
    named = jnp.any(routes[:, :, None] == expert_ids[None, None, :], axis=1)
    top_logit = jnp.max(jnp.where(named, logits, -jnp.inf), axis=1, keepdims=True)
    exp_logits = jnp.where(named, jnp.exp(jnp.where(named, logits - top_logit, 0.0)), 0.0)
    gates = exp_logits / jnp.sum(exp_logits, axis=1, keepdims=True)

    own_expert = 2 * z + core
    own_row = (expert_ids == own_expert)[:, None]
    normed_ring, gates_ring = [normed_moe], [gates.T]
    for _ in range(3):
        normed_ring.append(ring_z(normed_ring[-1]))
        gates_ring.append(ring_z(gates_ring[-1]))
    steps = []
    arrived_grad = arrived_gate = None
    for step in (1, 2, 3, 0):
        rows = jnp.concatenate([normed_ring[step], other_core(normed_ring[step])])
        all_gates = jnp.concatenate([gates_ring[step], other_core(gates_ring[step])], axis=1)
        weighting = jnp.sum(jnp.where(own_row, all_gates, 0.0), axis=0)[:, None]
        hidden, weighted, grad_out, grad_gate, grad_gate_up, grad_rows = expert_block(
            rows, upstream_units[step], weighting, up_matrix, down_matrix
        )
        steps.append((rows, hidden, grad_out, grad_gate_up, weighted))
        gate_rows = jnp.where(own_row, grad_gate[None, :], 0.0)
        unit_grad = sum_blocks(grad_rows[:count_of_rows], other_core(grad_rows[count_of_rows:]))
        unit_gate = gate_rows[:, :count_of_rows] + other_core(gate_rows[:, count_of_rows:])
        if arrived_grad is not None:
            unit_grad = unit_grad + arrived_grad.astype(jnp.float32)
            unit_gate = unit_gate + arrived_gate
        if step:
            arrived_grad = ring_z(unit_grad.astype(jnp.bfloat16))
            arrived_gate = ring_z(unit_gate)
    grad_normed, grad_gates = unit_grad, unit_gate.T
    all_rows, all_hidden, all_grad_out, all_grad_gate_up, _ = [
        jnp.concatenate(list(fields)) for fields in zip(*steps)
    ]
    term_down = jnp.dot(all_hidden.T, all_grad_out, preferred_element_type=jnp.float32)
    term_gate_up = jnp.dot(all_rows.T, all_grad_gate_up, preferred_element_type=jnp.float32)
    gate_up_grad = reduce_expert(term_gate_up, place)[None]
    down_grad = reduce_expert(term_down, place)[None]

    mean_term = jnp.sum(gates * grad_gates, axis=1, keepdims=True)
    grad_logits = (gates * (grad_gates - mean_term)).astype(jnp.bfloat16)
    term_router = jnp.dot(normed_moe.T, grad_logits, preferred_element_type=jnp.float32)
    grad_normed = grad_normed + jnp.dot(
        grad_logits, full_router.T, preferred_element_type=jnp.float32
    )
    grad_middle_norm, term_gain_second = norm_back(middle, inv_second, gain_second, grad_normed)
    grad_middle = upstream + grad_middle_norm
    grad_attn_out = grad_middle.astype(jnp.bfloat16)

    arrived = None
    for step in (0, 1, 2, 3):
        weighted = steps[step][4]
        unit = sum_blocks(weighted[:count_of_rows], other_core(weighted[count_of_rows:]))
        if arrived is not None:
            unit = unit + arrived.astype(jnp.float32)
        if step < 3:
            arrived = ring_z(unit.astype(jnp.bfloat16))
    final_rows = (middle + unit).astype(jnp.bfloat16)
    layer_out = to_dealt(permute(deal.T, final_rows))

    term_out = jnp.dot(attn_mix.T, grad_attn_out, preferred_element_type=jnp.float32)
    out_grad = reduce_weight(term_out.astype(jnp.bfloat16), place)
    grad_mix = (
        jnp.dot(grad_attn_out, full_out.T, preferred_element_type=jnp.float32)
        .astype(jnp.bfloat16)
        .reshape(count_of_rows, KEY_VALUE_HEADS, head_groups, HEAD_SIZE)
    )
    scores = masked_scores(query_matrix_rows, key_matrix_rows, segment, segment, 0)
    soft_probs = jnp.exp(scores - logsum[..., None])
    grad_probs = jnp.einsum(
        "ihgd,jhd->hgij", grad_mix, value_matrix_rows, preferred_element_type=jnp.float32
    )
    grad_value = jnp.einsum(
        "hgij,ihgd->jhd",
        soft_probs.astype(jnp.bfloat16),
        grad_mix,
        preferred_element_type=jnp.float32,
    )
    grad_scores = (
        soft_probs * (grad_probs - jnp.sum(soft_probs * grad_probs, axis=-1, keepdims=True))
    ).astype(jnp.bfloat16)
    grad_query = HEAD_SIZE ** (-0.5) * jnp.einsum(
        "hgij,jhd->ihgd", grad_scores, key_matrix_rows, preferred_element_type=jnp.float32
    )
    grad_key = HEAD_SIZE ** (-0.5) * jnp.einsum(
        "hgij,ihgd->jhd", grad_scores, query_matrix_rows, preferred_element_type=jnp.float32
    )
    grad_query = apply_rotation(
        grad_query.reshape(count_of_rows, QUERY_HEADS, HEAD_SIZE), token_position, -1.0
    )
    grad_key = apply_rotation(grad_key, token_position, -1.0)
    grad_projected = jnp.concatenate(
        [
            grad_query.reshape(count_of_rows, QUERY_HEADS * HEAD_SIZE),
            grad_key.reshape(count_of_rows, KEY_VALUE_HEADS * HEAD_SIZE),
            grad_value.reshape(count_of_rows, KEY_VALUE_HEADS * HEAD_SIZE),
        ],
        axis=1,
    ).astype(jnp.bfloat16)
    term_qkv = jnp.dot(normed_attn.T, grad_projected, preferred_element_type=jnp.float32)
    qkv_grad = reduce_weight(term_qkv.astype(jnp.bfloat16), place)
    grad_normed_attn = jnp.dot(grad_projected, full_qkv.T, preferred_element_type=jnp.float32)
    grad_resid_norm, term_gain_first = norm_back(residual, inv_first, gain_first, grad_normed_attn)
    grad_tokens = (grad_middle + grad_resid_norm).astype(jnp.bfloat16)
    input_gradient = to_dealt(permute(deal.T, grad_tokens))
    small_grad = reduce_small(
        jnp.concatenate([term_gain_first[None], term_gain_second[None], term_router.T], axis=0)
    )
    small_grad = lax.dynamic_slice_in_dim(
        small_grad, core * (model_width // 2), model_width // 2, axis=1
    )
    return (
        layer_out,
        input_gradient,
        small_grad[0],
        small_grad[1],
        qkv_grad,
        out_grad,
        small_grad[2:].T,
        gate_up_grad,
        down_grad,
    )


def solution(mesh):
    ringed = (mesh.shape["dp"], mesh.shape["expert"], mesh.shape["shard"]) == (2, 8, 2)
    shards = ring_shards if ringed else routed_shards
    return jax.shard_map(
        shards,
        mesh=mesh,
        in_specs=(
            P(("dp", "expert", "shard"), None),
            P(("dp", "expert", "shard"), None),
            P(("dp", "expert", "shard"), None),
            P(("dp", "expert", "shard"), None),
            P(("dp", "expert", "shard"), None),
            P("shard"),
            P("shard"),
            P("shard", None),
            P("shard", None),
            P("shard", None),
            P("expert", None, None),
            P("expert", None, None),
        ),
        out_specs=(
            P(("dp", "expert", "shard"), None),
            P(("dp", "expert", "shard"), None),
            P("shard"),
            P("shard"),
            P("shard", None),
            P("shard", None),
            P("shard", None),
            P("expert", ("dp", "shard"), None),
            P("expert", ("dp", "shard"), None),
        ),
        check_vma=False,
    )
```

```python
import functools

import jax
import jax.numpy as jnp
from jax import lax
from jax.experimental import pallas as pl
from jax.experimental.pallas import tpu as pltpu
from jax.sharding import PartitionSpec as P

QUERY_HEADS = 12
KEY_VALUE_HEADS = 2
HEAD_SIZE = 128
TOP = 4


EPS = 1e-06
THETA = 1000000.0


def positions_of(lengths_dev, count_of_rows):
    seq_ends = jnp.cumsum(lengths_dev)
    starts = seq_ends - lengths_dev
    places = jnp.arange(count_of_rows, dtype=jnp.int32)
    segment = jnp.sum((places[:, None] >= seq_ends[None, :]).astype(jnp.int32), axis=1)
    member = segment[:, None] == jnp.arange(lengths_dev.shape[0], dtype=jnp.int32)[None, :]
    start_of = jnp.sum(jnp.where(member, starts[None, :], 0), axis=1)
    return (segment, places - start_of)


def apply_rotation(field, token_position, direction):
    half_dim = field.shape[-1] // 2
    frequency = THETA ** (-jnp.arange(half_dim, dtype=jnp.float32) / half_dim)
    angles = token_position.astype(jnp.float32)[:, None] * frequency[None, :]
    cosine = jnp.cos(angles)[:, None, :]
    sine_term = direction * jnp.sin(angles)[:, None, :]
    lead_part = field[..., :half_dim]
    tail_part = field[..., half_dim:]
    return jnp.concatenate(
        [lead_part * cosine - tail_part * sine_term, tail_part * cosine + lead_part * sine_term],
        axis=-1,
    )


def masked_scores(query_block, key_matrix_rows, segment_block, segment, row_start):
    raw_scores = jnp.einsum(
        "ihgd,jhd->hgij", query_block, key_matrix_rows, preferred_element_type=jnp.float32
    ) * HEAD_SIZE ** (-0.5)
    query_at = row_start + jnp.arange(query_block.shape[0], dtype=jnp.int32)
    key_at = jnp.arange(key_matrix_rows.shape[0], dtype=jnp.int32)
    allowed = (segment_block[:, None] == segment[None, :]) & (key_at[None, :] <= query_at[:, None])
    return jnp.where(allowed, raw_scores, -1e30)


def norm_back(field, inv_scale, gain_vec, grad_normed):
    scaled = grad_normed * gain_vec
    grad_field = inv_scale * scaled - field * inv_scale**3 * jnp.mean(
        scaled * field, axis=1, keepdims=True
    )
    grad_gain = jnp.sum(field * inv_scale * grad_normed, axis=0)
    return (grad_field, grad_gain)


def activate(gate_up):
    hidden_width = gate_up.shape[1] // 2
    return jax.nn.gelu(gate_up[:, :hidden_width], approximate=True) * gate_up[:, hidden_width:]


def routed_shards(
    hidden_in,
    cotangent,
    deal_order,
    lengths,
    routes,
    attention_gain,
    expert_gain,
    qkv_weight,
    out_weight,
    router_weight,
    gate_up_weight,
    down_weight,
):
    count_of_rows = hidden_in.shape[0]
    model_width = hidden_in.shape[1]
    head_groups = QUERY_HEADS // KEY_VALUE_HEADS
    arrived_in, arrived_ct = (
        lax.all_to_all(hidden_in, "dp", split_axis=0, concat_axis=0, tiled=True),
        lax.all_to_all(cotangent, "dp", split_axis=0, concat_axis=0, tiled=True),
    )
    deal_rows = deal_order[0]
    tokens = arrived_in[deal_rows]
    upstream = arrived_ct[deal_rows].astype(jnp.float32)
    gain_first, gain_second, full_qkv, full_out, full_router = (
        lax.all_gather(attention_gain, "shard", axis=0, tiled=True),
        lax.all_gather(expert_gain, "shard", axis=0, tiled=True),
        lax.all_gather(qkv_weight, "shard", axis=0, tiled=True),
        lax.all_gather(out_weight, "shard", axis=0, tiled=True),
        lax.all_gather(router_weight, "shard", axis=0, tiled=True),
    )
    gain_first = gain_first.astype(jnp.float32)
    gain_second = gain_second.astype(jnp.float32)
    residual = tokens.astype(jnp.float32)
    inv_first = lax.rsqrt(jnp.mean(residual * residual, axis=1, keepdims=True) + EPS)
    normed_attn = (residual * inv_first * gain_first).astype(jnp.bfloat16)
    projected_rows = jnp.dot(normed_attn, full_qkv, preferred_element_type=jnp.float32)
    segment, token_position = positions_of(lengths[0], count_of_rows)
    query_matrix_rows = (
        apply_rotation(
            projected_rows[:, : QUERY_HEADS * HEAD_SIZE].reshape(
                count_of_rows, QUERY_HEADS, HEAD_SIZE
            ),
            token_position,
            1.0,
        )
        .astype(jnp.bfloat16)
        .reshape(count_of_rows, KEY_VALUE_HEADS, head_groups, HEAD_SIZE)
    )
    key_matrix_rows = apply_rotation(
        projected_rows[
            :, QUERY_HEADS * HEAD_SIZE : (QUERY_HEADS + KEY_VALUE_HEADS) * HEAD_SIZE
        ].reshape(count_of_rows, KEY_VALUE_HEADS, HEAD_SIZE),
        token_position,
        1.0,
    ).astype(jnp.bfloat16)
    value_matrix_rows = (
        projected_rows[:, (QUERY_HEADS + KEY_VALUE_HEADS) * HEAD_SIZE :]
        .reshape(count_of_rows, KEY_VALUE_HEADS, HEAD_SIZE)
        .astype(jnp.bfloat16)
    )
    block_rows = min(count_of_rows, 512)
    block_starts = jnp.arange(count_of_rows // block_rows, dtype=jnp.int32) * block_rows

    def forward_block(row_start):
        scores = masked_scores(query_matrix_rows, key_matrix_rows, segment, segment, row_start)
        row_max = jnp.max(scores, axis=-1, keepdims=True)
        exp_scores = jnp.exp(scores - row_max)
        exp_total = jnp.sum(exp_scores, axis=-1, keepdims=True)
        soft_probs = (exp_scores / exp_total).astype(jnp.bfloat16)
        mix_block = jnp.einsum(
            "hgij,jhd->ihgd", soft_probs, value_matrix_rows, preferred_element_type=jnp.float32
        )
        return (mix_block, (row_max + jnp.log(exp_total))[..., 0])

    mix_blocks, logsum = lax.map(forward_block, block_starts)
    attn_mix = mix_blocks.reshape(count_of_rows, QUERY_HEADS * HEAD_SIZE).astype(jnp.bfloat16)
    middle = residual + jnp.dot(attn_mix, full_out, preferred_element_type=jnp.float32)
    inv_second = lax.rsqrt(jnp.mean(middle * middle, axis=1, keepdims=True) + EPS)
    normed_moe = (middle * inv_second * gain_second).astype(jnp.bfloat16)
    logits = jnp.dot(normed_moe, full_router, preferred_element_type=jnp.float32)
    gate_probs = jax.nn.softmax(jnp.take_along_axis(logits, routes, axis=1), axis=-1)
    expert_count = full_router.shape[1]
    peer_count = lax.axis_size("expert")
    capacity = min(count_of_rows, max(2, 3 * count_of_rows * TOP // (2 * expert_count)))
    flat_routes = routes.reshape(-1)
    expert_ids = jnp.arange(expert_count, dtype=jnp.int32)
    onehot = (flat_routes[:, None] == expert_ids[None, :]).astype(jnp.int32)
    slot_rank = jnp.sum(jnp.cumsum(onehot, axis=0) * onehot, axis=1) - 1
    target = flat_routes * capacity + slot_rank
    pair_count = count_of_rows * TOP
    slot_pair = (
        jnp.full((expert_count * capacity,), pair_count, jnp.int32)
        .at[target]
        .set(jnp.arange(pair_count, dtype=jnp.int32))
    )
    padded = jnp.concatenate([normed_moe, jnp.zeros((1, model_width), jnp.bfloat16)], axis=0)
    sending = padded[slot_pair // TOP].reshape(peer_count, capacity, model_width)
    received = lax.all_to_all(sending, "expert", split_axis=0, concat_axis=0, tiled=True)
    rows_in = received.reshape(peer_count * capacity, model_width)
    gate_up = jnp.dot(rows_in, gate_up_weight[0], preferred_element_type=jnp.float32)
    hidden_rows = activate(gate_up).astype(jnp.bfloat16)
    expert_out = jnp.dot(hidden_rows, down_weight[0], preferred_element_type=jnp.float32).astype(
        jnp.bfloat16
    )
    returned = lax.all_to_all(
        expert_out.reshape(peer_count, capacity, model_width),
        "expert",
        split_axis=0,
        concat_axis=0,
        tiled=True,
    )
    per_pair = returned.reshape(peer_count * capacity, model_width)[target].reshape(
        count_of_rows, TOP, model_width
    )
    expert_sum = jnp.zeros((count_of_rows, model_width), jnp.float32)
    for choice_slot in range(TOP):
        expert_sum = expert_sum + gate_probs[:, choice_slot : choice_slot + 1] * per_pair[
            :, choice_slot
        ].astype(jnp.float32)
    final_rows = middle + expert_sum
    grad_pairs = (gate_probs[:, :, None] * upstream[:, None, :]).astype(jnp.bfloat16)
    grad_gates = jnp.stack(
        [
            jnp.sum(per_pair[:, choice_slot].astype(jnp.float32) * upstream, axis=1)
            for choice_slot in range(TOP)
        ],
        axis=1,
    )
    padded_grad = jnp.concatenate(
        [grad_pairs.reshape(pair_count, model_width), jnp.zeros((1, model_width), jnp.bfloat16)],
        axis=0,
    )
    sending_back = padded_grad[slot_pair].reshape(peer_count, capacity, model_width)
    grad_rows = lax.all_to_all(
        sending_back, "expert", split_axis=0, concat_axis=0, tiled=True
    ).reshape(peer_count * capacity, model_width)
    grad_hidden = jnp.dot(grad_rows, down_weight[0].T, preferred_element_type=jnp.float32)
    grad_gate_up = jax.vjp(activate, gate_up)[1](grad_hidden)[0].astype(jnp.bfloat16)
    term_down = jnp.dot(hidden_rows.T, grad_rows, preferred_element_type=jnp.float32)
    term_gate_up = jnp.dot(rows_in.T, grad_gate_up, preferred_element_type=jnp.float32)
    grad_rows_in = jnp.dot(
        grad_gate_up, gate_up_weight[0].T, preferred_element_type=jnp.float32
    ).astype(jnp.bfloat16)
    back_rows = lax.all_to_all(
        grad_rows_in.reshape(peer_count, capacity, model_width),
        "expert",
        split_axis=0,
        concat_axis=0,
        tiled=True,
    )
    back_pairs = back_rows.reshape(peer_count * capacity, model_width)[target].reshape(
        count_of_rows, TOP, model_width
    )
    grad_normed = jnp.zeros((count_of_rows, model_width), jnp.float32)
    for choice_slot in range(TOP):
        grad_normed = grad_normed + back_pairs[:, choice_slot].astype(jnp.float32)
    mean_term = jnp.sum(gate_probs * grad_gates, axis=1, keepdims=True)
    grad_chosen = gate_probs * (grad_gates - mean_term)
    grad_logits = jnp.sum(
        jnp.where(routes[:, :, None] == expert_ids[None, None, :], grad_chosen[:, :, None], 0.0),
        axis=1,
    ).astype(jnp.bfloat16)
    term_router = jnp.dot(normed_moe.T, grad_logits, preferred_element_type=jnp.float32)
    grad_normed = grad_normed + jnp.dot(
        grad_logits, full_router.T, preferred_element_type=jnp.float32
    )
    grad_middle_norm, term_gain_second = norm_back(middle, inv_second, gain_second, grad_normed)
    grad_middle = upstream + grad_middle_norm
    grad_attn_out = grad_middle.astype(jnp.bfloat16)
    term_out = jnp.dot(attn_mix.T, grad_attn_out, preferred_element_type=jnp.float32)
    grad_mix = (
        jnp.dot(grad_attn_out, full_out.T, preferred_element_type=jnp.float32)
        .astype(jnp.bfloat16)
        .reshape(count_of_rows, KEY_VALUE_HEADS, head_groups, HEAD_SIZE)
    )

    def backward_block(accums, inputs):
        acc_key, value_accumulator = accums
        row_start, logsum_block = inputs
        scores = masked_scores(query_matrix_rows, key_matrix_rows, segment, segment, row_start)
        soft_probs = jnp.exp(scores - logsum_block[..., None])
        grad_probs = jnp.einsum(
            "ihgd,jhd->hgij", grad_mix, value_matrix_rows, preferred_element_type=jnp.float32
        )
        value_accumulator = value_accumulator + jnp.einsum(
            "hgij,ihgd->jhd",
            soft_probs.astype(jnp.bfloat16),
            grad_mix,
            preferred_element_type=jnp.float32,
        )
        grad_scores = (
            soft_probs * (grad_probs - jnp.sum(soft_probs * grad_probs, axis=-1, keepdims=True))
        ).astype(jnp.bfloat16)
        grad_query = HEAD_SIZE ** (-0.5) * jnp.einsum(
            "hgij,jhd->ihgd", grad_scores, key_matrix_rows, preferred_element_type=jnp.float32
        )
        acc_key = acc_key + HEAD_SIZE ** (-0.5) * jnp.einsum(
            "hgij,ihgd->jhd", grad_scores, query_matrix_rows, preferred_element_type=jnp.float32
        )
        return ((acc_key, value_accumulator), grad_query)

    zero_key_value = jnp.zeros((count_of_rows, KEY_VALUE_HEADS, HEAD_SIZE), jnp.float32)
    (acc_key, value_accumulator), grad_query = lax.scan(
        backward_block, (zero_key_value, zero_key_value), (block_starts, logsum)
    )
    grad_query = apply_rotation(
        grad_query.reshape(count_of_rows, QUERY_HEADS, HEAD_SIZE), token_position, -1.0
    )
    key_gradient = apply_rotation(acc_key, token_position, -1.0)
    grad_projected = jnp.concatenate(
        [
            grad_query.reshape(count_of_rows, QUERY_HEADS * HEAD_SIZE),
            key_gradient.reshape(count_of_rows, KEY_VALUE_HEADS * HEAD_SIZE),
            value_accumulator.reshape(count_of_rows, KEY_VALUE_HEADS * HEAD_SIZE),
        ],
        axis=1,
    ).astype(jnp.bfloat16)
    term_qkv = jnp.dot(normed_attn.T, grad_projected, preferred_element_type=jnp.float32)
    grad_normed_attn = jnp.dot(grad_projected, full_qkv.T, preferred_element_type=jnp.float32)
    grad_resid_norm, term_gain_first = norm_back(residual, inv_first, gain_first, grad_normed_attn)
    grad_tokens = (grad_middle + grad_resid_norm).astype(jnp.bfloat16)
    inverse = (
        jnp.zeros((count_of_rows,), jnp.int32)
        .at[deal_rows]
        .set(jnp.arange(count_of_rows, dtype=jnp.int32))
    )
    layer_out, input_gradient = (
        lax.all_to_all(
            final_rows.astype(jnp.bfloat16)[inverse], "dp", split_axis=0, concat_axis=0, tiled=True
        ),
        lax.all_to_all(grad_tokens[inverse], "dp", split_axis=0, concat_axis=0, tiled=True),
    )
    shard_terms = (
        lax.psum_scatter(
            term_gain_first.astype(jnp.bfloat16), "shard", scatter_dimension=0, tiled=True
        ).astype(jnp.float32),
        lax.psum_scatter(
            term_gain_second.astype(jnp.bfloat16), "shard", scatter_dimension=0, tiled=True
        ).astype(jnp.float32),
        lax.psum_scatter(
            term_qkv.astype(jnp.bfloat16), "shard", scatter_dimension=0, tiled=True
        ).astype(jnp.float32),
        lax.psum_scatter(
            term_out.astype(jnp.bfloat16), "shard", scatter_dimension=0, tiled=True
        ).astype(jnp.float32),
        lax.psum_scatter(
            term_router.astype(jnp.bfloat16), "shard", scatter_dimension=0, tiled=True
        ).astype(jnp.float32),
    )
    gain_first_grad, gain_second_grad, qkv_grad, out_grad, router_grad = lax.psum(
        (shard_terms[0], shard_terms[1], shard_terms[2], shard_terms[3], shard_terms[4]),
        ("dp", "expert"),
    )
    gate_up_grad, down_grad = (
        lax.psum_scatter(
            term_gate_up[None].astype(jnp.bfloat16),
            ("dp", "shard"),
            scatter_dimension=1,
            tiled=True,
        ).astype(jnp.float32),
        lax.psum_scatter(
            term_down[None].astype(jnp.bfloat16), ("dp", "shard"), scatter_dimension=1, tiled=True
        ).astype(jnp.float32),
    )
    return (
        layer_out,
        input_gradient,
        gain_first_grad,
        gain_second_grad,
        qkv_grad,
        out_grad,
        router_grad,
        gate_up_grad,
        down_grad,
    )


RING_NEXT = (1, 3, 0, 2)
LAST_WITH_LAST = (((1,), (1,)), ((), ()))


def after(value, *earlier):
    return lax.optimization_barrier((value, *earlier))[0]


def part(*fields):
    return lax.optimization_barrier(fields)


def other_core(field):
    return lax.ppermute(field, "shard", [(0, 1), (1, 0)])


def other_dp(field):
    return lax.ppermute(field, "dp", [(0, 1), (1, 0)])


def across_x(field):
    return lax.ppermute(field, "expert", [(i, i ^ 1) for i in range(8)])


def across_dp_x(field):
    pairs = [(d * 8 + e, (1 - d) * 8 + (e ^ 1)) for d in range(2) for e in range(8)]
    return lax.ppermute(field, ("dp", "expert"), pairs)


def across_z(field, distance):
    return lax.ppermute(field, "expert", [(i, i ^ (2 * distance)) for i in range(8)])


def ring_z(field):
    pairs = [(2 * z + x, 2 * RING_NEXT[z] + x) for z in range(4) for x in range(2)]
    return lax.ppermute(field, "expert", pairs)


def to_owner(field):
    pairs = [(e * 2 + c, (e ^ 1) * 2 + c) for e in range(8) for c in range(2) if e % 2 != c]
    return lax.ppermute(field, ("expert", "shard"), pairs)


def from_owner(field):
    pairs = [(e * 2 + c, (e ^ 1) * 2 + c) for e in range(8) for c in range(2) if e % 2 == c]
    return lax.ppermute(field, ("expert", "shard"), pairs)


def in_order(first, own, received, axis=0):
    return jnp.where(
        first,
        jnp.concatenate([own, received], axis=axis),
        jnp.concatenate([received, own], axis=axis),
    )


def block(field, index, count):
    rows = field.shape[0] // count
    return lax.dynamic_slice_in_dim(field, index * rows, rows, axis=0)


def sum_blocks(*fields):
    total = fields[0].astype(jnp.float32)
    for field in fields[1:]:
        total = total + field.astype(jnp.float32)
    return total


def low(field):
    return field.astype(jnp.bfloat16)


def reduce_chip(term, core):
    return low(sum_blocks(block(term, core, 2), other_core(block(term, 1 - core, 2))))


def slab_first(part, place):
    dp, x, _, _ = place
    first, second = jnp.split(part, 2)
    return across_x(block(first, 1 - x, 2)), other_dp(block(second, 1 - dp, 2))


def slab_second(part, sent, place):
    dp, x, _, _ = place
    first, second = jnp.split(part, 2)
    first = low(sum_blocks(block(first, x, 2), sent[0]))
    second = low(sum_blocks(block(second, dp, 2), sent[1]))
    first = low(sum_blocks(block(first, dp, 2), other_dp(block(first, 1 - dp, 2))))
    second = low(sum_blocks(block(second, x, 2), across_x(block(second, 1 - x, 2))))
    return jnp.concatenate([first, second])


def reduce_line(part, z):
    return low(
        sum_blocks(
            block(part, z, 4), *[across_z(block(part, z ^ k, 4), k) for k in (1, 2, 3)]
        )
    )


def put_in_order(pieces, own):
    stacked = jnp.stack(pieces)
    return jnp.concatenate(
        [lax.dynamic_index_in_dim(stacked, own ^ b, 0, False) for b in range(len(pieces))]
    )


def spread_line(part, z):
    return put_in_order([part] + [across_z(part, k) for k in (1, 2, 3)], z)


def spread_first(part, place):
    dp, x, _, _ = place
    first, second = jnp.split(part, 2)
    return in_order(dp == 0, first, other_dp(first)), in_order(x == 0, second, across_x(second))


def spread_second(parts, place):
    dp, x, _, _ = place
    first, second = parts
    first = in_order(x == 0, first, across_x(first))
    second = in_order(dp == 0, second, other_dp(second))
    return jnp.concatenate([first, second])


def matmul(left, right, dims=(((1,), (0,)), ((), ()))):
    return lax.dot_general(left, right, dims, preferred_element_type=jnp.float32)


FIRST_WITH_FIRST = (((0,), (0,)), ((), ()))


def expert_kernel(
    is_own,
    own_rows,
    other_rows,
    own_ct,
    other_ct,
    weight_ref,
    up_own,
    up_other,
    down_own,
    down_other,
    *refs,
    columns,
):
    (
        own_sum,
        other_sum,
        own_back,
        other_back,
        gate_ref,
        hidden_ref,
        grad_out_ref,
        grad_up_ref,
        rows_ref,
        ct_ref,
        up_ref,
        down_ref,
        up_sem,
        down_sem,
    ) = refs[-14:]
    width = down_ref.shape[0]
    first = pl.program_id(0) == 0

    @pl.when(first & (is_own[0] == 1))
    def _():
        pltpu.make_async_copy(up_own, up_ref, up_sem).start()
        pltpu.make_async_copy(down_own, down_ref, down_sem).start()

    @pl.when(first & (is_own[0] == 0))
    def _():
        pltpu.make_async_copy(up_other, up_ref, up_sem).start()
        pltpu.make_async_copy(down_other, down_ref, down_sem).start()

    @pl.when(first)
    def _():
        rows_ref[...] = own_rows[...]
        ct_ref[...] = own_ct[...]
        pltpu.make_async_copy(up_own, up_ref, up_sem).wait()
        pltpu.make_async_copy(down_own, down_ref, down_sem).wait()

    @pl.when(pl.program_id(0) == 1)
    def _():
        rows_ref[...] = other_rows[...]
        ct_ref[...] = other_ct[...]

    rows, weighting = rows_ref[...], weight_ref[...]
    ct = ct_ref[...].astype(jnp.float32)
    grad_out = low(weighting * ct)
    grad_out_ref[...] = grad_out
    for start in range(0, width, columns):
        gate, up = pl.ds(start, columns), pl.ds(width + start, columns)
        a, b = matmul(rows, up_ref[:, gate]), matmul(rows, up_ref[:, up])
        tanh = jnp.tanh(0.7978845608028654 * (a + 0.044715 * a * a * a))
        half = 0.5 * (1.0 + tanh)
        gelu = a * half
        hidden_ref[:, gate] = low(gelu * b)
        grad_hidden = matmul(grad_out, down_ref[gate, :], LAST_WITH_LAST)
        slope = half + 0.5 * a * (1.0 - tanh * tanh) * (
            0.7978845608028654 * (1.0 + 3.0 * 0.044715 * a * a)
        )
        grad_up_ref[:, gate] = low(grad_hidden * b * slope)
        grad_up_ref[:, up] = low(grad_hidden * gelu)
    out = low(matmul(hidden_ref[...], down_ref[...])).astype(jnp.float32)
    gate_ref[...] = jnp.sum(ct * out, axis=1, keepdims=True)
    weighted = low(weighting * out)
    back = low(matmul(grad_up_ref[...], up_ref[...], LAST_WITH_LAST))

    @pl.when(pl.program_id(0) == 0)
    def _():
        own_sum[...], own_back[...] = weighted, back

    @pl.when(pl.program_id(0) == 1)
    def _():
        other_sum[...], other_back[...] = weighted, back


SHORT = pl.CostEstimate(flops=1000, bytes_accessed=1000, transcendentals=0)


def expert_step(step, is_own, rows, upstream, weighting, matrices, kept):
    tile, model_width = rows[0].shape
    width = matrices[2].shape[0]
    anywhere = pl.BlockSpec(memory_space=pl.ANY)

    def placed(columns):
        return pl.BlockSpec((tile, columns), lambda i: (2 * step + i, 0))

    def shape(count, columns, dtype=jnp.bfloat16):
        return jax.ShapeDtypeStruct((count * tile, columns), dtype)

    same = pl.BlockSpec((tile, model_width), lambda i: (0, 0))
    out_shape = [
        *[shape(1, model_width)] * 4,
        shape(2, 1, jnp.float32),
        shape(8, width),
        shape(8, model_width),
        shape(8, 2 * width),
        shape(8, model_width),
    ]
    operands = [is_own, *rows, *upstream, weighting, *matrices]
    in_specs = [pl.BlockSpec(memory_space=pltpu.SMEM)] + [same] * 4 + [placed(1)] + [anywhere] * 4
    aliases = {}
    if kept is not None:
        aliases = {len(operands) + i: 5 + i for i in range(4)}
        operands += list(kept)
        in_specs += [anywhere] * 4
    results = pl.pallas_call(
        functools.partial(expert_kernel, columns=256),
        grid=(2,),
        in_specs=in_specs,
        out_specs=[
            *[same] * 4,
            pl.BlockSpec((tile, 1), lambda i: (i, 0)),
            placed(width),
            placed(model_width),
            placed(2 * width),
            placed(model_width),
        ],
        out_shape=out_shape,
        scratch_shapes=[
            pltpu.VMEM((tile, model_width), jnp.bfloat16),
            pltpu.VMEM((model_width, 2 * width), jnp.bfloat16),
            pltpu.VMEM((width, model_width), jnp.bfloat16),
            pltpu.SemaphoreType.DMA,
            pltpu.SemaphoreType.DMA,
        ],
        input_output_aliases=aliases,
        compiler_params=pltpu.CompilerParams(vmem_limit_bytes=50 * 2**20),
        cost_estimate=SHORT,
    )(*operands)
    return results[:2], results[2:4], results[4], results[5:]


def middle_back_kernel(
    back_own,
    back_other,
    back_ring,
    logits_ref,
    router_ref,
    middle_ref,
    scale_ref,
    gain_ref,
    ct_ref,
    weight_ref,
    grad_ref,
    low_ref,
    mix_ref,
    gain_grad,
):
    rows = middle_ref.shape[0]
    total = jnp.zeros(gain_grad.shape, jnp.float32)
    for start in range(0, rows, HEAD_SIZE):
        at = pl.ds(start, HEAD_SIZE)
        grad = sum_blocks(back_own[at, :], back_other[at, :], back_ring[at, :])
        grad = grad + matmul(logits_ref[:, at], router_ref[...], FIRST_WITH_FIRST)
        middle, scale = middle_ref[at, :], scale_ref[at, :]
        scaled = grad * gain_ref[...]
        mean = jnp.mean(scaled * middle, axis=1, keepdims=True)
        out = ct_ref[at, :].astype(jnp.float32) + scale * scaled - middle * (scale**3 * mean)
        total = total + jnp.sum(middle * scale * grad, axis=0, keepdims=True)
        grad_ref[at, :] = out
        low_ref[at, :] = low(out)
    gain_grad[...] = total
    for start in range(0, weight_ref.shape[0], 256):
        at = pl.ds(start, 256)
        mix_ref[:, at] = low(matmul(low_ref[...], weight_ref[at, :], LAST_WITH_LAST))


def middle_back(back, logits, router, middle, scale, gain, upstream, out_weight):
    rows, model_width = middle.shape
    shapes = [
        ((rows, model_width), jnp.float32),
        ((rows, model_width), jnp.bfloat16),
        ((rows, out_weight.shape[0]), jnp.bfloat16),
        ((1, model_width), jnp.float32),
    ]
    return pl.pallas_call(
        middle_back_kernel,
        out_shape=[jax.ShapeDtypeStruct(*shape) for shape in shapes],
        compiler_params=pltpu.CompilerParams(vmem_limit_bytes=40 * 2**20),
        cost_estimate=SHORT,
    )(*back, logits, router, middle, scale, gain[None], upstream, out_weight)


def product_kernel(left_ref, right_ref, out_ref):
    out_ref[...] = low(matmul(left_ref[...], right_ref[...], FIRST_WITH_FIRST))


def product(left, right):
    depth, rows = left.shape
    columns = right.shape[1]
    tile = 384
    return pl.pallas_call(
        product_kernel,
        grid=(rows // tile,),
        in_specs=[
            pl.BlockSpec((depth, tile), lambda i: (0, i)),
            pl.BlockSpec((depth, columns), lambda i: (0, 0)),
        ],
        out_specs=pl.BlockSpec((tile, columns), lambda i: (i, 0)),
        out_shape=jax.ShapeDtypeStruct((rows, columns), jnp.bfloat16),
        compiler_params=pltpu.CompilerParams(vmem_limit_bytes=24 * 2**20),
        cost_estimate=SHORT,
    )(left, right)


def turn(field, cosine, sine):
    half = field.shape[1] // 2
    turned = jnp.concatenate([field[:, half:], field[:, :half]], axis=1)
    return field * cosine + turned * sine


def attend_kernel(query_in, key_in, value_in, cos_ref, sin_ref, seg_row, seg_column, *refs):
    query_ref, key_ref, value_ref, mix_ref = refs
    cosine, sine = cos_ref[...], sin_ref[...]
    query = low(turn(query_in[...], cosine, sine))
    key = low(turn(key_in[...], cosine, sine))
    value = low(value_in[...])
    query_ref[...], key_ref[...], value_ref[...] = query, key, value
    probs = probabilities(query, key, seg_row[...], seg_column[...])
    mix_ref[...] = low(matmul(low(probs), value, FIRST_WITH_FIRST))


def probabilities(query, key, seg_row, seg_column):
    scores = matmul(key, query, LAST_WITH_LAST) * HEAD_SIZE ** (-0.5)
    key_at = lax.broadcasted_iota(jnp.int32, scores.shape, 0)
    query_at = lax.broadcasted_iota(jnp.int32, scores.shape, 1)
    scores = jnp.where((seg_row == seg_column) & (key_at <= query_at), scores, -1e30)
    raised = jnp.exp(scores - jnp.max(scores, axis=0, keepdims=True))
    return raised / jnp.sum(raised, axis=0, keepdims=True)


def attend(projected, cosine, sine, segment):
    rows, width = projected.shape
    groups, heads = KEY_VALUE_HEADS, QUERY_HEADS

    def head(index):
        return pl.BlockSpec((rows, HEAD_SIZE), lambda i: (0, index(i)))

    def whole(*shape):
        return pl.BlockSpec(shape, lambda i: (0, 0))

    def shape(count):
        return jax.ShapeDtypeStruct((rows, count * HEAD_SIZE), jnp.bfloat16)

    group = lambda i: i // (heads // groups)
    return pl.pallas_call(
        attend_kernel,
        grid=(heads,),
        in_specs=[
            head(lambda i: i),
            head(lambda i: heads + group(i)),
            head(lambda i: heads + groups + group(i)),
            whole(rows, HEAD_SIZE),
            whole(rows, HEAD_SIZE),
            whole(1, rows),
            whole(rows, 1),
        ],
        out_specs=[head(lambda i: i), head(group), head(group), head(lambda i: i)],
        out_shape=[shape(heads), shape(groups), shape(groups), shape(heads)],
        compiler_params=pltpu.CompilerParams(vmem_limit_bytes=16 * 2**20),
        cost_estimate=SHORT,
    )(projected, projected, projected, cosine, sine, segment[None, :], segment[:, None])


def attend_back_kernel(
    query_ref, key_ref, value_ref, grad_ref, cos_ref, sin_ref, seg_row, seg_column, out_ref, *sums
):
    key_sum, value_sum = sums
    step = pl.program_id(0)
    heads = pl.num_programs(0)
    groups = KEY_VALUE_HEADS
    group, place = step // (heads // groups), step % (heads // groups)
    query, key, value, grad_mix = query_ref[...], key_ref[...], value_ref[...], grad_ref[...]
    probs = probabilities(query, key, seg_row[...], seg_column[...])
    grad_probs = matmul(value, grad_mix, LAST_WITH_LAST)
    grad_scores = low(
        probs * (grad_probs - jnp.sum(probs * grad_probs, axis=0, keepdims=True))
    )
    grad_query = matmul(grad_scores, key, FIRST_WITH_FIRST) * HEAD_SIZE ** (-0.5)
    grad_query = turn(grad_query, cos_ref[...], -sin_ref[...])
    grad_key = matmul(grad_scores, query) * HEAD_SIZE ** (-0.5)
    grad_value = matmul(low(probs), grad_mix)

    def put(head, field):
        at = pl.multiple_of(head * HEAD_SIZE, HEAD_SIZE)
        out_ref[:, pl.ds(at, HEAD_SIZE)] = low(field)

    put(step, grad_query)

    @pl.when(place == 0)
    def _():
        key_sum[...] = grad_key
        value_sum[...] = grad_value

    @pl.when(place > 0)
    def _():
        key_sum[...] += grad_key
        value_sum[...] += grad_value

    @pl.when(place == heads // groups - 1)
    def _():
        put(heads + group, turn(key_sum[...], cos_ref[...], -sin_ref[...]))
        put(heads + groups + group, value_sum[...])


def attend_back(query, key, value, grad_mix, cosine, sine, segment):
    rows = query.shape[0]
    heads, groups = QUERY_HEADS, KEY_VALUE_HEADS

    def whole(*shape):
        return pl.BlockSpec(shape, lambda i: (0, 0))

    head = pl.BlockSpec((rows, HEAD_SIZE), lambda i: (0, i))
    shared = pl.BlockSpec((rows, HEAD_SIZE), lambda i: (0, i // (heads // groups)))
    width = (heads + 2 * groups) * HEAD_SIZE
    return pl.pallas_call(
        attend_back_kernel,
        grid=(heads,),
        in_specs=[
            head,
            shared,
            shared,
            head,
            whole(rows, HEAD_SIZE),
            whole(rows, HEAD_SIZE),
            whole(1, rows),
            whole(rows, 1),
        ],
        out_specs=whole(rows, width),
        out_shape=jax.ShapeDtypeStruct((rows, width), jnp.bfloat16),
        scratch_shapes=[pltpu.VMEM((rows, HEAD_SIZE), jnp.float32)] * 2,
        compiler_params=pltpu.CompilerParams(vmem_limit_bytes=16 * 2**20),
        cost_estimate=SHORT,
    )(query, key, value, grad_mix, cosine, sine, segment[None, :], segment[:, None])


def ring_shards(
    hidden_in,
    cotangent,
    deal_order,
    lengths,
    routes,
    attention_gain,
    expert_gain,
    qkv_weight,
    out_weight,
    router_weight,
    gate_up_weight,
    down_weight,
):
    count_of_rows = hidden_in.shape[0]
    model_width = hidden_in.shape[1]
    half_rows = count_of_rows // 2
    expert_count = router_weight.shape[1]
    dp, core, at = lax.axis_index("dp"), lax.axis_index("shard"), lax.axis_index("expert")
    x, z = at % 2, at // 2
    place = (dp, x, z, core)
    expert_ids = jnp.arange(expert_count, dtype=jnp.int32)
    row_ids = jnp.arange(count_of_rows, dtype=jnp.int32)

    outer = (z == 0) | (z == 3)

    def by_step(k1, k2, k3):
        return [jnp.where(outer, k2, k1), k3, jnp.where(outer, k1, k2)]

    def held_at(deal_rows):
        return jnp.where(deal_rows // half_rows == dp, 0, half_rows) + deal_rows % half_rows

    def arrange(own_half, other_half, order):
        chosen = low(held_at(order)[:, None] == row_ids[None, :])
        return low(matmul(chosen, jnp.concatenate([own_half, other_half], axis=0)))

    def from_dealt(field, order):
        return arrange(block(field, dp, 2), other_dp(block(field, 1 - dp, 2)), order)

    def to_dealt(field):
        chosen = low(held_at(deal_order[0])[None, :] == row_ids[:, None])
        field = low(matmul(chosen, field))
        return in_order(dp == 0, field[:half_rows], other_dp(field[half_rows:]))

    hidden_out = block(hidden_in, 1 - dp, 2)
    hidden_arrived = other_dp(hidden_out)
    qkv_other, out_other, ct_1, up_other = (
        send(after(field, hidden_out))
        for send, field in (
            (other_core, qkv_weight),
            (other_core, out_weight),
            (ring_z, cotangent),
            (from_owner, gate_up_weight[0]),
        )
    )
    small = jnp.concatenate([attention_gain[None], expert_gain[None], router_weight.T], axis=0)
    small = in_order(core == 0, small, other_core(small), axis=1)
    full_qkv = in_order(core == 0, qkv_weight, qkv_other)
    full_out = in_order(core == 0, out_weight, out_other)
    gain_first, gain_second = small[0].astype(jnp.float32), small[1].astype(jnp.float32)
    full_router = small[2:].T
    segment, token_position = positions_of(lengths[0], count_of_rows)
    frequency = THETA ** (-jnp.arange(HEAD_SIZE // 2, dtype=jnp.float32) / (HEAD_SIZE // 2))
    angles = token_position.astype(jnp.float32)[:, None] * frequency[None, :]
    cosine = jnp.concatenate([jnp.cos(angles)] * 2, axis=1)
    sine = jnp.concatenate([-jnp.sin(angles), jnp.sin(angles)], axis=1)
    cosine, sine, full_qkv, hidden_arrived, gain_first, gain_second, full_router = part(
        cosine, sine, full_qkv, hidden_arrived, gain_first, gain_second, full_router
    )
    tokens = arrange(block(hidden_in, dp, 2), hidden_arrived, deal_order[0])
    residual = tokens.astype(jnp.float32)
    inv_first = lax.rsqrt(jnp.mean(residual * residual, axis=1, keepdims=True) + EPS)
    normed_attn = low(residual * inv_first * gain_first)
    projected = matmul(normed_attn, full_qkv)
    ct_1, projected, cotangent, full_out, down_own, routes = part(
        ct_1, projected, cotangent, full_out, down_weight[0], routes
    )

    ct_2 = ring_z(ct_1)
    down_other = from_owner(down_own)
    ct_0_other = other_dp(block(cotangent, 1 - dp, 2))
    query, key, value, attn_mix = attend(projected, cosine, sine, segment)
    middle = residual + matmul(attn_mix, full_out)
    inv_second = lax.rsqrt(jnp.mean(middle * middle, axis=1, keepdims=True) + EPS)
    normed_0 = low(middle * inv_second * gain_second)
    ct_2, ct_0_other, normed_0, up_other, deal_order = part(
        ct_2, ct_0_other, normed_0, up_other, deal_order
    )

    normed_1 = ring_z(normed_0)
    logits = matmul(normed_0, full_router)
    named = jnp.any(routes[:, :, None] == expert_ids[None, None, :], axis=1)
    top_logit = jnp.max(jnp.where(named, logits, -jnp.inf), axis=1, keepdims=True)
    exp_logits = jnp.where(named, jnp.exp(jnp.where(named, logits - top_logit, 0.0)), 0.0)
    gates = (exp_logits / jnp.sum(exp_logits, axis=1, keepdims=True)).T
    order_here = jnp.pad(deal_order.astype(jnp.float32), ((0, 7), (0, 0)))
    gates_here = jnp.concatenate([gates, order_here], axis=0)
    gates_here = [gates_here] + by_step(*[across_z(gates_here, k) for k in (1, 2, 3)])
    orders = [field[expert_count].astype(jnp.int32) for field in gates_here]
    gates_here = jnp.stack([field[:expert_count] for field in gates_here], axis=1)
    own_row = (expert_ids == 2 * z + core)[:, None]
    weighting = jnp.stack([gates_here, other_core(gates_here)], axis=2)
    weighting = jnp.sum(jnp.where(own_row[:, :, None, None], weighting, 0.0), axis=0)
    weighting = weighting.reshape(8 * count_of_rows, 1)
    ct_0 = arrange(block(cotangent, dp, 2), ct_0_other, deal_order[0])
    ct_0_other, normed_0_other = other_core(ct_0), other_core(normed_0)
    ct_1, ct_1_other = block(ct_1, dp, 2), other_dp(block(ct_1, 1 - dp, 2))
    (
        normed_1,
        weighting,
        ct_0_other,
        normed_0_other,
        ct_1,
        ct_1_other,
        ct_2,
        down_other,
    ) = part(
        normed_1,
        weighting,
        ct_0_other,
        normed_0_other,
        ct_1,
        ct_1_other,
        ct_2,
        down_other,
    )
    is_own = (core == x).astype(jnp.int32)[None]
    matrices = (gate_up_weight[0], up_other, down_weight[0], down_other)

    def expert(step, rows, ct, kept):
        return expert_step(step, is_own, rows, ct, weighting, matrices, kept)

    ct_3 = ring_z(ct_2)
    ct_2, ct_2_other = block(ct_2, dp, 2), other_dp(block(ct_2, 1 - dp, 2))
    ct_1 = arrange(ct_1, ct_1_other, orders[1])
    ct_1_other, normed_1_other = other_core(ct_1), other_core(normed_1)
    sums_0, back_0, gate_0, kept = expert(0, (normed_0, normed_0_other), (ct_0, ct_0_other), None)
    ct_3, ct_2, ct_2_other, ct_1, ct_1_other, normed_1, normed_1_other, kept = part(
        ct_3, ct_2, ct_2_other, ct_1, ct_1_other, normed_1, normed_1_other, kept
    )

    normed_2 = ring_z(normed_1)
    ct_3, ct_3_other = block(ct_3, dp, 2), other_dp(block(ct_3, 1 - dp, 2))
    ct_2 = arrange(ct_2, ct_2_other, orders[2])
    ct_2_other = other_core(ct_2)
    sums_1, back_1, gate_1, kept = expert(1, (normed_1, normed_1_other), (ct_1, ct_1_other), kept)
    normed_2, ct_3, ct_3_other, ct_2, ct_2_other, back_1, kept = part(
        normed_2, ct_3, ct_3_other, ct_2, ct_2_other, back_1, kept
    )

    normed_3 = ring_z(normed_2)
    back_1 = low(sum_blocks(back_1[0], other_core(back_1[1])))
    normed_2_other = other_core(normed_2)
    ct_3 = arrange(ct_3, ct_3_other, orders[3])
    ct_3_other = other_core(ct_3)
    sums_2, back_2, gate_2, kept = expert(2, (normed_2, normed_2_other), (ct_2, ct_2_other), kept)
    normed_3, back_1, ct_3, ct_3_other, back_2, kept = part(
        normed_3, back_1, ct_3, ct_3_other, back_2, kept
    )

    back_1 = ring_z(back_1)
    normed_3_other = other_core(normed_3)
    back_2_other = other_core(back_2[1])
    sums_1 = low(sum_blocks(sums_1[0], other_core(sums_1[1])))
    sums_3, back_3, gate_3, kept = expert(3, (normed_3, normed_3_other), (ct_3, ct_3_other), kept)
    back_1, back_2_other, back_3, sums_1, kept = part(back_1, back_2_other, back_3, sums_1, kept)

    back_2 = ring_z(low(sum_blocks(back_2[0], back_2_other, back_1)))
    back_3_other = other_core(back_3[1])
    all_hidden, all_grad_out, all_grad_up, all_rows = kept
    half_width = model_width // 2
    up_first = low(matmul(all_rows.T, all_grad_up[:, :half_width]))
    up_second = low(matmul(all_rows.T, all_grad_up[:, half_width:]))
    grad_gates = jnp.concatenate([gate_0, gate_1, gate_2, gate_3]).reshape(4, 2 * count_of_rows)
    other_gates = other_core(grad_gates[:, count_of_rows:])
    back_2, back_3_other, up_first, up_second, grad_gates, other_gates, sums_2 = part(
        back_2, back_3_other, up_first, up_second, grad_gates, other_gates, sums_2
    )

    back_3 = ring_z(low(sum_blocks(back_3[0], back_3_other, back_2)))
    up_first_other = to_owner(up_first)
    up_second_other = other_dp(block(up_second, 1 - dp, 2))
    back_0_other = other_core(back_0[1])
    pairs = in_order(core == 0, grad_gates[:, None, :count_of_rows], other_gates[:, None], axis=1)
    pairs = jnp.where((expert_ids // 2 == z)[None, :, None], jnp.tile(pairs, (1, 4, 1)), 0.0)
    home = jnp.where(outer, pairs[3], pairs[1]), jnp.where(outer, pairs[1], pairs[3]), pairs[2]
    home = [pairs[0]] + [across_z(home[k - 1], k) for k in (1, 2, 3)]
    down_first = low(matmul(all_hidden.T, all_grad_out[:, :half_width]))
    down_second = low(matmul(all_hidden.T, all_grad_out[:, half_width:]))
    (
        back_3,
        up_first,
        up_first_other,
        up_second,
        up_second_other,
        down_first,
        down_second,
        home,
        sums_1,
        back_0_other,
    ) = part(
        back_3,
        up_first,
        up_first_other,
        up_second,
        up_second_other,
        down_first,
        down_second,
        home,
        sums_1,
        back_0_other,
    )

    sums_1 = ring_z(sums_1)
    down_first_other = to_owner(down_first)
    down_second_other = other_dp(block(down_second, 1 - dp, 2))
    up_first = low(sum_blocks(up_first, up_first_other))
    up_second = low(sum_blocks(block(up_second, dp, 2), up_second_other))
    up_first_other = other_dp(block(up_first, 1 - dp, 2))
    up_second_other = to_owner(up_second)
    sums_2_other = other_core(sums_2[1])
    grad_gates = sum_blocks(*home)
    mean_term = jnp.sum(gates * grad_gates, axis=0, keepdims=True)
    grad_logits = low(gates * (grad_gates - mean_term))
    grad_middle, grad_attn_out, grad_mix, term_gain_second = middle_back(
        (back_0[0], back_0_other, back_3),
        grad_logits,
        full_router.T,
        middle,
        inv_second,
        gain_second,
        ct_0,
        full_out,
    )
    grad_projected = attend_back(query, key, value, grad_mix, cosine, sine, segment)
    term_out = product(attn_mix, grad_attn_out)
    term_qkv = product(normed_attn, grad_projected)
    (
        sums_1,
        down_first,
        down_first_other,
        down_second,
        down_second_other,
        up_first,
        up_first_other,
        up_second,
        up_second_other,
        sums_2_other,
        term_out,
        term_qkv,
        grad_projected,
    ) = part(
        sums_1,
        down_first,
        down_first_other,
        down_second,
        down_second_other,
        up_first,
        up_first_other,
        up_second,
        up_second_other,
        sums_2_other,
        term_out,
        term_qkv,
        grad_projected,
    )

    sums_2 = ring_z(low(sum_blocks(sums_2[0], sums_2_other, sums_1)))
    sums_3_other = other_core(sums_3[1])
    chip_out, chip_qkv = reduce_chip(term_out, core), reduce_chip(term_qkv, core)
    down_first = low(sum_blocks(down_first, down_first_other))
    down_second = low(sum_blocks(block(down_second, dp, 2), down_second_other))
    down_first_other = other_dp(block(down_first, 1 - dp, 2))
    down_second_other = to_owner(down_second)
    up_grad = [
        sum_blocks(block(up_first, dp, 2), up_first_other),
        sum_blocks(up_second, up_second_other),
    ]
    up_grad = low(jnp.concatenate(up_grad, axis=1))
    up_grad_other = other_core(block(up_grad, 1 - core, 2))
    grad_normed_attn = matmul(grad_projected, full_qkv, LAST_WITH_LAST)
    grad_resid_norm, term_gain_first = norm_back(residual, inv_first, gain_first, grad_normed_attn)
    grad_tokens = low(grad_middle + grad_resid_norm)
    term_router = matmul(grad_logits, normed_0)
    small_grad = jnp.concatenate([term_gain_first[None], term_gain_second, term_router])
    (
        sums_2,
        sums_3_other,
        chip_out,
        chip_qkv,
        down_first,
        down_first_other,
        down_second,
        down_second_other,
        up_grad,
        up_grad_other,
        grad_tokens,
        small_grad,
    ) = part(
        sums_2,
        sums_3_other,
        chip_out,
        chip_qkv,
        down_first,
        down_first_other,
        down_second,
        down_second_other,
        up_grad,
        up_grad_other,
        grad_tokens,
        small_grad,
    )

    sums_3 = ring_z(low(sum_blocks(sums_3[0], sums_3_other, sums_2)))
    sums_0_other = other_core(sums_0[1])
    out_sent, qkv_sent = slab_first(chip_out, place), slab_first(chip_qkv, place)
    down_grad = [
        sum_blocks(block(down_first, dp, 2), down_first_other),
        sum_blocks(down_second, down_second_other),
    ]
    down_grad = low(jnp.concatenate(down_grad, axis=1))
    down_grad_other = other_core(block(down_grad, 1 - core, 2))
    down_grad = jnp.where(core == x, block(down_grad, core, 2), down_grad_other)
    up_grad = jnp.where(core == x, block(up_grad, core, 2), up_grad_other)
    down_grad, gate_up_grad = (field[None].astype(jnp.float32) for field in (down_grad, up_grad))
    small_grad = small_grad + other_core(small_grad)
    sums_3, sums_0_other, out_sent, qkv_sent, small_grad, grad_tokens = part(
        sums_3, sums_0_other, out_sent, qkv_sent, small_grad, grad_tokens
    )

    slab_out, slab_qkv = (
        slab_second(chip, sent, place) for chip, sent in ((chip_out, out_sent), (chip_qkv, qkv_sent))
    )
    input_gradient = to_dealt(grad_tokens)
    layer_out = low(middle + sum_blocks(sums_0[0], sums_0_other, sums_3))
    small_sent = other_dp(small_grad), across_x(small_grad), across_dp_x(small_grad)
    slab_out, slab_qkv, small_grad, small_sent, layer_out = part(
        slab_out, slab_qkv, small_grad, small_sent, layer_out
    )

    line_out, line_qkv = reduce_line(slab_out, z), reduce_line(slab_qkv, z)
    layer_out = to_dealt(layer_out)
    small_grad = sum_blocks(small_grad, *small_sent)
    line_out, line_qkv, small_grad = part(line_out, line_qkv, small_grad)

    line_out, line_qkv = spread_line(line_out, z), spread_line(line_qkv, z)
    small_grad = sum_blocks(small_grad, *[across_z(small_grad, k) for k in (1, 2, 3)])
    line_out, line_qkv, small_grad = part(line_out, line_qkv, small_grad)

    out_parts, qkv_parts = spread_first(line_out, place), spread_first(line_qkv, place)
    out_parts, qkv_parts = part(out_parts, qkv_parts)
    out_grad = spread_second(out_parts, place).astype(jnp.float32)
    qkv_grad = spread_second(qkv_parts, place).astype(jnp.float32)
    small_grad = lax.dynamic_slice_in_dim(
        small_grad, core * (model_width // 2), model_width // 2, axis=1
    )
    return (
        layer_out,
        input_gradient,
        small_grad[0],
        small_grad[1],
        qkv_grad,
        out_grad,
        small_grad[2:].T,
        gate_up_grad,
        down_grad,
    )


def solution(mesh):
    ringed = (mesh.shape["dp"], mesh.shape["expert"], mesh.shape["shard"]) == (2, 8, 2)
    shards = ring_shards if ringed else routed_shards
    return jax.shard_map(
        shards,
        mesh=mesh,
        in_specs=(
            P(("dp", "expert", "shard"), None),
            P(("dp", "expert", "shard"), None),
            P(("dp", "expert", "shard"), None),
            P(("dp", "expert", "shard"), None),
            P(("dp", "expert", "shard"), None),
            P("shard"),
            P("shard"),
            P("shard", None),
            P("shard", None),
            P("shard", None),
            P("expert", None, None),
            P("expert", None, None),
        ),
        out_specs=(
            P(("dp", "expert", "shard"), None),
            P(("dp", "expert", "shard"), None),
            P("shard"),
            P("shard"),
            P("shard", None),
            P("shard", None),
            P("shard", None),
            P("expert", ("dp", "shard"), None),
            P("expert", ("dp", "shard"), None),
        ),
        check_vma=False,
    )
```

```python
import functools

import jax
import jax.numpy as jnp
from jax import lax
from jax.experimental import pallas as pl
from jax.experimental.pallas import tpu as pltpu
from jax.sharding import PartitionSpec as P

QUERY_HEADS = 12
KEY_VALUE_HEADS = 2
HEAD_SIZE = 128
TOP = 4


EPS = 1e-06
THETA = 1000000.0


def positions_of(lengths_dev, count_of_rows):
    seq_ends = jnp.cumsum(lengths_dev)
    starts = seq_ends - lengths_dev
    places = jnp.arange(count_of_rows, dtype=jnp.int32)
    segment = jnp.sum((places[:, None] >= seq_ends[None, :]).astype(jnp.int32), axis=1)
    member = segment[:, None] == jnp.arange(lengths_dev.shape[0], dtype=jnp.int32)[None, :]
    start_of = jnp.sum(jnp.where(member, starts[None, :], 0), axis=1)
    return (segment, places - start_of)


def apply_rotation(field, token_position, direction):
    half_dim = field.shape[-1] // 2
    frequency = THETA ** (-jnp.arange(half_dim, dtype=jnp.float32) / half_dim)
    angles = token_position.astype(jnp.float32)[:, None] * frequency[None, :]
    cosine = jnp.cos(angles)[:, None, :]
    sine_term = direction * jnp.sin(angles)[:, None, :]
    lead_part = field[..., :half_dim]
    tail_part = field[..., half_dim:]
    return jnp.concatenate(
        [lead_part * cosine - tail_part * sine_term, tail_part * cosine + lead_part * sine_term],
        axis=-1,
    )


def masked_scores(query_block, key_matrix_rows, segment_block, segment, row_start):
    raw_scores = jnp.einsum(
        "ihgd,jhd->hgij", query_block, key_matrix_rows, preferred_element_type=jnp.float32
    ) * HEAD_SIZE ** (-0.5)
    query_at = row_start + jnp.arange(query_block.shape[0], dtype=jnp.int32)
    key_at = jnp.arange(key_matrix_rows.shape[0], dtype=jnp.int32)
    allowed = (segment_block[:, None] == segment[None, :]) & (key_at[None, :] <= query_at[:, None])
    return jnp.where(allowed, raw_scores, -1e30)


def norm_back(field, inv_scale, gain_vec, grad_normed):
    scaled = grad_normed * gain_vec
    grad_field = inv_scale * scaled - field * inv_scale**3 * jnp.mean(
        scaled * field, axis=1, keepdims=True
    )
    grad_gain = jnp.sum(field * inv_scale * grad_normed, axis=0)
    return (grad_field, grad_gain)


def activate(gate_up):
    hidden_width = gate_up.shape[1] // 2
    return jax.nn.gelu(gate_up[:, :hidden_width], approximate=True) * gate_up[:, hidden_width:]


def routed_shards(
    hidden_in,
    cotangent,
    deal_order,
    lengths,
    routes,
    attention_gain,
    expert_gain,
    qkv_weight,
    out_weight,
    router_weight,
    gate_up_weight,
    down_weight,
):
    count_of_rows = hidden_in.shape[0]
    model_width = hidden_in.shape[1]
    head_groups = QUERY_HEADS // KEY_VALUE_HEADS
    arrived_in, arrived_ct = (
        lax.all_to_all(hidden_in, "dp", split_axis=0, concat_axis=0, tiled=True),
        lax.all_to_all(cotangent, "dp", split_axis=0, concat_axis=0, tiled=True),
    )
    deal_rows = deal_order[0]
    tokens = arrived_in[deal_rows]
    upstream = arrived_ct[deal_rows].astype(jnp.float32)
    gain_first, gain_second, full_qkv, full_out, full_router = (
        lax.all_gather(attention_gain, "shard", axis=0, tiled=True),
        lax.all_gather(expert_gain, "shard", axis=0, tiled=True),
        lax.all_gather(qkv_weight, "shard", axis=0, tiled=True),
        lax.all_gather(out_weight, "shard", axis=0, tiled=True),
        lax.all_gather(router_weight, "shard", axis=0, tiled=True),
    )
    gain_first = gain_first.astype(jnp.float32)
    gain_second = gain_second.astype(jnp.float32)
    residual = tokens.astype(jnp.float32)
    inv_first = lax.rsqrt(jnp.mean(residual * residual, axis=1, keepdims=True) + EPS)
    normed_attn = (residual * inv_first * gain_first).astype(jnp.bfloat16)
    projected_rows = jnp.dot(normed_attn, full_qkv, preferred_element_type=jnp.float32)
    segment, token_position = positions_of(lengths[0], count_of_rows)
    query_matrix_rows = (
        apply_rotation(
            projected_rows[:, : QUERY_HEADS * HEAD_SIZE].reshape(
                count_of_rows, QUERY_HEADS, HEAD_SIZE
            ),
            token_position,
            1.0,
        )
        .astype(jnp.bfloat16)
        .reshape(count_of_rows, KEY_VALUE_HEADS, head_groups, HEAD_SIZE)
    )
    key_matrix_rows = apply_rotation(
        projected_rows[
            :, QUERY_HEADS * HEAD_SIZE : (QUERY_HEADS + KEY_VALUE_HEADS) * HEAD_SIZE
        ].reshape(count_of_rows, KEY_VALUE_HEADS, HEAD_SIZE),
        token_position,
        1.0,
    ).astype(jnp.bfloat16)
    value_matrix_rows = (
        projected_rows[:, (QUERY_HEADS + KEY_VALUE_HEADS) * HEAD_SIZE :]
        .reshape(count_of_rows, KEY_VALUE_HEADS, HEAD_SIZE)
        .astype(jnp.bfloat16)
    )
    block_rows = min(count_of_rows, 512)
    block_starts = jnp.arange(count_of_rows // block_rows, dtype=jnp.int32) * block_rows

    def forward_block(row_start):
        scores = masked_scores(query_matrix_rows, key_matrix_rows, segment, segment, row_start)
        row_max = jnp.max(scores, axis=-1, keepdims=True)
        exp_scores = jnp.exp(scores - row_max)
        exp_total = jnp.sum(exp_scores, axis=-1, keepdims=True)
        soft_probs = (exp_scores / exp_total).astype(jnp.bfloat16)
        mix_block = jnp.einsum(
            "hgij,jhd->ihgd", soft_probs, value_matrix_rows, preferred_element_type=jnp.float32
        )
        return (mix_block, (row_max + jnp.log(exp_total))[..., 0])

    mix_blocks, logsum = lax.map(forward_block, block_starts)
    attn_mix = mix_blocks.reshape(count_of_rows, QUERY_HEADS * HEAD_SIZE).astype(jnp.bfloat16)
    middle = residual + jnp.dot(attn_mix, full_out, preferred_element_type=jnp.float32)
    inv_second = lax.rsqrt(jnp.mean(middle * middle, axis=1, keepdims=True) + EPS)
    normed_moe = (middle * inv_second * gain_second).astype(jnp.bfloat16)
    logits = jnp.dot(normed_moe, full_router, preferred_element_type=jnp.float32)
    gate_probs = jax.nn.softmax(jnp.take_along_axis(logits, routes, axis=1), axis=-1)
    expert_count = full_router.shape[1]
    peer_count = lax.axis_size("expert")
    capacity = min(count_of_rows, max(2, 3 * count_of_rows * TOP // (2 * expert_count)))
    flat_routes = routes.reshape(-1)
    expert_ids = jnp.arange(expert_count, dtype=jnp.int32)
    onehot = (flat_routes[:, None] == expert_ids[None, :]).astype(jnp.int32)
    slot_rank = jnp.sum(jnp.cumsum(onehot, axis=0) * onehot, axis=1) - 1
    target = flat_routes * capacity + slot_rank
    pair_count = count_of_rows * TOP
    slot_pair = (
        jnp.full((expert_count * capacity,), pair_count, jnp.int32)
        .at[target]
        .set(jnp.arange(pair_count, dtype=jnp.int32))
    )
    padded = jnp.concatenate([normed_moe, jnp.zeros((1, model_width), jnp.bfloat16)], axis=0)
    sending = padded[slot_pair // TOP].reshape(peer_count, capacity, model_width)
    received = lax.all_to_all(sending, "expert", split_axis=0, concat_axis=0, tiled=True)
    rows_in = received.reshape(peer_count * capacity, model_width)
    gate_up = jnp.dot(rows_in, gate_up_weight[0], preferred_element_type=jnp.float32)
    hidden_rows = activate(gate_up).astype(jnp.bfloat16)
    expert_out = jnp.dot(hidden_rows, down_weight[0], preferred_element_type=jnp.float32).astype(
        jnp.bfloat16
    )
    returned = lax.all_to_all(
        expert_out.reshape(peer_count, capacity, model_width),
        "expert",
        split_axis=0,
        concat_axis=0,
        tiled=True,
    )
    per_pair = returned.reshape(peer_count * capacity, model_width)[target].reshape(
        count_of_rows, TOP, model_width
    )
    expert_sum = jnp.zeros((count_of_rows, model_width), jnp.float32)
    for choice_slot in range(TOP):
        expert_sum = expert_sum + gate_probs[:, choice_slot : choice_slot + 1] * per_pair[
            :, choice_slot
        ].astype(jnp.float32)
    final_rows = middle + expert_sum
    grad_pairs = (gate_probs[:, :, None] * upstream[:, None, :]).astype(jnp.bfloat16)
    grad_gates = jnp.stack(
        [
            jnp.sum(per_pair[:, choice_slot].astype(jnp.float32) * upstream, axis=1)
            for choice_slot in range(TOP)
        ],
        axis=1,
    )
    padded_grad = jnp.concatenate(
        [grad_pairs.reshape(pair_count, model_width), jnp.zeros((1, model_width), jnp.bfloat16)],
        axis=0,
    )
    sending_back = padded_grad[slot_pair].reshape(peer_count, capacity, model_width)
    grad_rows = lax.all_to_all(
        sending_back, "expert", split_axis=0, concat_axis=0, tiled=True
    ).reshape(peer_count * capacity, model_width)
    grad_hidden = jnp.dot(grad_rows, down_weight[0].T, preferred_element_type=jnp.float32)
    grad_gate_up = jax.vjp(activate, gate_up)[1](grad_hidden)[0].astype(jnp.bfloat16)
    term_down = jnp.dot(hidden_rows.T, grad_rows, preferred_element_type=jnp.float32)
    term_gate_up = jnp.dot(rows_in.T, grad_gate_up, preferred_element_type=jnp.float32)
    grad_rows_in = jnp.dot(
        grad_gate_up, gate_up_weight[0].T, preferred_element_type=jnp.float32
    ).astype(jnp.bfloat16)
    back_rows = lax.all_to_all(
        grad_rows_in.reshape(peer_count, capacity, model_width),
        "expert",
        split_axis=0,
        concat_axis=0,
        tiled=True,
    )
    back_pairs = back_rows.reshape(peer_count * capacity, model_width)[target].reshape(
        count_of_rows, TOP, model_width
    )
    grad_normed = jnp.zeros((count_of_rows, model_width), jnp.float32)
    for choice_slot in range(TOP):
        grad_normed = grad_normed + back_pairs[:, choice_slot].astype(jnp.float32)
    mean_term = jnp.sum(gate_probs * grad_gates, axis=1, keepdims=True)
    grad_chosen = gate_probs * (grad_gates - mean_term)
    grad_logits = jnp.sum(
        jnp.where(routes[:, :, None] == expert_ids[None, None, :], grad_chosen[:, :, None], 0.0),
        axis=1,
    ).astype(jnp.bfloat16)
    term_router = jnp.dot(normed_moe.T, grad_logits, preferred_element_type=jnp.float32)
    grad_normed = grad_normed + jnp.dot(
        grad_logits, full_router.T, preferred_element_type=jnp.float32
    )
    grad_middle_norm, term_gain_second = norm_back(middle, inv_second, gain_second, grad_normed)
    grad_middle = upstream + grad_middle_norm
    grad_attn_out = grad_middle.astype(jnp.bfloat16)
    term_out = jnp.dot(attn_mix.T, grad_attn_out, preferred_element_type=jnp.float32)
    grad_mix = (
        jnp.dot(grad_attn_out, full_out.T, preferred_element_type=jnp.float32)
        .astype(jnp.bfloat16)
        .reshape(count_of_rows, KEY_VALUE_HEADS, head_groups, HEAD_SIZE)
    )

    def backward_block(accums, inputs):
        acc_key, value_accumulator = accums
        row_start, logsum_block = inputs
        scores = masked_scores(query_matrix_rows, key_matrix_rows, segment, segment, row_start)
        soft_probs = jnp.exp(scores - logsum_block[..., None])
        grad_probs = jnp.einsum(
            "ihgd,jhd->hgij", grad_mix, value_matrix_rows, preferred_element_type=jnp.float32
        )
        value_accumulator = value_accumulator + jnp.einsum(
            "hgij,ihgd->jhd",
            soft_probs.astype(jnp.bfloat16),
            grad_mix,
            preferred_element_type=jnp.float32,
        )
        grad_scores = (
            soft_probs * (grad_probs - jnp.sum(soft_probs * grad_probs, axis=-1, keepdims=True))
        ).astype(jnp.bfloat16)
        grad_query = HEAD_SIZE ** (-0.5) * jnp.einsum(
            "hgij,jhd->ihgd", grad_scores, key_matrix_rows, preferred_element_type=jnp.float32
        )
        acc_key = acc_key + HEAD_SIZE ** (-0.5) * jnp.einsum(
            "hgij,ihgd->jhd", grad_scores, query_matrix_rows, preferred_element_type=jnp.float32
        )
        return ((acc_key, value_accumulator), grad_query)

    zero_key_value = jnp.zeros((count_of_rows, KEY_VALUE_HEADS, HEAD_SIZE), jnp.float32)
    (acc_key, value_accumulator), grad_query = lax.scan(
        backward_block, (zero_key_value, zero_key_value), (block_starts, logsum)
    )
    grad_query = apply_rotation(
        grad_query.reshape(count_of_rows, QUERY_HEADS, HEAD_SIZE), token_position, -1.0
    )
    key_gradient = apply_rotation(acc_key, token_position, -1.0)
    grad_projected = jnp.concatenate(
        [
            grad_query.reshape(count_of_rows, QUERY_HEADS * HEAD_SIZE),
            key_gradient.reshape(count_of_rows, KEY_VALUE_HEADS * HEAD_SIZE),
            value_accumulator.reshape(count_of_rows, KEY_VALUE_HEADS * HEAD_SIZE),
        ],
        axis=1,
    ).astype(jnp.bfloat16)
    term_qkv = jnp.dot(normed_attn.T, grad_projected, preferred_element_type=jnp.float32)
    grad_normed_attn = jnp.dot(grad_projected, full_qkv.T, preferred_element_type=jnp.float32)
    grad_resid_norm, term_gain_first = norm_back(residual, inv_first, gain_first, grad_normed_attn)
    grad_tokens = (grad_middle + grad_resid_norm).astype(jnp.bfloat16)
    inverse = (
        jnp.zeros((count_of_rows,), jnp.int32)
        .at[deal_rows]
        .set(jnp.arange(count_of_rows, dtype=jnp.int32))
    )
    layer_out, input_gradient = (
        lax.all_to_all(
            final_rows.astype(jnp.bfloat16)[inverse], "dp", split_axis=0, concat_axis=0, tiled=True
        ),
        lax.all_to_all(grad_tokens[inverse], "dp", split_axis=0, concat_axis=0, tiled=True),
    )
    shard_terms = (
        lax.psum_scatter(
            term_gain_first.astype(jnp.bfloat16), "shard", scatter_dimension=0, tiled=True
        ).astype(jnp.float32),
        lax.psum_scatter(
            term_gain_second.astype(jnp.bfloat16), "shard", scatter_dimension=0, tiled=True
        ).astype(jnp.float32),
        lax.psum_scatter(
            term_qkv.astype(jnp.bfloat16), "shard", scatter_dimension=0, tiled=True
        ).astype(jnp.float32),
        lax.psum_scatter(
            term_out.astype(jnp.bfloat16), "shard", scatter_dimension=0, tiled=True
        ).astype(jnp.float32),
        lax.psum_scatter(
            term_router.astype(jnp.bfloat16), "shard", scatter_dimension=0, tiled=True
        ).astype(jnp.float32),
    )
    gain_first_grad, gain_second_grad, qkv_grad, out_grad, router_grad = lax.psum(
        (shard_terms[0], shard_terms[1], shard_terms[2], shard_terms[3], shard_terms[4]),
        ("dp", "expert"),
    )
    gate_up_grad, down_grad = (
        lax.psum_scatter(
            term_gate_up[None].astype(jnp.bfloat16),
            ("dp", "shard"),
            scatter_dimension=1,
            tiled=True,
        ).astype(jnp.float32),
        lax.psum_scatter(
            term_down[None].astype(jnp.bfloat16), ("dp", "shard"), scatter_dimension=1, tiled=True
        ).astype(jnp.float32),
    )
    return (
        layer_out,
        input_gradient,
        gain_first_grad,
        gain_second_grad,
        qkv_grad,
        out_grad,
        router_grad,
        gate_up_grad,
        down_grad,
    )


RING_NEXT = (1, 3, 0, 2)
LAST_WITH_LAST = (((1,), (1,)), ((), ()))


def after(value, *earlier):
    return lax.optimization_barrier((value, *earlier))[0]


def part(*fields):
    return lax.optimization_barrier(fields)


def other_core(field):
    return lax.ppermute(field, "shard", [(0, 1), (1, 0)])


def other_dp(field):
    return lax.ppermute(field, "dp", [(0, 1), (1, 0)])


def owners_dp(field):
    pairs = [
        ((d * 8 + e) * 2 + e % 2, ((1 - d) * 8 + e) * 2 + e % 2) for d in range(2) for e in range(8)
    ]
    return lax.ppermute(field, ("dp", "expert", "shard"), pairs)


def across_x(field):
    return lax.ppermute(field, "expert", [(i, i ^ 1) for i in range(8)])


def across_dp_x(field):
    pairs = [(d * 8 + e, (1 - d) * 8 + (e ^ 1)) for d in range(2) for e in range(8)]
    return lax.ppermute(field, ("dp", "expert"), pairs)


def across_z(field, distance):
    return lax.ppermute(field, "expert", [(i, i ^ (2 * distance)) for i in range(8)])


def ring_z(field):
    pairs = [(2 * z + x, 2 * RING_NEXT[z] + x) for z in range(4) for x in range(2)]
    return lax.ppermute(field, "expert", pairs)


def to_owner(field):
    pairs = [(e * 2 + c, (e ^ 1) * 2 + c) for e in range(8) for c in range(2) if e % 2 != c]
    return lax.ppermute(field, ("expert", "shard"), pairs)


def from_owner(field):
    pairs = [(e * 2 + c, (e ^ 1) * 2 + c) for e in range(8) for c in range(2) if e % 2 == c]
    return lax.ppermute(field, ("expert", "shard"), pairs)


def in_order(first, own, received, axis=0):
    return jnp.where(
        first,
        jnp.concatenate([own, received], axis=axis),
        jnp.concatenate([received, own], axis=axis),
    )


def block(field, index, count):
    rows = field.shape[0] // count
    return lax.dynamic_slice_in_dim(field, index * rows, rows, axis=0)


def sum_blocks(*fields):
    total = fields[0].astype(jnp.float32)
    for field in fields[1:]:
        total = total + field.astype(jnp.float32)
    return total


def low(field):
    return field.astype(jnp.bfloat16)


def chip_send(theirs, mine):
    return mine, other_core(theirs)


def slab_send(fields, place):
    dp, x, _, _ = place
    first, second = jnp.split(low(sum_blocks(*fields)), 2)
    return (
        (block(first, x, 2), across_x(block(first, 1 - x, 2))),
        (block(second, dp, 2), other_dp(block(second, 1 - dp, 2))),
    )


def slab_send_on(fields, place):
    dp, x, _, _ = place
    first, second = (low(sum_blocks(*pair)) for pair in fields)
    return (
        (block(first, dp, 2), other_dp(block(first, 1 - dp, 2))),
        (block(second, x, 2), across_x(block(second, 1 - x, 2))),
    )


def line_send(fields, z):
    part = low(jnp.concatenate([sum_blocks(*pair) for pair in fields]))
    return [block(part, z, 4)] + [across_z(block(part, z ^ k, 4), k) for k in (1, 2, 3)]


def put_in_order(pieces, own):
    stacked = jnp.stack(pieces)
    return jnp.concatenate(
        [lax.dynamic_index_in_dim(stacked, own ^ b, 0, False) for b in range(len(pieces))]
    )


def line_spread(fields):
    part = low(sum_blocks(*fields))
    return [part] + [across_z(part, k) for k in (1, 2, 3)]


def slab_spread(fields, z):
    first, second = jnp.split(put_in_order(fields, z), 2)
    return (first, other_dp(first)), (second, across_x(second))


def slab_spread_on(fields, place):
    dp, x, _, _ = place
    first, second = fields
    first, second = in_order(dp == 0, *first), in_order(x == 0, *second)
    return (first, across_x(first)), (second, other_dp(second))


def whole_of(fields, place):
    dp, x, _, _ = place
    first, second = fields
    return jnp.concatenate([in_order(x == 0, *first), in_order(dp == 0, *second)])


def matmul(left, right, dims=(((1,), (0,)), ((), ()))):
    return lax.dot_general(left, right, dims, preferred_element_type=jnp.float32)


FIRST_WITH_FIRST = (((0,), (0,)), ((), ()))


EXTRA = 16


def packed(field, columns):
    high = low(field)
    rest = low(field - high.astype(jnp.float32))
    pad = jnp.zeros((field.shape[0], columns - 2 * field.shape[1]), jnp.bfloat16)
    block = jnp.concatenate([high, rest, pad], axis=1)
    return jnp.concatenate([block, jnp.zeros((EXTRA - field.shape[0], columns), jnp.bfloat16)])


def unpacked(extra, rows):
    field = extra.astype(jnp.float32)[: EXTRA // 2]
    return field[:, :rows] + field[:, rows : 2 * rows]


def expert_kernel(
    choice,
    own_rows,
    other_rows,
    own_ct,
    other_ct,
    up_own,
    up_other,
    down_own,
    down_other,
    *refs,
    columns,
):
    (
        own_sum,
        other_sum,
        own_back,
        other_back,
        hidden_ref,
        grad_out_ref,
        grad_up_ref,
        rows_ref,
        unit_ref,
        ct_ref,
        up_ref,
        down_ref,
        up_sem,
        down_sem,
    ) = refs[-14:]
    width = down_ref.shape[0]
    first = pl.program_id(0) == 0

    @pl.when(first & (choice[0] == 1))
    def _():
        pltpu.make_async_copy(up_own, up_ref, up_sem).start()
        pltpu.make_async_copy(down_own, down_ref, down_sem).start()

    @pl.when(first & (choice[0] == 0))
    def _():
        pltpu.make_async_copy(up_other, up_ref, up_sem).start()
        pltpu.make_async_copy(down_other, down_ref, down_sem).start()

    @pl.when(first)
    def _():
        unit_ref[...] = own_rows[...]
        ct_ref[...] = own_ct[...]
        pltpu.make_async_copy(up_own, up_ref, up_sem).wait()
        pltpu.make_async_copy(down_own, down_ref, down_sem).wait()

    @pl.when(pl.program_id(0) == 1)
    def _():
        unit_ref[...] = other_rows[...]
        ct_ref[...] = other_ct[...]

    count = ct_ref.shape[0]
    rows = unit_ref[:count, :]
    rows_ref[...] = rows
    gates = unpacked(unit_ref[count:, :], count)
    mine = lax.broadcasted_iota(jnp.int32, gates.shape, 0) == choice[1]
    weighting = jnp.sum(jnp.where(mine, gates, 0.0), axis=0, keepdims=True)
    weighting = jnp.broadcast_to(weighting, (HEAD_SIZE, rows.shape[0])).T[:, :1]
    ct = ct_ref[...].astype(jnp.float32)
    grad_out = low(weighting * ct)
    grad_out_ref[...] = grad_out
    for start in range(0, width, columns):
        gate, up = pl.ds(start, columns), pl.ds(width + start, columns)
        a, b = matmul(rows, up_ref[:, gate]), matmul(rows, up_ref[:, up])
        tanh = jnp.tanh(0.7978845608028654 * (a + 0.044715 * a * a * a))
        half = 0.5 * (1.0 + tanh)
        gelu = a * half
        hidden_ref[:, gate] = low(gelu * b)
        grad_hidden = matmul(grad_out, down_ref[gate, :], LAST_WITH_LAST)
        slope = half + 0.5 * a * (1.0 - tanh * tanh) * (
            0.7978845608028654 * (1.0 + 3.0 * 0.044715 * a * a)
        )
        grad_up_ref[:, gate] = low(grad_hidden * b * slope)
        grad_up_ref[:, up] = low(grad_hidden * gelu)
    out = low(matmul(hidden_ref[...], down_ref[...])).astype(jnp.float32)
    grad = jnp.sum(ct * out, axis=1, keepdims=True)
    grad = jnp.broadcast_to(grad, (rows.shape[0], HEAD_SIZE)).T[: mine.shape[0], :]
    grad = packed(jnp.where(mine, grad, 0.0), rows.shape[1])
    weighted = low(weighting * out)
    back = low(matmul(grad_up_ref[...], up_ref[...], LAST_WITH_LAST))

    @pl.when(pl.program_id(0) == 0)
    def _():
        own_sum[...], own_back[:count, :], own_back[count:, :] = weighted, back, grad

    @pl.when(pl.program_id(0) == 1)
    def _():
        other_sum[...], other_back[:count, :], other_back[count:, :] = weighted, back, grad


SHORT = pl.CostEstimate(flops=1000, bytes_accessed=1000, transcendentals=0)


def expert_step(step, choice, rows, upstream, matrices, kept):
    tile, model_width = upstream[0].shape
    width = matrices[2].shape[0]
    anywhere = pl.BlockSpec(memory_space=pl.ANY)

    def placed(columns):
        return pl.BlockSpec((tile, columns), lambda i: (2 * step + i, 0))

    def shape(count, columns, dtype=jnp.bfloat16):
        return jax.ShapeDtypeStruct((count * tile, columns), dtype)

    same = pl.BlockSpec((tile, model_width), lambda i: (0, 0))
    unit = pl.BlockSpec((tile + EXTRA, model_width), lambda i: (0, 0))
    out_shape = [
        *[shape(1, model_width)] * 2,
        *[jax.ShapeDtypeStruct((tile + EXTRA, model_width), jnp.bfloat16)] * 2,
        shape(8, width),
        shape(8, model_width),
        shape(8, 2 * width),
        shape(8, model_width),
    ]
    operands = [choice, *rows, *upstream, *matrices]
    in_specs = [pl.BlockSpec(memory_space=pltpu.SMEM), unit, unit, same, same] + [anywhere] * 4
    aliases = {}
    if kept is not None:
        aliases = {len(operands) + i: 4 + i for i in range(4)}
        operands += list(kept)
        in_specs += [anywhere] * 4
    results = pl.pallas_call(
        functools.partial(expert_kernel, columns=256),
        grid=(2,),
        in_specs=in_specs,
        out_specs=[
            *[same] * 2,
            *[unit] * 2,
            placed(width),
            placed(model_width),
            placed(2 * width),
            placed(model_width),
        ],
        out_shape=out_shape,
        scratch_shapes=[
            pltpu.VMEM((tile + EXTRA, model_width), jnp.bfloat16),
            pltpu.VMEM((tile, model_width), jnp.bfloat16),
            pltpu.VMEM((model_width, 2 * width), jnp.bfloat16),
            pltpu.VMEM((width, model_width), jnp.bfloat16),
            pltpu.SemaphoreType.DMA,
            pltpu.SemaphoreType.DMA,
        ],
        input_output_aliases=aliases,
        compiler_params=pltpu.CompilerParams(vmem_limit_bytes=50 * 2**20),
        cost_estimate=SHORT,
    )(*operands)
    return results[:2], results[2:4], results[4:]


def middle_back_kernel(
    back_own,
    back_other,
    back_ring,
    gates_ref,
    router_ref,
    middle_ref,
    scale_ref,
    gain_ref,
    ct_ref,
    weight_ref,
    grad_ref,
    low_ref,
    mix_ref,
    gain_grad,
    logits_grad,
    weight_here,
    weight_sem,
):
    rows = middle_ref.shape[0]
    pltpu.make_async_copy(weight_ref, weight_here, weight_sem).start()
    gates = gates_ref[...]
    grad_gates = unpacked(
        sum_blocks(back_own[rows:, :], back_other[rows:, :], back_ring[rows:, :]), rows
    )
    mean_term = jnp.sum(gates * grad_gates, axis=0, keepdims=True)
    logits = low(gates * (grad_gates - mean_term))
    logits_grad[...] = logits
    total = jnp.zeros(gain_grad.shape, jnp.float32)
    for start in range(0, rows, HEAD_SIZE):
        at = pl.ds(start, HEAD_SIZE)
        grad = sum_blocks(back_own[at, :], back_other[at, :], back_ring[at, :])
        grad = grad + matmul(logits[:, start : start + HEAD_SIZE], router_ref[...], FIRST_WITH_FIRST)
        middle, scale = middle_ref[at, :], scale_ref[at, :]
        scaled = grad * gain_ref[...]
        mean = jnp.mean(scaled * middle, axis=1, keepdims=True)
        out = ct_ref[at, :].astype(jnp.float32) + scale * scaled - middle * (scale**3 * mean)
        total = total + jnp.sum(middle * scale * grad, axis=0, keepdims=True)
        grad_ref[at, :] = out
        low_ref[at, :] = low(out)
    gain_grad[...] = total
    pltpu.make_async_copy(weight_ref, weight_here, weight_sem).wait()
    for start in range(0, weight_here.shape[0], 256):
        at = pl.ds(start, 256)
        mix_ref[:, at] = low(matmul(low_ref[...], weight_here[at, :], LAST_WITH_LAST))


def middle_back(back, gates, router, middle, scale, gain, upstream, out_weight):
    rows, model_width = middle.shape
    shapes = [
        ((rows, model_width), jnp.float32),
        ((rows, model_width), jnp.bfloat16),
        ((rows, out_weight.shape[0]), jnp.bfloat16),
        ((1, model_width), jnp.float32),
        (gates.shape, jnp.bfloat16),
    ]
    return pl.pallas_call(
        middle_back_kernel,
        in_specs=[pl.BlockSpec(memory_space=pltpu.VMEM)] * 9 + [pl.BlockSpec(memory_space=pl.ANY)],
        out_shape=[jax.ShapeDtypeStruct(*shape) for shape in shapes],
        scratch_shapes=[pltpu.VMEM(out_weight.shape, jnp.bfloat16), pltpu.SemaphoreType.DMA],
        compiler_params=pltpu.CompilerParams(vmem_limit_bytes=60 * 2**20),
        cost_estimate=SHORT,
    )(*back, gates, router, middle, scale, gain, upstream, out_weight)


def middle_kernel(
    mix_ref, weight_ref, tokens_ref, gain_ref, router_ref, routes_ref, *outs
):
    middle_ref, scale_ref, unit_ref, gates_ref = outs
    rows, columns = tokens_ref.shape
    for start in range(0, columns, 256):
        at = pl.ds(start, 256)
        middle_ref[:, at] = tokens_ref[:, at].astype(jnp.float32) + matmul(
            mix_ref[...], weight_ref[:, at]
        )
    for start in range(0, rows, HEAD_SIZE):
        at = pl.ds(start, HEAD_SIZE)
        middle = middle_ref[at, :]
        scale = lax.rsqrt(jnp.mean(middle * middle, axis=1, keepdims=True) + EPS)
        scale_ref[at, :] = scale
        unit_ref[at, :] = low(middle * scale * gain_ref[...])
    logits = matmul(router_ref[...], unit_ref[:rows, :], LAST_WITH_LAST)
    expert = lax.broadcasted_iota(jnp.int32, logits.shape, 0)
    named = expert == routes_ref[0:1, :]
    for choice in range(1, routes_ref.shape[0]):
        named = named | (expert == routes_ref[choice : choice + 1, :])
    logits = jnp.where(named, logits, -1e30)
    raised = jnp.exp(logits - jnp.max(logits, axis=0, keepdims=True))
    raised = jnp.where(named, raised, 0.0)
    gates = raised / jnp.sum(raised, axis=0, keepdims=True)
    gates_ref[...] = gates
    unit_ref[rows:, :] = packed(gates, columns)


def middle_of(mix, out_weight, tokens, gain, router, routes):
    rows, columns = tokens.shape
    shapes = [
        ((rows, columns), jnp.float32),
        ((rows, 1), jnp.float32),
        ((rows + EXTRA, columns), jnp.bfloat16),
        ((router.shape[0], rows), jnp.float32),
    ]
    return pl.pallas_call(
        middle_kernel,
        out_shape=[jax.ShapeDtypeStruct(*shape) for shape in shapes],
        compiler_params=pltpu.CompilerParams(vmem_limit_bytes=32 * 2**20),
        cost_estimate=SHORT,
    )(mix, out_weight, tokens, gain, router, routes)


def tokens_back_kernel(
    grad_ref, weight_ref, tokens_ref, scale_ref, gain_ref, middle_grad, out_ref, normed
):
    rows, columns = tokens_ref.shape
    for start in range(0, columns, 256):
        at = pl.ds(start, 256)
        normed[:, at] = matmul(grad_ref[...], weight_ref[at, :], LAST_WITH_LAST)
    for start in range(0, rows, HEAD_SIZE):
        at = pl.ds(start, HEAD_SIZE)
        tokens, scale, grad = tokens_ref[at, :].astype(jnp.float32), scale_ref[at, :], normed[at, :]
        scaled = grad * gain_ref[...]
        mean = jnp.mean(scaled * tokens, axis=1, keepdims=True)
        out_ref[at, :] = low(
            middle_grad[at, :] + scale * scaled - tokens * (scale**3 * mean)
        )


def tokens_back(grad_projected, qkv_weight, tokens, scale, gain, grad_middle):
    return pl.pallas_call(
        tokens_back_kernel,
        out_shape=jax.ShapeDtypeStruct(tokens.shape, jnp.bfloat16),
        scratch_shapes=[pltpu.VMEM(tokens.shape, jnp.float32)],
        compiler_params=pltpu.CompilerParams(vmem_limit_bytes=40 * 2**20),
        cost_estimate=SHORT,
    )(grad_projected, qkv_weight, tokens, scale, gain, grad_middle)


def halves_kernel(fill, core_ref, *refs):
    theirs_ref, mine_ref = refs[-2:]

    @pl.when(pl.program_id(0) == 0)
    def _():
        fill(*refs[:-2], theirs_ref)

    @pl.when(pl.program_id(0) == 1)
    def _():
        fill(*refs[:-2], mine_ref)


def in_halves(fill, core, tiled, whole, total):
    columns = tiled[0].shape[1]
    tile = columns // 4

    def chosen(half, i, core_ref):
        return jnp.where(half == 1, core_ref[0], 1 - core_ref[0]) * 2 + i

    def cut(field):
        return pl.BlockSpec(
            (field.shape[0], tile), lambda half, i, core_ref: (0, chosen(half, i, core_ref))
        )

    def kept(field):
        return pl.BlockSpec(field.shape, lambda half, i, core_ref: (0, 0))

    return pl.pallas_call(
        functools.partial(halves_kernel, fill),
        grid_spec=pltpu.PrefetchScalarGridSpec(
            num_scalar_prefetch=1,
            grid=(2, 2),
            in_specs=[cut(field) for field in tiled] + [kept(field) for field in whole],
            out_specs=[
                pl.BlockSpec((tile, total), lambda half, i, core_ref: (jnp.where(half == 0, i, 1), 0)),
                pl.BlockSpec((tile, total), lambda half, i, core_ref: (jnp.where(half == 1, i, 0), 0)),
            ],
        ),
        out_shape=[jax.ShapeDtypeStruct((columns // 2, total), jnp.bfloat16)] * 2,
        compiler_params=pltpu.CompilerParams(vmem_limit_bytes=24 * 2**20),
        cost_estimate=SHORT,
    )(core[None].astype(jnp.int32), *tiled, *whole)


def fill_product(left_ref, right_ref, out_ref):
    out_ref[...] = low(matmul(left_ref[...], right_ref[...], FIRST_WITH_FIRST))


def product(left, right, core):
    return in_halves(fill_product, core, [left], [right], right.shape[1])


def fill_out_grads(mix_ref, rows_ref, gain_ref, grad_out, logits_ref, out_ref):
    rows, width = grad_out.shape
    out_ref[:, :width] = low(matmul(mix_ref[...], grad_out[...], FIRST_WITH_FIRST))
    logits = logits_ref[...]
    experts = logits.shape[0]
    logits = jnp.concatenate([logits] + [jnp.zeros_like(logits)] * (HEAD_SIZE // experts - 1))
    small = matmul(rows_ref[:rows, :], logits, (((0,), (1,)), ((), ())))
    lane = lax.broadcasted_iota(jnp.int32, small.shape, 1)
    gain = jnp.broadcast_to(gain_ref[...], (HEAD_SIZE, small.shape[0])).T
    out_ref[:, width:] = low(jnp.where(lane == experts, gain, small))


def out_grads(mix, grad_out, unit, logits, gain, core):
    total = grad_out.shape[1] + HEAD_SIZE
    return in_halves(fill_out_grads, core, [mix, unit, gain], [grad_out, logits], total)


def finish_kernel(place_ref, own_0, got_0, own_1, got_1, weight_ref, gain_ref, out_ref, grad_ref):
    step = pl.program_id(0)

    def put(field):
        field = field[...].astype(jnp.float32)
        out_ref[...] = field
        total = jnp.sum(field * weight_ref[...].astype(jnp.float32), axis=1, keepdims=True)
        grad_ref[...] = total / gain_ref[...]

    for half, (own, got) in enumerate(((own_0, got_0), (own_1, got_1))):
        here = 2 * half + place_ref[half]
        pl.when(step == here)(functools.partial(put, own))
        pl.when(step == 4 * half + 1 - here)(functools.partial(put, got))


def finish(fields, place, weight, gain):
    dp, x, _, _ = place
    (own_0, got_0), (own_1, got_1) = fields
    rows, columns = own_0.shape
    whole = pl.BlockSpec((rows, columns), lambda i: (0, 0))
    return pl.pallas_call(
        finish_kernel,
        grid=(4,),
        in_specs=[
            pl.BlockSpec(memory_space=pltpu.SMEM),
            *[whole] * 4,
            pl.BlockSpec((rows, columns), lambda i: (i, 0)),
            pl.BlockSpec((rows, 1), lambda i: (i, 0)),
        ],
        out_specs=[
            pl.BlockSpec((rows, columns), lambda i: (i, 0)),
            pl.BlockSpec((rows, 1), lambda i: (i, 0)),
        ],
        out_shape=[
            jax.ShapeDtypeStruct((4 * rows, columns), jnp.float32),
            jax.ShapeDtypeStruct((4 * rows, 1), jnp.float32),
        ],
        compiler_params=pltpu.CompilerParams(vmem_limit_bytes=24 * 2**20),
        cost_estimate=SHORT,
    )(jnp.stack([x, dp]).astype(jnp.int32), own_0, got_0, own_1, got_1, weight, gain)


def turn(field, cosine, sine):
    half = field.shape[1] // 2
    turned = jnp.concatenate([field[:, half:], field[:, :half]], axis=1)
    return field * cosine + turned * sine


HEADS_AT_ONCE = 2


def attend_kernel(query_in, key_in, value_in, cos_ref, sin_ref, seg_row, seg_column, *refs):
    query_ref, key_ref, value_ref, mix_ref = refs
    cosine, sine = cos_ref[...], sin_ref[...]
    key = low(turn(key_in[...], cosine, sine))
    value = low(value_in[...])
    key_ref[...], value_ref[...] = key, value
    for half in range(HEADS_AT_ONCE):
        columns = slice(half * HEAD_SIZE, (half + 1) * HEAD_SIZE)
        query = low(turn(query_in[:, columns], cosine, sine))
        query_ref[:, columns] = query
        probs = probabilities(query, key, seg_row[...], seg_column[...])
        mix_ref[:, columns] = low(matmul(low(probs), value, FIRST_WITH_FIRST))


def probabilities(query, key, seg_row, seg_column):
    scores = matmul(key, query, LAST_WITH_LAST) * HEAD_SIZE ** (-0.5)
    key_at = lax.broadcasted_iota(jnp.int32, scores.shape, 0)
    query_at = lax.broadcasted_iota(jnp.int32, scores.shape, 1)
    scores = jnp.where((seg_row == seg_column) & (key_at <= query_at), scores, -1e30)
    raised = jnp.exp(scores - jnp.max(scores, axis=0, keepdims=True))
    return raised / jnp.sum(raised, axis=0, keepdims=True)


def attend(projected, cosine, sine, segment):
    rows, width = projected.shape
    groups, heads = KEY_VALUE_HEADS, QUERY_HEADS

    steps = heads // HEADS_AT_ONCE

    def one(index):
        return pl.BlockSpec((rows, HEAD_SIZE), lambda i: (0, index(i)))

    def whole(*shape):
        return pl.BlockSpec(shape, lambda i: (0, 0))

    def shape(count):
        return jax.ShapeDtypeStruct((rows, count * HEAD_SIZE), jnp.bfloat16)

    def group(i):
        return i // (steps // groups)

    head = pl.BlockSpec((rows, HEADS_AT_ONCE * HEAD_SIZE), lambda i: (0, i))
    return pl.pallas_call(
        attend_kernel,
        grid=(steps,),
        in_specs=[
            head,
            one(lambda i: heads + group(i)),
            one(lambda i: heads + groups + group(i)),
            whole(rows, HEAD_SIZE),
            whole(rows, HEAD_SIZE),
            whole(1, rows),
            whole(rows, 1),
        ],
        out_specs=[head, one(group), one(group), head],
        out_shape=[shape(heads), shape(groups), shape(groups), shape(heads)],
        compiler_params=pltpu.CompilerParams(vmem_limit_bytes=24 * 2**20),
        cost_estimate=SHORT,
    )(projected, projected, projected, cosine, sine, segment[None, :], segment[:, None])


def attend_back_kernel(
    query_ref, key_ref, value_ref, grad_ref, cos_ref, sin_ref, seg_row, seg_column, out_ref, *sums
):
    key_sum, value_sum = sums
    step = pl.program_id(0)
    heads, groups = QUERY_HEADS, KEY_VALUE_HEADS
    steps = pl.num_programs(0) // groups
    group, place = step // steps, step % steps
    key, value = key_ref[...], value_ref[...]
    cosine, sine = cos_ref[...], -sin_ref[...]

    def put(head, field):
        at = pl.multiple_of(head * HEAD_SIZE, HEAD_SIZE)
        out_ref[:, pl.ds(at, HEAD_SIZE)] = low(field)

    grad_key = grad_value = 0.0
    for half in range(HEADS_AT_ONCE):
        columns = slice(half * HEAD_SIZE, (half + 1) * HEAD_SIZE)
        query, grad_mix = query_ref[:, columns], grad_ref[:, columns]
        probs = probabilities(query, key, seg_row[...], seg_column[...])
        grad_probs = matmul(value, grad_mix, LAST_WITH_LAST)
        grad_scores = low(
            probs * (grad_probs - jnp.sum(probs * grad_probs, axis=0, keepdims=True))
        )
        grad_query = matmul(grad_scores, key, FIRST_WITH_FIRST) * HEAD_SIZE ** (-0.5)
        put(step * HEADS_AT_ONCE + half, turn(grad_query, cosine, sine))
        grad_key = grad_key + matmul(grad_scores, query) * HEAD_SIZE ** (-0.5)
        grad_value = grad_value + matmul(low(probs), grad_mix)

    @pl.when(place == 0)
    def _():
        key_sum[...] = grad_key
        value_sum[...] = grad_value

    @pl.when(place > 0)
    def _():
        key_sum[...] += grad_key
        value_sum[...] += grad_value

    @pl.when(place == steps - 1)
    def _():
        put(heads + group, turn(key_sum[...], cosine, sine))
        put(heads + groups + group, value_sum[...])


def attend_back(query, key, value, grad_mix, cosine, sine, segment):
    rows = query.shape[0]
    heads, groups = QUERY_HEADS, KEY_VALUE_HEADS
    steps = heads // HEADS_AT_ONCE

    def whole(*shape):
        return pl.BlockSpec(shape, lambda i: (0, 0))

    head = pl.BlockSpec((rows, HEADS_AT_ONCE * HEAD_SIZE), lambda i: (0, i))
    shared = pl.BlockSpec((rows, HEAD_SIZE), lambda i: (0, i // (steps // groups)))
    width = (heads + 2 * groups) * HEAD_SIZE
    return pl.pallas_call(
        attend_back_kernel,
        grid=(steps,),
        in_specs=[
            head,
            shared,
            shared,
            head,
            whole(rows, HEAD_SIZE),
            whole(rows, HEAD_SIZE),
            whole(1, rows),
            whole(rows, 1),
        ],
        out_specs=whole(rows, width),
        out_shape=jax.ShapeDtypeStruct((rows, width), jnp.bfloat16),
        scratch_shapes=[pltpu.VMEM((rows, HEAD_SIZE), jnp.float32)] * 2,
        compiler_params=pltpu.CompilerParams(vmem_limit_bytes=24 * 2**20),
        cost_estimate=SHORT,
    )(query, key, value, grad_mix, cosine, sine, segment[None, :], segment[:, None])


def ring_shards(
    hidden_in,
    cotangent,
    deal_order,
    lengths,
    routes,
    attention_gain,
    expert_gain,
    qkv_weight,
    out_weight,
    router_weight,
    gate_up_weight,
    down_weight,
):
    count_of_rows = hidden_in.shape[0]
    model_width = hidden_in.shape[1]
    half_rows = count_of_rows // 2
    expert_count = router_weight.shape[1]
    dp, core, at = lax.axis_index("dp"), lax.axis_index("shard"), lax.axis_index("expert")
    x, z = at % 2, at // 2
    place = (dp, x, z, core)
    row_ids = jnp.arange(count_of_rows, dtype=jnp.int32)

    def half_of(field, index):
        return lax.dynamic_slice_in_dim(field, index * half_rows, half_rows, axis=0)

    def sent_dealt(field):
        return half_of(field, dp), other_dp(half_of(field, 1 - dp)), field[count_of_rows:]

    def arrange(own_half, other_half, order):
        held_at = jnp.where(order[1, :count_of_rows] == dp, 0, half_rows)
        held_at = held_at + order[0, :count_of_rows].astype(jnp.int32)
        chosen = low(held_at[:, None] == row_ids[None, :])
        return low(matmul(chosen, jnp.concatenate([own_half, other_half], axis=0)))

    def swapped(field):
        return field, other_core(field)

    def to_dealt(field):
        held_at = jnp.where(deal_order[0] // half_rows == dp, 0, half_rows)
        held_at = held_at + deal_order[0] % half_rows
        chosen = low(held_at[None, :] == row_ids[:, None])
        field = low(matmul(chosen, field))
        return in_order(dp == 0, field[:half_rows], other_dp(field[half_rows:]))

    order = jnp.concatenate([deal_order % half_rows, deal_order // half_rows])
    order = jnp.pad(low(order), ((0, EXTRA - 2), (0, model_width - count_of_rows)))
    ct_0 = jnp.concatenate([cotangent, order])
    ct_1 = ring_z(ct_0)
    hidden_out = half_of(after(hidden_in, ct_0), 1 - dp)
    hidden_arrived = other_dp(hidden_out)
    qkv_other, out_other, up_other = (
        send(after(field, hidden_out))
        for send, field in (
            (other_core, qkv_weight),
            (other_core, out_weight),
            (from_owner, gate_up_weight[0]),
        )
    )
    small = jnp.concatenate(
        [router_weight.T, attention_gain[None], expert_gain[None], jnp.zeros_like(router_weight.T[:6])]
    )
    small = in_order(core == 0, small, other_core(small), axis=1)
    router = small[:expert_count]
    gain_first = small[expert_count : expert_count + 1].astype(jnp.float32)
    gain_second = small[expert_count + 1 : expert_count + 2].astype(jnp.float32)
    full_qkv = in_order(core == 0, qkv_weight, qkv_other)
    segment, token_position = positions_of(lengths[0], count_of_rows)
    frequency = THETA ** (-jnp.arange(HEAD_SIZE // 2, dtype=jnp.float32) / (HEAD_SIZE // 2))
    angles = token_position.astype(jnp.float32)[:, None] * frequency[None, :]
    cosine = jnp.concatenate([jnp.cos(angles)] * 2, axis=1)
    sine = jnp.concatenate([-jnp.sin(angles), jnp.sin(angles)], axis=1)
    cosine, sine, full_qkv, hidden_arrived, gain_first, gain_second, router, routes = part(
        cosine, sine, full_qkv, hidden_arrived, gain_first, gain_second, router, routes.T
    )
    tokens = arrange(half_of(hidden_in, dp), hidden_arrived, order)
    residual = tokens.astype(jnp.float32)
    inv_first = lax.rsqrt(jnp.mean(residual * residual, axis=1, keepdims=True) + EPS)
    normed_attn = low(residual * inv_first * gain_first)
    projected = matmul(normed_attn, full_qkv)
    ct_1, projected, ct_0, out_other, down_own = part(
        ct_1, projected, ct_0, out_other, down_weight[0]
    )

    ct_2 = ring_z(ct_1)
    ct_0 = sent_dealt(ct_0)
    down_other = from_owner(down_own)
    full_out = in_order(core == 0, out_weight, out_other)
    query, key, value, attn_mix = attend(projected, cosine, sine, segment)
    middle, inv_second, unit_0, gates = middle_of(
        attn_mix, full_out, tokens, gain_second, router, routes
    )
    ct_2, ct_0, ct_1, unit_0, up_other = part(ct_2, ct_0, ct_1, unit_0, up_other)

    normed_1 = ring_z(unit_0)
    normed_0 = swapped(unit_0)
    ct_1 = sent_dealt(ct_1)
    ct_0 = swapped(arrange(*ct_0))
    normed_1, normed_0, ct_0, ct_1, ct_2, down_other = part(
        normed_1, normed_0, ct_0, ct_1, ct_2, down_other
    )
    choice = jnp.stack([(core == x).astype(jnp.int32), (2 * z + core).astype(jnp.int32)])
    matrices = (gate_up_weight[0], up_other, down_weight[0], down_other)

    ct_3 = ring_z(ct_2)
    ct_2 = sent_dealt(ct_2)
    ct_1, normed_1 = swapped(arrange(*ct_1)), swapped(normed_1)
    sums_0, back_0, kept = expert_step(0, choice, normed_0, ct_0, matrices, None)
    ct_3, ct_1, normed_1, ct_2, kept = part(ct_3, ct_1, normed_1, ct_2, kept)

    normed_2 = ring_z(normed_1[0])
    ct_3 = sent_dealt(ct_3)
    ct_2 = swapped(arrange(*ct_2))
    sums_1, back_1, kept = expert_step(1, choice, normed_1, ct_1, matrices, kept)
    normed_2, ct_3, ct_2, back_1, kept = part(normed_2, ct_3, ct_2, back_1, kept)

    normed_3 = ring_z(normed_2)
    normed_2, back_1_other = swapped(normed_2), other_core(back_1[1])
    ct_3 = swapped(arrange(*ct_3))
    sums_2, back_2, kept = expert_step(2, choice, normed_2, ct_2, matrices, kept)
    back_1 = low(sum_blocks(back_1[0], back_1_other))
    normed_3, back_1, ct_3, back_2, kept = part(normed_3, back_1, ct_3, back_2, kept)

    back_1 = ring_z(back_1)
    normed_3, back_2_other = swapped(normed_3), other_core(back_2[1])
    sums_3, back_3, kept = expert_step(3, choice, normed_3, ct_3, matrices, kept)
    back_1, back_2_other, back_3, kept = part(back_1, back_2_other, back_3, kept)

    back_2 = ring_z(low(sum_blocks(back_2[0], back_2_other, back_1)))
    back_3_other, back_0_other = other_core(back_3[1]), other_core(back_0[1])
    sums_1_other = other_core(sums_1[1])
    all_hidden, all_grad_out, all_grad_up, all_rows = kept
    half_width = model_width // 2
    up_first = low(matmul(all_rows.T, all_grad_up[:, :half_width]))
    up_second = low(matmul(all_rows.T, all_grad_up[:, half_width:]))
    back_2, back_3_other, back_0_other, sums_1_other, up_first, up_second, all_grad_out = part(
        back_2, back_3_other, back_0_other, sums_1_other, up_first, up_second, all_grad_out
    )

    back_3 = ring_z(low(sum_blocks(back_3[0], back_3_other, back_2)))
    down_first = low(matmul(all_hidden.T, all_grad_out[:, :half_width]))
    down_second = low(matmul(all_hidden.T, all_grad_out[:, half_width:]))
    sums_1 = low(sum_blocks(sums_1[0], sums_1_other))
    sums_2_other = other_core(sums_2[1])
    back_3, up_first, up_second, down_first, down_second, sums_1, sums_2_other = part(
        back_3, up_first, up_second, down_first, down_second, sums_1, sums_2_other
    )

    sums_1 = ring_z(sums_1)
    up_first = up_first, to_owner(up_first)
    up_second = block(up_second, dp, 2), other_dp(block(up_second, 1 - dp, 2))
    sums_3_other = other_core(sums_3[1])
    grad_middle, grad_attn_out, grad_mix, term_gain_second, grad_logits = middle_back(
        (back_0[0], back_0_other, back_3),
        gates,
        router,
        middle,
        inv_second,
        gain_second,
        ct_0[0],
        full_out,
    )
    out = out_grads(attn_mix, grad_attn_out, unit_0, grad_logits, term_gain_second, core)
    grad_projected = attend_back(query, key, value, grad_mix, cosine, sine, segment)
    qkv = product(normed_attn, grad_projected, core)
    sums_1, sums_3_other, out, qkv, grad_projected, up_first, up_second = part(
        sums_1, sums_3_other, out, qkv, grad_projected, up_first, up_second
    )

    sums_2 = ring_z(low(sum_blocks(sums_2[0], sums_2_other, sums_1)))
    out, qkv = chip_send(*out), chip_send(*qkv)
    down_first = down_first, to_owner(down_first)
    down_second = block(down_second, dp, 2), other_dp(block(down_second, 1 - dp, 2))
    up_first, up_second = low(sum_blocks(*up_first)), low(sum_blocks(*up_second))
    sums_2, out, qkv, down_first, down_second, up_first, up_second, grad_projected = part(
        sums_2, out, qkv, down_first, down_second, up_first, up_second, grad_projected
    )

    sums_3 = ring_z(low(sum_blocks(sums_3[0], sums_3_other, sums_2)))
    out = slab_send(out, place)
    up_first = block(up_first, dp, 2), owners_dp(block(up_first, 1 - dp, 2))
    up_second = up_second, to_owner(up_second)
    qkv = low(sum_blocks(*qkv))
    down_first, down_second = low(sum_blocks(*down_first)), low(sum_blocks(*down_second))
    grad_tokens = tokens_back(
        grad_projected, full_qkv, tokens, inv_first, gain_first, grad_middle
    )
    sums_3, out, qkv, up_first, up_second, down_first, down_second, grad_tokens = part(
        sums_3, out, qkv, up_first, up_second, down_first, down_second, grad_tokens
    )

    out = slab_send_on(out, place)
    down_first = block(down_first, dp, 2), owners_dp(block(down_first, 1 - dp, 2))
    down_second = down_second, to_owner(down_second)
    sums_0_other = other_core(sums_0[1])
    up_grad = low(jnp.concatenate([sum_blocks(*up_first), sum_blocks(*up_second)], axis=1))
    out, qkv, down_first, down_second, sums_0_other, up_grad, grad_tokens = part(
        out, qkv, down_first, down_second, sums_0_other, up_grad, grad_tokens
    )

    out, qkv = line_send(out, z), slab_send((qkv,), place)
    layer_out = low(middle + sum_blocks(sums_0[0], sums_0_other, sums_3))
    down_grad = low(jnp.concatenate([sum_blocks(*down_first), sum_blocks(*down_second)], axis=1))
    out, qkv, layer_out, down_grad, grad_tokens, up_grad = part(
        out, qkv, layer_out, down_grad, grad_tokens, up_grad
    )

    out, qkv = line_spread(out), slab_send_on(qkv, place)
    layer_out = to_dealt(layer_out)
    out, qkv, layer_out, grad_tokens, up_grad = part(out, qkv, layer_out, grad_tokens, up_grad)

    out, qkv = slab_spread(out, z), line_send(qkv, z)
    input_gradient = to_dealt(grad_tokens)
    out, qkv, input_gradient, up_grad, down_grad = part(
        out, qkv, input_gradient, up_grad, down_grad
    )

    out, qkv = slab_spread_on(out, place), line_spread(qkv)
    up_grad = up_grad, other_core(block(up_grad, 1 - core, 2))
    out, qkv, up_grad, down_grad = part(out, qkv, up_grad, down_grad)

    qkv = slab_spread(qkv, z)
    down_grad = down_grad, other_core(block(down_grad, 1 - core, 2))
    out = whole_of(out, place).astype(jnp.float32)
    qkv, out, up_grad, down_grad = part(qkv, out, up_grad, down_grad)
    qkv = slab_spread_on(qkv, place)
    gate_up_grad, down_grad = (
        jnp.where(core == x, block(field, core, 2), received)[None].astype(jnp.float32)
        for field, received in (up_grad, down_grad)
    )
    gain = attention_gain.astype(jnp.float32)[:, None]
    qkv_grad, gain_first_grad = finish(qkv, place, qkv_weight, gain)
    return (
        layer_out,
        input_gradient,
        gain_first_grad[:, 0],
        out[:, model_width + expert_count],
        qkv_grad,
        out[:, :model_width],
        out[:, model_width : model_width + expert_count],
        gate_up_grad,
        down_grad,
    )


def solution(mesh):
    ringed = (mesh.shape["dp"], mesh.shape["expert"], mesh.shape["shard"]) == (2, 8, 2)
    shards = ring_shards if ringed else routed_shards
    return jax.shard_map(
        shards,
        mesh=mesh,
        in_specs=(
            P(("dp", "expert", "shard"), None),
            P(("dp", "expert", "shard"), None),
            P(("dp", "expert", "shard"), None),
            P(("dp", "expert", "shard"), None),
            P(("dp", "expert", "shard"), None),
            P("shard"),
            P("shard"),
            P("shard", None),
            P("shard", None),
            P("shard", None),
            P("expert", None, None),
            P("expert", None, None),
        ),
        out_specs=(
            P(("dp", "expert", "shard"), None),
            P(("dp", "expert", "shard"), None),
            P("shard"),
            P("shard"),
            P("shard", None),
            P("shard", None),
            P("shard", None),
            P("expert", ("dp", "shard"), None),
            P("expert", ("dp", "shard"), None),
        ),
        check_vma=False,
    )
```

```python
import functools

import jax
import jax.numpy as jnp
from jax import lax
from jax.experimental import pallas as pl
from jax.experimental.pallas import tpu as pltpu
from jax.sharding import PartitionSpec as P

QUERY_HEADS = 12
KEY_VALUE_HEADS = 2
HEAD_SIZE = 128
TOP = 4


EPS = 1e-06
THETA = 1000000.0


def positions_of(lengths_dev, count_of_rows):
    seq_ends = jnp.cumsum(lengths_dev)
    starts = seq_ends - lengths_dev
    places = jnp.arange(count_of_rows, dtype=jnp.int32)
    segment = jnp.sum((places[:, None] >= seq_ends[None, :]).astype(jnp.int32), axis=1)
    member = segment[:, None] == jnp.arange(lengths_dev.shape[0], dtype=jnp.int32)[None, :]
    start_of = jnp.sum(jnp.where(member, starts[None, :], 0), axis=1)
    return (segment, places - start_of)


def apply_rotation(field, token_position, direction):
    half_dim = field.shape[-1] // 2
    frequency = THETA ** (-jnp.arange(half_dim, dtype=jnp.float32) / half_dim)
    angles = token_position.astype(jnp.float32)[:, None] * frequency[None, :]
    cosine = jnp.cos(angles)[:, None, :]
    sine_term = direction * jnp.sin(angles)[:, None, :]
    lead_part = field[..., :half_dim]
    tail_part = field[..., half_dim:]
    return jnp.concatenate(
        [lead_part * cosine - tail_part * sine_term, tail_part * cosine + lead_part * sine_term],
        axis=-1,
    )


def masked_scores(query_block, key_matrix_rows, segment_block, segment, row_start):
    raw_scores = jnp.einsum(
        "ihgd,jhd->hgij", query_block, key_matrix_rows, preferred_element_type=jnp.float32
    ) * HEAD_SIZE ** (-0.5)
    query_at = row_start + jnp.arange(query_block.shape[0], dtype=jnp.int32)
    key_at = jnp.arange(key_matrix_rows.shape[0], dtype=jnp.int32)
    allowed = (segment_block[:, None] == segment[None, :]) & (key_at[None, :] <= query_at[:, None])
    return jnp.where(allowed, raw_scores, -1e30)


def norm_back(field, inv_scale, gain_vec, grad_normed):
    scaled = grad_normed * gain_vec
    grad_field = inv_scale * scaled - field * inv_scale**3 * jnp.mean(
        scaled * field, axis=1, keepdims=True
    )
    grad_gain = jnp.sum(field * inv_scale * grad_normed, axis=0)
    return (grad_field, grad_gain)


def activate(gate_up):
    hidden_width = gate_up.shape[1] // 2
    return jax.nn.gelu(gate_up[:, :hidden_width], approximate=True) * gate_up[:, hidden_width:]


def routed_shards(
    hidden_in,
    cotangent,
    deal_order,
    lengths,
    routes,
    attention_gain,
    expert_gain,
    qkv_weight,
    out_weight,
    router_weight,
    gate_up_weight,
    down_weight,
):
    count_of_rows = hidden_in.shape[0]
    model_width = hidden_in.shape[1]
    head_groups = QUERY_HEADS // KEY_VALUE_HEADS
    arrived_in, arrived_ct = (
        lax.all_to_all(hidden_in, "dp", split_axis=0, concat_axis=0, tiled=True),
        lax.all_to_all(cotangent, "dp", split_axis=0, concat_axis=0, tiled=True),
    )
    deal_rows = deal_order[0]
    tokens = arrived_in[deal_rows]
    upstream = arrived_ct[deal_rows].astype(jnp.float32)
    gain_first, gain_second, full_qkv, full_out, full_router = (
        lax.all_gather(attention_gain, "shard", axis=0, tiled=True),
        lax.all_gather(expert_gain, "shard", axis=0, tiled=True),
        lax.all_gather(qkv_weight, "shard", axis=0, tiled=True),
        lax.all_gather(out_weight, "shard", axis=0, tiled=True),
        lax.all_gather(router_weight, "shard", axis=0, tiled=True),
    )
    gain_first = gain_first.astype(jnp.float32)
    gain_second = gain_second.astype(jnp.float32)
    residual = tokens.astype(jnp.float32)
    inv_first = lax.rsqrt(jnp.mean(residual * residual, axis=1, keepdims=True) + EPS)
    normed_attn = (residual * inv_first * gain_first).astype(jnp.bfloat16)
    projected_rows = jnp.dot(normed_attn, full_qkv, preferred_element_type=jnp.float32)
    segment, token_position = positions_of(lengths[0], count_of_rows)
    query_matrix_rows = (
        apply_rotation(
            projected_rows[:, : QUERY_HEADS * HEAD_SIZE].reshape(
                count_of_rows, QUERY_HEADS, HEAD_SIZE
            ),
            token_position,
            1.0,
        )
        .astype(jnp.bfloat16)
        .reshape(count_of_rows, KEY_VALUE_HEADS, head_groups, HEAD_SIZE)
    )
    key_matrix_rows = apply_rotation(
        projected_rows[
            :, QUERY_HEADS * HEAD_SIZE : (QUERY_HEADS + KEY_VALUE_HEADS) * HEAD_SIZE
        ].reshape(count_of_rows, KEY_VALUE_HEADS, HEAD_SIZE),
        token_position,
        1.0,
    ).astype(jnp.bfloat16)
    value_matrix_rows = (
        projected_rows[:, (QUERY_HEADS + KEY_VALUE_HEADS) * HEAD_SIZE :]
        .reshape(count_of_rows, KEY_VALUE_HEADS, HEAD_SIZE)
        .astype(jnp.bfloat16)
    )
    block_rows = min(count_of_rows, 512)
    block_starts = jnp.arange(count_of_rows // block_rows, dtype=jnp.int32) * block_rows

    def forward_block(row_start):
        scores = masked_scores(query_matrix_rows, key_matrix_rows, segment, segment, row_start)
        row_max = jnp.max(scores, axis=-1, keepdims=True)
        exp_scores = jnp.exp(scores - row_max)
        exp_total = jnp.sum(exp_scores, axis=-1, keepdims=True)
        soft_probs = (exp_scores / exp_total).astype(jnp.bfloat16)
        mix_block = jnp.einsum(
            "hgij,jhd->ihgd", soft_probs, value_matrix_rows, preferred_element_type=jnp.float32
        )
        return (mix_block, (row_max + jnp.log(exp_total))[..., 0])

    mix_blocks, logsum = lax.map(forward_block, block_starts)
    attn_mix = mix_blocks.reshape(count_of_rows, QUERY_HEADS * HEAD_SIZE).astype(jnp.bfloat16)
    middle = residual + jnp.dot(attn_mix, full_out, preferred_element_type=jnp.float32)
    inv_second = lax.rsqrt(jnp.mean(middle * middle, axis=1, keepdims=True) + EPS)
    normed_moe = (middle * inv_second * gain_second).astype(jnp.bfloat16)
    logits = jnp.dot(normed_moe, full_router, preferred_element_type=jnp.float32)
    gate_probs = jax.nn.softmax(jnp.take_along_axis(logits, routes, axis=1), axis=-1)
    expert_count = full_router.shape[1]
    peer_count = lax.axis_size("expert")
    capacity = min(count_of_rows, max(2, 3 * count_of_rows * TOP // (2 * expert_count)))
    flat_routes = routes.reshape(-1)
    expert_ids = jnp.arange(expert_count, dtype=jnp.int32)
    onehot = (flat_routes[:, None] == expert_ids[None, :]).astype(jnp.int32)
    slot_rank = jnp.sum(jnp.cumsum(onehot, axis=0) * onehot, axis=1) - 1
    target = flat_routes * capacity + slot_rank
    pair_count = count_of_rows * TOP
    slot_pair = (
        jnp.full((expert_count * capacity,), pair_count, jnp.int32)
        .at[target]
        .set(jnp.arange(pair_count, dtype=jnp.int32))
    )
    padded = jnp.concatenate([normed_moe, jnp.zeros((1, model_width), jnp.bfloat16)], axis=0)
    sending = padded[slot_pair // TOP].reshape(peer_count, capacity, model_width)
    received = lax.all_to_all(sending, "expert", split_axis=0, concat_axis=0, tiled=True)
    rows_in = received.reshape(peer_count * capacity, model_width)
    gate_up = jnp.dot(rows_in, gate_up_weight[0], preferred_element_type=jnp.float32)
    hidden_rows = activate(gate_up).astype(jnp.bfloat16)
    expert_out = jnp.dot(hidden_rows, down_weight[0], preferred_element_type=jnp.float32).astype(
        jnp.bfloat16
    )
    returned = lax.all_to_all(
        expert_out.reshape(peer_count, capacity, model_width),
        "expert",
        split_axis=0,
        concat_axis=0,
        tiled=True,
    )
    per_pair = returned.reshape(peer_count * capacity, model_width)[target].reshape(
        count_of_rows, TOP, model_width
    )
    expert_sum = jnp.zeros((count_of_rows, model_width), jnp.float32)
    for choice_slot in range(TOP):
        expert_sum = expert_sum + gate_probs[:, choice_slot : choice_slot + 1] * per_pair[
            :, choice_slot
        ].astype(jnp.float32)
    final_rows = middle + expert_sum
    grad_pairs = (gate_probs[:, :, None] * upstream[:, None, :]).astype(jnp.bfloat16)
    grad_gates = jnp.stack(
        [
            jnp.sum(per_pair[:, choice_slot].astype(jnp.float32) * upstream, axis=1)
            for choice_slot in range(TOP)
        ],
        axis=1,
    )
    padded_grad = jnp.concatenate(
        [grad_pairs.reshape(pair_count, model_width), jnp.zeros((1, model_width), jnp.bfloat16)],
        axis=0,
    )
    sending_back = padded_grad[slot_pair].reshape(peer_count, capacity, model_width)
    grad_rows = lax.all_to_all(
        sending_back, "expert", split_axis=0, concat_axis=0, tiled=True
    ).reshape(peer_count * capacity, model_width)
    grad_hidden = jnp.dot(grad_rows, down_weight[0].T, preferred_element_type=jnp.float32)
    grad_gate_up = jax.vjp(activate, gate_up)[1](grad_hidden)[0].astype(jnp.bfloat16)
    term_down = jnp.dot(hidden_rows.T, grad_rows, preferred_element_type=jnp.float32)
    term_gate_up = jnp.dot(rows_in.T, grad_gate_up, preferred_element_type=jnp.float32)
    grad_rows_in = jnp.dot(
        grad_gate_up, gate_up_weight[0].T, preferred_element_type=jnp.float32
    ).astype(jnp.bfloat16)
    back_rows = lax.all_to_all(
        grad_rows_in.reshape(peer_count, capacity, model_width),
        "expert",
        split_axis=0,
        concat_axis=0,
        tiled=True,
    )
    back_pairs = back_rows.reshape(peer_count * capacity, model_width)[target].reshape(
        count_of_rows, TOP, model_width
    )
    grad_normed = jnp.zeros((count_of_rows, model_width), jnp.float32)
    for choice_slot in range(TOP):
        grad_normed = grad_normed + back_pairs[:, choice_slot].astype(jnp.float32)
    mean_term = jnp.sum(gate_probs * grad_gates, axis=1, keepdims=True)
    grad_chosen = gate_probs * (grad_gates - mean_term)
    grad_logits = jnp.sum(
        jnp.where(routes[:, :, None] == expert_ids[None, None, :], grad_chosen[:, :, None], 0.0),
        axis=1,
    ).astype(jnp.bfloat16)
    term_router = jnp.dot(normed_moe.T, grad_logits, preferred_element_type=jnp.float32)
    grad_normed = grad_normed + jnp.dot(
        grad_logits, full_router.T, preferred_element_type=jnp.float32
    )
    grad_middle_norm, term_gain_second = norm_back(middle, inv_second, gain_second, grad_normed)
    grad_middle = upstream + grad_middle_norm
    grad_attn_out = grad_middle.astype(jnp.bfloat16)
    term_out = jnp.dot(attn_mix.T, grad_attn_out, preferred_element_type=jnp.float32)
    grad_mix = (
        jnp.dot(grad_attn_out, full_out.T, preferred_element_type=jnp.float32)
        .astype(jnp.bfloat16)
        .reshape(count_of_rows, KEY_VALUE_HEADS, head_groups, HEAD_SIZE)
    )

    def backward_block(accums, inputs):
        acc_key, value_accumulator = accums
        row_start, logsum_block = inputs
        scores = masked_scores(query_matrix_rows, key_matrix_rows, segment, segment, row_start)
        soft_probs = jnp.exp(scores - logsum_block[..., None])
        grad_probs = jnp.einsum(
            "ihgd,jhd->hgij", grad_mix, value_matrix_rows, preferred_element_type=jnp.float32
        )
        value_accumulator = value_accumulator + jnp.einsum(
            "hgij,ihgd->jhd",
            soft_probs.astype(jnp.bfloat16),
            grad_mix,
            preferred_element_type=jnp.float32,
        )
        grad_scores = (
            soft_probs * (grad_probs - jnp.sum(soft_probs * grad_probs, axis=-1, keepdims=True))
        ).astype(jnp.bfloat16)
        grad_query = HEAD_SIZE ** (-0.5) * jnp.einsum(
            "hgij,jhd->ihgd", grad_scores, key_matrix_rows, preferred_element_type=jnp.float32
        )
        acc_key = acc_key + HEAD_SIZE ** (-0.5) * jnp.einsum(
            "hgij,ihgd->jhd", grad_scores, query_matrix_rows, preferred_element_type=jnp.float32
        )
        return ((acc_key, value_accumulator), grad_query)

    zero_key_value = jnp.zeros((count_of_rows, KEY_VALUE_HEADS, HEAD_SIZE), jnp.float32)
    (acc_key, value_accumulator), grad_query = lax.scan(
        backward_block, (zero_key_value, zero_key_value), (block_starts, logsum)
    )
    grad_query = apply_rotation(
        grad_query.reshape(count_of_rows, QUERY_HEADS, HEAD_SIZE), token_position, -1.0
    )
    key_gradient = apply_rotation(acc_key, token_position, -1.0)
    grad_projected = jnp.concatenate(
        [
            grad_query.reshape(count_of_rows, QUERY_HEADS * HEAD_SIZE),
            key_gradient.reshape(count_of_rows, KEY_VALUE_HEADS * HEAD_SIZE),
            value_accumulator.reshape(count_of_rows, KEY_VALUE_HEADS * HEAD_SIZE),
        ],
        axis=1,
    ).astype(jnp.bfloat16)
    term_qkv = jnp.dot(normed_attn.T, grad_projected, preferred_element_type=jnp.float32)
    grad_normed_attn = jnp.dot(grad_projected, full_qkv.T, preferred_element_type=jnp.float32)
    grad_resid_norm, term_gain_first = norm_back(residual, inv_first, gain_first, grad_normed_attn)
    grad_tokens = (grad_middle + grad_resid_norm).astype(jnp.bfloat16)
    inverse = (
        jnp.zeros((count_of_rows,), jnp.int32)
        .at[deal_rows]
        .set(jnp.arange(count_of_rows, dtype=jnp.int32))
    )
    layer_out, input_gradient = (
        lax.all_to_all(
            final_rows.astype(jnp.bfloat16)[inverse], "dp", split_axis=0, concat_axis=0, tiled=True
        ),
        lax.all_to_all(grad_tokens[inverse], "dp", split_axis=0, concat_axis=0, tiled=True),
    )
    shard_terms = (
        lax.psum_scatter(
            term_gain_first.astype(jnp.bfloat16), "shard", scatter_dimension=0, tiled=True
        ).astype(jnp.float32),
        lax.psum_scatter(
            term_gain_second.astype(jnp.bfloat16), "shard", scatter_dimension=0, tiled=True
        ).astype(jnp.float32),
        lax.psum_scatter(
            term_qkv.astype(jnp.bfloat16), "shard", scatter_dimension=0, tiled=True
        ).astype(jnp.float32),
        lax.psum_scatter(
            term_out.astype(jnp.bfloat16), "shard", scatter_dimension=0, tiled=True
        ).astype(jnp.float32),
        lax.psum_scatter(
            term_router.astype(jnp.bfloat16), "shard", scatter_dimension=0, tiled=True
        ).astype(jnp.float32),
    )
    gain_first_grad, gain_second_grad, qkv_grad, out_grad, router_grad = lax.psum(
        (shard_terms[0], shard_terms[1], shard_terms[2], shard_terms[3], shard_terms[4]),
        ("dp", "expert"),
    )
    gate_up_grad, down_grad = (
        lax.psum_scatter(
            term_gate_up[None].astype(jnp.bfloat16),
            ("dp", "shard"),
            scatter_dimension=1,
            tiled=True,
        ).astype(jnp.float32),
        lax.psum_scatter(
            term_down[None].astype(jnp.bfloat16), ("dp", "shard"), scatter_dimension=1, tiled=True
        ).astype(jnp.float32),
    )
    return (
        layer_out,
        input_gradient,
        gain_first_grad,
        gain_second_grad,
        qkv_grad,
        out_grad,
        router_grad,
        gate_up_grad,
        down_grad,
    )


RING_NEXT = (1, 3, 0, 2)
LAST_WITH_LAST = (((1,), (1,)), ((), ()))


def after(value, *earlier):
    return lax.optimization_barrier((value, *earlier))[0]


def part(*fields):
    return lax.optimization_barrier(fields)


def other_core(field):
    return lax.ppermute(field, "shard", [(0, 1), (1, 0)])


def other_dp(field):
    return lax.ppermute(field, "dp", [(0, 1), (1, 0)])


def owners_dp(field):
    pairs = [
        ((d * 8 + e) * 2 + e % 2, ((1 - d) * 8 + e) * 2 + e % 2) for d in range(2) for e in range(8)
    ]
    return lax.ppermute(field, ("dp", "expert", "shard"), pairs)


def across_x(field):
    return lax.ppermute(field, "expert", [(i, i ^ 1) for i in range(8)])


def across_dp_x(field):
    pairs = [(d * 8 + e, (1 - d) * 8 + (e ^ 1)) for d in range(2) for e in range(8)]
    return lax.ppermute(field, ("dp", "expert"), pairs)


def across_z(field, distance):
    return lax.ppermute(field, "expert", [(i, i ^ (2 * distance)) for i in range(8)])


def ring_z(field):
    pairs = [(2 * z + x, 2 * RING_NEXT[z] + x) for z in range(4) for x in range(2)]
    return lax.ppermute(field, "expert", pairs)


def to_owner(field):
    pairs = [(e * 2 + c, (e ^ 1) * 2 + c) for e in range(8) for c in range(2) if e % 2 != c]
    return lax.ppermute(field, ("expert", "shard"), pairs)


def from_owner(field):
    pairs = [(e * 2 + c, (e ^ 1) * 2 + c) for e in range(8) for c in range(2) if e % 2 == c]
    return lax.ppermute(field, ("expert", "shard"), pairs)


def in_order(first, own, received, axis=0):
    return jnp.where(
        first,
        jnp.concatenate([own, received], axis=axis),
        jnp.concatenate([received, own], axis=axis),
    )


def block(field, index, count):
    rows = field.shape[0] // count
    return lax.dynamic_slice_in_dim(field, index * rows, rows, axis=0)


def sum_blocks(*fields):
    total = fields[0].astype(jnp.float32)
    for field in fields[1:]:
        total = total + field.astype(jnp.float32)
    return total


def low(field):
    return field.astype(jnp.bfloat16)


def slab_cut(first, second, at, other):
    return (
        (block(first, at, 2), block(first, 1 - at, 2)),
        (block(second, other, 2), block(second, 1 - other, 2)),
    )


def slab_sum(cuts, place):
    dp, x, _, _ = place
    (first, first_out), (second, second_out) = cuts
    first = low(sum_blocks(first, across_x(first_out)))
    second = low(sum_blocks(second, other_dp(second_out)))
    return slab_cut(first, second, dp, x)


def slab_sum_on(cuts, place):
    z = place[2]
    (first, first_out), (second, second_out) = cuts
    first = sum_blocks(first, other_dp(first_out))
    second = sum_blocks(second, across_x(second_out))
    part = low(jnp.concatenate([first, second]))
    return [block(part, z ^ k, 4) for k in range(4)]


def line_sum(cuts):
    return low(sum_blocks(cuts[0], *[across_z(cuts[k], k) for k in (1, 2, 3)]))


def put_in_order(pieces, own):
    stacked = jnp.stack(pieces)
    return jnp.concatenate(
        [lax.dynamic_index_in_dim(stacked, own ^ b, 0, False) for b in range(len(pieces))]
    )


def line_spread(part, place):
    part = put_in_order([part] + [across_z(part, k) for k in (1, 2, 3)], place[2])
    return jnp.split(part, 2)


def slab_spread(halves, place):
    dp, x, _, _ = place
    first, second = halves
    return in_order(dp == 0, first, other_dp(first)), in_order(x == 0, second, across_x(second))


def slab_spread_on(halves):
    first, second = halves
    return (first, across_x(first)), (second, other_dp(second))


def matmul(left, right, dims=(((1,), (0,)), ((), ()))):
    return lax.dot_general(left, right, dims, preferred_element_type=jnp.float32)


FIRST_WITH_FIRST = (((0,), (0,)), ((), ()))


EXTRA = 16


def packed(field, columns):
    high = low(field)
    rest = low(field - high.astype(jnp.float32))
    pad = jnp.zeros((field.shape[0], columns - 2 * field.shape[1]), jnp.bfloat16)
    block = jnp.concatenate([high, rest, pad], axis=1)
    return jnp.concatenate([block, jnp.zeros((EXTRA - field.shape[0], columns), jnp.bfloat16)])


def unpacked(extra, rows):
    field = extra.astype(jnp.float32)[: EXTRA // 2]
    return field[:, :rows] + field[:, rows : 2 * rows]


def expert_kernel(
    choice,
    own_rows,
    other_rows,
    own_ct,
    other_ct,
    up_own,
    up_other,
    down_own,
    down_other,
    *refs,
    columns,
):
    (
        own_sum,
        other_sum,
        own_back,
        other_back,
        hidden_ref,
        grad_out_ref,
        grad_up_ref,
        rows_ref,
        unit_ref,
        ct_ref,
        up_ref,
        down_ref,
        up_sem,
        down_sem,
    ) = refs[-14:]
    width = down_ref.shape[0]
    first = pl.program_id(0) == 0

    @pl.when(first & (choice[0] == 1))
    def _():
        pltpu.make_async_copy(up_own, up_ref, up_sem).start()
        pltpu.make_async_copy(down_own, down_ref, down_sem).start()

    @pl.when(first & (choice[0] == 0))
    def _():
        pltpu.make_async_copy(up_other, up_ref, up_sem).start()
        pltpu.make_async_copy(down_other, down_ref, down_sem).start()

    @pl.when(first)
    def _():
        unit_ref[...] = own_rows[...]
        ct_ref[...] = own_ct[...]
        pltpu.make_async_copy(up_own, up_ref, up_sem).wait()
        pltpu.make_async_copy(down_own, down_ref, down_sem).wait()

    @pl.when(pl.program_id(0) == 1)
    def _():
        unit_ref[...] = other_rows[...]
        ct_ref[...] = other_ct[...]

    count = ct_ref.shape[0]
    rows = unit_ref[:count, :]
    rows_ref[...] = rows
    gates = unpacked(unit_ref[count:, :], count)
    mine = lax.broadcasted_iota(jnp.int32, gates.shape, 0) == choice[1]
    weighting = jnp.sum(jnp.where(mine, gates, 0.0), axis=0, keepdims=True)
    weighting = jnp.broadcast_to(weighting, (HEAD_SIZE, rows.shape[0])).T[:, :1]
    ct = ct_ref[...].astype(jnp.float32)
    grad_out = low(weighting * ct)
    grad_out_ref[...] = grad_out
    for start in range(0, width, columns):
        gate, up = pl.ds(start, columns), pl.ds(width + start, columns)
        a, b = matmul(rows, up_ref[:, gate]), matmul(rows, up_ref[:, up])
        tanh = jnp.tanh(0.7978845608028654 * (a + 0.044715 * a * a * a))
        half = 0.5 * (1.0 + tanh)
        gelu = a * half
        hidden_ref[:, gate] = low(gelu * b)
        grad_hidden = matmul(grad_out, down_ref[gate, :], LAST_WITH_LAST)
        slope = half + 0.5 * a * (1.0 - tanh * tanh) * (
            0.7978845608028654 * (1.0 + 3.0 * 0.044715 * a * a)
        )
        grad_up_ref[:, gate] = low(grad_hidden * b * slope)
        grad_up_ref[:, up] = low(grad_hidden * gelu)
    out = low(matmul(hidden_ref[...], down_ref[...])).astype(jnp.float32)
    grad = jnp.sum(ct * out, axis=1, keepdims=True)
    grad = jnp.broadcast_to(grad, (rows.shape[0], HEAD_SIZE)).T[: mine.shape[0], :]
    grad = packed(jnp.where(mine, grad, 0.0), rows.shape[1])
    weighted = low(weighting * out)
    back = low(matmul(grad_up_ref[...], up_ref[...], LAST_WITH_LAST))

    @pl.when(pl.program_id(0) == 0)
    def _():
        own_sum[...], own_back[:count, :], own_back[count:, :] = weighted, back, grad

    @pl.when(pl.program_id(0) == 1)
    def _():
        other_sum[...], other_back[:count, :], other_back[count:, :] = weighted, back, grad


SHORT = pl.CostEstimate(flops=1000, bytes_accessed=1000, transcendentals=0)


def expert_step(step, choice, rows, upstream, matrices, kept):
    tile, model_width = upstream[0].shape
    width = matrices[2].shape[0]
    anywhere = pl.BlockSpec(memory_space=pl.ANY)

    def placed(columns):
        return pl.BlockSpec((tile, columns), lambda i: (2 * step + i, 0))

    def shape(count, columns, dtype=jnp.bfloat16):
        return jax.ShapeDtypeStruct((count * tile, columns), dtype)

    same = pl.BlockSpec((tile, model_width), lambda i: (0, 0))
    unit = pl.BlockSpec((tile + EXTRA, model_width), lambda i: (0, 0))
    out_shape = [
        *[shape(1, model_width)] * 2,
        *[jax.ShapeDtypeStruct((tile + EXTRA, model_width), jnp.bfloat16)] * 2,
        shape(8, width),
        shape(8, model_width),
        shape(8, 2 * width),
        shape(8, model_width),
    ]
    operands = [choice, *rows, *upstream, *matrices]
    in_specs = [pl.BlockSpec(memory_space=pltpu.SMEM), unit, unit, same, same] + [anywhere] * 4
    aliases = {}
    if kept is not None:
        aliases = {len(operands) + i: 4 + i for i in range(4)}
        operands += list(kept)
        in_specs += [anywhere] * 4
    results = pl.pallas_call(
        functools.partial(expert_kernel, columns=256),
        grid=(2,),
        in_specs=in_specs,
        out_specs=[
            *[same] * 2,
            *[unit] * 2,
            placed(width),
            placed(model_width),
            placed(2 * width),
            placed(model_width),
        ],
        out_shape=out_shape,
        scratch_shapes=[
            pltpu.VMEM((tile + EXTRA, model_width), jnp.bfloat16),
            pltpu.VMEM((tile, model_width), jnp.bfloat16),
            pltpu.VMEM((model_width, 2 * width), jnp.bfloat16),
            pltpu.VMEM((width, model_width), jnp.bfloat16),
            pltpu.SemaphoreType.DMA,
            pltpu.SemaphoreType.DMA,
        ],
        input_output_aliases=aliases,
        compiler_params=pltpu.CompilerParams(vmem_limit_bytes=50 * 2**20),
        cost_estimate=SHORT,
    )(*operands)
    return results[:2], results[2:4], results[4:]


def middle_back_kernel(
    back_own,
    back_other,
    back_ring,
    extra_own,
    extra_other,
    extra_ring,
    gates_ref,
    router_ref,
    middle_ref,
    scale_ref,
    gain_ref,
    ct_ref,
    weight_ref,
    grad_ref,
    unit_ref,
    mix_ref,
    gain_grad,
    logits_ref,
    weight_here,
    weight_sem,
):
    step, tile = pl.program_id(0), middle_ref.shape[0]
    at = pl.multiple_of(step * tile, tile)
    copy = pltpu.make_async_copy(weight_ref, weight_here, weight_sem)

    @pl.when(step == 0)
    def _():
        copy.start()
        gates = gates_ref[...]
        grad_gates = sum_blocks(extra_own[...], extra_other[...], extra_ring[...])
        grad_gates = unpacked(grad_gates, gates.shape[1])
        mean_term = jnp.sum(gates * grad_gates, axis=0, keepdims=True)
        logits_ref[...] = low(gates * (grad_gates - mean_term))
        gain_grad[...] = jnp.zeros(gain_grad.shape, jnp.float32)

    grad = sum_blocks(back_own[...], back_other[...], back_ring[...])
    grad = grad + matmul(logits_ref[:, pl.ds(at, tile)], router_ref[...], FIRST_WITH_FIRST)
    middle, scale = middle_ref[...], scale_ref[...]
    scaled = grad * gain_ref[...]
    mean = jnp.mean(scaled * middle, axis=1, keepdims=True)
    out = ct_ref[...].astype(jnp.float32) + scale * scaled - middle * (scale**3 * mean)
    gain_grad[...] += jnp.sum(middle * scale * grad, axis=0, keepdims=True)
    grad_ref[...] = out
    unit_ref[pl.ds(at, tile), :] = low(out)

    @pl.when(step == pl.num_programs(0) - 1)
    def _():
        count, columns = unit_ref.shape[0] - EXTRA, unit_ref.shape[1]
        gain = gain_grad[...]
        high = low(gain).astype(jnp.float32)
        logits = logits_ref[...].astype(jnp.float32)
        experts = logits.shape[0]
        pad = jnp.zeros((experts, columns - logits.shape[1]), jnp.float32)
        behind = jnp.concatenate([logits, pad], axis=1)
        behind = jnp.concatenate([jnp.zeros((EXTRA - experts, columns), jnp.float32), behind])
        row = lax.broadcasted_iota(jnp.int32, behind.shape, 0)
        behind = jnp.where(row == 0, high, jnp.where(row == 1, gain - high, behind))
        unit_ref[count:, :] = low(behind)
        copy.wait()
        for start in range(0, weight_here.shape[0], 256):
            part = pl.ds(start, 256)
            mix_ref[:, part] = low(
                matmul(unit_ref[:count, :], weight_here[part, :], LAST_WITH_LAST)
            )


def middle_back(back, gates, router, middle, scale, gain, upstream, out_weight):
    rows, columns = middle.shape
    tile = HEAD_SIZE

    def whole(*shape):
        return pl.BlockSpec(shape, lambda i: (0, 0))

    def cut(width):
        return pl.BlockSpec((tile, width), lambda i: (i, 0))

    extra = pl.BlockSpec((EXTRA, columns), lambda i: (rows // EXTRA, 0))
    shapes = [
        ((rows, columns), jnp.float32),
        ((rows + EXTRA, columns), jnp.bfloat16),
        ((rows, out_weight.shape[0]), jnp.bfloat16),
    ]
    return pl.pallas_call(
        middle_back_kernel,
        grid=(rows // tile,),
        in_specs=[
            *[cut(columns)] * 3,
            *[extra] * 3,
            whole(*gates.shape),
            whole(*router.shape),
            cut(columns),
            cut(1),
            whole(*gain.shape),
            cut(columns),
            pl.BlockSpec(memory_space=pl.ANY),
        ],
        out_specs=[
            cut(columns),
            whole(rows + EXTRA, columns),
            whole(rows, out_weight.shape[0]),
        ],
        out_shape=[jax.ShapeDtypeStruct(*shape) for shape in shapes],
        scratch_shapes=[
            pltpu.VMEM((1, columns), jnp.float32),
            pltpu.VMEM(gates.shape, jnp.bfloat16),
            pltpu.VMEM(out_weight.shape, jnp.bfloat16),
            pltpu.SemaphoreType.DMA,
        ],
        compiler_params=pltpu.CompilerParams(vmem_limit_bytes=60 * 2**20),
        cost_estimate=SHORT,
    )(*back, *back, gates, router, middle, scale, gain, upstream, out_weight)


def middle_kernel(
    mix_ref, weight_ref, tokens_ref, gain_ref, router_ref, routes_ref, *outs
):
    middle_ref, scale_ref, unit_ref, gates_ref = outs
    rows, columns = tokens_ref.shape
    for start in range(0, columns, 256):
        at = pl.ds(start, 256)
        middle_ref[:, at] = tokens_ref[:, at].astype(jnp.float32) + matmul(
            mix_ref[...], weight_ref[:, at]
        )
    for start in range(0, rows, HEAD_SIZE):
        at = pl.ds(start, HEAD_SIZE)
        middle = middle_ref[at, :]
        scale = lax.rsqrt(jnp.mean(middle * middle, axis=1, keepdims=True) + EPS)
        scale_ref[at, :] = scale
        unit_ref[at, :] = low(middle * scale * gain_ref[...])
    logits = matmul(router_ref[...], unit_ref[:rows, :], LAST_WITH_LAST)
    expert = lax.broadcasted_iota(jnp.int32, logits.shape, 0)
    named = expert == routes_ref[0:1, :]
    for choice in range(1, routes_ref.shape[0]):
        named = named | (expert == routes_ref[choice : choice + 1, :])
    logits = jnp.where(named, logits, -1e30)
    raised = jnp.exp(logits - jnp.max(logits, axis=0, keepdims=True))
    raised = jnp.where(named, raised, 0.0)
    gates = raised / jnp.sum(raised, axis=0, keepdims=True)
    gates_ref[...] = gates
    unit_ref[rows:, :] = packed(gates, columns)


def middle_of(mix, out_weight, tokens, gain, router, routes):
    rows, columns = tokens.shape
    shapes = [
        ((rows, columns), jnp.float32),
        ((rows, 1), jnp.float32),
        ((rows + EXTRA, columns), jnp.bfloat16),
        ((router.shape[0], rows), jnp.float32),
    ]
    return pl.pallas_call(
        middle_kernel,
        out_shape=[jax.ShapeDtypeStruct(*shape) for shape in shapes],
        compiler_params=pltpu.CompilerParams(vmem_limit_bytes=32 * 2**20),
        cost_estimate=SHORT,
    )(mix, out_weight, tokens, gain, router, routes)


def tokens_back_kernel(
    grad_ref, weight_ref, tokens_ref, scale_ref, gain_ref, middle_grad, out_ref, normed
):
    rows, columns = tokens_ref.shape
    for start in range(0, columns, 256):
        at = pl.ds(start, 256)
        normed[:, at] = matmul(grad_ref[...], weight_ref[at, :], LAST_WITH_LAST)
    for start in range(0, rows, HEAD_SIZE):
        at = pl.ds(start, HEAD_SIZE)
        tokens, scale, grad = tokens_ref[at, :].astype(jnp.float32), scale_ref[at, :], normed[at, :]
        scaled = grad * gain_ref[...]
        mean = jnp.mean(scaled * tokens, axis=1, keepdims=True)
        out_ref[at, :] = low(
            middle_grad[at, :] + scale * scaled - tokens * (scale**3 * mean)
        )


def tokens_back(grad_projected, qkv_weight, tokens, scale, gain, grad_middle):
    return pl.pallas_call(
        tokens_back_kernel,
        out_shape=jax.ShapeDtypeStruct(tokens.shape, jnp.bfloat16),
        scratch_shapes=[pltpu.VMEM(tokens.shape, jnp.float32)],
        compiler_params=pltpu.CompilerParams(vmem_limit_bytes=40 * 2**20),
        cost_estimate=SHORT,
    )(grad_projected, qkv_weight, tokens, scale, gain, grad_middle)


def put_pieces(half, place_ref, field, pieces):
    rows = field.shape[0] // 2
    stays, sent = pieces[2 * half : 2 * half + 2]

    @pl.when((pl.program_id(0) == half) & (place_ref[half] == 0))
    def _():
        stays[...], sent[...] = field[:rows], field[rows:]

    @pl.when((pl.program_id(0) == half) & (place_ref[half] == 1))
    def _():
        stays[...], sent[...] = field[rows:], field[:rows]


def qkv_grads_kernel(place_ref, left_own, left_other, right_own, right_other, *pieces):
    field = matmul(left_own[...], right_own[...], FIRST_WITH_FIRST)
    field = low(field + matmul(left_other[...], right_other[...], FIRST_WITH_FIRST))
    for half in range(2):
        put_pieces(half, place_ref, field, pieces)


def out_grads_kernel(place_ref, *refs):
    field = small = gain = 0.0
    for mix, rows, grad, logits, behind in (refs[0:5], refs[5:10]):
        field = field + matmul(mix[...], grad[...], FIRST_WITH_FIRST)
        experts = EXTRA // 2
        chosen = logits[...][EXTRA - experts :]
        pad = [jnp.zeros_like(chosen)] * (HEAD_SIZE // experts - 1)
        chosen = jnp.concatenate([chosen] + pad)
        small = small + matmul(rows[...], chosen, (((0,), (1,)), ((), ())))
        behind = behind[...].astype(jnp.float32)
        gain = gain + behind[0:1] + behind[1:2]
    lane = lax.broadcasted_iota(jnp.int32, small.shape, 1)
    gain = jnp.broadcast_to(gain, (HEAD_SIZE, small.shape[0])).T
    small = jnp.where(lane == EXTRA // 2, gain, small)
    field = low(jnp.concatenate([field, small], axis=1))
    for half in range(2):
        put_pieces(half, place_ref, field, refs[10:])


def chip_grads(kernel, place, operands, total):
    dp, x, _, core = place
    tile = operands[0][0].shape[1] // 4

    def spec(field, rows, at, is_cut):
        if is_cut:
            return pl.BlockSpec((rows, tile), lambda i, place_ref: (at, 2 * place_ref[2] + i))
        columns = operands[0][0].shape[0] if rows == EXTRA else field.shape[1]
        return pl.BlockSpec((rows, columns), lambda i, place_ref: (at, 0))

    piece = (tile // 2, total)
    pieces = pl.pallas_call(
        kernel,
        grid_spec=pltpu.PrefetchScalarGridSpec(
            num_scalar_prefetch=1,
            grid=(2,),
            in_specs=[spec(*operand) for operand in operands],
            out_specs=[pl.BlockSpec(piece, lambda i, place_ref: (0, 0))] * 4,
        ),
        out_shape=[jax.ShapeDtypeStruct(piece, jnp.bfloat16)] * 4,
        compiler_params=pltpu.CompilerParams(vmem_limit_bytes=24 * 2**20),
        cost_estimate=SHORT,
    )(jnp.stack([x, dp, core]).astype(jnp.int32), *[operand[0] for operand in operands])
    return pieces[0:2], pieces[2:4]


def qkv_grads(normed, grads, place):
    rows = grads[0].shape[0]
    operands = [(field, rows, 0, True) for field in normed]
    operands += [(field, rows, 0, False) for field in grads]
    return chip_grads(qkv_grads_kernel, place, operands, grads[0].shape[1])


def out_grads(mixes, units, grads, place):
    rows = mixes[0].shape[0]
    operands = []
    for mix, unit, grad in zip(mixes, units, grads):
        operands += [
            (mix, rows, 0, True),
            (unit, rows, 0, True),
            (grad, rows, 0, False),
            (grad, EXTRA, rows // EXTRA, False),
            (grad, EXTRA, rows // EXTRA, True),
        ]
    return chip_grads(out_grads_kernel, place, operands, grads[0].shape[1] + HEAD_SIZE)


def from_pieces(put, place_ref, pieces):
    step = pl.program_id(0)
    for half in range(2):
        here = 2 * half + place_ref[half]
        pl.when(step == here)(functools.partial(put, pieces[2 * half]))
        pl.when(step == 4 * half + 1 - here)(functools.partial(put, pieces[2 * half + 1]))


def finish_qkv_kernel(place_ref, *refs):
    weight_ref, gain_ref, out_ref, grad_ref = refs[4:]

    def put(field):
        field = field[...].astype(jnp.float32)
        out_ref[...] = field
        total = jnp.sum(field * weight_ref[...].astype(jnp.float32), axis=1, keepdims=True)
        grad_ref[...] = total / gain_ref[...]

    from_pieces(put, place_ref, refs[:4])


def finish_out_kernel(place_ref, *refs):
    out_ref, small_ref = refs[4:]
    width = out_ref.shape[1]

    def put(field):
        out_ref[...] = field[:, :width].astype(jnp.float32)
        small_ref[...] = field[:, width:].astype(jnp.float32)

    from_pieces(put, place_ref, refs[:4])


def finish(kernel, fields, place, extras, widths):
    dp, x, _, _ = place
    pieces = [*fields[0], *fields[1]]
    rows = pieces[0].shape[0]

    def cut(width):
        return pl.BlockSpec((rows, width), lambda i: (i, 0))

    return pl.pallas_call(
        kernel,
        grid=(4,),
        in_specs=[
            pl.BlockSpec(memory_space=pltpu.SMEM),
            *[pl.BlockSpec(piece.shape, lambda i: (0, 0)) for piece in pieces],
            *[cut(extra.shape[1]) for extra in extras],
        ],
        out_specs=[cut(width) for width in widths],
        out_shape=[jax.ShapeDtypeStruct((4 * rows, width), jnp.float32) for width in widths],
        compiler_params=pltpu.CompilerParams(vmem_limit_bytes=24 * 2**20),
        cost_estimate=SHORT,
    )(jnp.stack([x, dp]).astype(jnp.int32), *pieces, *extras)


def turn(field, cosine, sine):
    half = field.shape[1] // 2
    turned = jnp.concatenate([field[:, half:], field[:, :half]], axis=1)
    return field * cosine + turned * sine


HEADS_AT_ONCE = 2


def attend_kernel(query_in, key_in, value_in, cos_ref, sin_ref, seg_row, seg_column, *refs):
    query_ref, key_ref, value_ref, mix_ref = refs
    cosine, sine = cos_ref[...], sin_ref[...]
    key = low(turn(key_in[...], cosine, sine))
    value = low(value_in[...])
    key_ref[...], value_ref[...] = key, value
    for half in range(HEADS_AT_ONCE):
        columns = slice(half * HEAD_SIZE, (half + 1) * HEAD_SIZE)
        query = low(turn(query_in[:, columns], cosine, sine))
        query_ref[:, columns] = query
        probs = probabilities(query, key, seg_row[...], seg_column[...])
        mix_ref[:, columns] = low(matmul(low(probs), value, FIRST_WITH_FIRST))


def probabilities(query, key, seg_row, seg_column):
    scores = matmul(key, query, LAST_WITH_LAST) * HEAD_SIZE ** (-0.5)
    square = key.shape[0], key.shape[0]
    key_at = lax.broadcasted_iota(jnp.int32, square, 0)
    query_at = lax.broadcasted_iota(jnp.int32, square, 1)
    hidden = jnp.where((seg_row == seg_column) & (key_at <= query_at), 0.0, -1e30)
    hidden = jnp.concatenate([hidden] * (scores.shape[1] // key.shape[0]), axis=1)
    scores = jnp.where(hidden < 0.0, -1e30, scores)
    raised = jnp.exp(scores - jnp.max(scores, axis=0, keepdims=True))
    return raised / jnp.sum(raised, axis=0, keepdims=True)


def attend(projected, cosine, sine, segment):
    rows, width = projected.shape
    groups, heads = KEY_VALUE_HEADS, QUERY_HEADS

    steps = heads // HEADS_AT_ONCE

    def one(index):
        return pl.BlockSpec((rows, HEAD_SIZE), lambda i: (0, index(i)))

    def whole(*shape):
        return pl.BlockSpec(shape, lambda i: (0, 0))

    def shape(count):
        return jax.ShapeDtypeStruct((rows, count * HEAD_SIZE), jnp.bfloat16)

    def group(i):
        return i // (steps // groups)

    head = pl.BlockSpec((rows, HEADS_AT_ONCE * HEAD_SIZE), lambda i: (0, i))
    return pl.pallas_call(
        attend_kernel,
        grid=(steps,),
        in_specs=[
            head,
            one(lambda i: heads + group(i)),
            one(lambda i: heads + groups + group(i)),
            whole(rows, HEAD_SIZE),
            whole(rows, HEAD_SIZE),
            whole(1, rows),
            whole(rows, 1),
        ],
        out_specs=[head, one(group), one(group), head],
        out_shape=[shape(heads), shape(groups), shape(groups), shape(heads)],
        compiler_params=pltpu.CompilerParams(vmem_limit_bytes=24 * 2**20),
        cost_estimate=SHORT,
    )(projected, projected, projected, cosine, sine, segment[None, :], segment[:, None])


def attend_back_kernel(
    query_ref, key_ref, value_ref, grad_ref, cos_ref, sin_ref, seg_row, seg_column, out_ref, *sums
):
    key_sum, value_sum = sums
    step = pl.program_id(0)
    heads, groups = QUERY_HEADS, KEY_VALUE_HEADS
    steps = pl.num_programs(0) // groups
    group, place = step // steps, step % steps
    key, value = key_ref[...], value_ref[...]
    cosine, sine = cos_ref[...], -sin_ref[...]

    def put(head, field):
        at = pl.multiple_of(head * HEAD_SIZE, HEAD_SIZE)
        out_ref[:, pl.ds(at, HEAD_SIZE)] = low(field)

    def stacked(ref):
        return jnp.concatenate(
            [ref[:, at * HEAD_SIZE : (at + 1) * HEAD_SIZE] for at in range(HEADS_AT_ONCE)]
        )

    query, grad_mix = stacked(query_ref), stacked(grad_ref)
    rows = key.shape[0]
    probs = probabilities(query, key, seg_row[...], seg_column[...])
    grad_probs = matmul(value, grad_mix, LAST_WITH_LAST)
    grad_scores = low(
        probs * (grad_probs - jnp.sum(probs * grad_probs, axis=0, keepdims=True))
    )
    grad_query = matmul(grad_scores, key, FIRST_WITH_FIRST) * HEAD_SIZE ** (-0.5)
    for at in range(HEADS_AT_ONCE):
        head = grad_query[at * rows : (at + 1) * rows]
        put(step * HEADS_AT_ONCE + at, turn(head, cosine, sine))
    grad_key = matmul(grad_scores, query) * HEAD_SIZE ** (-0.5)
    grad_value = matmul(low(probs), grad_mix)

    @pl.when(place == 0)
    def _():
        key_sum[...] = grad_key
        value_sum[...] = grad_value

    @pl.when(place > 0)
    def _():
        key_sum[...] += grad_key
        value_sum[...] += grad_value

    @pl.when(place == steps - 1)
    def _():
        put(heads + group, turn(key_sum[...], cosine, sine))
        put(heads + groups + group, value_sum[...])


def attend_back(query, key, value, grad_mix, cosine, sine, segment):
    rows = query.shape[0]
    heads, groups = QUERY_HEADS, KEY_VALUE_HEADS
    steps = heads // HEADS_AT_ONCE

    def whole(*shape):
        return pl.BlockSpec(shape, lambda i: (0, 0))

    head = pl.BlockSpec((rows, HEADS_AT_ONCE * HEAD_SIZE), lambda i: (0, i))
    shared = pl.BlockSpec((rows, HEAD_SIZE), lambda i: (0, i // (steps // groups)))
    width = (heads + 2 * groups) * HEAD_SIZE
    return pl.pallas_call(
        attend_back_kernel,
        grid=(steps,),
        in_specs=[
            head,
            shared,
            shared,
            head,
            whole(rows, HEAD_SIZE),
            whole(rows, HEAD_SIZE),
            whole(1, rows),
            whole(rows, 1),
        ],
        out_specs=whole(rows, width),
        out_shape=jax.ShapeDtypeStruct((rows, width), jnp.bfloat16),
        scratch_shapes=[pltpu.VMEM((rows, HEAD_SIZE), jnp.float32)] * 2,
        compiler_params=pltpu.CompilerParams(vmem_limit_bytes=24 * 2**20),
        cost_estimate=SHORT,
    )(query, key, value, grad_mix, cosine, sine, segment[None, :], segment[:, None])


def ring_shards(
    hidden_in,
    cotangent,
    deal_order,
    lengths,
    routes,
    attention_gain,
    expert_gain,
    qkv_weight,
    out_weight,
    router_weight,
    gate_up_weight,
    down_weight,
):
    count_of_rows = hidden_in.shape[0]
    model_width = hidden_in.shape[1]
    half_rows = count_of_rows // 2
    expert_count = router_weight.shape[1]
    dp, core, at = lax.axis_index("dp"), lax.axis_index("shard"), lax.axis_index("expert")
    x, z = at % 2, at // 2
    place = (dp, x, z, core)
    row_ids = jnp.arange(count_of_rows, dtype=jnp.int32)

    def half_of(field, index):
        return lax.dynamic_slice_in_dim(field, index * half_rows, half_rows, axis=0)

    def sent_dealt(field):
        return half_of(field, dp), other_dp(half_of(field, 1 - dp)), field[count_of_rows:]

    def arrange(own_half, other_half, order):
        held_at = jnp.where(order[1, :count_of_rows] == dp, 0, half_rows)
        held_at = held_at + order[0, :count_of_rows].astype(jnp.int32)
        chosen = low(held_at[:, None] == row_ids[None, :])
        return low(matmul(chosen, jnp.concatenate([own_half, other_half], axis=0)))

    def swapped(field):
        return field, other_core(field)

    def to_dealt(field):
        held_at = jnp.where(deal_order[0] // half_rows == dp, 0, half_rows)
        held_at = held_at + deal_order[0] % half_rows
        chosen = low(held_at[None, :] == row_ids[:, None])
        field = low(matmul(chosen, field))
        return in_order(dp == 0, field[:half_rows], other_dp(field[half_rows:]))

    order = jnp.concatenate([deal_order % half_rows, deal_order // half_rows])
    order = jnp.pad(low(order), ((0, EXTRA - 2), (0, model_width - count_of_rows)))
    ct_0 = jnp.concatenate([cotangent, order])
    ct_1 = ring_z(ct_0)
    hidden_out = half_of(after(hidden_in, ct_0), 1 - dp)
    hidden_arrived = other_dp(hidden_out)
    qkv_other, out_other, up_other = (
        send(after(field, hidden_out))
        for send, field in (
            (other_core, qkv_weight),
            (other_core, out_weight),
            (from_owner, gate_up_weight[0]),
        )
    )
    small = jnp.concatenate(
        [router_weight.T, attention_gain[None], expert_gain[None], jnp.zeros_like(router_weight.T[:6])]
    )
    small = in_order(core == 0, small, other_core(small), axis=1)
    router = small[:expert_count]
    gain_first = small[expert_count : expert_count + 1].astype(jnp.float32)
    gain_second = small[expert_count + 1 : expert_count + 2].astype(jnp.float32)
    full_qkv = in_order(core == 0, qkv_weight, qkv_other)
    segment, token_position = positions_of(lengths[0], count_of_rows)
    frequency = THETA ** (-jnp.arange(HEAD_SIZE // 2, dtype=jnp.float32) / (HEAD_SIZE // 2))
    angles = token_position.astype(jnp.float32)[:, None] * frequency[None, :]
    cosine = jnp.concatenate([jnp.cos(angles)] * 2, axis=1)
    sine = jnp.concatenate([-jnp.sin(angles), jnp.sin(angles)], axis=1)
    cosine, sine, full_qkv, hidden_arrived, gain_first, gain_second, router, routes = part(
        cosine, sine, full_qkv, hidden_arrived, gain_first, gain_second, router, routes.T
    )
    tokens = arrange(half_of(hidden_in, dp), hidden_arrived, order)
    residual = tokens.astype(jnp.float32)
    inv_first = lax.rsqrt(jnp.mean(residual * residual, axis=1, keepdims=True) + EPS)
    normed_attn = low(residual * inv_first * gain_first)
    projected = matmul(normed_attn, full_qkv)
    ct_1, projected, ct_0, out_other, down_own = part(
        ct_1, projected, ct_0, out_other, down_weight[0]
    )

    ct_2 = ring_z(ct_1)
    ct_0 = sent_dealt(ct_0)
    down_other = from_owner(down_own)
    full_out = in_order(core == 0, out_weight, out_other)
    query, key, value, attn_mix = attend(projected, cosine, sine, segment)
    middle, inv_second, unit_0, gates = middle_of(
        attn_mix, full_out, tokens, gain_second, router, routes
    )
    ct_2, ct_0, ct_1, unit_0, up_other = part(ct_2, ct_0, ct_1, unit_0, up_other)

    normed_1 = ring_z(unit_0)
    normed_0 = swapped(unit_0)
    ct_1 = sent_dealt(ct_1)
    ct_0 = swapped(arrange(*ct_0))
    normed_1, normed_0, ct_0, ct_1, ct_2, down_other = part(
        normed_1, normed_0, ct_0, ct_1, ct_2, down_other
    )
    choice = jnp.stack([(core == x).astype(jnp.int32), (2 * z + core).astype(jnp.int32)])
    matrices = (gate_up_weight[0], up_other, down_weight[0], down_other)

    ct_3 = ring_z(ct_2)
    ct_2 = sent_dealt(ct_2)
    ct_1, normed_1 = swapped(arrange(*ct_1)), swapped(normed_1)
    sums_0, back_0, kept = expert_step(0, choice, normed_0, ct_0, matrices, None)
    ct_3, ct_1, normed_1, ct_2, kept = part(ct_3, ct_1, normed_1, ct_2, kept)

    normed_2 = ring_z(normed_1[0])
    ct_3 = sent_dealt(ct_3)
    ct_2 = swapped(arrange(*ct_2))
    mixes, normeds = swapped(attn_mix), swapped(normed_attn)
    sums_1, back_1, kept = expert_step(1, choice, normed_1, ct_1, matrices, kept)
    normed_2, ct_3, ct_2, back_1, kept, mixes, normeds = part(
        normed_2, ct_3, ct_2, back_1, kept, mixes, normeds
    )

    normed_3 = ring_z(normed_2)
    normed_2, back_1_other = swapped(normed_2), other_core(back_1[1])
    ct_3 = swapped(arrange(*ct_3))
    sums_2, back_2, kept = expert_step(2, choice, normed_2, ct_2, matrices, kept)
    back_1 = low(sum_blocks(back_1[0], back_1_other))
    normed_3, back_1, ct_3, back_2, kept = part(normed_3, back_1, ct_3, back_2, kept)

    back_1 = ring_z(back_1)
    normed_3, back_2_other = swapped(normed_3), other_core(back_2[1])
    sums_3, back_3, kept = expert_step(3, choice, normed_3, ct_3, matrices, kept)
    back_1, back_2_other, back_3, kept = part(back_1, back_2_other, back_3, kept)

    back_2 = ring_z(low(sum_blocks(back_2[0], back_2_other, back_1)))
    back_3_other, back_0_other = other_core(back_3[1]), other_core(back_0[1])
    sums_1_other = other_core(sums_1[1])
    all_hidden, all_grad_out, all_grad_up, all_rows = kept
    half_width = model_width // 2
    up_first = low(matmul(all_rows.T, all_grad_up[:, :half_width]))
    up_second = low(matmul(all_rows.T, all_grad_up[:, half_width:]))
    back_2, back_3_other, back_0_other, sums_1_other, up_first, up_second, all_grad_out = part(
        back_2, back_3_other, back_0_other, sums_1_other, up_first, up_second, all_grad_out
    )

    back_3 = ring_z(low(sum_blocks(back_3[0], back_3_other, back_2)))
    down_first = low(matmul(all_hidden.T, all_grad_out[:, :half_width]))
    down_second = low(matmul(all_hidden.T, all_grad_out[:, half_width:]))
    sums_1 = low(sum_blocks(sums_1[0], sums_1_other))
    sums_2_other = other_core(sums_2[1])
    up_second = block(up_second, dp, 2), block(up_second, 1 - dp, 2)
    down_second = block(down_second, dp, 2), block(down_second, 1 - dp, 2)
    back_3, up_first, up_second, down_first, down_second, sums_1, sums_2_other = part(
        back_3, up_first, up_second, down_first, down_second, sums_1, sums_2_other
    )

    sums_1 = ring_z(sums_1)
    up_first = up_first, to_owner(up_first)
    up_second = up_second[0], other_dp(up_second[1])
    sums_0_other, sums_3_other = other_core(sums_0[1]), other_core(sums_3[1])
    grad_middle, grad_unit, grad_mix = middle_back(
        (back_0[0], back_0_other, back_3),
        gates,
        router,
        middle,
        inv_second,
        gain_second,
        ct_0[0],
        full_out,
    )
    grad_projected = attend_back(query, key, value, grad_mix, cosine, sine, segment)
    (
        sums_0_other,
        sums_1,
        sums_3_other,
        grad_projected,
        grad_unit,
        up_first,
        up_second,
        down_first,
        down_second,
    ) = part(
        sums_0_other,
        sums_1,
        sums_3_other,
        grad_projected,
        grad_unit,
        up_first,
        up_second,
        down_first,
        down_second,
    )

    grads_projected, grad_units = swapped(grad_projected), swapped(grad_unit)
    down_first = down_first, to_owner(down_first)
    down_second = down_second[0], other_dp(down_second[1])
    up_first, up_second = low(sum_blocks(*up_first)), low(sum_blocks(*up_second))
    up_first = block(up_first, dp, 2), block(up_first, 1 - dp, 2)
    sums_2 = low(sum_blocks(sums_2[0], sums_2_other, sums_1))
    qkv = qkv_grads(normeds, grads_projected, place)
    sums_2, grad_units, qkv, down_first, down_second, up_first, up_second, grad_projected = part(
        sums_2, grad_units, qkv, down_first, down_second, up_first, up_second, grad_projected
    )

    sums_2 = ring_z(sums_2)
    qkv = slab_sum(qkv, place)
    up_first = up_first[0], owners_dp(up_first[1])
    up_second = up_second, to_owner(up_second)
    down_first, down_second, qkv = part(down_first, down_second, qkv)
    down_first, down_second = low(sum_blocks(*down_first)), low(sum_blocks(*down_second))
    down_first = block(down_first, dp, 2), block(down_first, 1 - dp, 2)
    grad_tokens = tokens_back(
        grad_projected, full_qkv, tokens, inv_first, gain_first, grad_middle
    )
    out = out_grads(mixes, normed_0, grad_units, place)
    sums_3 = low(sum_blocks(sums_3[0], sums_3_other, after(sums_2, qkv)))
    sums_3, out, qkv, up_first, up_second, down_first, down_second, grad_tokens = part(
        sums_3, out, qkv, up_first, up_second, down_first, down_second, grad_tokens
    )

    sums_3 = ring_z(sums_3)
    qkv = slab_sum_on(qkv, place)
    down_first = down_first[0], owners_dp(down_first[1])
    down_second = down_second, to_owner(down_second)
    input_gradient = to_dealt(grad_tokens)
    up_grad = low(jnp.concatenate([sum_blocks(*up_first), sum_blocks(*up_second)], axis=1))
    up_grad = block(up_grad, core, 2), block(up_grad, 1 - core, 2)
    layer_out = low(middle + sum_blocks(sums_0[0], sums_0_other, after(sums_3, qkv)))
    out, qkv, up_grad, down_first, down_second, layer_out, input_gradient = part(
        out, qkv, up_grad, down_first, down_second, layer_out, input_gradient
    )

    qkv, out = line_sum(qkv), slab_sum(out, place)
    down_grad = low(jnp.concatenate([sum_blocks(*down_first), sum_blocks(*down_second)], axis=1))
    down_grad = block(down_grad, core, 2), block(down_grad, 1 - core, 2)
    out, qkv, up_grad, down_grad, layer_out = part(out, qkv, up_grad, down_grad, layer_out)

    qkv, out = line_spread(qkv, place), slab_sum_on(out, place)
    layer_out = to_dealt(layer_out)
    out, qkv, layer_out, up_grad, down_grad = part(out, qkv, layer_out, up_grad, down_grad)

    qkv, out = slab_spread(qkv, place), line_sum(out)
    out, qkv, up_grad, down_grad = part(out, qkv, up_grad, down_grad)

    qkv, out = slab_spread_on(qkv), line_spread(out, place)
    out, qkv, up_grad, down_grad = part(out, qkv, up_grad, down_grad)

    out = slab_spread(out, place)
    up_grad, down_grad = (
        jnp.where(core == x, field[0], other_core(field[1])) for field in (up_grad, down_grad)
    )
    gain = attention_gain.astype(jnp.float32)[:, None]
    qkv_grad, gain_first_grad = finish(
        finish_qkv_kernel, qkv, place, [qkv_weight, gain], [qkv_weight.shape[1], 1]
    )
    out, qkv_grad, gain_first_grad, up_grad, down_grad = part(
        out, qkv_grad, gain_first_grad, up_grad, down_grad
    )

    out = slab_spread_on(out)
    gate_up_grad, down_grad = (field[None].astype(jnp.float32) for field in (up_grad, down_grad))
    out_grad, small_grad = finish(finish_out_kernel, out, place, [], [model_width, HEAD_SIZE])
    return (
        layer_out,
        input_gradient,
        gain_first_grad[:, 0],
        small_grad[:, expert_count],
        qkv_grad,
        out_grad,
        small_grad[:, :expert_count],
        gate_up_grad,
        down_grad,
    )


def solution(mesh):
    ringed = (mesh.shape["dp"], mesh.shape["expert"], mesh.shape["shard"]) == (2, 8, 2)
    shards = ring_shards if ringed else routed_shards
    return jax.shard_map(
        shards,
        mesh=mesh,
        in_specs=(
            P(("dp", "expert", "shard"), None),
            P(("dp", "expert", "shard"), None),
            P(("dp", "expert", "shard"), None),
            P(("dp", "expert", "shard"), None),
            P(("dp", "expert", "shard"), None),
            P("shard"),
            P("shard"),
            P("shard", None),
            P("shard", None),
            P("shard", None),
            P("expert", None, None),
            P("expert", None, None),
        ),
        out_specs=(
            P(("dp", "expert", "shard"), None),
            P(("dp", "expert", "shard"), None),
            P("shard"),
            P("shard"),
            P("shard", None),
            P("shard", None),
            P("shard", None),
            P("expert", ("dp", "shard"), None),
            P("expert", ("dp", "shard"), None),
        ),
        check_vma=False,
    )
```

```python
import functools

import jax
import jax.numpy as jnp
from jax import lax
from jax.experimental import pallas as pl
from jax.experimental.pallas import tpu as pltpu
from jax.sharding import PartitionSpec as P

QUERY_HEADS = 12
KEY_VALUE_HEADS = 2
HEAD_SIZE = 128
TOP = 4


EPS = 1e-06
THETA = 1000000.0


def positions_of(lengths_dev, count_of_rows):
    seq_ends = jnp.cumsum(lengths_dev)
    starts = seq_ends - lengths_dev
    places = jnp.arange(count_of_rows, dtype=jnp.int32)
    segment = jnp.sum((places[:, None] >= seq_ends[None, :]).astype(jnp.int32), axis=1)
    member = segment[:, None] == jnp.arange(lengths_dev.shape[0], dtype=jnp.int32)[None, :]
    start_of = jnp.sum(jnp.where(member, starts[None, :], 0), axis=1)
    return (segment, places - start_of)


def apply_rotation(field, token_position, direction):
    half_dim = field.shape[-1] // 2
    frequency = THETA ** (-jnp.arange(half_dim, dtype=jnp.float32) / half_dim)
    angles = token_position.astype(jnp.float32)[:, None] * frequency[None, :]
    cosine = jnp.cos(angles)[:, None, :]
    sine_term = direction * jnp.sin(angles)[:, None, :]
    lead_part = field[..., :half_dim]
    tail_part = field[..., half_dim:]
    return jnp.concatenate(
        [lead_part * cosine - tail_part * sine_term, tail_part * cosine + lead_part * sine_term],
        axis=-1,
    )


def masked_scores(query_block, key_matrix_rows, segment_block, segment, row_start):
    raw_scores = jnp.einsum(
        "ihgd,jhd->hgij", query_block, key_matrix_rows, preferred_element_type=jnp.float32
    ) * HEAD_SIZE ** (-0.5)
    query_at = row_start + jnp.arange(query_block.shape[0], dtype=jnp.int32)
    key_at = jnp.arange(key_matrix_rows.shape[0], dtype=jnp.int32)
    allowed = (segment_block[:, None] == segment[None, :]) & (key_at[None, :] <= query_at[:, None])
    return jnp.where(allowed, raw_scores, -1e30)


def norm_back(field, inv_scale, gain_vec, grad_normed):
    scaled = grad_normed * gain_vec
    grad_field = inv_scale * scaled - field * inv_scale**3 * jnp.mean(
        scaled * field, axis=1, keepdims=True
    )
    grad_gain = jnp.sum(field * inv_scale * grad_normed, axis=0)
    return (grad_field, grad_gain)


def activate(gate_up):
    hidden_width = gate_up.shape[1] // 2
    return jax.nn.gelu(gate_up[:, :hidden_width], approximate=True) * gate_up[:, hidden_width:]


def routed_shards(
    hidden_in,
    cotangent,
    deal_order,
    lengths,
    routes,
    attention_gain,
    expert_gain,
    qkv_weight,
    out_weight,
    router_weight,
    gate_up_weight,
    down_weight,
):
    count_of_rows = hidden_in.shape[0]
    model_width = hidden_in.shape[1]
    head_groups = QUERY_HEADS // KEY_VALUE_HEADS
    arrived_in, arrived_ct = (
        lax.all_to_all(hidden_in, "dp", split_axis=0, concat_axis=0, tiled=True),
        lax.all_to_all(cotangent, "dp", split_axis=0, concat_axis=0, tiled=True),
    )
    deal_rows = deal_order[0]
    tokens = arrived_in[deal_rows]
    upstream = arrived_ct[deal_rows].astype(jnp.float32)
    gain_first, gain_second, full_qkv, full_out, full_router = (
        lax.all_gather(attention_gain, "shard", axis=0, tiled=True),
        lax.all_gather(expert_gain, "shard", axis=0, tiled=True),
        lax.all_gather(qkv_weight, "shard", axis=0, tiled=True),
        lax.all_gather(out_weight, "shard", axis=0, tiled=True),
        lax.all_gather(router_weight, "shard", axis=0, tiled=True),
    )
    gain_first = gain_first.astype(jnp.float32)
    gain_second = gain_second.astype(jnp.float32)
    residual = tokens.astype(jnp.float32)
    inv_first = lax.rsqrt(jnp.mean(residual * residual, axis=1, keepdims=True) + EPS)
    normed_attn = (residual * inv_first * gain_first).astype(jnp.bfloat16)
    projected_rows = jnp.dot(normed_attn, full_qkv, preferred_element_type=jnp.float32)
    segment, token_position = positions_of(lengths[0], count_of_rows)
    query_matrix_rows = (
        apply_rotation(
            projected_rows[:, : QUERY_HEADS * HEAD_SIZE].reshape(
                count_of_rows, QUERY_HEADS, HEAD_SIZE
            ),
            token_position,
            1.0,
        )
        .astype(jnp.bfloat16)
        .reshape(count_of_rows, KEY_VALUE_HEADS, head_groups, HEAD_SIZE)
    )
    key_matrix_rows = apply_rotation(
        projected_rows[
            :, QUERY_HEADS * HEAD_SIZE : (QUERY_HEADS + KEY_VALUE_HEADS) * HEAD_SIZE
        ].reshape(count_of_rows, KEY_VALUE_HEADS, HEAD_SIZE),
        token_position,
        1.0,
    ).astype(jnp.bfloat16)
    value_matrix_rows = (
        projected_rows[:, (QUERY_HEADS + KEY_VALUE_HEADS) * HEAD_SIZE :]
        .reshape(count_of_rows, KEY_VALUE_HEADS, HEAD_SIZE)
        .astype(jnp.bfloat16)
    )
    block_rows = min(count_of_rows, 512)
    block_starts = jnp.arange(count_of_rows // block_rows, dtype=jnp.int32) * block_rows

    def forward_block(row_start):
        scores = masked_scores(query_matrix_rows, key_matrix_rows, segment, segment, row_start)
        row_max = jnp.max(scores, axis=-1, keepdims=True)
        exp_scores = jnp.exp(scores - row_max)
        exp_total = jnp.sum(exp_scores, axis=-1, keepdims=True)
        soft_probs = (exp_scores / exp_total).astype(jnp.bfloat16)
        mix_block = jnp.einsum(
            "hgij,jhd->ihgd", soft_probs, value_matrix_rows, preferred_element_type=jnp.float32
        )
        return (mix_block, (row_max + jnp.log(exp_total))[..., 0])

    mix_blocks, logsum = lax.map(forward_block, block_starts)
    attn_mix = mix_blocks.reshape(count_of_rows, QUERY_HEADS * HEAD_SIZE).astype(jnp.bfloat16)
    middle = residual + jnp.dot(attn_mix, full_out, preferred_element_type=jnp.float32)
    inv_second = lax.rsqrt(jnp.mean(middle * middle, axis=1, keepdims=True) + EPS)
    normed_moe = (middle * inv_second * gain_second).astype(jnp.bfloat16)
    logits = jnp.dot(normed_moe, full_router, preferred_element_type=jnp.float32)
    gate_probs = jax.nn.softmax(jnp.take_along_axis(logits, routes, axis=1), axis=-1)
    expert_count = full_router.shape[1]
    peer_count = lax.axis_size("expert")
    capacity = min(count_of_rows, max(2, 3 * count_of_rows * TOP // (2 * expert_count)))
    flat_routes = routes.reshape(-1)
    expert_ids = jnp.arange(expert_count, dtype=jnp.int32)
    onehot = (flat_routes[:, None] == expert_ids[None, :]).astype(jnp.int32)
    slot_rank = jnp.sum(jnp.cumsum(onehot, axis=0) * onehot, axis=1) - 1
    target = flat_routes * capacity + slot_rank
    pair_count = count_of_rows * TOP
    slot_pair = (
        jnp.full((expert_count * capacity,), pair_count, jnp.int32)
        .at[target]
        .set(jnp.arange(pair_count, dtype=jnp.int32))
    )
    padded = jnp.concatenate([normed_moe, jnp.zeros((1, model_width), jnp.bfloat16)], axis=0)
    sending = padded[slot_pair // TOP].reshape(peer_count, capacity, model_width)
    received = lax.all_to_all(sending, "expert", split_axis=0, concat_axis=0, tiled=True)
    rows_in = received.reshape(peer_count * capacity, model_width)
    gate_up = jnp.dot(rows_in, gate_up_weight[0], preferred_element_type=jnp.float32)
    hidden_rows = activate(gate_up).astype(jnp.bfloat16)
    expert_out = jnp.dot(hidden_rows, down_weight[0], preferred_element_type=jnp.float32).astype(
        jnp.bfloat16
    )
    returned = lax.all_to_all(
        expert_out.reshape(peer_count, capacity, model_width),
        "expert",
        split_axis=0,
        concat_axis=0,
        tiled=True,
    )
    per_pair = returned.reshape(peer_count * capacity, model_width)[target].reshape(
        count_of_rows, TOP, model_width
    )
    expert_sum = jnp.zeros((count_of_rows, model_width), jnp.float32)
    for choice_slot in range(TOP):
        expert_sum = expert_sum + gate_probs[:, choice_slot : choice_slot + 1] * per_pair[
            :, choice_slot
        ].astype(jnp.float32)
    final_rows = middle + expert_sum
    grad_pairs = (gate_probs[:, :, None] * upstream[:, None, :]).astype(jnp.bfloat16)
    grad_gates = jnp.stack(
        [
            jnp.sum(per_pair[:, choice_slot].astype(jnp.float32) * upstream, axis=1)
            for choice_slot in range(TOP)
        ],
        axis=1,
    )
    padded_grad = jnp.concatenate(
        [grad_pairs.reshape(pair_count, model_width), jnp.zeros((1, model_width), jnp.bfloat16)],
        axis=0,
    )
    sending_back = padded_grad[slot_pair].reshape(peer_count, capacity, model_width)
    grad_rows = lax.all_to_all(
        sending_back, "expert", split_axis=0, concat_axis=0, tiled=True
    ).reshape(peer_count * capacity, model_width)
    grad_hidden = jnp.dot(grad_rows, down_weight[0].T, preferred_element_type=jnp.float32)
    grad_gate_up = jax.vjp(activate, gate_up)[1](grad_hidden)[0].astype(jnp.bfloat16)
    term_down = jnp.dot(hidden_rows.T, grad_rows, preferred_element_type=jnp.float32)
    term_gate_up = jnp.dot(rows_in.T, grad_gate_up, preferred_element_type=jnp.float32)
    grad_rows_in = jnp.dot(
        grad_gate_up, gate_up_weight[0].T, preferred_element_type=jnp.float32
    ).astype(jnp.bfloat16)
    back_rows = lax.all_to_all(
        grad_rows_in.reshape(peer_count, capacity, model_width),
        "expert",
        split_axis=0,
        concat_axis=0,
        tiled=True,
    )
    back_pairs = back_rows.reshape(peer_count * capacity, model_width)[target].reshape(
        count_of_rows, TOP, model_width
    )
    grad_normed = jnp.zeros((count_of_rows, model_width), jnp.float32)
    for choice_slot in range(TOP):
        grad_normed = grad_normed + back_pairs[:, choice_slot].astype(jnp.float32)
    mean_term = jnp.sum(gate_probs * grad_gates, axis=1, keepdims=True)
    grad_chosen = gate_probs * (grad_gates - mean_term)
    grad_logits = jnp.sum(
        jnp.where(routes[:, :, None] == expert_ids[None, None, :], grad_chosen[:, :, None], 0.0),
        axis=1,
    ).astype(jnp.bfloat16)
    term_router = jnp.dot(normed_moe.T, grad_logits, preferred_element_type=jnp.float32)
    grad_normed = grad_normed + jnp.dot(
        grad_logits, full_router.T, preferred_element_type=jnp.float32
    )
    grad_middle_norm, term_gain_second = norm_back(middle, inv_second, gain_second, grad_normed)
    grad_middle = upstream + grad_middle_norm
    grad_attn_out = grad_middle.astype(jnp.bfloat16)
    term_out = jnp.dot(attn_mix.T, grad_attn_out, preferred_element_type=jnp.float32)
    grad_mix = (
        jnp.dot(grad_attn_out, full_out.T, preferred_element_type=jnp.float32)
        .astype(jnp.bfloat16)
        .reshape(count_of_rows, KEY_VALUE_HEADS, head_groups, HEAD_SIZE)
    )

    def backward_block(accums, inputs):
        acc_key, value_accumulator = accums
        row_start, logsum_block = inputs
        scores = masked_scores(query_matrix_rows, key_matrix_rows, segment, segment, row_start)
        soft_probs = jnp.exp(scores - logsum_block[..., None])
        grad_probs = jnp.einsum(
            "ihgd,jhd->hgij", grad_mix, value_matrix_rows, preferred_element_type=jnp.float32
        )
        value_accumulator = value_accumulator + jnp.einsum(
            "hgij,ihgd->jhd",
            soft_probs.astype(jnp.bfloat16),
            grad_mix,
            preferred_element_type=jnp.float32,
        )
        grad_scores = (
            soft_probs * (grad_probs - jnp.sum(soft_probs * grad_probs, axis=-1, keepdims=True))
        ).astype(jnp.bfloat16)
        grad_query = HEAD_SIZE ** (-0.5) * jnp.einsum(
            "hgij,jhd->ihgd", grad_scores, key_matrix_rows, preferred_element_type=jnp.float32
        )
        acc_key = acc_key + HEAD_SIZE ** (-0.5) * jnp.einsum(
            "hgij,ihgd->jhd", grad_scores, query_matrix_rows, preferred_element_type=jnp.float32
        )
        return ((acc_key, value_accumulator), grad_query)

    zero_key_value = jnp.zeros((count_of_rows, KEY_VALUE_HEADS, HEAD_SIZE), jnp.float32)
    (acc_key, value_accumulator), grad_query = lax.scan(
        backward_block, (zero_key_value, zero_key_value), (block_starts, logsum)
    )
    grad_query = apply_rotation(
        grad_query.reshape(count_of_rows, QUERY_HEADS, HEAD_SIZE), token_position, -1.0
    )
    key_gradient = apply_rotation(acc_key, token_position, -1.0)
    grad_projected = jnp.concatenate(
        [
            grad_query.reshape(count_of_rows, QUERY_HEADS * HEAD_SIZE),
            key_gradient.reshape(count_of_rows, KEY_VALUE_HEADS * HEAD_SIZE),
            value_accumulator.reshape(count_of_rows, KEY_VALUE_HEADS * HEAD_SIZE),
        ],
        axis=1,
    ).astype(jnp.bfloat16)
    term_qkv = jnp.dot(normed_attn.T, grad_projected, preferred_element_type=jnp.float32)
    grad_normed_attn = jnp.dot(grad_projected, full_qkv.T, preferred_element_type=jnp.float32)
    grad_resid_norm, term_gain_first = norm_back(residual, inv_first, gain_first, grad_normed_attn)
    grad_tokens = (grad_middle + grad_resid_norm).astype(jnp.bfloat16)
    inverse = (
        jnp.zeros((count_of_rows,), jnp.int32)
        .at[deal_rows]
        .set(jnp.arange(count_of_rows, dtype=jnp.int32))
    )
    layer_out, input_gradient = (
        lax.all_to_all(
            final_rows.astype(jnp.bfloat16)[inverse], "dp", split_axis=0, concat_axis=0, tiled=True
        ),
        lax.all_to_all(grad_tokens[inverse], "dp", split_axis=0, concat_axis=0, tiled=True),
    )
    shard_terms = (
        lax.psum_scatter(
            term_gain_first.astype(jnp.bfloat16), "shard", scatter_dimension=0, tiled=True
        ).astype(jnp.float32),
        lax.psum_scatter(
            term_gain_second.astype(jnp.bfloat16), "shard", scatter_dimension=0, tiled=True
        ).astype(jnp.float32),
        lax.psum_scatter(
            term_qkv.astype(jnp.bfloat16), "shard", scatter_dimension=0, tiled=True
        ).astype(jnp.float32),
        lax.psum_scatter(
            term_out.astype(jnp.bfloat16), "shard", scatter_dimension=0, tiled=True
        ).astype(jnp.float32),
        lax.psum_scatter(
            term_router.astype(jnp.bfloat16), "shard", scatter_dimension=0, tiled=True
        ).astype(jnp.float32),
    )
    gain_first_grad, gain_second_grad, qkv_grad, out_grad, router_grad = lax.psum(
        (shard_terms[0], shard_terms[1], shard_terms[2], shard_terms[3], shard_terms[4]),
        ("dp", "expert"),
    )
    gate_up_grad, down_grad = (
        lax.psum_scatter(
            term_gate_up[None].astype(jnp.bfloat16),
            ("dp", "shard"),
            scatter_dimension=1,
            tiled=True,
        ).astype(jnp.float32),
        lax.psum_scatter(
            term_down[None].astype(jnp.bfloat16), ("dp", "shard"), scatter_dimension=1, tiled=True
        ).astype(jnp.float32),
    )
    return (
        layer_out,
        input_gradient,
        gain_first_grad,
        gain_second_grad,
        qkv_grad,
        out_grad,
        router_grad,
        gate_up_grad,
        down_grad,
    )


RING_NEXT = (1, 3, 0, 2)
LAST_WITH_LAST = (((1,), (1,)), ((), ()))


def after(value, *earlier):
    return lax.optimization_barrier((value, *earlier))[0]


def part(*fields):
    return lax.optimization_barrier(fields)


def other_core(field):
    return lax.ppermute(field, "shard", [(0, 1), (1, 0)])


def other_dp(field):
    return lax.ppermute(field, "dp", [(0, 1), (1, 0)])


def owners_dp(field):
    pairs = [
        ((d * 8 + e) * 2 + e % 2, ((1 - d) * 8 + e) * 2 + e % 2) for d in range(2) for e in range(8)
    ]
    return lax.ppermute(field, ("dp", "expert", "shard"), pairs)


def across_x(field):
    return lax.ppermute(field, "expert", [(i, i ^ 1) for i in range(8)])


def across_dp_x(field):
    pairs = [(d * 8 + e, (1 - d) * 8 + (e ^ 1)) for d in range(2) for e in range(8)]
    return lax.ppermute(field, ("dp", "expert"), pairs)


def across_z(field, distance):
    return lax.ppermute(field, "expert", [(i, i ^ (2 * distance)) for i in range(8)])


def ring_z(field):
    pairs = [(2 * z + x, 2 * RING_NEXT[z] + x) for z in range(4) for x in range(2)]
    return lax.ppermute(field, "expert", pairs)


def to_owner(field):
    pairs = [(e * 2 + c, (e ^ 1) * 2 + c) for e in range(8) for c in range(2) if e % 2 != c]
    return lax.ppermute(field, ("expert", "shard"), pairs)


def from_owner(field):
    pairs = [(e * 2 + c, (e ^ 1) * 2 + c) for e in range(8) for c in range(2) if e % 2 == c]
    return lax.ppermute(field, ("expert", "shard"), pairs)


def in_order(first, own, received, axis=0):
    return jnp.where(
        first,
        jnp.concatenate([own, received], axis=axis),
        jnp.concatenate([received, own], axis=axis),
    )


def block(field, index, count):
    rows = field.shape[0] // count
    return lax.dynamic_slice_in_dim(field, index * rows, rows, axis=0)


def sum_blocks(*fields):
    total = fields[0].astype(jnp.float32)
    for field in fields[1:]:
        total = total + field.astype(jnp.float32)
    return total


def low(field):
    return field.astype(jnp.bfloat16)


def slab_cut(first, second, at, other):
    return (
        (block(first, at, 2), block(first, 1 - at, 2)),
        (block(second, other, 2), block(second, 1 - other, 2)),
    )


def slab_sum(cuts, place):
    dp, x, _, _ = place
    (first, first_out), (second, second_out) = cuts
    first = low(sum_blocks(first, across_x(first_out)))
    second = low(sum_blocks(second, other_dp(second_out)))
    return slab_cut(first, second, dp, x)


def slab_sum_on(cuts, place):
    z = place[2]
    (first, first_out), (second, second_out) = cuts
    first = sum_blocks(first, other_dp(first_out))
    second = sum_blocks(second, across_x(second_out))
    part = low(jnp.concatenate([first, second]))
    return [block(part, z ^ k, 4) for k in range(4)]


def line_sum(cuts):
    return low(sum_blocks(cuts[0], *[across_z(cuts[k], k) for k in (1, 2, 3)]))


def put_in_order(pieces, own):
    stacked = jnp.stack(pieces)
    return jnp.concatenate(
        [lax.dynamic_index_in_dim(stacked, own ^ b, 0, False) for b in range(len(pieces))]
    )


def line_spread(part, place):
    part = put_in_order([part] + [across_z(part, k) for k in (1, 2, 3)], place[2])
    return jnp.split(part, 2)


def slab_spread(halves, place):
    dp, x, _, _ = place
    first, second = halves
    return in_order(dp == 0, first, other_dp(first)), in_order(x == 0, second, across_x(second))


def slab_spread_on(halves):
    first, second = halves
    return (first, across_x(first)), (second, other_dp(second))


def matmul(left, right, dims=(((1,), (0,)), ((), ()))):
    return lax.dot_general(left, right, dims, preferred_element_type=jnp.float32)


FIRST_WITH_FIRST = (((0,), (0,)), ((), ()))


EXTRA = 16


def packed(field, columns):
    high = low(field)
    rest = low(field - high.astype(jnp.float32))
    pad = jnp.zeros((field.shape[0], columns - 2 * field.shape[1]), jnp.bfloat16)
    block = jnp.concatenate([high, rest, pad], axis=1)
    return jnp.concatenate([block, jnp.zeros((EXTRA - field.shape[0], columns), jnp.bfloat16)])


def unpacked(extra, rows):
    field = extra.astype(jnp.float32)[: EXTRA // 2]
    return field[:, :rows] + field[:, rows : 2 * rows]


def expert_kernel(
    choice,
    own_rows,
    other_rows,
    own_ct,
    other_ct,
    up_own,
    up_other,
    down_own,
    down_other,
    *refs,
    columns,
):
    (
        own_sum,
        other_sum,
        own_back,
        other_back,
        hidden_ref,
        grad_out_ref,
        grad_up_ref,
        rows_ref,
        unit_ref,
        ct_ref,
        up_ref,
        down_ref,
        up_sem,
        down_sem,
    ) = refs[-14:]
    width = down_ref.shape[0]
    first = pl.program_id(0) == 0

    @pl.when(first & (choice[0] == 1))
    def _():
        pltpu.make_async_copy(up_own, up_ref, up_sem).start()
        pltpu.make_async_copy(down_own, down_ref, down_sem).start()

    @pl.when(first & (choice[0] == 0))
    def _():
        pltpu.make_async_copy(up_other, up_ref, up_sem).start()
        pltpu.make_async_copy(down_other, down_ref, down_sem).start()

    @pl.when(first)
    def _():
        unit_ref[...] = own_rows[...]
        ct_ref[...] = own_ct[...]
        pltpu.make_async_copy(up_own, up_ref, up_sem).wait()
        pltpu.make_async_copy(down_own, down_ref, down_sem).wait()

    @pl.when(pl.program_id(0) == 1)
    def _():
        unit_ref[...] = other_rows[...]
        ct_ref[...] = other_ct[...]

    count = ct_ref.shape[0]
    rows = unit_ref[:count, :]
    rows_ref[...] = rows
    gates = unpacked(unit_ref[count:, :], count)
    mine = lax.broadcasted_iota(jnp.int32, gates.shape, 0) == choice[1]
    weighting = jnp.sum(jnp.where(mine, gates, 0.0), axis=0, keepdims=True)
    weighting = jnp.broadcast_to(weighting, (HEAD_SIZE, rows.shape[0])).T[:, :1]
    ct = ct_ref[...].astype(jnp.float32)
    grad_out = low(weighting * ct)
    grad_out_ref[...] = grad_out
    for start in range(0, width, columns):
        gate, up = pl.ds(start, columns), pl.ds(width + start, columns)
        a, b = matmul(rows, up_ref[:, gate]), matmul(rows, up_ref[:, up])
        tanh = jnp.tanh(0.7978845608028654 * (a + 0.044715 * a * a * a))
        half = 0.5 * (1.0 + tanh)
        gelu = a * half
        hidden_ref[:, gate] = low(gelu * b)
        grad_hidden = matmul(grad_out, down_ref[gate, :], LAST_WITH_LAST)
        slope = half + 0.5 * a * (1.0 - tanh * tanh) * (
            0.7978845608028654 * (1.0 + 3.0 * 0.044715 * a * a)
        )
        grad_up_ref[:, gate] = low(grad_hidden * b * slope)
        grad_up_ref[:, up] = low(grad_hidden * gelu)
    out = low(matmul(hidden_ref[...], down_ref[...])).astype(jnp.float32)
    grad = jnp.sum(ct * out, axis=1, keepdims=True)
    grad = jnp.broadcast_to(grad, (rows.shape[0], HEAD_SIZE)).T[: mine.shape[0], :]
    grad = packed(jnp.where(mine, grad, 0.0), rows.shape[1])
    weighted = low(weighting * out)
    back = low(matmul(grad_up_ref[...], up_ref[...], LAST_WITH_LAST))

    @pl.when(pl.program_id(0) == 0)
    def _():
        own_sum[...], own_back[:count, :], own_back[count:, :] = weighted, back, grad

    @pl.when(pl.program_id(0) == 1)
    def _():
        other_sum[...], other_back[:count, :], other_back[count:, :] = weighted, back, grad


SHORT = pl.CostEstimate(flops=1000, bytes_accessed=1000, transcendentals=0)


def expert_step(step, choice, rows, upstream, matrices, kept):
    tile, model_width = upstream[0].shape
    width = matrices[2].shape[0]
    anywhere = pl.BlockSpec(memory_space=pl.ANY)

    def placed(columns):
        return pl.BlockSpec((tile, columns), lambda i: (2 * step + i, 0))

    def shape(count, columns, dtype=jnp.bfloat16):
        return jax.ShapeDtypeStruct((count * tile, columns), dtype)

    same = pl.BlockSpec((tile, model_width), lambda i: (0, 0))
    unit = pl.BlockSpec((tile + EXTRA, model_width), lambda i: (0, 0))
    out_shape = [
        *[shape(1, model_width)] * 2,
        *[jax.ShapeDtypeStruct((tile + EXTRA, model_width), jnp.bfloat16)] * 2,
        shape(8, width),
        shape(8, model_width),
        shape(8, 2 * width),
        shape(8, model_width),
    ]
    operands = [choice, *rows, *upstream, *matrices]
    in_specs = [pl.BlockSpec(memory_space=pltpu.SMEM), unit, unit, same, same] + [anywhere] * 4
    aliases = {}
    if kept is not None:
        aliases = {len(operands) + i: 4 + i for i in range(4)}
        operands += list(kept)
        in_specs += [anywhere] * 4
    results = pl.pallas_call(
        functools.partial(expert_kernel, columns=256),
        grid=(2,),
        in_specs=in_specs,
        out_specs=[
            *[same] * 2,
            *[unit] * 2,
            placed(width),
            placed(model_width),
            placed(2 * width),
            placed(model_width),
        ],
        out_shape=out_shape,
        scratch_shapes=[
            pltpu.VMEM((tile + EXTRA, model_width), jnp.bfloat16),
            pltpu.VMEM((tile, model_width), jnp.bfloat16),
            pltpu.VMEM((model_width, 2 * width), jnp.bfloat16),
            pltpu.VMEM((width, model_width), jnp.bfloat16),
            pltpu.SemaphoreType.DMA,
            pltpu.SemaphoreType.DMA,
        ],
        input_output_aliases=aliases,
        compiler_params=pltpu.CompilerParams(vmem_limit_bytes=50 * 2**20),
        cost_estimate=SHORT,
    )(*operands)
    return results[:2], results[2:4], results[4:]


def middle_back_kernel(
    back_own,
    back_other,
    back_ring,
    extra_own,
    extra_other,
    extra_ring,
    gates_ref,
    router_ref,
    middle_ref,
    scale_ref,
    gain_ref,
    ct_ref,
    weight_ref,
    grad_ref,
    unit_ref,
    mix_ref,
    gain_grad,
    logits_ref,
    weight_here,
    weight_sem,
):
    step, tile = pl.program_id(0), middle_ref.shape[0]
    at = pl.multiple_of(step * tile, tile)
    copy = pltpu.make_async_copy(weight_ref, weight_here, weight_sem)

    @pl.when(step == 0)
    def _():
        copy.start()
        gates = gates_ref[...]
        grad_gates = sum_blocks(extra_own[...], extra_other[...], extra_ring[...])
        grad_gates = unpacked(grad_gates, gates.shape[1])
        mean_term = jnp.sum(gates * grad_gates, axis=0, keepdims=True)
        logits_ref[...] = low(gates * (grad_gates - mean_term))
        gain_grad[...] = jnp.zeros(gain_grad.shape, jnp.float32)

    grad = sum_blocks(back_own[...], back_other[...], back_ring[...])
    grad = grad + matmul(logits_ref[:, pl.ds(at, tile)], router_ref[...], FIRST_WITH_FIRST)
    middle, scale = middle_ref[...], scale_ref[...]
    scaled = grad * gain_ref[...]
    mean = jnp.mean(scaled * middle, axis=1, keepdims=True)
    out = ct_ref[...].astype(jnp.float32) + scale * scaled - middle * (scale**3 * mean)
    gain_grad[...] += jnp.sum(middle * scale * grad, axis=0, keepdims=True)
    grad_ref[...] = out
    unit_ref[pl.ds(at, tile), :] = low(out)

    @pl.when(step == pl.num_programs(0) - 1)
    def _():
        count, columns = unit_ref.shape[0] - EXTRA, unit_ref.shape[1]
        gain = gain_grad[...]
        high = low(gain).astype(jnp.float32)
        logits = logits_ref[...].astype(jnp.float32)
        experts = logits.shape[0]
        pad = jnp.zeros((experts, columns - logits.shape[1]), jnp.float32)
        behind = jnp.concatenate([logits, pad], axis=1)
        behind = jnp.concatenate([jnp.zeros((EXTRA - experts, columns), jnp.float32), behind])
        row = lax.broadcasted_iota(jnp.int32, behind.shape, 0)
        behind = jnp.where(row == 0, high, jnp.where(row == 1, gain - high, behind))
        unit_ref[count:, :] = low(behind)
        copy.wait()
        for start in range(0, weight_here.shape[0], 256):
            part = pl.ds(start, 256)
            mix_ref[:, part] = low(
                matmul(unit_ref[:count, :], weight_here[part, :], LAST_WITH_LAST)
            )


def middle_back(back, gates, router, middle, scale, gain, upstream, out_weight):
    rows, columns = middle.shape
    tile = HEAD_SIZE

    def whole(*shape):
        return pl.BlockSpec(shape, lambda i: (0, 0))

    def cut(width):
        return pl.BlockSpec((tile, width), lambda i: (i, 0))

    extra = pl.BlockSpec((EXTRA, columns), lambda i: (rows // EXTRA, 0))
    shapes = [
        ((rows, columns), jnp.float32),
        ((rows + EXTRA, columns), jnp.bfloat16),
        ((rows, out_weight.shape[0]), jnp.bfloat16),
    ]
    return pl.pallas_call(
        middle_back_kernel,
        grid=(rows // tile,),
        in_specs=[
            *[cut(columns)] * 3,
            *[extra] * 3,
            whole(*gates.shape),
            whole(*router.shape),
            cut(columns),
            cut(1),
            whole(*gain.shape),
            cut(columns),
            pl.BlockSpec(memory_space=pl.ANY),
        ],
        out_specs=[
            cut(columns),
            whole(rows + EXTRA, columns),
            whole(rows, out_weight.shape[0]),
        ],
        out_shape=[jax.ShapeDtypeStruct(*shape) for shape in shapes],
        scratch_shapes=[
            pltpu.VMEM((1, columns), jnp.float32),
            pltpu.VMEM(gates.shape, jnp.bfloat16),
            pltpu.VMEM(out_weight.shape, jnp.bfloat16),
            pltpu.SemaphoreType.DMA,
        ],
        compiler_params=pltpu.CompilerParams(vmem_limit_bytes=60 * 2**20),
        cost_estimate=SHORT,
    )(*back, *back, gates, router, middle, scale, gain, upstream, out_weight)


def middle_kernel(
    mix_ref, weight_ref, tokens_ref, gain_ref, router_ref, routes_ref, *outs
):
    middle_ref, scale_ref, unit_ref, gates_ref = outs
    rows, columns = tokens_ref.shape
    for start in range(0, columns, 256):
        at = pl.ds(start, 256)
        middle_ref[:, at] = tokens_ref[:, at].astype(jnp.float32) + matmul(
            mix_ref[...], weight_ref[:, at]
        )
    for start in range(0, rows, HEAD_SIZE):
        at = pl.ds(start, HEAD_SIZE)
        middle = middle_ref[at, :]
        scale = lax.rsqrt(jnp.mean(middle * middle, axis=1, keepdims=True) + EPS)
        scale_ref[at, :] = scale
        unit_ref[at, :] = low(middle * scale * gain_ref[...])
    logits = matmul(router_ref[...], unit_ref[:rows, :], LAST_WITH_LAST)
    expert = lax.broadcasted_iota(jnp.int32, logits.shape, 0)
    named = expert == routes_ref[0:1, :]
    for choice in range(1, routes_ref.shape[0]):
        named = named | (expert == routes_ref[choice : choice + 1, :])
    logits = jnp.where(named, logits, -1e30)
    raised = jnp.exp(logits - jnp.max(logits, axis=0, keepdims=True))
    raised = jnp.where(named, raised, 0.0)
    gates = raised / jnp.sum(raised, axis=0, keepdims=True)
    gates_ref[...] = gates
    unit_ref[rows:, :] = packed(gates, columns)


def middle_of(mix, out_weight, tokens, gain, router, routes):
    rows, columns = tokens.shape
    shapes = [
        ((rows, columns), jnp.float32),
        ((rows, 1), jnp.float32),
        ((rows + EXTRA, columns), jnp.bfloat16),
        ((router.shape[0], rows), jnp.float32),
    ]
    return pl.pallas_call(
        middle_kernel,
        out_shape=[jax.ShapeDtypeStruct(*shape) for shape in shapes],
        compiler_params=pltpu.CompilerParams(vmem_limit_bytes=32 * 2**20),
        cost_estimate=SHORT,
    )(mix, out_weight, tokens, gain, router, routes)


def tokens_back_kernel(
    grad_ref, weight_ref, tokens_ref, scale_ref, gain_ref, middle_grad, out_ref, normed
):
    rows, columns = tokens_ref.shape
    for start in range(0, columns, 256):
        at = pl.ds(start, 256)
        normed[:, at] = matmul(grad_ref[...], weight_ref[at, :], LAST_WITH_LAST)
    for start in range(0, rows, HEAD_SIZE):
        at = pl.ds(start, HEAD_SIZE)
        tokens, scale, grad = tokens_ref[at, :].astype(jnp.float32), scale_ref[at, :], normed[at, :]
        scaled = grad * gain_ref[...]
        mean = jnp.mean(scaled * tokens, axis=1, keepdims=True)
        out_ref[at, :] = low(
            middle_grad[at, :] + scale * scaled - tokens * (scale**3 * mean)
        )


def tokens_back(grad_projected, qkv_weight, tokens, scale, gain, grad_middle):
    return pl.pallas_call(
        tokens_back_kernel,
        out_shape=jax.ShapeDtypeStruct(tokens.shape, jnp.bfloat16),
        scratch_shapes=[pltpu.VMEM(tokens.shape, jnp.float32)],
        compiler_params=pltpu.CompilerParams(vmem_limit_bytes=40 * 2**20),
        cost_estimate=SHORT,
    )(grad_projected, qkv_weight, tokens, scale, gain, grad_middle)


def put_pieces(half, place_ref, field, pieces):
    rows = field.shape[0] // 2
    stays, sent = pieces[2 * half : 2 * half + 2]

    @pl.when((pl.program_id(0) == half) & (place_ref[half] == 0))
    def _():
        stays[...], sent[...] = field[:rows], field[rows:]

    @pl.when((pl.program_id(0) == half) & (place_ref[half] == 1))
    def _():
        stays[...], sent[...] = field[rows:], field[:rows]


def qkv_grads_kernel(place_ref, left_own, left_other, right_own, right_other, *pieces):
    field = matmul(left_own[...], right_own[...], FIRST_WITH_FIRST)
    field = low(field + matmul(left_other[...], right_other[...], FIRST_WITH_FIRST))
    for half in range(2):
        put_pieces(half, place_ref, field, pieces)


def out_grads_kernel(place_ref, *refs):
    field = small = gain = 0.0
    for mix, rows, grad, logits, behind in (refs[0:5], refs[5:10]):
        field = field + matmul(mix[...], grad[...], FIRST_WITH_FIRST)
        experts = EXTRA // 2
        chosen = logits[...][EXTRA - experts :]
        pad = [jnp.zeros_like(chosen)] * (HEAD_SIZE // experts - 1)
        chosen = jnp.concatenate([chosen] + pad)
        small = small + matmul(rows[...], chosen, (((0,), (1,)), ((), ())))
        behind = behind[...].astype(jnp.float32)
        gain = gain + behind[0:1] + behind[1:2]
    lane = lax.broadcasted_iota(jnp.int32, small.shape, 1)
    gain = jnp.broadcast_to(gain, (HEAD_SIZE, small.shape[0])).T
    small = jnp.where(lane == EXTRA // 2, gain, small)
    field = low(jnp.concatenate([field, small], axis=1))
    for half in range(2):
        put_pieces(half, place_ref, field, refs[10:])


def chip_grads(kernel, place, operands, total):
    dp, x, _, core = place
    tile = operands[0][0].shape[1] // 4

    def spec(field, rows, at, is_cut):
        if is_cut:
            return pl.BlockSpec((rows, tile), lambda i, place_ref: (at, 2 * place_ref[2] + i))
        columns = operands[0][0].shape[0] if rows == EXTRA else field.shape[1]
        return pl.BlockSpec((rows, columns), lambda i, place_ref: (at, 0))

    piece = (tile // 2, total)
    pieces = pl.pallas_call(
        kernel,
        grid_spec=pltpu.PrefetchScalarGridSpec(
            num_scalar_prefetch=1,
            grid=(2,),
            in_specs=[spec(*operand) for operand in operands],
            out_specs=[pl.BlockSpec(piece, lambda i, place_ref: (0, 0))] * 4,
        ),
        out_shape=[jax.ShapeDtypeStruct(piece, jnp.bfloat16)] * 4,
        compiler_params=pltpu.CompilerParams(vmem_limit_bytes=24 * 2**20),
        cost_estimate=SHORT,
    )(jnp.stack([x, dp, core]).astype(jnp.int32), *[operand[0] for operand in operands])
    return pieces[0:2], pieces[2:4]


def qkv_grads(normed, grads, place):
    rows = grads[0].shape[0]
    operands = [(field, rows, 0, True) for field in normed]
    operands += [(field, rows, 0, False) for field in grads]
    return chip_grads(qkv_grads_kernel, place, operands, grads[0].shape[1])


def out_grads(mixes, units, grads, place):
    rows = mixes[0].shape[0]
    operands = []
    for mix, unit, grad in zip(mixes, units, grads):
        operands += [
            (mix, rows, 0, True),
            (unit, rows, 0, True),
            (grad, rows, 0, False),
            (grad, EXTRA, rows // EXTRA, False),
            (grad, EXTRA, rows // EXTRA, True),
        ]
    return chip_grads(out_grads_kernel, place, operands, grads[0].shape[1] + HEAD_SIZE)


def dealt_kernel(rows_ref, order_ref, out_ref):
    count, columns = rows_ref.shape
    half = count // 2
    order = order_ref[...]
    second = order >= half
    place = jnp.where(second, order - half, order).astype(jnp.float32)
    pad = jnp.zeros((1, columns - count), jnp.float32)
    place = jnp.concatenate([place, pad], axis=1)
    second = jnp.concatenate([jnp.where(second, 1.0, 0.0), pad], axis=1)
    row = lax.broadcasted_iota(jnp.int32, (EXTRA, columns), 0)
    out_ref[:count, :] = rows_ref[...]
    out_ref[count:, :] = low(jnp.where(row == 0, place, jnp.where(row == 1, second, 0.0)))


def dealt_unit(rows, order):
    count, columns = rows.shape
    return pl.pallas_call(
        dealt_kernel,
        out_shape=jax.ShapeDtypeStruct((count + EXTRA, columns), rows.dtype),
        compiler_params=pltpu.CompilerParams(vmem_limit_bytes=16 * 2**20),
        cost_estimate=SHORT,
    )(rows, order)


def settle_kernel(held_ref, middle_ref, own_ref, other_ref, ring_ref, first_ref, second_ref):
    field = low(middle_ref[...] + sum_blocks(own_ref[...], other_ref[...], ring_ref[...]))
    rows = field.shape[0]
    place = lax.broadcasted_iota(jnp.int32, (rows, rows), 0)
    chosen = low(jnp.where(held_ref[...] == place, 1.0, 0.0))
    dealt = low(matmul(chosen, field))
    first_ref[...], second_ref[...] = dealt[: rows // 2], dealt[rows // 2 :]


def settle(held_at, middle, *sums):
    rows, columns = middle.shape
    half = jax.ShapeDtypeStruct((rows // 2, columns), jnp.bfloat16)
    return pl.pallas_call(
        settle_kernel,
        out_shape=[half] * 2,
        compiler_params=pltpu.CompilerParams(vmem_limit_bytes=24 * 2**20),
        cost_estimate=SHORT,
    )(held_at, middle, *sums)


def from_pieces(put, place_ref, pieces):
    step = pl.program_id(0)
    for half in range(2):
        here = 2 * half + place_ref[half]
        pl.when(step == here)(functools.partial(put, pieces[2 * half]))
        pl.when(step == 4 * half + 1 - here)(functools.partial(put, pieces[2 * half + 1]))


def finish_qkv_kernel(place_ref, *refs):
    weight_ref, gain_ref, out_ref, grad_ref = refs[4:]

    def put(field):
        field = field[...].astype(jnp.float32)
        out_ref[...] = field
        total = jnp.sum(field * weight_ref[...].astype(jnp.float32), axis=1, keepdims=True)
        grad_ref[...] = total / gain_ref[...]

    from_pieces(put, place_ref, refs[:4])


def finish_out_kernel(place_ref, first, second, *refs):
    out_ref, small_ref = refs[-2:]
    width = out_ref.shape[1]

    def put(field):
        out_ref[...] = field[:, :width].astype(jnp.float32)
        small_ref[...] = field[:, width:].astype(jnp.float32)

    pl.when(pl.program_id(0) == 0)(functools.partial(put, first))
    pl.when(pl.program_id(0) == 1)(functools.partial(put, second))


def finish_out(pieces, place, is_own, kept):
    dp, x, _, _ = place
    at = jnp.stack([x, dp]).astype(jnp.int32)
    at = at if is_own else 1 - at
    rows, total = pieces[0].shape
    widths = total - HEAD_SIZE, HEAD_SIZE
    whole = pl.BlockSpec((rows, total), lambda i, place_ref: (0, 0))
    return pl.pallas_call(
        finish_out_kernel,
        grid_spec=pltpu.PrefetchScalarGridSpec(
            num_scalar_prefetch=1,
            grid=(2,),
            in_specs=[whole] * 2 + [pl.BlockSpec(memory_space=pl.ANY)] * len(kept),
            out_specs=[
                pl.BlockSpec((rows, width), lambda i, place_ref: (2 * i + place_ref[i], 0))
                for width in widths
            ],
        ),
        out_shape=[jax.ShapeDtypeStruct((4 * rows, width), jnp.float32) for width in widths],
        input_output_aliases={3 + i: i for i in range(len(kept))},
        compiler_params=pltpu.CompilerParams(vmem_limit_bytes=24 * 2**20),
        cost_estimate=SHORT,
    )(at, *pieces, *kept)


def finish(kernel, fields, place, extras, widths):
    dp, x, _, _ = place
    pieces = [*fields[0], *fields[1]]
    rows = pieces[0].shape[0]

    def cut(width):
        return pl.BlockSpec((rows, width), lambda i: (i, 0))

    return pl.pallas_call(
        kernel,
        grid=(4,),
        in_specs=[
            pl.BlockSpec(memory_space=pltpu.SMEM),
            *[pl.BlockSpec(piece.shape, lambda i: (0, 0)) for piece in pieces],
            *[cut(extra.shape[1]) for extra in extras],
        ],
        out_specs=[cut(width) for width in widths],
        out_shape=[jax.ShapeDtypeStruct((4 * rows, width), jnp.float32) for width in widths],
        compiler_params=pltpu.CompilerParams(vmem_limit_bytes=24 * 2**20),
        cost_estimate=SHORT,
    )(jnp.stack([x, dp]).astype(jnp.int32), *pieces, *extras)


def turn(field, cosine, sine):
    half = field.shape[1] // 2
    turned = jnp.concatenate([field[:, half:], field[:, :half]], axis=1)
    return field * cosine + turned * sine


HEADS_AT_ONCE = 2


def attend_kernel(query_in, key_in, value_in, cos_ref, sin_ref, seg_row, seg_column, *refs):
    query_ref, key_ref, value_ref, mix_ref = refs
    cosine, sine = cos_ref[...], sin_ref[...]
    key = low(turn(key_in[...], cosine, sine))
    value = low(value_in[...])
    key_ref[...], value_ref[...] = key, value
    for half in range(HEADS_AT_ONCE):
        columns = slice(half * HEAD_SIZE, (half + 1) * HEAD_SIZE)
        query = low(turn(query_in[:, columns], cosine, sine))
        query_ref[:, columns] = query
        probs = probabilities(query, key, seg_row[...], seg_column[...])
        mix_ref[:, columns] = low(matmul(low(probs), value, FIRST_WITH_FIRST))


def probabilities(query, key, seg_row, seg_column):
    scores = matmul(key, query, LAST_WITH_LAST) * HEAD_SIZE ** (-0.5)
    square = key.shape[0], key.shape[0]
    key_at = lax.broadcasted_iota(jnp.int32, square, 0)
    query_at = lax.broadcasted_iota(jnp.int32, square, 1)
    hidden = jnp.where((seg_row == seg_column) & (key_at <= query_at), 0.0, -1e30)
    hidden = jnp.concatenate([hidden] * (scores.shape[1] // key.shape[0]), axis=1)
    scores = jnp.where(hidden < 0.0, -1e30, scores)
    raised = jnp.exp(scores - jnp.max(scores, axis=0, keepdims=True))
    return raised / jnp.sum(raised, axis=0, keepdims=True)


def attend(projected, cosine, sine, segment):
    rows, width = projected.shape
    groups, heads = KEY_VALUE_HEADS, QUERY_HEADS

    steps = heads // HEADS_AT_ONCE

    def one(index):
        return pl.BlockSpec((rows, HEAD_SIZE), lambda i: (0, index(i)))

    def whole(*shape):
        return pl.BlockSpec(shape, lambda i: (0, 0))

    def shape(count):
        return jax.ShapeDtypeStruct((rows, count * HEAD_SIZE), jnp.bfloat16)

    def group(i):
        return i // (steps // groups)

    head = pl.BlockSpec((rows, HEADS_AT_ONCE * HEAD_SIZE), lambda i: (0, i))
    return pl.pallas_call(
        attend_kernel,
        grid=(steps,),
        in_specs=[
            head,
            one(lambda i: heads + group(i)),
            one(lambda i: heads + groups + group(i)),
            whole(rows, HEAD_SIZE),
            whole(rows, HEAD_SIZE),
            whole(1, rows),
            whole(rows, 1),
        ],
        out_specs=[head, one(group), one(group), head],
        out_shape=[shape(heads), shape(groups), shape(groups), shape(heads)],
        compiler_params=pltpu.CompilerParams(vmem_limit_bytes=24 * 2**20),
        cost_estimate=SHORT,
    )(projected, projected, projected, cosine, sine, segment[None, :], segment[:, None])


def attend_back_kernel(
    query_ref, key_ref, value_ref, grad_ref, cos_ref, sin_ref, seg_row, seg_column, out_ref, *sums
):
    key_sum, value_sum = sums
    step = pl.program_id(0)
    heads, groups = QUERY_HEADS, KEY_VALUE_HEADS
    steps = pl.num_programs(0) // groups
    group, place = step // steps, step % steps
    key, value = key_ref[...], value_ref[...]
    cosine, sine = cos_ref[...], -sin_ref[...]

    def put(head, field):
        at = pl.multiple_of(head * HEAD_SIZE, HEAD_SIZE)
        out_ref[:, pl.ds(at, HEAD_SIZE)] = low(field)

    def stacked(ref):
        return jnp.concatenate(
            [ref[:, at * HEAD_SIZE : (at + 1) * HEAD_SIZE] for at in range(HEADS_AT_ONCE)]
        )

    query, grad_mix = stacked(query_ref), stacked(grad_ref)
    rows = key.shape[0]
    probs = probabilities(query, key, seg_row[...], seg_column[...])
    grad_probs = matmul(value, grad_mix, LAST_WITH_LAST)
    grad_scores = low(
        probs * (grad_probs - jnp.sum(probs * grad_probs, axis=0, keepdims=True))
    )
    grad_query = matmul(grad_scores, key, FIRST_WITH_FIRST) * HEAD_SIZE ** (-0.5)
    for at in range(HEADS_AT_ONCE):
        head = grad_query[at * rows : (at + 1) * rows]
        put(step * HEADS_AT_ONCE + at, turn(head, cosine, sine))
    grad_key = matmul(grad_scores, query) * HEAD_SIZE ** (-0.5)
    grad_value = matmul(low(probs), grad_mix)

    @pl.when(place == 0)
    def _():
        key_sum[...] = grad_key
        value_sum[...] = grad_value

    @pl.when(place > 0)
    def _():
        key_sum[...] += grad_key
        value_sum[...] += grad_value

    @pl.when(place == steps - 1)
    def _():
        put(heads + group, turn(key_sum[...], cosine, sine))
        put(heads + groups + group, value_sum[...])


def attend_back(query, key, value, grad_mix, cosine, sine, segment):
    rows = query.shape[0]
    heads, groups = QUERY_HEADS, KEY_VALUE_HEADS
    steps = heads // HEADS_AT_ONCE

    def whole(*shape):
        return pl.BlockSpec(shape, lambda i: (0, 0))

    head = pl.BlockSpec((rows, HEADS_AT_ONCE * HEAD_SIZE), lambda i: (0, i))
    shared = pl.BlockSpec((rows, HEAD_SIZE), lambda i: (0, i // (steps // groups)))
    width = (heads + 2 * groups) * HEAD_SIZE
    return pl.pallas_call(
        attend_back_kernel,
        grid=(steps,),
        in_specs=[
            head,
            shared,
            shared,
            head,
            whole(rows, HEAD_SIZE),
            whole(rows, HEAD_SIZE),
            whole(1, rows),
            whole(rows, 1),
        ],
        out_specs=whole(rows, width),
        out_shape=jax.ShapeDtypeStruct((rows, width), jnp.bfloat16),
        scratch_shapes=[pltpu.VMEM((rows, HEAD_SIZE), jnp.float32)] * 2,
        compiler_params=pltpu.CompilerParams(vmem_limit_bytes=24 * 2**20),
        cost_estimate=SHORT,
    )(query, key, value, grad_mix, cosine, sine, segment[None, :], segment[:, None])


def ring_shards(
    hidden_in,
    cotangent,
    deal_order,
    lengths,
    routes,
    attention_gain,
    expert_gain,
    qkv_weight,
    out_weight,
    router_weight,
    gate_up_weight,
    down_weight,
):
    count_of_rows = hidden_in.shape[0]
    model_width = hidden_in.shape[1]
    half_rows = count_of_rows // 2
    expert_count = router_weight.shape[1]
    dp, core, at = lax.axis_index("dp"), lax.axis_index("shard"), lax.axis_index("expert")
    x, z = at % 2, at // 2
    place = (dp, x, z, core)
    row_ids = jnp.arange(count_of_rows, dtype=jnp.int32)

    def half_of(field, index):
        return lax.dynamic_slice_in_dim(field, index * half_rows, half_rows, axis=0)

    def sent_dealt(field):
        return half_of(field, dp), other_dp(half_of(field, 1 - dp)), field[count_of_rows:]

    def arrange(own_half, other_half, order):
        held_at = jnp.where(order[1, :count_of_rows] == dp, 0, half_rows)
        held_at = held_at + order[0, :count_of_rows].astype(jnp.int32)
        chosen = low(held_at[:, None] == row_ids[None, :])
        return low(matmul(chosen, jnp.concatenate([own_half, other_half], axis=0)))

    def swapped(field):
        return field, other_core(field)

    held_at = jnp.where(deal_order // half_rows == dp, 0, half_rows) + deal_order % half_rows

    def deal(field):
        field = low(matmul(low(held_at == row_ids[:, None]), field))
        return field[:half_rows], field[half_rows:]

    def to_dealt(halves):
        return in_order(dp == 0, halves[0], other_dp(halves[1]))

    ct_0 = dealt_unit(cotangent, deal_order)
    order = ct_0[count_of_rows:]
    ct_1 = ring_z(ct_0)
    hidden_out = half_of(after(hidden_in, ct_0), 1 - dp)
    hidden_arrived = other_dp(hidden_out)
    qkv_other, out_other, up_other = (
        send(after(field, hidden_out))
        for send, field in (
            (other_core, qkv_weight),
            (other_core, out_weight),
            (from_owner, gate_up_weight[0]),
        )
    )
    small = jnp.concatenate(
        [router_weight.T, attention_gain[None], expert_gain[None], jnp.zeros_like(router_weight.T[:6])]
    )
    small = in_order(core == 0, small, other_core(small), axis=1)
    router = small[:expert_count]
    gain_first = small[expert_count : expert_count + 1].astype(jnp.float32)
    gain_second = small[expert_count + 1 : expert_count + 2].astype(jnp.float32)
    full_qkv = in_order(core == 0, qkv_weight, qkv_other)
    segment, token_position = positions_of(lengths[0], count_of_rows)
    frequency = THETA ** (-jnp.arange(HEAD_SIZE // 2, dtype=jnp.float32) / (HEAD_SIZE // 2))
    angles = token_position.astype(jnp.float32)[:, None] * frequency[None, :]
    cosine = jnp.concatenate([jnp.cos(angles)] * 2, axis=1)
    sine = jnp.concatenate([-jnp.sin(angles), jnp.sin(angles)], axis=1)
    cosine, sine, full_qkv, hidden_arrived, gain_first, gain_second, router, routes = part(
        cosine, sine, full_qkv, hidden_arrived, gain_first, gain_second, router, routes.T
    )
    tokens = arrange(half_of(hidden_in, dp), hidden_arrived, order)
    residual = tokens.astype(jnp.float32)
    inv_first = lax.rsqrt(jnp.mean(residual * residual, axis=1, keepdims=True) + EPS)
    normed_attn = low(residual * inv_first * gain_first)
    projected = matmul(normed_attn, full_qkv)
    ct_1, projected, ct_0, out_other, down_own = part(
        ct_1, projected, ct_0, out_other, down_weight[0]
    )

    ct_2 = ring_z(ct_1)
    ct_0 = sent_dealt(ct_0)
    down_other = from_owner(down_own)
    full_out = in_order(core == 0, out_weight, out_other)
    query, key, value, attn_mix = attend(projected, cosine, sine, segment)
    middle, inv_second, unit_0, gates = middle_of(
        attn_mix, full_out, tokens, gain_second, router, routes
    )
    ct_2, ct_0, ct_1, unit_0, up_other = part(ct_2, ct_0, ct_1, unit_0, up_other)

    normed_1 = ring_z(unit_0)
    normed_0 = swapped(unit_0)
    ct_1 = sent_dealt(ct_1)
    ct_0 = swapped(arrange(*ct_0))
    normed_1, normed_0, ct_0, ct_1, ct_2, down_other = part(
        normed_1, normed_0, ct_0, ct_1, ct_2, down_other
    )
    choice = jnp.stack([(core == x).astype(jnp.int32), (2 * z + core).astype(jnp.int32)])
    matrices = (gate_up_weight[0], up_other, down_weight[0], down_other)

    ct_3 = ring_z(ct_2)
    ct_2 = sent_dealt(ct_2)
    ct_1, normed_1 = swapped(arrange(*ct_1)), swapped(normed_1)
    sums_0, back_0, kept = expert_step(0, choice, normed_0, ct_0, matrices, None)
    ct_3, ct_1, normed_1, ct_2, kept = part(ct_3, ct_1, normed_1, ct_2, kept)

    normed_2 = ring_z(normed_1[0])
    ct_3 = sent_dealt(ct_3)
    ct_2 = swapped(arrange(*ct_2))
    mixes, normeds = swapped(attn_mix), swapped(normed_attn)
    sums_1, back_1, kept = expert_step(1, choice, normed_1, ct_1, matrices, kept)
    normed_2, ct_3, ct_2, back_1, kept, mixes, normeds = part(
        normed_2, ct_3, ct_2, back_1, kept, mixes, normeds
    )

    normed_3 = ring_z(normed_2)
    normed_2, back_1_other = swapped(normed_2), other_core(back_1[1])
    ct_3 = swapped(arrange(*ct_3))
    sums_2, back_2, kept = expert_step(2, choice, normed_2, ct_2, matrices, kept)
    back_1 = low(sum_blocks(back_1[0], back_1_other))
    normed_3, back_1, ct_3, back_2, kept = part(normed_3, back_1, ct_3, back_2, kept)

    back_1 = ring_z(back_1)
    normed_3, back_2_other = swapped(normed_3), other_core(back_2[1])
    sums_3, back_3, kept = expert_step(3, choice, normed_3, ct_3, matrices, kept)
    back_1, back_2_other, back_3, kept = part(back_1, back_2_other, back_3, kept)

    back_2 = ring_z(low(sum_blocks(back_2[0], back_2_other, back_1)))
    back_3_other, back_0_other = other_core(back_3[1]), other_core(back_0[1])
    sums_1_other = other_core(sums_1[1])
    all_hidden, all_grad_out, all_grad_up, all_rows = kept
    half_width = model_width // 2
    up_first = low(matmul(all_rows.T, all_grad_up[:, :half_width]))
    up_second = low(matmul(all_rows.T, all_grad_up[:, half_width:]))
    back_2, back_3_other, back_0_other, sums_1_other, up_first, up_second, all_grad_out = part(
        back_2, back_3_other, back_0_other, sums_1_other, up_first, up_second, all_grad_out
    )

    back_3 = ring_z(low(sum_blocks(back_3[0], back_3_other, back_2)))
    down_first = low(matmul(all_hidden.T, all_grad_out[:, :half_width]))
    down_second = low(matmul(all_hidden.T, all_grad_out[:, half_width:]))
    sums_1 = low(sum_blocks(sums_1[0], sums_1_other))
    sums_2_other = other_core(sums_2[1])
    up_second = block(up_second, dp, 2), block(up_second, 1 - dp, 2)
    down_second = block(down_second, dp, 2), block(down_second, 1 - dp, 2)
    back_3, up_first, up_second, down_first, down_second, sums_1, sums_2_other = part(
        back_3, up_first, up_second, down_first, down_second, sums_1, sums_2_other
    )

    sums_1 = ring_z(sums_1)
    up_first = up_first, to_owner(up_first)
    up_second = up_second[0], other_dp(up_second[1])
    sums_0_other, sums_3_other = other_core(sums_0[1]), other_core(sums_3[1])
    grad_middle, grad_unit, grad_mix = middle_back(
        (back_0[0], back_0_other, back_3),
        gates,
        router,
        middle,
        inv_second,
        gain_second,
        ct_0[0],
        full_out,
    )
    grad_projected = attend_back(query, key, value, grad_mix, cosine, sine, segment)
    (
        sums_0_other,
        sums_1,
        sums_3_other,
        grad_projected,
        grad_unit,
        up_first,
        up_second,
        down_first,
        down_second,
    ) = part(
        sums_0_other,
        sums_1,
        sums_3_other,
        grad_projected,
        grad_unit,
        up_first,
        up_second,
        down_first,
        down_second,
    )

    grads_projected, grad_units = swapped(grad_projected), swapped(grad_unit)
    down_first = down_first, to_owner(down_first)
    down_second = down_second[0], other_dp(down_second[1])
    up_first, up_second = low(sum_blocks(*up_first)), low(sum_blocks(*up_second))
    up_first = block(up_first, dp, 2), block(up_first, 1 - dp, 2)
    sums_2 = low(sum_blocks(sums_2[0], sums_2_other, sums_1))
    qkv = qkv_grads(normeds, grads_projected, place)
    sums_2, grad_units, qkv, down_first, down_second, up_first, up_second, grad_projected = part(
        sums_2, grad_units, qkv, down_first, down_second, up_first, up_second, grad_projected
    )

    sums_2 = ring_z(sums_2)
    qkv = slab_sum(qkv, place)
    up_first = up_first[0], owners_dp(up_first[1])
    up_second = up_second, to_owner(up_second)
    down_first, down_second, qkv = part(down_first, down_second, qkv)
    down_first, down_second = low(sum_blocks(*down_first)), low(sum_blocks(*down_second))
    down_first = block(down_first, dp, 2), block(down_first, 1 - dp, 2)
    grad_tokens = tokens_back(
        grad_projected, full_qkv, tokens, inv_first, gain_first, grad_middle
    )
    out = out_grads(mixes, normed_0, grad_units, place)
    grad_tokens = deal(grad_tokens)
    sums_3 = low(sum_blocks(sums_3[0], sums_3_other, sums_2))
    sums_3, out, qkv, up_first, up_second, down_first, down_second, grad_tokens = part(
        sums_3, out, qkv, up_first, up_second, down_first, down_second, grad_tokens
    )

    sums_3 = ring_z(sums_3)
    qkv = slab_sum_on(qkv, place)
    down_first = down_first[0], owners_dp(down_first[1])
    down_second = down_second, to_owner(down_second)
    input_gradient = to_dealt(grad_tokens)
    up_grad = low(jnp.concatenate([sum_blocks(*up_first), sum_blocks(*up_second)], axis=1))
    up_grad = block(up_grad, core, 2), block(up_grad, 1 - core, 2)
    out, qkv, up_grad, down_first, down_second, sums_3, input_gradient = part(
        out, qkv, up_grad, down_first, down_second, sums_3, input_gradient
    )

    qkv, out = line_sum(qkv), slab_sum(out, place)
    down_grad = low(jnp.concatenate([sum_blocks(*down_first), sum_blocks(*down_second)], axis=1))
    down_grad = block(down_grad, core, 2), block(down_grad, 1 - core, 2)
    layer_out = settle(held_at, middle, sums_0[0], sums_0_other, sums_3)
    out, qkv, up_grad, down_grad, layer_out = part(out, qkv, up_grad, down_grad, layer_out)

    qkv, out = line_spread(qkv, place), slab_sum_on(out, place)
    layer_out = to_dealt(layer_out)
    out, qkv, layer_out, up_grad, down_grad = part(out, qkv, layer_out, up_grad, down_grad)

    qkv, out = slab_spread(qkv, place), line_sum(out)
    out, qkv, up_grad, down_grad = part(out, qkv, up_grad, down_grad)

    qkv, out = slab_spread_on(qkv), line_spread(out, place)
    out, qkv, up_grad, down_grad = part(out, qkv, up_grad, down_grad)

    out = slab_spread(out, place)
    up_grad, down_grad = (
        jnp.where(core == x, field[0], other_core(field[1])) for field in (up_grad, down_grad)
    )
    gain = attention_gain.astype(jnp.float32)[:, None]
    qkv_grad, gain_first_grad = finish(
        finish_qkv_kernel, qkv, place, [qkv_weight, gain], [qkv_weight.shape[1], 1]
    )
    out, qkv_grad, gain_first_grad, up_grad, down_grad = part(
        out, qkv_grad, gain_first_grad, up_grad, down_grad
    )

    out_grad, small_grad = finish_out(out, place, True, [])
    (_, first), (_, second) = slab_spread_on(out)
    out_grad, small_grad = finish_out([first, second], place, False, [out_grad, small_grad])
    gate_up_grad, down_grad = (field[None].astype(jnp.float32) for field in (up_grad, down_grad))
    return (
        layer_out,
        input_gradient,
        gain_first_grad[:, 0],
        small_grad[:, expert_count],
        qkv_grad,
        out_grad,
        small_grad[:, :expert_count],
        gate_up_grad,
        down_grad,
    )


def solution(mesh):
    ringed = (mesh.shape["dp"], mesh.shape["expert"], mesh.shape["shard"]) == (2, 8, 2)
    shards = ring_shards if ringed else routed_shards
    return jax.shard_map(
        shards,
        mesh=mesh,
        in_specs=(
            P(("dp", "expert", "shard"), None),
            P(("dp", "expert", "shard"), None),
            P(("dp", "expert", "shard"), None),
            P(("dp", "expert", "shard"), None),
            P(("dp", "expert", "shard"), None),
            P("shard"),
            P("shard"),
            P("shard", None),
            P("shard", None),
            P("shard", None),
            P("expert", None, None),
            P("expert", None, None),
        ),
        out_specs=(
            P(("dp", "expert", "shard"), None),
            P(("dp", "expert", "shard"), None),
            P("shard"),
            P("shard"),
            P("shard", None),
            P("shard", None),
            P("shard", None),
            P("expert", ("dp", "shard"), None),
            P("expert", ("dp", "shard"), None),
        ),
        check_vma=False,
    )
```

```python
import functools

import jax
import jax.numpy as jnp
from jax import lax
from jax.experimental import pallas as pl
from jax.experimental.pallas import tpu as pltpu
from jax.sharding import PartitionSpec as P

QUERY_HEADS = 12
KEY_VALUE_HEADS = 2
HEAD_SIZE = 128
TOP = 4


EPS = 1e-06
THETA = 1000000.0


def positions_of(lengths_dev, count_of_rows):
    seq_ends = jnp.cumsum(lengths_dev)
    starts = seq_ends - lengths_dev
    places = jnp.arange(count_of_rows, dtype=jnp.int32)
    segment = jnp.sum((places[:, None] >= seq_ends[None, :]).astype(jnp.int32), axis=1)
    member = segment[:, None] == jnp.arange(lengths_dev.shape[0], dtype=jnp.int32)[None, :]
    start_of = jnp.sum(jnp.where(member, starts[None, :], 0), axis=1)
    return (segment, places - start_of)


def apply_rotation(field, token_position, direction):
    half_dim = field.shape[-1] // 2
    frequency = THETA ** (-jnp.arange(half_dim, dtype=jnp.float32) / half_dim)
    angles = token_position.astype(jnp.float32)[:, None] * frequency[None, :]
    cosine = jnp.cos(angles)[:, None, :]
    sine_term = direction * jnp.sin(angles)[:, None, :]
    lead_part = field[..., :half_dim]
    tail_part = field[..., half_dim:]
    return jnp.concatenate(
        [lead_part * cosine - tail_part * sine_term, tail_part * cosine + lead_part * sine_term],
        axis=-1,
    )


def masked_scores(query_block, key_matrix_rows, segment_block, segment, row_start):
    raw_scores = jnp.einsum(
        "ihgd,jhd->hgij", query_block, key_matrix_rows, preferred_element_type=jnp.float32
    ) * HEAD_SIZE ** (-0.5)
    query_at = row_start + jnp.arange(query_block.shape[0], dtype=jnp.int32)
    key_at = jnp.arange(key_matrix_rows.shape[0], dtype=jnp.int32)
    allowed = (segment_block[:, None] == segment[None, :]) & (key_at[None, :] <= query_at[:, None])
    return jnp.where(allowed, raw_scores, -1e30)


def norm_back(field, inv_scale, gain_vec, grad_normed):
    scaled = grad_normed * gain_vec
    grad_field = inv_scale * scaled - field * inv_scale**3 * jnp.mean(
        scaled * field, axis=1, keepdims=True
    )
    grad_gain = jnp.sum(field * inv_scale * grad_normed, axis=0)
    return (grad_field, grad_gain)


def activate(gate_up):
    hidden_width = gate_up.shape[1] // 2
    return jax.nn.gelu(gate_up[:, :hidden_width], approximate=True) * gate_up[:, hidden_width:]


def routed_shards(
    hidden_in,
    cotangent,
    deal_order,
    lengths,
    routes,
    attention_gain,
    expert_gain,
    qkv_weight,
    out_weight,
    router_weight,
    gate_up_weight,
    down_weight,
):
    count_of_rows = hidden_in.shape[0]
    model_width = hidden_in.shape[1]
    head_groups = QUERY_HEADS // KEY_VALUE_HEADS
    arrived_in, arrived_ct = (
        lax.all_to_all(hidden_in, "dp", split_axis=0, concat_axis=0, tiled=True),
        lax.all_to_all(cotangent, "dp", split_axis=0, concat_axis=0, tiled=True),
    )
    deal_rows = deal_order[0]
    tokens = arrived_in[deal_rows]
    upstream = arrived_ct[deal_rows].astype(jnp.float32)
    gain_first, gain_second, full_qkv, full_out, full_router = (
        lax.all_gather(attention_gain, "shard", axis=0, tiled=True),
        lax.all_gather(expert_gain, "shard", axis=0, tiled=True),
        lax.all_gather(qkv_weight, "shard", axis=0, tiled=True),
        lax.all_gather(out_weight, "shard", axis=0, tiled=True),
        lax.all_gather(router_weight, "shard", axis=0, tiled=True),
    )
    gain_first = gain_first.astype(jnp.float32)
    gain_second = gain_second.astype(jnp.float32)
    residual = tokens.astype(jnp.float32)
    inv_first = lax.rsqrt(jnp.mean(residual * residual, axis=1, keepdims=True) + EPS)
    normed_attn = (residual * inv_first * gain_first).astype(jnp.bfloat16)
    projected_rows = jnp.dot(normed_attn, full_qkv, preferred_element_type=jnp.float32)
    segment, token_position = positions_of(lengths[0], count_of_rows)
    query_matrix_rows = (
        apply_rotation(
            projected_rows[:, : QUERY_HEADS * HEAD_SIZE].reshape(
                count_of_rows, QUERY_HEADS, HEAD_SIZE
            ),
            token_position,
            1.0,
        )
        .astype(jnp.bfloat16)
        .reshape(count_of_rows, KEY_VALUE_HEADS, head_groups, HEAD_SIZE)
    )
    key_matrix_rows = apply_rotation(
        projected_rows[
            :, QUERY_HEADS * HEAD_SIZE : (QUERY_HEADS + KEY_VALUE_HEADS) * HEAD_SIZE
        ].reshape(count_of_rows, KEY_VALUE_HEADS, HEAD_SIZE),
        token_position,
        1.0,
    ).astype(jnp.bfloat16)
    value_matrix_rows = (
        projected_rows[:, (QUERY_HEADS + KEY_VALUE_HEADS) * HEAD_SIZE :]
        .reshape(count_of_rows, KEY_VALUE_HEADS, HEAD_SIZE)
        .astype(jnp.bfloat16)
    )
    block_rows = min(count_of_rows, 512)
    block_starts = jnp.arange(count_of_rows // block_rows, dtype=jnp.int32) * block_rows

    def forward_block(row_start):
        scores = masked_scores(query_matrix_rows, key_matrix_rows, segment, segment, row_start)
        row_max = jnp.max(scores, axis=-1, keepdims=True)
        exp_scores = jnp.exp(scores - row_max)
        exp_total = jnp.sum(exp_scores, axis=-1, keepdims=True)
        soft_probs = (exp_scores / exp_total).astype(jnp.bfloat16)
        mix_block = jnp.einsum(
            "hgij,jhd->ihgd", soft_probs, value_matrix_rows, preferred_element_type=jnp.float32
        )
        return (mix_block, (row_max + jnp.log(exp_total))[..., 0])

    mix_blocks, logsum = lax.map(forward_block, block_starts)
    attn_mix = mix_blocks.reshape(count_of_rows, QUERY_HEADS * HEAD_SIZE).astype(jnp.bfloat16)
    middle = residual + jnp.dot(attn_mix, full_out, preferred_element_type=jnp.float32)
    inv_second = lax.rsqrt(jnp.mean(middle * middle, axis=1, keepdims=True) + EPS)
    normed_moe = (middle * inv_second * gain_second).astype(jnp.bfloat16)
    logits = jnp.dot(normed_moe, full_router, preferred_element_type=jnp.float32)
    gate_probs = jax.nn.softmax(jnp.take_along_axis(logits, routes, axis=1), axis=-1)
    expert_count = full_router.shape[1]
    peer_count = lax.axis_size("expert")
    capacity = min(count_of_rows, max(2, 3 * count_of_rows * TOP // (2 * expert_count)))
    flat_routes = routes.reshape(-1)
    expert_ids = jnp.arange(expert_count, dtype=jnp.int32)
    onehot = (flat_routes[:, None] == expert_ids[None, :]).astype(jnp.int32)
    slot_rank = jnp.sum(jnp.cumsum(onehot, axis=0) * onehot, axis=1) - 1
    target = flat_routes * capacity + slot_rank
    pair_count = count_of_rows * TOP
    slot_pair = (
        jnp.full((expert_count * capacity,), pair_count, jnp.int32)
        .at[target]
        .set(jnp.arange(pair_count, dtype=jnp.int32))
    )
    padded = jnp.concatenate([normed_moe, jnp.zeros((1, model_width), jnp.bfloat16)], axis=0)
    sending = padded[slot_pair // TOP].reshape(peer_count, capacity, model_width)
    received = lax.all_to_all(sending, "expert", split_axis=0, concat_axis=0, tiled=True)
    rows_in = received.reshape(peer_count * capacity, model_width)
    gate_up = jnp.dot(rows_in, gate_up_weight[0], preferred_element_type=jnp.float32)
    hidden_rows = activate(gate_up).astype(jnp.bfloat16)
    expert_out = jnp.dot(hidden_rows, down_weight[0], preferred_element_type=jnp.float32).astype(
        jnp.bfloat16
    )
    returned = lax.all_to_all(
        expert_out.reshape(peer_count, capacity, model_width),
        "expert",
        split_axis=0,
        concat_axis=0,
        tiled=True,
    )
    per_pair = returned.reshape(peer_count * capacity, model_width)[target].reshape(
        count_of_rows, TOP, model_width
    )
    expert_sum = jnp.zeros((count_of_rows, model_width), jnp.float32)
    for choice_slot in range(TOP):
        expert_sum = expert_sum + gate_probs[:, choice_slot : choice_slot + 1] * per_pair[
            :, choice_slot
        ].astype(jnp.float32)
    final_rows = middle + expert_sum
    grad_pairs = (gate_probs[:, :, None] * upstream[:, None, :]).astype(jnp.bfloat16)
    grad_gates = jnp.stack(
        [
            jnp.sum(per_pair[:, choice_slot].astype(jnp.float32) * upstream, axis=1)
            for choice_slot in range(TOP)
        ],
        axis=1,
    )
    padded_grad = jnp.concatenate(
        [grad_pairs.reshape(pair_count, model_width), jnp.zeros((1, model_width), jnp.bfloat16)],
        axis=0,
    )
    sending_back = padded_grad[slot_pair].reshape(peer_count, capacity, model_width)
    grad_rows = lax.all_to_all(
        sending_back, "expert", split_axis=0, concat_axis=0, tiled=True
    ).reshape(peer_count * capacity, model_width)
    grad_hidden = jnp.dot(grad_rows, down_weight[0].T, preferred_element_type=jnp.float32)
    grad_gate_up = jax.vjp(activate, gate_up)[1](grad_hidden)[0].astype(jnp.bfloat16)
    term_down = jnp.dot(hidden_rows.T, grad_rows, preferred_element_type=jnp.float32)
    term_gate_up = jnp.dot(rows_in.T, grad_gate_up, preferred_element_type=jnp.float32)
    grad_rows_in = jnp.dot(
        grad_gate_up, gate_up_weight[0].T, preferred_element_type=jnp.float32
    ).astype(jnp.bfloat16)
    back_rows = lax.all_to_all(
        grad_rows_in.reshape(peer_count, capacity, model_width),
        "expert",
        split_axis=0,
        concat_axis=0,
        tiled=True,
    )
    back_pairs = back_rows.reshape(peer_count * capacity, model_width)[target].reshape(
        count_of_rows, TOP, model_width
    )
    grad_normed = jnp.zeros((count_of_rows, model_width), jnp.float32)
    for choice_slot in range(TOP):
        grad_normed = grad_normed + back_pairs[:, choice_slot].astype(jnp.float32)
    mean_term = jnp.sum(gate_probs * grad_gates, axis=1, keepdims=True)
    grad_chosen = gate_probs * (grad_gates - mean_term)
    grad_logits = jnp.sum(
        jnp.where(routes[:, :, None] == expert_ids[None, None, :], grad_chosen[:, :, None], 0.0),
        axis=1,
    ).astype(jnp.bfloat16)
    term_router = jnp.dot(normed_moe.T, grad_logits, preferred_element_type=jnp.float32)
    grad_normed = grad_normed + jnp.dot(
        grad_logits, full_router.T, preferred_element_type=jnp.float32
    )
    grad_middle_norm, term_gain_second = norm_back(middle, inv_second, gain_second, grad_normed)
    grad_middle = upstream + grad_middle_norm
    grad_attn_out = grad_middle.astype(jnp.bfloat16)
    term_out = jnp.dot(attn_mix.T, grad_attn_out, preferred_element_type=jnp.float32)
    grad_mix = (
        jnp.dot(grad_attn_out, full_out.T, preferred_element_type=jnp.float32)
        .astype(jnp.bfloat16)
        .reshape(count_of_rows, KEY_VALUE_HEADS, head_groups, HEAD_SIZE)
    )

    def backward_block(accums, inputs):
        acc_key, value_accumulator = accums
        row_start, logsum_block = inputs
        scores = masked_scores(query_matrix_rows, key_matrix_rows, segment, segment, row_start)
        soft_probs = jnp.exp(scores - logsum_block[..., None])
        grad_probs = jnp.einsum(
            "ihgd,jhd->hgij", grad_mix, value_matrix_rows, preferred_element_type=jnp.float32
        )
        value_accumulator = value_accumulator + jnp.einsum(
            "hgij,ihgd->jhd",
            soft_probs.astype(jnp.bfloat16),
            grad_mix,
            preferred_element_type=jnp.float32,
        )
        grad_scores = (
            soft_probs * (grad_probs - jnp.sum(soft_probs * grad_probs, axis=-1, keepdims=True))
        ).astype(jnp.bfloat16)
        grad_query = HEAD_SIZE ** (-0.5) * jnp.einsum(
            "hgij,jhd->ihgd", grad_scores, key_matrix_rows, preferred_element_type=jnp.float32
        )
        acc_key = acc_key + HEAD_SIZE ** (-0.5) * jnp.einsum(
            "hgij,ihgd->jhd", grad_scores, query_matrix_rows, preferred_element_type=jnp.float32
        )
        return ((acc_key, value_accumulator), grad_query)

    zero_key_value = jnp.zeros((count_of_rows, KEY_VALUE_HEADS, HEAD_SIZE), jnp.float32)
    (acc_key, value_accumulator), grad_query = lax.scan(
        backward_block, (zero_key_value, zero_key_value), (block_starts, logsum)
    )
    grad_query = apply_rotation(
        grad_query.reshape(count_of_rows, QUERY_HEADS, HEAD_SIZE), token_position, -1.0
    )
    key_gradient = apply_rotation(acc_key, token_position, -1.0)
    grad_projected = jnp.concatenate(
        [
            grad_query.reshape(count_of_rows, QUERY_HEADS * HEAD_SIZE),
            key_gradient.reshape(count_of_rows, KEY_VALUE_HEADS * HEAD_SIZE),
            value_accumulator.reshape(count_of_rows, KEY_VALUE_HEADS * HEAD_SIZE),
        ],
        axis=1,
    ).astype(jnp.bfloat16)
    term_qkv = jnp.dot(normed_attn.T, grad_projected, preferred_element_type=jnp.float32)
    grad_normed_attn = jnp.dot(grad_projected, full_qkv.T, preferred_element_type=jnp.float32)
    grad_resid_norm, term_gain_first = norm_back(residual, inv_first, gain_first, grad_normed_attn)
    grad_tokens = (grad_middle + grad_resid_norm).astype(jnp.bfloat16)
    inverse = (
        jnp.zeros((count_of_rows,), jnp.int32)
        .at[deal_rows]
        .set(jnp.arange(count_of_rows, dtype=jnp.int32))
    )
    layer_out, input_gradient = (
        lax.all_to_all(
            final_rows.astype(jnp.bfloat16)[inverse], "dp", split_axis=0, concat_axis=0, tiled=True
        ),
        lax.all_to_all(grad_tokens[inverse], "dp", split_axis=0, concat_axis=0, tiled=True),
    )
    shard_terms = (
        lax.psum_scatter(
            term_gain_first.astype(jnp.bfloat16), "shard", scatter_dimension=0, tiled=True
        ).astype(jnp.float32),
        lax.psum_scatter(
            term_gain_second.astype(jnp.bfloat16), "shard", scatter_dimension=0, tiled=True
        ).astype(jnp.float32),
        lax.psum_scatter(
            term_qkv.astype(jnp.bfloat16), "shard", scatter_dimension=0, tiled=True
        ).astype(jnp.float32),
        lax.psum_scatter(
            term_out.astype(jnp.bfloat16), "shard", scatter_dimension=0, tiled=True
        ).astype(jnp.float32),
        lax.psum_scatter(
            term_router.astype(jnp.bfloat16), "shard", scatter_dimension=0, tiled=True
        ).astype(jnp.float32),
    )
    gain_first_grad, gain_second_grad, qkv_grad, out_grad, router_grad = lax.psum(
        (shard_terms[0], shard_terms[1], shard_terms[2], shard_terms[3], shard_terms[4]),
        ("dp", "expert"),
    )
    gate_up_grad, down_grad = (
        lax.psum_scatter(
            term_gate_up[None].astype(jnp.bfloat16),
            ("dp", "shard"),
            scatter_dimension=1,
            tiled=True,
        ).astype(jnp.float32),
        lax.psum_scatter(
            term_down[None].astype(jnp.bfloat16), ("dp", "shard"), scatter_dimension=1, tiled=True
        ).astype(jnp.float32),
    )
    return (
        layer_out,
        input_gradient,
        gain_first_grad,
        gain_second_grad,
        qkv_grad,
        out_grad,
        router_grad,
        gate_up_grad,
        down_grad,
    )


RING_NEXT = (1, 3, 0, 2)
LAST_WITH_LAST = (((1,), (1,)), ((), ()))


def after(value, *earlier):
    return lax.optimization_barrier((value, *earlier))[0]


def part(*fields):
    return lax.optimization_barrier(fields)


def other_core(field):
    return lax.ppermute(field, "shard", [(0, 1), (1, 0)])


def other_dp(field):
    return lax.ppermute(field, "dp", [(0, 1), (1, 0)])


def owners_dp(field):
    pairs = [
        ((d * 8 + e) * 2 + e % 2, ((1 - d) * 8 + e) * 2 + e % 2) for d in range(2) for e in range(8)
    ]
    return lax.ppermute(field, ("dp", "expert", "shard"), pairs)


def across_x(field):
    return lax.ppermute(field, "expert", [(i, i ^ 1) for i in range(8)])


def across_dp_x(field):
    pairs = [(d * 8 + e, (1 - d) * 8 + (e ^ 1)) for d in range(2) for e in range(8)]
    return lax.ppermute(field, ("dp", "expert"), pairs)


def across_z(field, distance):
    return lax.ppermute(field, "expert", [(i, i ^ (2 * distance)) for i in range(8)])


def ring_z(field):
    pairs = [(2 * z + x, 2 * RING_NEXT[z] + x) for z in range(4) for x in range(2)]
    return lax.ppermute(field, "expert", pairs)


def to_owner(field):
    pairs = [(e * 2 + c, (e ^ 1) * 2 + c) for e in range(8) for c in range(2) if e % 2 != c]
    return lax.ppermute(field, ("expert", "shard"), pairs)


def from_owner(field):
    pairs = [(e * 2 + c, (e ^ 1) * 2 + c) for e in range(8) for c in range(2) if e % 2 == c]
    return lax.ppermute(field, ("expert", "shard"), pairs)


def in_order(first, own, received, axis=0):
    return jnp.where(
        first,
        jnp.concatenate([own, received], axis=axis),
        jnp.concatenate([received, own], axis=axis),
    )


def block(field, index, count):
    rows = field.shape[0] // count
    return lax.dynamic_slice_in_dim(field, index * rows, rows, axis=0)


def sum_blocks(*fields):
    total = fields[0].astype(jnp.float32)
    for field in fields[1:]:
        total = total + field.astype(jnp.float32)
    return total


def low(field):
    return field.astype(jnp.bfloat16)


def slab_cut(first, second, at, other):
    return (
        (block(first, at, 2), block(first, 1 - at, 2)),
        (block(second, other, 2), block(second, 1 - other, 2)),
    )


def slab_sum(cuts, place):
    dp, x, _, _ = place
    (first, first_out), (second, second_out) = cuts
    first = low(sum_blocks(first, across_x(first_out)))
    second = low(sum_blocks(second, other_dp(second_out)))
    return slab_cut(first, second, dp, x)


def slab_sum_on(cuts, place):
    z = place[2]
    (first, first_out), (second, second_out) = cuts
    first = sum_blocks(first, other_dp(first_out))
    second = sum_blocks(second, across_x(second_out))
    part = low(jnp.concatenate([first, second]))
    return [block(part, z ^ k, 4) for k in range(4)]


def line_sum(cuts):
    return low(sum_blocks(cuts[0], *[across_z(cuts[k], k) for k in (1, 2, 3)]))


def put_in_order(pieces, own):
    stacked = jnp.stack(pieces)
    return jnp.concatenate(
        [lax.dynamic_index_in_dim(stacked, own ^ b, 0, False) for b in range(len(pieces))]
    )


def line_spread(part, place):
    part = put_in_order([part] + [across_z(part, k) for k in (1, 2, 3)], place[2])
    return jnp.split(part, 2)


def slab_spread(halves, place):
    dp, x, _, _ = place
    first, second = halves
    return in_order(dp == 0, first, other_dp(first)), in_order(x == 0, second, across_x(second))


def slab_spread_on(halves):
    first, second = halves
    return (first, across_x(first)), (second, other_dp(second))


def matmul(left, right, dims=(((1,), (0,)), ((), ()))):
    return lax.dot_general(left, right, dims, preferred_element_type=jnp.float32)


FIRST_WITH_FIRST = (((0,), (0,)), ((), ()))


EXTRA = 16


def packed(field, columns):
    high = low(field)
    rest = low(field - high.astype(jnp.float32))
    pad = jnp.zeros((field.shape[0], columns - 2 * field.shape[1]), jnp.bfloat16)
    block = jnp.concatenate([high, rest, pad], axis=1)
    return jnp.concatenate([block, jnp.zeros((EXTRA - field.shape[0], columns), jnp.bfloat16)])


def unpacked(extra, rows):
    field = extra.astype(jnp.float32)[: EXTRA // 2]
    return field[:, :rows] + field[:, rows : 2 * rows]


def expert_kernel(
    choice,
    own_rows,
    other_rows,
    own_ct,
    other_ct,
    up_own,
    up_other,
    down_own,
    down_other,
    *refs,
    columns,
):
    (
        own_sum,
        other_sum,
        own_back,
        other_back,
        hidden_ref,
        grad_out_ref,
        grad_up_ref,
        rows_ref,
        unit_ref,
        ct_ref,
        up_ref,
        down_ref,
        up_sem,
        down_sem,
    ) = refs[-14:]
    width = down_ref.shape[0]
    first = pl.program_id(0) == 0

    @pl.when(first & (choice[0] == 1))
    def _():
        pltpu.make_async_copy(up_own, up_ref, up_sem).start()
        pltpu.make_async_copy(down_own, down_ref, down_sem).start()

    @pl.when(first & (choice[0] == 0))
    def _():
        pltpu.make_async_copy(up_other, up_ref, up_sem).start()
        pltpu.make_async_copy(down_other, down_ref, down_sem).start()

    @pl.when(first)
    def _():
        unit_ref[...] = own_rows[...]
        ct_ref[...] = own_ct[...]
        pltpu.make_async_copy(up_own, up_ref, up_sem).wait()
        pltpu.make_async_copy(down_own, down_ref, down_sem).wait()

    @pl.when(pl.program_id(0) == 1)
    def _():
        unit_ref[...] = other_rows[...]
        ct_ref[...] = other_ct[...]

    count = ct_ref.shape[0]
    rows = unit_ref[:count, :]
    rows_ref[...] = rows
    gates = unpacked(unit_ref[count:, :], count)
    mine = lax.broadcasted_iota(jnp.int32, gates.shape, 0) == choice[1]
    weighting = jnp.sum(jnp.where(mine, gates, 0.0), axis=0, keepdims=True)
    weighting = jnp.broadcast_to(weighting, (HEAD_SIZE, rows.shape[0])).T[:, :1]
    ct = ct_ref[...].astype(jnp.float32)
    grad_out = low(weighting * ct)
    grad_out_ref[...] = grad_out
    for start in range(0, width, columns):
        gate, up = pl.ds(start, columns), pl.ds(width + start, columns)
        a, b = matmul(rows, up_ref[:, gate]), matmul(rows, up_ref[:, up])
        tanh = jnp.tanh(0.7978845608028654 * (a + 0.044715 * a * a * a))
        half = 0.5 * (1.0 + tanh)
        gelu = a * half
        hidden_ref[:, gate] = low(gelu * b)
        grad_hidden = matmul(grad_out, down_ref[gate, :], LAST_WITH_LAST)
        slope = half + 0.5 * a * (1.0 - tanh * tanh) * (
            0.7978845608028654 * (1.0 + 3.0 * 0.044715 * a * a)
        )
        grad_up_ref[:, gate] = low(grad_hidden * b * slope)
        grad_up_ref[:, up] = low(grad_hidden * gelu)
    out = low(matmul(hidden_ref[...], down_ref[...])).astype(jnp.float32)
    grad = jnp.sum(ct * out, axis=1, keepdims=True)
    grad = jnp.broadcast_to(grad, (rows.shape[0], HEAD_SIZE)).T[: mine.shape[0], :]
    grad = packed(jnp.where(mine, grad, 0.0), rows.shape[1])
    weighted = low(weighting * out)
    back = low(matmul(grad_up_ref[...], up_ref[...], LAST_WITH_LAST))

    @pl.when(pl.program_id(0) == 0)
    def _():
        own_sum[...], own_back[:count, :], own_back[count:, :] = weighted, back, grad

    @pl.when(pl.program_id(0) == 1)
    def _():
        other_sum[...], other_back[:count, :], other_back[count:, :] = weighted, back, grad


SHORT = pl.CostEstimate(flops=1000, bytes_accessed=1000, transcendentals=0)


def expert_step(step, choice, rows, upstream, matrices, kept):
    tile, model_width = upstream[0].shape
    width = matrices[2].shape[0]
    anywhere = pl.BlockSpec(memory_space=pl.ANY)

    def placed(columns):
        return pl.BlockSpec((tile, columns), lambda i: (2 * step + i, 0))

    def shape(count, columns, dtype=jnp.bfloat16):
        return jax.ShapeDtypeStruct((count * tile, columns), dtype)

    same = pl.BlockSpec((tile, model_width), lambda i: (0, 0))
    unit = pl.BlockSpec((tile + EXTRA, model_width), lambda i: (0, 0))
    out_shape = [
        *[shape(1, model_width)] * 2,
        *[jax.ShapeDtypeStruct((tile + EXTRA, model_width), jnp.bfloat16)] * 2,
        shape(8, width),
        shape(8, model_width),
        shape(8, 2 * width),
        shape(8, model_width),
    ]
    operands = [choice, *rows, *upstream, *matrices]
    in_specs = [pl.BlockSpec(memory_space=pltpu.SMEM), unit, unit, same, same] + [anywhere] * 4
    aliases = {}
    if kept is not None:
        aliases = {len(operands) + i: 4 + i for i in range(4)}
        operands += list(kept)
        in_specs += [anywhere] * 4
    results = pl.pallas_call(
        functools.partial(expert_kernel, columns=256),
        grid=(2,),
        in_specs=in_specs,
        out_specs=[
            *[same] * 2,
            *[unit] * 2,
            placed(width),
            placed(model_width),
            placed(2 * width),
            placed(model_width),
        ],
        out_shape=out_shape,
        scratch_shapes=[
            pltpu.VMEM((tile + EXTRA, model_width), jnp.bfloat16),
            pltpu.VMEM((tile, model_width), jnp.bfloat16),
            pltpu.VMEM((model_width, 2 * width), jnp.bfloat16),
            pltpu.VMEM((width, model_width), jnp.bfloat16),
            pltpu.SemaphoreType.DMA,
            pltpu.SemaphoreType.DMA,
        ],
        input_output_aliases=aliases,
        compiler_params=pltpu.CompilerParams(vmem_limit_bytes=50 * 2**20),
        cost_estimate=SHORT,
    )(*operands)
    return results[:2], results[2:4], results[4:]


def middle_back_kernel(
    back_own,
    back_other,
    back_ring,
    extra_own,
    extra_other,
    extra_ring,
    gates_ref,
    router_ref,
    middle_ref,
    scale_ref,
    gain_ref,
    ct_ref,
    weight_ref,
    grad_ref,
    unit_ref,
    mix_ref,
    gain_grad,
    logits_ref,
    weight_here,
    weight_sem,
):
    step, tile = pl.program_id(0), middle_ref.shape[0]
    at = pl.multiple_of(step * tile, tile)
    copy = pltpu.make_async_copy(weight_ref, weight_here, weight_sem)

    @pl.when(step == 0)
    def _():
        copy.start()
        gates = gates_ref[...]
        grad_gates = sum_blocks(extra_own[...], extra_other[...], extra_ring[...])
        grad_gates = unpacked(grad_gates, gates.shape[1])
        mean_term = jnp.sum(gates * grad_gates, axis=0, keepdims=True)
        logits_ref[...] = low(gates * (grad_gates - mean_term))
        gain_grad[...] = jnp.zeros(gain_grad.shape, jnp.float32)

    grad = sum_blocks(back_own[...], back_other[...], back_ring[...])
    grad = grad + matmul(logits_ref[:, pl.ds(at, tile)], router_ref[...], FIRST_WITH_FIRST)
    middle, scale = middle_ref[...], scale_ref[...]
    scaled = grad * gain_ref[...]
    mean = jnp.mean(scaled * middle, axis=1, keepdims=True)
    out = ct_ref[...].astype(jnp.float32) + scale * scaled - middle * (scale**3 * mean)
    gain_grad[...] += jnp.sum(middle * scale * grad, axis=0, keepdims=True)
    grad_ref[...] = out
    unit_ref[pl.ds(at, tile), :] = low(out)

    @pl.when(step == pl.num_programs(0) - 1)
    def _():
        count, columns = unit_ref.shape[0] - EXTRA, unit_ref.shape[1]
        gain = gain_grad[...]
        high = low(gain).astype(jnp.float32)
        logits = logits_ref[...].astype(jnp.float32)
        experts = logits.shape[0]
        pad = jnp.zeros((experts, columns - logits.shape[1]), jnp.float32)
        behind = jnp.concatenate([logits, pad], axis=1)
        behind = jnp.concatenate([jnp.zeros((EXTRA - experts, columns), jnp.float32), behind])
        row = lax.broadcasted_iota(jnp.int32, behind.shape, 0)
        behind = jnp.where(row == 0, high, jnp.where(row == 1, gain - high, behind))
        unit_ref[count:, :] = low(behind)
        copy.wait()
        for start in range(0, weight_here.shape[0], 256):
            part = pl.ds(start, 256)
            mix_ref[:, part] = low(
                matmul(unit_ref[:count, :], weight_here[part, :], LAST_WITH_LAST)
            )


def middle_back(back, gates, router, middle, scale, gain, upstream, out_weight):
    rows, columns = middle.shape
    tile = HEAD_SIZE

    def whole(*shape):
        return pl.BlockSpec(shape, lambda i: (0, 0))

    def cut(width):
        return pl.BlockSpec((tile, width), lambda i: (i, 0))

    extra = pl.BlockSpec((EXTRA, columns), lambda i: (rows // EXTRA, 0))
    shapes = [
        ((rows, columns), jnp.float32),
        ((rows + EXTRA, columns), jnp.bfloat16),
        ((rows, out_weight.shape[0]), jnp.bfloat16),
    ]
    return pl.pallas_call(
        middle_back_kernel,
        grid=(rows // tile,),
        in_specs=[
            *[cut(columns)] * 3,
            *[extra] * 3,
            whole(*gates.shape),
            whole(*router.shape),
            cut(columns),
            cut(1),
            whole(*gain.shape),
            cut(columns),
            pl.BlockSpec(memory_space=pl.ANY),
        ],
        out_specs=[
            cut(columns),
            whole(rows + EXTRA, columns),
            whole(rows, out_weight.shape[0]),
        ],
        out_shape=[jax.ShapeDtypeStruct(*shape) for shape in shapes],
        scratch_shapes=[
            pltpu.VMEM((1, columns), jnp.float32),
            pltpu.VMEM(gates.shape, jnp.bfloat16),
            pltpu.VMEM(out_weight.shape, jnp.bfloat16),
            pltpu.SemaphoreType.DMA,
        ],
        compiler_params=pltpu.CompilerParams(vmem_limit_bytes=60 * 2**20),
        cost_estimate=SHORT,
    )(*back, *back, gates, router, middle, scale, gain, upstream, out_weight)


def middle_kernel(
    mix_ref, weight_ref, tokens_ref, gain_ref, router_ref, routes_ref, *outs
):
    middle_ref, scale_ref, unit_ref, gates_ref = outs
    rows, columns = tokens_ref.shape
    for start in range(0, columns, 256):
        at = pl.ds(start, 256)
        middle_ref[:, at] = tokens_ref[:, at].astype(jnp.float32) + matmul(
            mix_ref[...], weight_ref[:, at]
        )
    for start in range(0, rows, HEAD_SIZE):
        at = pl.ds(start, HEAD_SIZE)
        middle = middle_ref[at, :]
        scale = lax.rsqrt(jnp.mean(middle * middle, axis=1, keepdims=True) + EPS)
        scale_ref[at, :] = scale
        unit_ref[at, :] = low(middle * scale * gain_ref[...])
    logits = matmul(router_ref[...], unit_ref[:rows, :], LAST_WITH_LAST)
    expert = lax.broadcasted_iota(jnp.int32, logits.shape, 0)
    named = expert == routes_ref[0:1, :]
    for choice in range(1, routes_ref.shape[0]):
        named = named | (expert == routes_ref[choice : choice + 1, :])
    logits = jnp.where(named, logits, -1e30)
    raised = jnp.exp(logits - jnp.max(logits, axis=0, keepdims=True))
    raised = jnp.where(named, raised, 0.0)
    gates = raised / jnp.sum(raised, axis=0, keepdims=True)
    gates_ref[...] = gates
    unit_ref[rows:, :] = packed(gates, columns)


def middle_of(mix, out_weight, tokens, gain, router, routes):
    rows, columns = tokens.shape
    shapes = [
        ((rows, columns), jnp.float32),
        ((rows, 1), jnp.float32),
        ((rows + EXTRA, columns), jnp.bfloat16),
        ((router.shape[0], rows), jnp.float32),
    ]
    return pl.pallas_call(
        middle_kernel,
        out_shape=[jax.ShapeDtypeStruct(*shape) for shape in shapes],
        compiler_params=pltpu.CompilerParams(vmem_limit_bytes=32 * 2**20),
        cost_estimate=SHORT,
    )(mix, out_weight, tokens, gain, router, routes)


def tokens_back_kernel(
    grad_ref, weight_ref, tokens_ref, scale_ref, gain_ref, middle_grad, out_ref, normed
):
    rows, columns = tokens_ref.shape
    for start in range(0, columns, 256):
        at = pl.ds(start, 256)
        normed[:, at] = matmul(grad_ref[...], weight_ref[at, :], LAST_WITH_LAST)
    for start in range(0, rows, HEAD_SIZE):
        at = pl.ds(start, HEAD_SIZE)
        tokens, scale, grad = tokens_ref[at, :].astype(jnp.float32), scale_ref[at, :], normed[at, :]
        scaled = grad * gain_ref[...]
        mean = jnp.mean(scaled * tokens, axis=1, keepdims=True)
        out_ref[at, :] = low(
            middle_grad[at, :] + scale * scaled - tokens * (scale**3 * mean)
        )


def tokens_back(grad_projected, qkv_weight, tokens, scale, gain, grad_middle):
    return pl.pallas_call(
        tokens_back_kernel,
        out_shape=jax.ShapeDtypeStruct(tokens.shape, jnp.bfloat16),
        scratch_shapes=[pltpu.VMEM(tokens.shape, jnp.float32)],
        compiler_params=pltpu.CompilerParams(vmem_limit_bytes=40 * 2**20),
        cost_estimate=SHORT,
    )(grad_projected, qkv_weight, tokens, scale, gain, grad_middle)


def put_pieces(half, place_ref, field, pieces):
    rows = field.shape[0] // 2
    stays, sent = pieces[2 * half : 2 * half + 2]

    @pl.when((pl.program_id(0) == half) & (place_ref[half] == 0))
    def _():
        stays[...], sent[...] = field[:rows], field[rows:]

    @pl.when((pl.program_id(0) == half) & (place_ref[half] == 1))
    def _():
        stays[...], sent[...] = field[rows:], field[:rows]


def qkv_grads_kernel(place_ref, left_own, left_other, right_own, right_other, *pieces):
    field = matmul(left_own[...], right_own[...], FIRST_WITH_FIRST)
    field = low(field + matmul(left_other[...], right_other[...], FIRST_WITH_FIRST))
    for half in range(2):
        put_pieces(half, place_ref, field, pieces)


def out_grads_kernel(place_ref, *refs):
    field = small = gain = 0.0
    for mix, rows, grad, logits, behind in (refs[0:5], refs[5:10]):
        field = field + matmul(mix[...], grad[...], FIRST_WITH_FIRST)
        experts = EXTRA // 2
        chosen = logits[...][EXTRA - experts :]
        pad = [jnp.zeros_like(chosen)] * (HEAD_SIZE // experts - 1)
        chosen = jnp.concatenate([chosen] + pad)
        small = small + matmul(rows[...], chosen, (((0,), (1,)), ((), ())))
        behind = behind[...].astype(jnp.float32)
        gain = gain + behind[0:1] + behind[1:2]
    lane = lax.broadcasted_iota(jnp.int32, small.shape, 1)
    gain = jnp.broadcast_to(gain, (HEAD_SIZE, small.shape[0])).T
    small = jnp.where(lane == EXTRA // 2, gain, small)
    field = low(jnp.concatenate([field, small], axis=1))
    for half in range(2):
        put_pieces(half, place_ref, field, refs[10:])


def chip_grads(kernel, place, operands, total):
    dp, x, _, core = place
    tile = operands[0][0].shape[1] // 4

    def spec(field, rows, at, is_cut):
        if is_cut:
            return pl.BlockSpec((rows, tile), lambda i, place_ref: (at, 2 * place_ref[2] + i))
        columns = operands[0][0].shape[0] if rows == EXTRA else field.shape[1]
        return pl.BlockSpec((rows, columns), lambda i, place_ref: (at, 0))

    piece = (tile // 2, total)
    pieces = pl.pallas_call(
        kernel,
        grid_spec=pltpu.PrefetchScalarGridSpec(
            num_scalar_prefetch=1,
            grid=(2,),
            in_specs=[spec(*operand) for operand in operands],
            out_specs=[pl.BlockSpec(piece, lambda i, place_ref: (0, 0))] * 4,
        ),
        out_shape=[jax.ShapeDtypeStruct(piece, jnp.bfloat16)] * 4,
        compiler_params=pltpu.CompilerParams(vmem_limit_bytes=24 * 2**20),
        cost_estimate=SHORT,
    )(jnp.stack([x, dp, core]).astype(jnp.int32), *[operand[0] for operand in operands])
    return pieces[0:2], pieces[2:4]


def qkv_grads(normed, grads, place):
    rows = grads[0].shape[0]
    operands = [(field, rows, 0, True) for field in normed]
    operands += [(field, rows, 0, False) for field in grads]
    return chip_grads(qkv_grads_kernel, place, operands, grads[0].shape[1])


def out_grads(mixes, units, grads, place):
    rows = mixes[0].shape[0]
    operands = []
    for mix, unit, grad in zip(mixes, units, grads):
        operands += [
            (mix, rows, 0, True),
            (unit, rows, 0, True),
            (grad, rows, 0, False),
            (grad, EXTRA, rows // EXTRA, False),
            (grad, EXTRA, rows // EXTRA, True),
        ]
    return chip_grads(out_grads_kernel, place, operands, grads[0].shape[1] + HEAD_SIZE)


def dealt_kernel(rows_ref, order_ref, out_ref):
    count, columns = rows_ref.shape
    half = count // 2
    order = order_ref[...]
    second = order >= half
    place = jnp.where(second, order - half, order).astype(jnp.float32)
    pad = jnp.zeros((1, columns - count), jnp.float32)
    place = jnp.concatenate([place, pad], axis=1)
    second = jnp.concatenate([jnp.where(second, 1.0, 0.0), pad], axis=1)
    row = lax.broadcasted_iota(jnp.int32, (EXTRA, columns), 0)
    out_ref[:count, :] = rows_ref[...]
    out_ref[count:, :] = low(jnp.where(row == 0, place, jnp.where(row == 1, second, 0.0)))


def dealt_unit(rows, order):
    count, columns = rows.shape
    return pl.pallas_call(
        dealt_kernel,
        out_shape=jax.ShapeDtypeStruct((count + EXTRA, columns), rows.dtype),
        compiler_params=pltpu.CompilerParams(vmem_limit_bytes=16 * 2**20),
        cost_estimate=SHORT,
    )(rows, order)


def settle_kernel(held_ref, middle_ref, own_ref, other_ref, ring_ref, first_ref, second_ref):
    field = low(middle_ref[...] + sum_blocks(own_ref[...], other_ref[...], ring_ref[...]))
    rows = field.shape[0]
    place = lax.broadcasted_iota(jnp.int32, (rows, rows), 0)
    chosen = low(jnp.where(held_ref[...] == place, 1.0, 0.0))
    dealt = low(matmul(chosen, field))
    first_ref[...], second_ref[...] = dealt[: rows // 2], dealt[rows // 2 :]


def settle(held_at, middle, *sums):
    rows, columns = middle.shape
    half = jax.ShapeDtypeStruct((rows // 2, columns), jnp.bfloat16)
    return pl.pallas_call(
        settle_kernel,
        out_shape=[half] * 2,
        compiler_params=pltpu.CompilerParams(vmem_limit_bytes=24 * 2**20),
        cost_estimate=SHORT,
    )(held_at, middle, *sums)


def add_cut_kernel(dp_ref, own_ref, got_ref, sent_ref, kept_ref):
    field = low(sum_blocks(own_ref[...], got_ref[...]))

    @pl.when(pl.program_id(0) == 0)
    def _():
        sent_ref[...] = field

    @pl.when(pl.program_id(0) == 1)
    def _():
        kept_ref[...] = field


def add_cut(own, got, dp):
    rows, columns = own.shape

    def half(i, dp_ref):
        return jnp.where(i == 0, 1 - dp_ref[0], dp_ref[0]), 0

    block_of = pl.BlockSpec((rows // 2, columns), half)
    whole = pl.BlockSpec((rows // 2, columns), lambda i, dp_ref: (0, 0))
    sent, kept = pl.pallas_call(
        add_cut_kernel,
        grid_spec=pltpu.PrefetchScalarGridSpec(
            num_scalar_prefetch=1, grid=(2,), in_specs=[block_of] * 2, out_specs=[whole] * 2
        ),
        out_shape=[jax.ShapeDtypeStruct((rows // 2, columns), jnp.bfloat16)] * 2,
        compiler_params=pltpu.CompilerParams(vmem_limit_bytes=24 * 2**20),
        cost_estimate=SHORT,
    )(dp[None].astype(jnp.int32), own, got)
    return kept, sent


def from_pieces(put, place_ref, pieces):
    step = pl.program_id(0)
    for half in range(2):
        here = 2 * half + place_ref[half]
        pl.when(step == here)(functools.partial(put, pieces[2 * half]))
        pl.when(step == 4 * half + 1 - here)(functools.partial(put, pieces[2 * half + 1]))


def finish_qkv_kernel(place_ref, *refs):
    weight_ref, gain_ref, out_ref, grad_ref = refs[4:]

    def put(field):
        field = field[...].astype(jnp.float32)
        out_ref[...] = field
        total = jnp.sum(field * weight_ref[...].astype(jnp.float32), axis=1, keepdims=True)
        grad_ref[...] = total / gain_ref[...]

    from_pieces(put, place_ref, refs[:4])


def finish_out_kernel(place_ref, first, second, *refs):
    out_ref, small_ref = refs[-2:]
    width = out_ref.shape[1]

    def put(field):
        out_ref[...] = field[:, :width].astype(jnp.float32)
        small_ref[...] = field[:, width:].astype(jnp.float32)

    pl.when(pl.program_id(0) == 0)(functools.partial(put, first))
    pl.when(pl.program_id(0) == 1)(functools.partial(put, second))


def finish_out(pieces, place, is_own, kept):
    dp, x, _, _ = place
    at = jnp.stack([x, dp]).astype(jnp.int32)
    at = at if is_own else 1 - at
    rows, total = pieces[0].shape
    widths = total - HEAD_SIZE, HEAD_SIZE
    whole = pl.BlockSpec((rows, total), lambda i, place_ref: (0, 0))
    return pl.pallas_call(
        finish_out_kernel,
        grid_spec=pltpu.PrefetchScalarGridSpec(
            num_scalar_prefetch=1,
            grid=(2,),
            in_specs=[whole] * 2 + [pl.BlockSpec(memory_space=pl.ANY)] * len(kept),
            out_specs=[
                pl.BlockSpec((rows, width), lambda i, place_ref: (2 * i + place_ref[i], 0))
                for width in widths
            ],
        ),
        out_shape=[jax.ShapeDtypeStruct((4 * rows, width), jnp.float32) for width in widths],
        input_output_aliases={3 + i: i for i in range(len(kept))},
        compiler_params=pltpu.CompilerParams(vmem_limit_bytes=24 * 2**20),
        cost_estimate=SHORT,
    )(at, *pieces, *kept)


def finish(kernel, fields, place, extras, widths):
    dp, x, _, _ = place
    pieces = [*fields[0], *fields[1]]
    rows = pieces[0].shape[0]

    def cut(width):
        return pl.BlockSpec((rows, width), lambda i: (i, 0))

    return pl.pallas_call(
        kernel,
        grid=(4,),
        in_specs=[
            pl.BlockSpec(memory_space=pltpu.SMEM),
            *[pl.BlockSpec(piece.shape, lambda i: (0, 0)) for piece in pieces],
            *[cut(extra.shape[1]) for extra in extras],
        ],
        out_specs=[cut(width) for width in widths],
        out_shape=[jax.ShapeDtypeStruct((4 * rows, width), jnp.float32) for width in widths],
        compiler_params=pltpu.CompilerParams(vmem_limit_bytes=24 * 2**20),
        cost_estimate=SHORT,
    )(jnp.stack([x, dp]).astype(jnp.int32), *pieces, *extras)


def turn(field, cosine, sine):
    half = field.shape[1] // 2
    turned = jnp.concatenate([field[:, half:], field[:, :half]], axis=1)
    return field * cosine + turned * sine


HEADS_AT_ONCE = 2


def attend_kernel(query_in, key_in, value_in, cos_ref, sin_ref, seg_row, seg_column, *refs):
    query_ref, key_ref, value_ref, mix_ref = refs
    cosine, sine = cos_ref[...], sin_ref[...]
    key = low(turn(key_in[...], cosine, sine))
    value = low(value_in[...])
    key_ref[...], value_ref[...] = key, value
    for half in range(HEADS_AT_ONCE):
        columns = slice(half * HEAD_SIZE, (half + 1) * HEAD_SIZE)
        query = low(turn(query_in[:, columns], cosine, sine))
        query_ref[:, columns] = query
        probs = probabilities(query, key, seg_row[...], seg_column[...])
        mix_ref[:, columns] = low(matmul(low(probs), value, FIRST_WITH_FIRST))


def probabilities(query, key, seg_row, seg_column):
    scores = matmul(key, query, LAST_WITH_LAST) * HEAD_SIZE ** (-0.5)
    square = key.shape[0], key.shape[0]
    key_at = lax.broadcasted_iota(jnp.int32, square, 0)
    query_at = lax.broadcasted_iota(jnp.int32, square, 1)
    hidden = jnp.where((seg_row == seg_column) & (key_at <= query_at), 0.0, -1e30)
    hidden = jnp.concatenate([hidden] * (scores.shape[1] // key.shape[0]), axis=1)
    scores = jnp.where(hidden < 0.0, -1e30, scores)
    raised = jnp.exp(scores - jnp.max(scores, axis=0, keepdims=True))
    return raised / jnp.sum(raised, axis=0, keepdims=True)


def attend(projected, cosine, sine, segment):
    rows, width = projected.shape
    groups, heads = KEY_VALUE_HEADS, QUERY_HEADS

    steps = heads // HEADS_AT_ONCE

    def one(index):
        return pl.BlockSpec((rows, HEAD_SIZE), lambda i: (0, index(i)))

    def whole(*shape):
        return pl.BlockSpec(shape, lambda i: (0, 0))

    def shape(count):
        return jax.ShapeDtypeStruct((rows, count * HEAD_SIZE), jnp.bfloat16)

    def group(i):
        return i // (steps // groups)

    head = pl.BlockSpec((rows, HEADS_AT_ONCE * HEAD_SIZE), lambda i: (0, i))
    return pl.pallas_call(
        attend_kernel,
        grid=(steps,),
        in_specs=[
            head,
            one(lambda i: heads + group(i)),
            one(lambda i: heads + groups + group(i)),
            whole(rows, HEAD_SIZE),
            whole(rows, HEAD_SIZE),
            whole(1, rows),
            whole(rows, 1),
        ],
        out_specs=[head, one(group), one(group), head],
        out_shape=[shape(heads), shape(groups), shape(groups), shape(heads)],
        compiler_params=pltpu.CompilerParams(vmem_limit_bytes=24 * 2**20),
        cost_estimate=SHORT,
    )(projected, projected, projected, cosine, sine, segment[None, :], segment[:, None])


def attend_back_kernel(
    query_ref, key_ref, value_ref, grad_ref, cos_ref, sin_ref, seg_row, seg_column, out_ref, *sums
):
    key_sum, value_sum = sums
    step = pl.program_id(0)
    heads, groups = QUERY_HEADS, KEY_VALUE_HEADS
    steps = pl.num_programs(0) // groups
    group, place = step // steps, step % steps
    key, value = key_ref[...], value_ref[...]
    cosine, sine = cos_ref[...], -sin_ref[...]

    def put(head, field):
        at = pl.multiple_of(head * HEAD_SIZE, HEAD_SIZE)
        out_ref[:, pl.ds(at, HEAD_SIZE)] = low(field)

    def stacked(ref):
        return jnp.concatenate(
            [ref[:, at * HEAD_SIZE : (at + 1) * HEAD_SIZE] for at in range(HEADS_AT_ONCE)]
        )

    query, grad_mix = stacked(query_ref), stacked(grad_ref)
    rows = key.shape[0]
    probs = probabilities(query, key, seg_row[...], seg_column[...])
    grad_probs = matmul(value, grad_mix, LAST_WITH_LAST)
    grad_scores = low(
        probs * (grad_probs - jnp.sum(probs * grad_probs, axis=0, keepdims=True))
    )
    grad_query = matmul(grad_scores, key, FIRST_WITH_FIRST) * HEAD_SIZE ** (-0.5)
    for at in range(HEADS_AT_ONCE):
        head = grad_query[at * rows : (at + 1) * rows]
        put(step * HEADS_AT_ONCE + at, turn(head, cosine, sine))
    grad_key = matmul(grad_scores, query) * HEAD_SIZE ** (-0.5)
    grad_value = matmul(low(probs), grad_mix)

    @pl.when(place == 0)
    def _():
        key_sum[...] = grad_key
        value_sum[...] = grad_value

    @pl.when(place > 0)
    def _():
        key_sum[...] += grad_key
        value_sum[...] += grad_value

    @pl.when(place == steps - 1)
    def _():
        put(heads + group, turn(key_sum[...], cosine, sine))
        put(heads + groups + group, value_sum[...])


def attend_back(query, key, value, grad_mix, cosine, sine, segment):
    rows = query.shape[0]
    heads, groups = QUERY_HEADS, KEY_VALUE_HEADS
    steps = heads // HEADS_AT_ONCE

    def whole(*shape):
        return pl.BlockSpec(shape, lambda i: (0, 0))

    head = pl.BlockSpec((rows, HEADS_AT_ONCE * HEAD_SIZE), lambda i: (0, i))
    shared = pl.BlockSpec((rows, HEAD_SIZE), lambda i: (0, i // (steps // groups)))
    width = (heads + 2 * groups) * HEAD_SIZE
    return pl.pallas_call(
        attend_back_kernel,
        grid=(steps,),
        in_specs=[
            head,
            shared,
            shared,
            head,
            whole(rows, HEAD_SIZE),
            whole(rows, HEAD_SIZE),
            whole(1, rows),
            whole(rows, 1),
        ],
        out_specs=whole(rows, width),
        out_shape=jax.ShapeDtypeStruct((rows, width), jnp.bfloat16),
        scratch_shapes=[pltpu.VMEM((rows, HEAD_SIZE), jnp.float32)] * 2,
        compiler_params=pltpu.CompilerParams(vmem_limit_bytes=24 * 2**20),
        cost_estimate=SHORT,
    )(query, key, value, grad_mix, cosine, sine, segment[None, :], segment[:, None])


def ring_shards(
    hidden_in,
    cotangent,
    deal_order,
    lengths,
    routes,
    attention_gain,
    expert_gain,
    qkv_weight,
    out_weight,
    router_weight,
    gate_up_weight,
    down_weight,
):
    count_of_rows = hidden_in.shape[0]
    model_width = hidden_in.shape[1]
    half_rows = count_of_rows // 2
    expert_count = router_weight.shape[1]
    dp, core, at = lax.axis_index("dp"), lax.axis_index("shard"), lax.axis_index("expert")
    x, z = at % 2, at // 2
    place = (dp, x, z, core)
    row_ids = jnp.arange(count_of_rows, dtype=jnp.int32)

    def half_of(field, index):
        return lax.dynamic_slice_in_dim(field, index * half_rows, half_rows, axis=0)

    def sent_dealt(field):
        return half_of(field, dp), other_dp(half_of(field, 1 - dp)), field[count_of_rows:]

    def arrange(own_half, other_half, order):
        held_at = jnp.where(order[1, :count_of_rows] == dp, 0, half_rows)
        held_at = held_at + order[0, :count_of_rows].astype(jnp.int32)
        chosen = low(held_at[:, None] == row_ids[None, :])
        return low(matmul(chosen, jnp.concatenate([own_half, other_half], axis=0)))

    def swapped(field):
        return field, other_core(field)

    held_at = jnp.where(deal_order // half_rows == dp, 0, half_rows) + deal_order % half_rows

    def deal(field):
        field = low(matmul(low(held_at == row_ids[:, None]), field))
        return field[:half_rows], field[half_rows:]

    def to_dealt(halves):
        return halves[0], other_dp(halves[1])

    ct_0 = dealt_unit(cotangent, deal_order)
    order = ct_0[count_of_rows:]
    ct_1 = ring_z(ct_0)
    hidden_out = half_of(after(hidden_in, ct_0), 1 - dp)
    hidden_arrived = other_dp(hidden_out)
    qkv_other, out_other, up_other = (
        send(after(field, hidden_out))
        for send, field in (
            (other_core, qkv_weight),
            (other_core, out_weight),
            (from_owner, gate_up_weight[0]),
        )
    )
    small = jnp.concatenate(
        [router_weight.T, attention_gain[None], expert_gain[None], jnp.zeros_like(router_weight.T[:6])]
    )
    small = in_order(core == 0, small, other_core(small), axis=1)
    router = small[:expert_count]
    gain_first = small[expert_count : expert_count + 1].astype(jnp.float32)
    gain_second = small[expert_count + 1 : expert_count + 2].astype(jnp.float32)
    full_qkv = in_order(core == 0, qkv_weight, qkv_other)
    segment, token_position = positions_of(lengths[0], count_of_rows)
    frequency = THETA ** (-jnp.arange(HEAD_SIZE // 2, dtype=jnp.float32) / (HEAD_SIZE // 2))
    angles = token_position.astype(jnp.float32)[:, None] * frequency[None, :]
    cosine = jnp.concatenate([jnp.cos(angles)] * 2, axis=1)
    sine = jnp.concatenate([-jnp.sin(angles), jnp.sin(angles)], axis=1)
    cosine, sine, full_qkv, hidden_arrived, gain_first, gain_second, router, routes = part(
        cosine, sine, full_qkv, hidden_arrived, gain_first, gain_second, router, routes.T
    )
    tokens = arrange(half_of(hidden_in, dp), hidden_arrived, order)
    residual = tokens.astype(jnp.float32)
    inv_first = lax.rsqrt(jnp.mean(residual * residual, axis=1, keepdims=True) + EPS)
    normed_attn = low(residual * inv_first * gain_first)
    projected = matmul(normed_attn, full_qkv)
    ct_1, projected, ct_0, out_other, down_own = part(
        ct_1, projected, ct_0, out_other, down_weight[0]
    )

    ct_2 = ring_z(ct_1)
    ct_0 = sent_dealt(ct_0)
    down_other = from_owner(down_own)
    full_out = in_order(core == 0, out_weight, out_other)
    query, key, value, attn_mix = attend(projected, cosine, sine, segment)
    middle, inv_second, unit_0, gates = middle_of(
        attn_mix, full_out, tokens, gain_second, router, routes
    )
    ct_2, ct_0, ct_1, unit_0, up_other = part(ct_2, ct_0, ct_1, unit_0, up_other)

    normed_1 = ring_z(unit_0)
    normed_0 = swapped(unit_0)
    ct_1 = sent_dealt(ct_1)
    ct_0 = swapped(arrange(*ct_0))
    normed_1, normed_0, ct_0, ct_1, ct_2, down_other = part(
        normed_1, normed_0, ct_0, ct_1, ct_2, down_other
    )
    choice = jnp.stack([(core == x).astype(jnp.int32), (2 * z + core).astype(jnp.int32)])
    matrices = (gate_up_weight[0], up_other, down_weight[0], down_other)

    ct_3 = ring_z(ct_2)
    ct_2 = sent_dealt(ct_2)
    ct_1, normed_1 = swapped(arrange(*ct_1)), swapped(normed_1)
    sums_0, back_0, kept = expert_step(0, choice, normed_0, ct_0, matrices, None)
    ct_3, ct_1, normed_1, ct_2, kept = part(ct_3, ct_1, normed_1, ct_2, kept)

    normed_2 = ring_z(normed_1[0])
    ct_3 = sent_dealt(ct_3)
    ct_2 = swapped(arrange(*ct_2))
    mixes, normeds = swapped(attn_mix), swapped(normed_attn)
    sums_1, back_1, kept = expert_step(1, choice, normed_1, ct_1, matrices, kept)
    normed_2, ct_3, ct_2, back_1, kept, mixes, normeds = part(
        normed_2, ct_3, ct_2, back_1, kept, mixes, normeds
    )

    normed_3 = ring_z(normed_2)
    normed_2, back_1_other = swapped(normed_2), other_core(back_1[1])
    ct_3 = swapped(arrange(*ct_3))
    sums_2, back_2, kept = expert_step(2, choice, normed_2, ct_2, matrices, kept)
    back_1 = low(sum_blocks(back_1[0], back_1_other))
    normed_3, back_1, ct_3, back_2, kept = part(normed_3, back_1, ct_3, back_2, kept)

    back_1 = ring_z(back_1)
    normed_3, back_2_other = swapped(normed_3), other_core(back_2[1])
    sums_3, back_3, kept = expert_step(3, choice, normed_3, ct_3, matrices, kept)
    back_1, back_2_other, back_3, kept = part(back_1, back_2_other, back_3, kept)

    back_2 = ring_z(low(sum_blocks(back_2[0], back_2_other, back_1)))
    back_3_other, back_0_other = other_core(back_3[1]), other_core(back_0[1])
    sums_1_other, sums_0_other = other_core(sums_1[1]), other_core(sums_0[1])
    all_hidden, all_grad_out, all_grad_up, all_rows = kept
    half_width = model_width // 2
    up_first = low(matmul(all_rows.T, all_grad_up[:, :half_width]))
    up_second = low(matmul(all_rows.T, all_grad_up[:, half_width:]))
    (
        back_2,
        back_3_other,
        back_0_other,
        sums_1_other,
        sums_0_other,
        up_first,
        up_second,
        all_grad_out,
    ) = part(
        back_2,
        back_3_other,
        back_0_other,
        sums_1_other,
        sums_0_other,
        up_first,
        up_second,
        all_grad_out,
    )

    back_3 = ring_z(low(sum_blocks(back_3[0], back_3_other, back_2)))
    down_first = low(matmul(all_hidden.T, all_grad_out[:, :half_width]))
    down_second = low(matmul(all_hidden.T, all_grad_out[:, half_width:]))
    sums_1 = low(sum_blocks(sums_1[0], sums_1_other))
    sums_2_other, sums_3_other = other_core(sums_2[1]), other_core(sums_3[1])
    up_second = block(up_second, dp, 2), block(up_second, 1 - dp, 2)
    down_second = block(down_second, dp, 2), block(down_second, 1 - dp, 2)
    (
        back_3,
        up_first,
        up_second,
        down_first,
        down_second,
        sums_1,
        sums_2_other,
        sums_3_other,
    ) = part(
        back_3,
        up_first,
        up_second,
        down_first,
        down_second,
        sums_1,
        sums_2_other,
        sums_3_other,
    )

    sums_1 = ring_z(sums_1)
    up_first = up_first, to_owner(up_first)
    up_second = up_second[0], other_dp(up_second[1])
    grad_middle, grad_unit, grad_mix = middle_back(
        (back_0[0], back_0_other, back_3),
        gates,
        router,
        middle,
        inv_second,
        gain_second,
        ct_0[0],
        full_out,
    )
    grad_projected = attend_back(query, key, value, grad_mix, cosine, sine, segment)
    sums_1, grad_projected, grad_unit, up_first, up_second, down_first, down_second = part(
        sums_1, grad_projected, grad_unit, up_first, up_second, down_first, down_second
    )

    grads_projected, grad_units = swapped(grad_projected), swapped(grad_unit)
    down_first = down_first, to_owner(down_first)
    down_second = down_second[0], other_dp(down_second[1])
    up_first, up_second = add_cut(*up_first, dp), low(sum_blocks(*up_second))
    sums_2 = low(sum_blocks(sums_2[0], sums_2_other, sums_1))
    qkv = qkv_grads(normeds, grads_projected, place)
    sums_2, grad_units, qkv, down_first, down_second, up_first, up_second, grad_projected = part(
        sums_2, grad_units, qkv, down_first, down_second, up_first, up_second, grad_projected
    )

    sums_2 = ring_z(sums_2)
    qkv = slab_sum(qkv, place)
    up_first = up_first[0], owners_dp(up_first[1])
    up_second = up_second, to_owner(up_second)
    down_first, down_second, qkv = part(down_first, down_second, qkv)
    down_first, down_second = low(sum_blocks(*down_first)), low(sum_blocks(*down_second))
    down_first = block(down_first, dp, 2), block(down_first, 1 - dp, 2)
    grad_tokens = tokens_back(
        grad_projected, full_qkv, tokens, inv_first, gain_first, grad_middle
    )
    out = out_grads(mixes, normed_0, grad_units, place)
    grad_tokens = deal(grad_tokens)
    sums_3 = low(sum_blocks(sums_3[0], sums_3_other, sums_2))
    sums_3, out, qkv, up_first, up_second, down_first, down_second, grad_tokens = part(
        sums_3, out, qkv, up_first, up_second, down_first, down_second, grad_tokens
    )

    sums_3 = ring_z(sums_3)
    qkv = slab_sum_on(qkv, place)
    down_first = down_first[0], owners_dp(down_first[1])
    down_second = down_second, to_owner(down_second)
    input_gradient = to_dealt(grad_tokens)
    up_grad = low(jnp.concatenate([sum_blocks(*up_first), sum_blocks(*up_second)], axis=1))
    up_grad = block(up_grad, core, 2), block(up_grad, 1 - core, 2)
    out, qkv, up_grad, down_first, down_second, sums_3, input_gradient = part(
        out, qkv, up_grad, down_first, down_second, sums_3, input_gradient
    )

    qkv, out = line_sum(qkv), slab_sum(out, place)
    down_grad = low(jnp.concatenate([sum_blocks(*down_first), sum_blocks(*down_second)], axis=1))
    down_grad = block(down_grad, core, 2), block(down_grad, 1 - core, 2)
    layer_out = settle(held_at, middle, sums_0[0], sums_0_other, sums_3)
    out, qkv, up_grad, down_grad, layer_out = part(out, qkv, up_grad, down_grad, layer_out)

    qkv, out = line_spread(qkv, place), slab_sum_on(out, place)
    layer_out = to_dealt(layer_out)
    out, qkv, layer_out, up_grad, down_grad = part(out, qkv, layer_out, up_grad, down_grad)

    qkv, out = slab_spread(qkv, place), line_sum(out)
    out, qkv, up_grad, down_grad = part(out, qkv, up_grad, down_grad)

    qkv, out = slab_spread_on(qkv), line_spread(out, place)
    out, qkv, up_grad, down_grad = part(out, qkv, up_grad, down_grad)

    out = slab_spread(out, place)
    up_grad, down_grad = (
        jnp.where(core == x, field[0], other_core(field[1])) for field in (up_grad, down_grad)
    )
    gain = attention_gain.astype(jnp.float32)[:, None]
    qkv_grad, gain_first_grad = finish(
        finish_qkv_kernel, qkv, place, [qkv_weight, gain], [qkv_weight.shape[1], 1]
    )
    out, qkv_grad, gain_first_grad, up_grad, down_grad, layer_out, input_gradient = part(
        out, qkv_grad, gain_first_grad, up_grad, down_grad, layer_out, input_gradient
    )

    layer_out, input_gradient = (
        in_order(dp == 0, *field) for field in (layer_out, input_gradient)
    )
    out_grad, small_grad = finish_out(out, place, True, [])
    (_, first), (_, second) = slab_spread_on(out)
    out_grad, small_grad = finish_out([first, second], place, False, [out_grad, small_grad])
    gate_up_grad, down_grad = (field[None].astype(jnp.float32) for field in (up_grad, down_grad))
    return (
        layer_out,
        input_gradient,
        gain_first_grad[:, 0],
        small_grad[:, expert_count],
        qkv_grad,
        out_grad,
        small_grad[:, :expert_count],
        gate_up_grad,
        down_grad,
    )


def solution(mesh):
    ringed = (mesh.shape["dp"], mesh.shape["expert"], mesh.shape["shard"]) == (2, 8, 2)
    shards = ring_shards if ringed else routed_shards
    return jax.shard_map(
        shards,
        mesh=mesh,
        in_specs=(
            P(("dp", "expert", "shard"), None),
            P(("dp", "expert", "shard"), None),
            P(("dp", "expert", "shard"), None),
            P(("dp", "expert", "shard"), None),
            P(("dp", "expert", "shard"), None),
            P("shard"),
            P("shard"),
            P("shard", None),
            P("shard", None),
            P("shard", None),
            P("expert", None, None),
            P("expert", None, None),
        ),
        out_specs=(
            P(("dp", "expert", "shard"), None),
            P(("dp", "expert", "shard"), None),
            P("shard"),
            P("shard"),
            P("shard", None),
            P("shard", None),
            P("shard", None),
            P("expert", ("dp", "shard"), None),
            P("expert", ("dp", "shard"), None),
        ),
        check_vma=False,
    )
```

```python
import functools

import jax
import jax.numpy as jnp
from jax import lax
from jax.experimental import pallas as pl
from jax.experimental.pallas import tpu as pltpu
from jax.sharding import PartitionSpec as P

QUERY_HEADS = 12
KEY_VALUE_HEADS = 2
HEAD_SIZE = 128
TOP = 4


EPS = 1e-06
THETA = 1000000.0


def positions_of(lengths_dev, count_of_rows):
    seq_ends = jnp.cumsum(lengths_dev)
    starts = seq_ends - lengths_dev
    places = jnp.arange(count_of_rows, dtype=jnp.int32)
    segment = jnp.sum((places[:, None] >= seq_ends[None, :]).astype(jnp.int32), axis=1)
    member = segment[:, None] == jnp.arange(lengths_dev.shape[0], dtype=jnp.int32)[None, :]
    start_of = jnp.sum(jnp.where(member, starts[None, :], 0), axis=1)
    return (segment, places - start_of)


def apply_rotation(field, token_position, direction):
    half_dim = field.shape[-1] // 2
    frequency = THETA ** (-jnp.arange(half_dim, dtype=jnp.float32) / half_dim)
    angles = token_position.astype(jnp.float32)[:, None] * frequency[None, :]
    cosine = jnp.cos(angles)[:, None, :]
    sine_term = direction * jnp.sin(angles)[:, None, :]
    lead_part = field[..., :half_dim]
    tail_part = field[..., half_dim:]
    return jnp.concatenate(
        [lead_part * cosine - tail_part * sine_term, tail_part * cosine + lead_part * sine_term],
        axis=-1,
    )


def masked_scores(query_block, key_matrix_rows, segment_block, segment, row_start):
    raw_scores = jnp.einsum(
        "ihgd,jhd->hgij", query_block, key_matrix_rows, preferred_element_type=jnp.float32
    ) * HEAD_SIZE ** (-0.5)
    query_at = row_start + jnp.arange(query_block.shape[0], dtype=jnp.int32)
    key_at = jnp.arange(key_matrix_rows.shape[0], dtype=jnp.int32)
    allowed = (segment_block[:, None] == segment[None, :]) & (key_at[None, :] <= query_at[:, None])
    return jnp.where(allowed, raw_scores, -1e30)


def norm_back(field, inv_scale, gain_vec, grad_normed):
    scaled = grad_normed * gain_vec
    grad_field = inv_scale * scaled - field * inv_scale**3 * jnp.mean(
        scaled * field, axis=1, keepdims=True
    )
    grad_gain = jnp.sum(field * inv_scale * grad_normed, axis=0)
    return (grad_field, grad_gain)


def activate(gate_up):
    hidden_width = gate_up.shape[1] // 2
    return jax.nn.gelu(gate_up[:, :hidden_width], approximate=True) * gate_up[:, hidden_width:]


def routed_shards(
    hidden_in,
    cotangent,
    deal_order,
    lengths,
    routes,
    attention_gain,
    expert_gain,
    qkv_weight,
    out_weight,
    router_weight,
    gate_up_weight,
    down_weight,
):
    count_of_rows = hidden_in.shape[0]
    model_width = hidden_in.shape[1]
    head_groups = QUERY_HEADS // KEY_VALUE_HEADS
    arrived_in, arrived_ct = (
        lax.all_to_all(hidden_in, "dp", split_axis=0, concat_axis=0, tiled=True),
        lax.all_to_all(cotangent, "dp", split_axis=0, concat_axis=0, tiled=True),
    )
    deal_rows = deal_order[0]
    tokens = arrived_in[deal_rows]
    upstream = arrived_ct[deal_rows].astype(jnp.float32)
    gain_first, gain_second, full_qkv, full_out, full_router = (
        lax.all_gather(attention_gain, "shard", axis=0, tiled=True),
        lax.all_gather(expert_gain, "shard", axis=0, tiled=True),
        lax.all_gather(qkv_weight, "shard", axis=0, tiled=True),
        lax.all_gather(out_weight, "shard", axis=0, tiled=True),
        lax.all_gather(router_weight, "shard", axis=0, tiled=True),
    )
    gain_first = gain_first.astype(jnp.float32)
    gain_second = gain_second.astype(jnp.float32)
    residual = tokens.astype(jnp.float32)
    inv_first = lax.rsqrt(jnp.mean(residual * residual, axis=1, keepdims=True) + EPS)
    normed_attn = (residual * inv_first * gain_first).astype(jnp.bfloat16)
    projected_rows = jnp.dot(normed_attn, full_qkv, preferred_element_type=jnp.float32)
    segment, token_position = positions_of(lengths[0], count_of_rows)
    query_matrix_rows = (
        apply_rotation(
            projected_rows[:, : QUERY_HEADS * HEAD_SIZE].reshape(
                count_of_rows, QUERY_HEADS, HEAD_SIZE
            ),
            token_position,
            1.0,
        )
        .astype(jnp.bfloat16)
        .reshape(count_of_rows, KEY_VALUE_HEADS, head_groups, HEAD_SIZE)
    )
    key_matrix_rows = apply_rotation(
        projected_rows[
            :, QUERY_HEADS * HEAD_SIZE : (QUERY_HEADS + KEY_VALUE_HEADS) * HEAD_SIZE
        ].reshape(count_of_rows, KEY_VALUE_HEADS, HEAD_SIZE),
        token_position,
        1.0,
    ).astype(jnp.bfloat16)
    value_matrix_rows = (
        projected_rows[:, (QUERY_HEADS + KEY_VALUE_HEADS) * HEAD_SIZE :]
        .reshape(count_of_rows, KEY_VALUE_HEADS, HEAD_SIZE)
        .astype(jnp.bfloat16)
    )
    block_rows = min(count_of_rows, 512)
    block_starts = jnp.arange(count_of_rows // block_rows, dtype=jnp.int32) * block_rows

    def forward_block(row_start):
        scores = masked_scores(query_matrix_rows, key_matrix_rows, segment, segment, row_start)
        row_max = jnp.max(scores, axis=-1, keepdims=True)
        exp_scores = jnp.exp(scores - row_max)
        exp_total = jnp.sum(exp_scores, axis=-1, keepdims=True)
        soft_probs = (exp_scores / exp_total).astype(jnp.bfloat16)
        mix_block = jnp.einsum(
            "hgij,jhd->ihgd", soft_probs, value_matrix_rows, preferred_element_type=jnp.float32
        )
        return (mix_block, (row_max + jnp.log(exp_total))[..., 0])

    mix_blocks, logsum = lax.map(forward_block, block_starts)
    attn_mix = mix_blocks.reshape(count_of_rows, QUERY_HEADS * HEAD_SIZE).astype(jnp.bfloat16)
    middle = residual + jnp.dot(attn_mix, full_out, preferred_element_type=jnp.float32)
    inv_second = lax.rsqrt(jnp.mean(middle * middle, axis=1, keepdims=True) + EPS)
    normed_moe = (middle * inv_second * gain_second).astype(jnp.bfloat16)
    logits = jnp.dot(normed_moe, full_router, preferred_element_type=jnp.float32)
    gate_probs = jax.nn.softmax(jnp.take_along_axis(logits, routes, axis=1), axis=-1)
    expert_count = full_router.shape[1]
    peer_count = lax.axis_size("expert")
    capacity = min(count_of_rows, max(2, 3 * count_of_rows * TOP // (2 * expert_count)))
    flat_routes = routes.reshape(-1)
    expert_ids = jnp.arange(expert_count, dtype=jnp.int32)
    onehot = (flat_routes[:, None] == expert_ids[None, :]).astype(jnp.int32)
    slot_rank = jnp.sum(jnp.cumsum(onehot, axis=0) * onehot, axis=1) - 1
    target = flat_routes * capacity + slot_rank
    pair_count = count_of_rows * TOP
    slot_pair = (
        jnp.full((expert_count * capacity,), pair_count, jnp.int32)
        .at[target]
        .set(jnp.arange(pair_count, dtype=jnp.int32))
    )
    padded = jnp.concatenate([normed_moe, jnp.zeros((1, model_width), jnp.bfloat16)], axis=0)
    sending = padded[slot_pair // TOP].reshape(peer_count, capacity, model_width)
    received = lax.all_to_all(sending, "expert", split_axis=0, concat_axis=0, tiled=True)
    rows_in = received.reshape(peer_count * capacity, model_width)
    gate_up = jnp.dot(rows_in, gate_up_weight[0], preferred_element_type=jnp.float32)
    hidden_rows = activate(gate_up).astype(jnp.bfloat16)
    expert_out = jnp.dot(hidden_rows, down_weight[0], preferred_element_type=jnp.float32).astype(
        jnp.bfloat16
    )
    returned = lax.all_to_all(
        expert_out.reshape(peer_count, capacity, model_width),
        "expert",
        split_axis=0,
        concat_axis=0,
        tiled=True,
    )
    per_pair = returned.reshape(peer_count * capacity, model_width)[target].reshape(
        count_of_rows, TOP, model_width
    )
    expert_sum = jnp.zeros((count_of_rows, model_width), jnp.float32)
    for choice_slot in range(TOP):
        expert_sum = expert_sum + gate_probs[:, choice_slot : choice_slot + 1] * per_pair[
            :, choice_slot
        ].astype(jnp.float32)
    final_rows = middle + expert_sum
    grad_pairs = (gate_probs[:, :, None] * upstream[:, None, :]).astype(jnp.bfloat16)
    grad_gates = jnp.stack(
        [
            jnp.sum(per_pair[:, choice_slot].astype(jnp.float32) * upstream, axis=1)
            for choice_slot in range(TOP)
        ],
        axis=1,
    )
    padded_grad = jnp.concatenate(
        [grad_pairs.reshape(pair_count, model_width), jnp.zeros((1, model_width), jnp.bfloat16)],
        axis=0,
    )
    sending_back = padded_grad[slot_pair].reshape(peer_count, capacity, model_width)
    grad_rows = lax.all_to_all(
        sending_back, "expert", split_axis=0, concat_axis=0, tiled=True
    ).reshape(peer_count * capacity, model_width)
    grad_hidden = jnp.dot(grad_rows, down_weight[0].T, preferred_element_type=jnp.float32)
    grad_gate_up = jax.vjp(activate, gate_up)[1](grad_hidden)[0].astype(jnp.bfloat16)
    term_down = jnp.dot(hidden_rows.T, grad_rows, preferred_element_type=jnp.float32)
    term_gate_up = jnp.dot(rows_in.T, grad_gate_up, preferred_element_type=jnp.float32)
    grad_rows_in = jnp.dot(
        grad_gate_up, gate_up_weight[0].T, preferred_element_type=jnp.float32
    ).astype(jnp.bfloat16)
    back_rows = lax.all_to_all(
        grad_rows_in.reshape(peer_count, capacity, model_width),
        "expert",
        split_axis=0,
        concat_axis=0,
        tiled=True,
    )
    back_pairs = back_rows.reshape(peer_count * capacity, model_width)[target].reshape(
        count_of_rows, TOP, model_width
    )
    grad_normed = jnp.zeros((count_of_rows, model_width), jnp.float32)
    for choice_slot in range(TOP):
        grad_normed = grad_normed + back_pairs[:, choice_slot].astype(jnp.float32)
    mean_term = jnp.sum(gate_probs * grad_gates, axis=1, keepdims=True)
    grad_chosen = gate_probs * (grad_gates - mean_term)
    grad_logits = jnp.sum(
        jnp.where(routes[:, :, None] == expert_ids[None, None, :], grad_chosen[:, :, None], 0.0),
        axis=1,
    ).astype(jnp.bfloat16)
    term_router = jnp.dot(normed_moe.T, grad_logits, preferred_element_type=jnp.float32)
    grad_normed = grad_normed + jnp.dot(
        grad_logits, full_router.T, preferred_element_type=jnp.float32
    )
    grad_middle_norm, term_gain_second = norm_back(middle, inv_second, gain_second, grad_normed)
    grad_middle = upstream + grad_middle_norm
    grad_attn_out = grad_middle.astype(jnp.bfloat16)
    term_out = jnp.dot(attn_mix.T, grad_attn_out, preferred_element_type=jnp.float32)
    grad_mix = (
        jnp.dot(grad_attn_out, full_out.T, preferred_element_type=jnp.float32)
        .astype(jnp.bfloat16)
        .reshape(count_of_rows, KEY_VALUE_HEADS, head_groups, HEAD_SIZE)
    )

    def backward_block(accums, inputs):
        acc_key, value_accumulator = accums
        row_start, logsum_block = inputs
        scores = masked_scores(query_matrix_rows, key_matrix_rows, segment, segment, row_start)
        soft_probs = jnp.exp(scores - logsum_block[..., None])
        grad_probs = jnp.einsum(
            "ihgd,jhd->hgij", grad_mix, value_matrix_rows, preferred_element_type=jnp.float32
        )
        value_accumulator = value_accumulator + jnp.einsum(
            "hgij,ihgd->jhd",
            soft_probs.astype(jnp.bfloat16),
            grad_mix,
            preferred_element_type=jnp.float32,
        )
        grad_scores = (
            soft_probs * (grad_probs - jnp.sum(soft_probs * grad_probs, axis=-1, keepdims=True))
        ).astype(jnp.bfloat16)
        grad_query = HEAD_SIZE ** (-0.5) * jnp.einsum(
            "hgij,jhd->ihgd", grad_scores, key_matrix_rows, preferred_element_type=jnp.float32
        )
        acc_key = acc_key + HEAD_SIZE ** (-0.5) * jnp.einsum(
            "hgij,ihgd->jhd", grad_scores, query_matrix_rows, preferred_element_type=jnp.float32
        )
        return ((acc_key, value_accumulator), grad_query)

    zero_key_value = jnp.zeros((count_of_rows, KEY_VALUE_HEADS, HEAD_SIZE), jnp.float32)
    (acc_key, value_accumulator), grad_query = lax.scan(
        backward_block, (zero_key_value, zero_key_value), (block_starts, logsum)
    )
    grad_query = apply_rotation(
        grad_query.reshape(count_of_rows, QUERY_HEADS, HEAD_SIZE), token_position, -1.0
    )
    key_gradient = apply_rotation(acc_key, token_position, -1.0)
    grad_projected = jnp.concatenate(
        [
            grad_query.reshape(count_of_rows, QUERY_HEADS * HEAD_SIZE),
            key_gradient.reshape(count_of_rows, KEY_VALUE_HEADS * HEAD_SIZE),
            value_accumulator.reshape(count_of_rows, KEY_VALUE_HEADS * HEAD_SIZE),
        ],
        axis=1,
    ).astype(jnp.bfloat16)
    term_qkv = jnp.dot(normed_attn.T, grad_projected, preferred_element_type=jnp.float32)
    grad_normed_attn = jnp.dot(grad_projected, full_qkv.T, preferred_element_type=jnp.float32)
    grad_resid_norm, term_gain_first = norm_back(residual, inv_first, gain_first, grad_normed_attn)
    grad_tokens = (grad_middle + grad_resid_norm).astype(jnp.bfloat16)
    inverse = (
        jnp.zeros((count_of_rows,), jnp.int32)
        .at[deal_rows]
        .set(jnp.arange(count_of_rows, dtype=jnp.int32))
    )
    layer_out, input_gradient = (
        lax.all_to_all(
            final_rows.astype(jnp.bfloat16)[inverse], "dp", split_axis=0, concat_axis=0, tiled=True
        ),
        lax.all_to_all(grad_tokens[inverse], "dp", split_axis=0, concat_axis=0, tiled=True),
    )
    shard_terms = (
        lax.psum_scatter(
            term_gain_first.astype(jnp.bfloat16), "shard", scatter_dimension=0, tiled=True
        ).astype(jnp.float32),
        lax.psum_scatter(
            term_gain_second.astype(jnp.bfloat16), "shard", scatter_dimension=0, tiled=True
        ).astype(jnp.float32),
        lax.psum_scatter(
            term_qkv.astype(jnp.bfloat16), "shard", scatter_dimension=0, tiled=True
        ).astype(jnp.float32),
        lax.psum_scatter(
            term_out.astype(jnp.bfloat16), "shard", scatter_dimension=0, tiled=True
        ).astype(jnp.float32),
        lax.psum_scatter(
            term_router.astype(jnp.bfloat16), "shard", scatter_dimension=0, tiled=True
        ).astype(jnp.float32),
    )
    gain_first_grad, gain_second_grad, qkv_grad, out_grad, router_grad = lax.psum(
        (shard_terms[0], shard_terms[1], shard_terms[2], shard_terms[3], shard_terms[4]),
        ("dp", "expert"),
    )
    gate_up_grad, down_grad = (
        lax.psum_scatter(
            term_gate_up[None].astype(jnp.bfloat16),
            ("dp", "shard"),
            scatter_dimension=1,
            tiled=True,
        ).astype(jnp.float32),
        lax.psum_scatter(
            term_down[None].astype(jnp.bfloat16), ("dp", "shard"), scatter_dimension=1, tiled=True
        ).astype(jnp.float32),
    )
    return (
        layer_out,
        input_gradient,
        gain_first_grad,
        gain_second_grad,
        qkv_grad,
        out_grad,
        router_grad,
        gate_up_grad,
        down_grad,
    )


RING_NEXT = (1, 3, 0, 2)
LAST_WITH_LAST = (((1,), (1,)), ((), ()))


def after(value, *earlier):
    return lax.optimization_barrier((value, *earlier))[0]


def part(*fields):
    return lax.optimization_barrier(fields)


def other_core(field):
    return lax.ppermute(field, "shard", [(0, 1), (1, 0)])


def other_dp(field):
    return lax.ppermute(field, "dp", [(0, 1), (1, 0)])


def owners_dp(field):
    pairs = [
        ((d * 8 + e) * 2 + e % 2, ((1 - d) * 8 + e) * 2 + e % 2) for d in range(2) for e in range(8)
    ]
    return lax.ppermute(field, ("dp", "expert", "shard"), pairs)


def across_x(field):
    return lax.ppermute(field, "expert", [(i, i ^ 1) for i in range(8)])


def across_dp_x(field):
    pairs = [(d * 8 + e, (1 - d) * 8 + (e ^ 1)) for d in range(2) for e in range(8)]
    return lax.ppermute(field, ("dp", "expert"), pairs)


def across_z(field, distance):
    return lax.ppermute(field, "expert", [(i, i ^ (2 * distance)) for i in range(8)])


def ring_z(field):
    pairs = [(2 * z + x, 2 * RING_NEXT[z] + x) for z in range(4) for x in range(2)]
    return lax.ppermute(field, "expert", pairs)


def to_owner(field):
    pairs = [(e * 2 + c, (e ^ 1) * 2 + c) for e in range(8) for c in range(2) if e % 2 != c]
    return lax.ppermute(field, ("expert", "shard"), pairs)


def from_owner(field):
    pairs = [(e * 2 + c, (e ^ 1) * 2 + c) for e in range(8) for c in range(2) if e % 2 == c]
    return lax.ppermute(field, ("expert", "shard"), pairs)


def in_order(first, own, received, axis=0):
    return jnp.where(
        first,
        jnp.concatenate([own, received], axis=axis),
        jnp.concatenate([received, own], axis=axis),
    )


def block(field, index, count):
    rows = field.shape[0] // count
    return lax.dynamic_slice_in_dim(field, index * rows, rows, axis=0)


def sum_blocks(*fields):
    total = fields[0].astype(jnp.float32)
    for field in fields[1:]:
        total = total + field.astype(jnp.float32)
    return total


def low(field):
    return field.astype(jnp.bfloat16)


def slab_cut(first, second, at, other):
    return (
        (block(first, at, 2), block(first, 1 - at, 2)),
        (block(second, other, 2), block(second, 1 - other, 2)),
    )


def slab_sum(cuts, place):
    dp, x, _, _ = place
    (first, first_out), (second, second_out) = cuts
    first = low(sum_blocks(first, across_x(first_out)))
    second = low(sum_blocks(second, other_dp(second_out)))
    return slab_cut(first, second, dp, x)


def slab_sum_on(cuts, place):
    z = place[2]
    (first, first_out), (second, second_out) = cuts
    first = sum_blocks(first, other_dp(first_out))
    second = sum_blocks(second, across_x(second_out))
    part = low(jnp.concatenate([first, second]))
    return [block(part, z ^ k, 4) for k in range(4)]


def line_sum(cuts):
    return low(sum_blocks(cuts[0], *[across_z(cuts[k], k) for k in (1, 2, 3)]))


def put_in_order(pieces, own):
    stacked = jnp.stack(pieces)
    return jnp.concatenate(
        [lax.dynamic_index_in_dim(stacked, own ^ b, 0, False) for b in range(len(pieces))]
    )


def line_spread(part, place):
    part = put_in_order([part] + [across_z(part, k) for k in (1, 2, 3)], place[2])
    return jnp.split(part, 2)


def slab_spread(halves, place):
    dp, x, _, _ = place
    first, second = halves
    return in_order(dp == 0, first, other_dp(first)), in_order(x == 0, second, across_x(second))


def slab_spread_on(halves):
    first, second = halves
    return (first, across_x(first)), (second, other_dp(second))


def matmul(left, right, dims=(((1,), (0,)), ((), ()))):
    return lax.dot_general(left, right, dims, preferred_element_type=jnp.float32)


FIRST_WITH_FIRST = (((0,), (0,)), ((), ()))


EXTRA = 16


def packed(field, columns):
    high = low(field)
    rest = low(field - high.astype(jnp.float32))
    pad = jnp.zeros((field.shape[0], columns - 2 * field.shape[1]), jnp.bfloat16)
    block = jnp.concatenate([high, rest, pad], axis=1)
    return jnp.concatenate([block, jnp.zeros((EXTRA - field.shape[0], columns), jnp.bfloat16)])


def unpacked(extra, rows):
    field = extra.astype(jnp.float32)[: EXTRA // 2]
    return field[:, :rows] + field[:, rows : 2 * rows]


def expert_kernel(
    choice,
    own_rows,
    other_rows,
    own_ct,
    other_ct,
    up_own,
    up_other,
    down_own,
    down_other,
    *refs,
    columns,
):
    (
        own_sum,
        other_sum,
        own_back,
        other_back,
        hidden_ref,
        grad_out_ref,
        grad_up_ref,
        rows_ref,
        unit_ref,
        ct_ref,
        up_ref,
        down_ref,
        up_sem,
        down_sem,
    ) = refs[-14:]
    width = down_ref.shape[0]
    first = pl.program_id(0) == 0

    @pl.when(first & (choice[0] == 1))
    def _():
        pltpu.make_async_copy(up_own, up_ref, up_sem).start()
        pltpu.make_async_copy(down_own, down_ref, down_sem).start()

    @pl.when(first & (choice[0] == 0))
    def _():
        pltpu.make_async_copy(up_other, up_ref, up_sem).start()
        pltpu.make_async_copy(down_other, down_ref, down_sem).start()

    @pl.when(first)
    def _():
        unit_ref[...] = own_rows[...]
        ct_ref[...] = own_ct[...]
        pltpu.make_async_copy(up_own, up_ref, up_sem).wait()
        pltpu.make_async_copy(down_own, down_ref, down_sem).wait()

    @pl.when(pl.program_id(0) == 1)
    def _():
        unit_ref[...] = other_rows[...]
        ct_ref[...] = other_ct[...]

    count = ct_ref.shape[0]
    rows = unit_ref[:count, :]
    rows_ref[...] = rows
    gates = unpacked(unit_ref[count:, :], count)
    mine = lax.broadcasted_iota(jnp.int32, gates.shape, 0) == choice[1]
    weighting = jnp.sum(jnp.where(mine, gates, 0.0), axis=0, keepdims=True)
    weighting = jnp.broadcast_to(weighting, (HEAD_SIZE, rows.shape[0])).T[:, :1]
    ct = ct_ref[...].astype(jnp.float32)
    grad_out = low(weighting * ct)
    grad_out_ref[...] = grad_out
    for start in range(0, width, columns):
        gate, up = pl.ds(start, columns), pl.ds(width + start, columns)
        a, b = matmul(rows, up_ref[:, gate]), matmul(rows, up_ref[:, up])
        tanh = jnp.tanh(0.7978845608028654 * (a + 0.044715 * a * a * a))
        half = 0.5 * (1.0 + tanh)
        gelu = a * half
        hidden_ref[:, gate] = low(gelu * b)
        grad_hidden = matmul(grad_out, down_ref[gate, :], LAST_WITH_LAST)
        slope = half + 0.5 * a * (1.0 - tanh * tanh) * (
            0.7978845608028654 * (1.0 + 3.0 * 0.044715 * a * a)
        )
        grad_up_ref[:, gate] = low(grad_hidden * b * slope)
        grad_up_ref[:, up] = low(grad_hidden * gelu)
    out = low(matmul(hidden_ref[...], down_ref[...])).astype(jnp.float32)
    grad = jnp.sum(ct * out, axis=1, keepdims=True)
    grad = jnp.broadcast_to(grad, (rows.shape[0], HEAD_SIZE)).T[: mine.shape[0], :]
    grad = packed(jnp.where(mine, grad, 0.0), rows.shape[1])
    weighted = low(weighting * out)
    back = low(matmul(grad_up_ref[...], up_ref[...], LAST_WITH_LAST))

    @pl.when(pl.program_id(0) == 0)
    def _():
        own_sum[...], own_back[:count, :], own_back[count:, :] = weighted, back, grad

    @pl.when(pl.program_id(0) == 1)
    def _():
        other_sum[...], other_back[:count, :], other_back[count:, :] = weighted, back, grad


SHORT = pl.CostEstimate(flops=1000, bytes_accessed=1000, transcendentals=0)


def expert_step(step, choice, rows, upstream, matrices, kept):
    tile, model_width = upstream[0].shape
    width = matrices[2].shape[0]
    anywhere = pl.BlockSpec(memory_space=pl.ANY)

    def placed(columns):
        return pl.BlockSpec((tile, columns), lambda i: (2 * step + i, 0))

    def shape(count, columns, dtype=jnp.bfloat16):
        return jax.ShapeDtypeStruct((count * tile, columns), dtype)

    same = pl.BlockSpec((tile, model_width), lambda i: (0, 0))
    unit = pl.BlockSpec((tile + EXTRA, model_width), lambda i: (0, 0))
    out_shape = [
        *[shape(1, model_width)] * 2,
        *[jax.ShapeDtypeStruct((tile + EXTRA, model_width), jnp.bfloat16)] * 2,
        shape(8, width),
        shape(8, model_width),
        shape(8, 2 * width),
        shape(8, model_width),
    ]
    operands = [choice, *rows, *upstream, *matrices]
    in_specs = [pl.BlockSpec(memory_space=pltpu.SMEM), unit, unit, same, same] + [anywhere] * 4
    aliases = {}
    if kept is not None:
        aliases = {len(operands) + i: 4 + i for i in range(4)}
        operands += list(kept)
        in_specs += [anywhere] * 4
    results = pl.pallas_call(
        functools.partial(expert_kernel, columns=256),
        grid=(2,),
        in_specs=in_specs,
        out_specs=[
            *[same] * 2,
            *[unit] * 2,
            placed(width),
            placed(model_width),
            placed(2 * width),
            placed(model_width),
        ],
        out_shape=out_shape,
        scratch_shapes=[
            pltpu.VMEM((tile + EXTRA, model_width), jnp.bfloat16),
            pltpu.VMEM((tile, model_width), jnp.bfloat16),
            pltpu.VMEM((model_width, 2 * width), jnp.bfloat16),
            pltpu.VMEM((width, model_width), jnp.bfloat16),
            pltpu.SemaphoreType.DMA,
            pltpu.SemaphoreType.DMA,
        ],
        input_output_aliases=aliases,
        compiler_params=pltpu.CompilerParams(vmem_limit_bytes=50 * 2**20),
        cost_estimate=SHORT,
    )(*operands)
    return results[:2], results[2:4], results[4:]


def middle_back_kernel(
    back_own,
    back_other,
    back_ring,
    extra_own,
    extra_other,
    extra_ring,
    gates_ref,
    router_ref,
    middle_ref,
    scale_ref,
    gain_ref,
    ct_ref,
    weight_ref,
    grad_ref,
    unit_ref,
    mix_ref,
    gain_grad,
    logits_ref,
    weight_here,
    weight_sem,
):
    step, tile = pl.program_id(0), middle_ref.shape[0]
    at = pl.multiple_of(step * tile, tile)
    copy = pltpu.make_async_copy(weight_ref, weight_here, weight_sem)

    @pl.when(step == 0)
    def _():
        copy.start()
        gates = gates_ref[...]
        grad_gates = sum_blocks(extra_own[...], extra_other[...], extra_ring[...])
        grad_gates = unpacked(grad_gates, gates.shape[1])
        mean_term = jnp.sum(gates * grad_gates, axis=0, keepdims=True)
        logits_ref[...] = low(gates * (grad_gates - mean_term))
        gain_grad[...] = jnp.zeros(gain_grad.shape, jnp.float32)

    grad = sum_blocks(back_own[...], back_other[...], back_ring[...])
    grad = grad + matmul(logits_ref[:, pl.ds(at, tile)], router_ref[...], FIRST_WITH_FIRST)
    middle, scale = middle_ref[...], scale_ref[...]
    scaled = grad * gain_ref[...]
    mean = jnp.mean(scaled * middle, axis=1, keepdims=True)
    out = ct_ref[...].astype(jnp.float32) + scale * scaled - middle * (scale**3 * mean)
    gain_grad[...] += jnp.sum(middle * scale * grad, axis=0, keepdims=True)
    grad_ref[...] = out
    unit_ref[pl.ds(at, tile), :] = low(out)

    @pl.when(step == pl.num_programs(0) - 1)
    def _():
        count, columns = unit_ref.shape[0] - EXTRA, unit_ref.shape[1]
        gain = gain_grad[...]
        high = low(gain).astype(jnp.float32)
        logits = logits_ref[...].astype(jnp.float32)
        experts = logits.shape[0]
        pad = jnp.zeros((experts, columns - logits.shape[1]), jnp.float32)
        behind = jnp.concatenate([logits, pad], axis=1)
        behind = jnp.concatenate([jnp.zeros((EXTRA - experts, columns), jnp.float32), behind])
        row = lax.broadcasted_iota(jnp.int32, behind.shape, 0)
        behind = jnp.where(row == 0, high, jnp.where(row == 1, gain - high, behind))
        unit_ref[count:, :] = low(behind)
        copy.wait()
        for start in range(0, weight_here.shape[0], 256):
            part = pl.ds(start, 256)
            mix_ref[:, part] = low(
                matmul(unit_ref[:count, :], weight_here[part, :], LAST_WITH_LAST)
            )


def middle_back(back, gates, router, middle, scale, gain, upstream, out_weight):
    rows, columns = middle.shape
    tile = HEAD_SIZE

    def whole(*shape):
        return pl.BlockSpec(shape, lambda i: (0, 0))

    def cut(width):
        return pl.BlockSpec((tile, width), lambda i: (i, 0))

    extra = pl.BlockSpec((EXTRA, columns), lambda i: (rows // EXTRA, 0))
    shapes = [
        ((rows, columns), jnp.float32),
        ((rows + EXTRA, columns), jnp.bfloat16),
        ((rows, out_weight.shape[0]), jnp.bfloat16),
    ]
    return pl.pallas_call(
        middle_back_kernel,
        grid=(rows // tile,),
        in_specs=[
            *[cut(columns)] * 3,
            *[extra] * 3,
            whole(*gates.shape),
            whole(*router.shape),
            cut(columns),
            cut(1),
            whole(*gain.shape),
            cut(columns),
            pl.BlockSpec(memory_space=pl.ANY),
        ],
        out_specs=[
            cut(columns),
            whole(rows + EXTRA, columns),
            whole(rows, out_weight.shape[0]),
        ],
        out_shape=[jax.ShapeDtypeStruct(*shape) for shape in shapes],
        scratch_shapes=[
            pltpu.VMEM((1, columns), jnp.float32),
            pltpu.VMEM(gates.shape, jnp.bfloat16),
            pltpu.VMEM(out_weight.shape, jnp.bfloat16),
            pltpu.SemaphoreType.DMA,
        ],
        compiler_params=pltpu.CompilerParams(vmem_limit_bytes=60 * 2**20),
        cost_estimate=SHORT,
    )(*back, *back, gates, router, middle, scale, gain, upstream, out_weight)


def middle_kernel(
    mix_ref, weight_ref, tokens_ref, gain_ref, router_ref, routes_ref, *outs
):
    middle_ref, scale_ref, unit_ref, gates_ref = outs
    rows, columns = tokens_ref.shape
    for start in range(0, columns, 256):
        at = pl.ds(start, 256)
        middle_ref[:, at] = tokens_ref[:, at].astype(jnp.float32) + matmul(
            mix_ref[...], weight_ref[:, at]
        )
    for start in range(0, rows, HEAD_SIZE):
        at = pl.ds(start, HEAD_SIZE)
        middle = middle_ref[at, :]
        scale = lax.rsqrt(jnp.mean(middle * middle, axis=1, keepdims=True) + EPS)
        scale_ref[at, :] = scale
        unit_ref[at, :] = low(middle * scale * gain_ref[...])
    logits = matmul(router_ref[...], unit_ref[:rows, :], LAST_WITH_LAST)
    expert = lax.broadcasted_iota(jnp.int32, logits.shape, 0)
    named = expert == routes_ref[0:1, :]
    for choice in range(1, routes_ref.shape[0]):
        named = named | (expert == routes_ref[choice : choice + 1, :])
    logits = jnp.where(named, logits, -1e30)
    raised = jnp.exp(logits - jnp.max(logits, axis=0, keepdims=True))
    raised = jnp.where(named, raised, 0.0)
    gates = raised / jnp.sum(raised, axis=0, keepdims=True)
    gates_ref[...] = gates
    unit_ref[rows:, :] = packed(gates, columns)


def middle_of(mix, out_weight, tokens, gain, router, routes):
    rows, columns = tokens.shape
    shapes = [
        ((rows, columns), jnp.float32),
        ((rows, 1), jnp.float32),
        ((rows + EXTRA, columns), jnp.bfloat16),
        ((router.shape[0], rows), jnp.float32),
    ]
    return pl.pallas_call(
        middle_kernel,
        out_shape=[jax.ShapeDtypeStruct(*shape) for shape in shapes],
        compiler_params=pltpu.CompilerParams(vmem_limit_bytes=32 * 2**20),
        cost_estimate=SHORT,
    )(mix, out_weight, tokens, gain, router, routes)


def tokens_back_kernel(
    grad_ref, weight_ref, tokens_ref, scale_ref, gain_ref, middle_grad, out_ref, normed
):
    rows, columns = tokens_ref.shape
    for start in range(0, columns, 256):
        at = pl.ds(start, 256)
        normed[:, at] = matmul(grad_ref[...], weight_ref[at, :], LAST_WITH_LAST)
    for start in range(0, rows, HEAD_SIZE):
        at = pl.ds(start, HEAD_SIZE)
        tokens, scale, grad = tokens_ref[at, :].astype(jnp.float32), scale_ref[at, :], normed[at, :]
        scaled = grad * gain_ref[...]
        mean = jnp.mean(scaled * tokens, axis=1, keepdims=True)
        out_ref[at, :] = low(
            middle_grad[at, :] + scale * scaled - tokens * (scale**3 * mean)
        )


def tokens_back(grad_projected, qkv_weight, tokens, scale, gain, grad_middle):
    return pl.pallas_call(
        tokens_back_kernel,
        out_shape=jax.ShapeDtypeStruct(tokens.shape, jnp.bfloat16),
        scratch_shapes=[pltpu.VMEM(tokens.shape, jnp.float32)],
        compiler_params=pltpu.CompilerParams(vmem_limit_bytes=40 * 2**20),
        cost_estimate=SHORT,
    )(grad_projected, qkv_weight, tokens, scale, gain, grad_middle)


def put_pieces(half, place_ref, field, pieces):
    rows = field.shape[0] // 2
    stays, sent = pieces[2 * half : 2 * half + 2]

    @pl.when((pl.program_id(0) == half) & (place_ref[half] == 0))
    def _():
        stays[...], sent[...] = field[:rows], field[rows:]

    @pl.when((pl.program_id(0) == half) & (place_ref[half] == 1))
    def _():
        stays[...], sent[...] = field[rows:], field[:rows]


def qkv_grads_kernel(place_ref, left_own, left_other, right_own, right_other, *pieces):
    field = matmul(left_own[...], right_own[...], FIRST_WITH_FIRST)
    field = low(field + matmul(left_other[...], right_other[...], FIRST_WITH_FIRST))
    for half in range(2):
        put_pieces(half, place_ref, field, pieces)


def out_grads_kernel(place_ref, *refs):
    field = small = gain = 0.0
    for mix, rows, grad, logits, behind in (refs[0:5], refs[5:10]):
        field = field + matmul(mix[...], grad[...], FIRST_WITH_FIRST)
        experts = EXTRA // 2
        chosen = logits[...][EXTRA - experts :]
        pad = [jnp.zeros_like(chosen)] * (HEAD_SIZE // experts - 1)
        chosen = jnp.concatenate([chosen] + pad)
        small = small + matmul(rows[...], chosen, (((0,), (1,)), ((), ())))
        behind = behind[...].astype(jnp.float32)
        gain = gain + behind[0:1] + behind[1:2]
    lane = lax.broadcasted_iota(jnp.int32, small.shape, 1)
    gain = jnp.broadcast_to(gain, (HEAD_SIZE, small.shape[0])).T
    small = jnp.where(lane == EXTRA // 2, gain, small)
    field = low(jnp.concatenate([field, small], axis=1))
    for half in range(2):
        put_pieces(half, place_ref, field, refs[10:])


def chip_grads(kernel, place, operands, total):
    dp, x, _, core = place
    tile = operands[0][0].shape[1] // 4

    def spec(field, rows, at, is_cut):
        if is_cut:
            return pl.BlockSpec((rows, tile), lambda i, place_ref: (at, 2 * place_ref[2] + i))
        columns = operands[0][0].shape[0] if rows == EXTRA else field.shape[1]
        return pl.BlockSpec((rows, columns), lambda i, place_ref: (at, 0))

    piece = (tile // 2, total)
    pieces = pl.pallas_call(
        kernel,
        grid_spec=pltpu.PrefetchScalarGridSpec(
            num_scalar_prefetch=1,
            grid=(2,),
            in_specs=[spec(*operand) for operand in operands],
            out_specs=[pl.BlockSpec(piece, lambda i, place_ref: (0, 0))] * 4,
        ),
        out_shape=[jax.ShapeDtypeStruct(piece, jnp.bfloat16)] * 4,
        compiler_params=pltpu.CompilerParams(vmem_limit_bytes=24 * 2**20),
        cost_estimate=SHORT,
    )(jnp.stack([x, dp, core]).astype(jnp.int32), *[operand[0] for operand in operands])
    return pieces[0:2], pieces[2:4]


def qkv_grads(normed, grads, place):
    rows = grads[0].shape[0]
    operands = [(field, rows, 0, True) for field in normed]
    operands += [(field, rows, 0, False) for field in grads]
    return chip_grads(qkv_grads_kernel, place, operands, grads[0].shape[1])


def out_grads(mixes, units, grads, place):
    rows = mixes[0].shape[0]
    operands = []
    for mix, unit, grad in zip(mixes, units, grads):
        operands += [
            (mix, rows, 0, True),
            (unit, rows, 0, True),
            (grad, rows, 0, False),
            (grad, EXTRA, rows // EXTRA, False),
            (grad, EXTRA, rows // EXTRA, True),
        ]
    return chip_grads(out_grads_kernel, place, operands, grads[0].shape[1] + HEAD_SIZE)


def dealt_kernel(rows_ref, order_ref, out_ref):
    count, columns = rows_ref.shape
    half = count // 2
    order = order_ref[...]
    second = order >= half
    place = jnp.where(second, order - half, order).astype(jnp.float32)
    pad = jnp.zeros((1, columns - count), jnp.float32)
    place = jnp.concatenate([place, pad], axis=1)
    second = jnp.concatenate([jnp.where(second, 1.0, 0.0), pad], axis=1)
    row = lax.broadcasted_iota(jnp.int32, (EXTRA, columns), 0)
    out_ref[:count, :] = rows_ref[...]
    out_ref[count:, :] = low(jnp.where(row == 0, place, jnp.where(row == 1, second, 0.0)))


def dealt_unit(rows, order):
    count, columns = rows.shape
    return pl.pallas_call(
        dealt_kernel,
        out_shape=jax.ShapeDtypeStruct((count + EXTRA, columns), rows.dtype),
        compiler_params=pltpu.CompilerParams(vmem_limit_bytes=16 * 2**20),
        cost_estimate=SHORT,
    )(rows, order)


def settle_kernel(held_ref, middle_ref, own_ref, other_ref, ring_ref, first_ref, second_ref):
    field = low(middle_ref[...] + sum_blocks(own_ref[...], other_ref[...], ring_ref[...]))
    rows = field.shape[0]
    place = lax.broadcasted_iota(jnp.int32, (rows, rows), 0)
    chosen = low(jnp.where(held_ref[...] == place, 1.0, 0.0))
    dealt = low(matmul(chosen, field))
    first_ref[...], second_ref[...] = dealt[: rows // 2], dealt[rows // 2 :]


def settle(held_at, middle, *sums):
    rows, columns = middle.shape
    half = jax.ShapeDtypeStruct((rows // 2, columns), jnp.bfloat16)
    return pl.pallas_call(
        settle_kernel,
        out_shape=[half] * 2,
        compiler_params=pltpu.CompilerParams(vmem_limit_bytes=24 * 2**20),
        cost_estimate=SHORT,
    )(held_at, middle, *sums)


def add_cut_kernel(dp_ref, own_ref, got_ref, sent_ref, kept_ref):
    field = low(sum_blocks(own_ref[...], got_ref[...]))

    @pl.when(pl.program_id(0) == 0)
    def _():
        sent_ref[...] = field

    @pl.when(pl.program_id(0) == 1)
    def _():
        kept_ref[...] = field


def add_cut(own, got, dp):
    rows, columns = own.shape

    def half(i, dp_ref):
        return jnp.where(i == 0, 1 - dp_ref[0], dp_ref[0]), 0

    block_of = pl.BlockSpec((rows // 2, columns), half)
    whole = pl.BlockSpec((rows // 2, columns), lambda i, dp_ref: (0, 0))
    sent, kept = pl.pallas_call(
        add_cut_kernel,
        grid_spec=pltpu.PrefetchScalarGridSpec(
            num_scalar_prefetch=1, grid=(2,), in_specs=[block_of] * 2, out_specs=[whole] * 2
        ),
        out_shape=[jax.ShapeDtypeStruct((rows // 2, columns), jnp.bfloat16)] * 2,
        compiler_params=pltpu.CompilerParams(vmem_limit_bytes=24 * 2**20),
        cost_estimate=SHORT,
    )(dp[None].astype(jnp.int32), own, got)
    return kept, sent


def from_pieces(put, place_ref, pieces):
    step = pl.program_id(0)
    for half in range(2):
        here = 2 * half + place_ref[half]
        pl.when(step == here)(functools.partial(put, pieces[2 * half]))
        pl.when(step == 4 * half + 1 - here)(functools.partial(put, pieces[2 * half + 1]))


def finish_qkv_kernel(place_ref, *refs):
    weight_ref, gain_ref, out_ref, grad_ref = refs[4:]

    def put(field):
        field = field[...].astype(jnp.float32)
        out_ref[...] = field
        total = jnp.sum(field * weight_ref[...].astype(jnp.float32), axis=1, keepdims=True)
        grad_ref[...] = total / gain_ref[...]

    from_pieces(put, place_ref, refs[:4])


def finish_out_kernel(place_ref, first, second, *refs):
    out_ref, small_ref = refs[-2:]
    width = out_ref.shape[1]

    def put(field):
        out_ref[...] = field[:, :width].astype(jnp.float32)
        small_ref[...] = field[:, width:].astype(jnp.float32)

    pl.when(pl.program_id(0) == 0)(functools.partial(put, first))
    pl.when(pl.program_id(0) == 1)(functools.partial(put, second))


def finish_out(pieces, place, is_own, kept):
    dp, x, _, _ = place
    at = jnp.stack([x, dp]).astype(jnp.int32)
    at = at if is_own else 1 - at
    rows, total = pieces[0].shape
    widths = total - HEAD_SIZE, HEAD_SIZE
    whole = pl.BlockSpec((rows, total), lambda i, place_ref: (0, 0))
    return pl.pallas_call(
        finish_out_kernel,
        grid_spec=pltpu.PrefetchScalarGridSpec(
            num_scalar_prefetch=1,
            grid=(2,),
            in_specs=[whole] * 2 + [pl.BlockSpec(memory_space=pl.ANY)] * len(kept),
            out_specs=[
                pl.BlockSpec((rows, width), lambda i, place_ref: (2 * i + place_ref[i], 0))
                for width in widths
            ],
        ),
        out_shape=[jax.ShapeDtypeStruct((4 * rows, width), jnp.float32) for width in widths],
        input_output_aliases={3 + i: i for i in range(len(kept))},
        compiler_params=pltpu.CompilerParams(vmem_limit_bytes=24 * 2**20),
        cost_estimate=SHORT,
    )(at, *pieces, *kept)


def finish(kernel, fields, place, extras, widths):
    dp, x, _, _ = place
    pieces = [*fields[0], *fields[1]]
    rows = pieces[0].shape[0]

    def cut(width):
        return pl.BlockSpec((rows, width), lambda i: (i, 0))

    return pl.pallas_call(
        kernel,
        grid=(4,),
        in_specs=[
            pl.BlockSpec(memory_space=pltpu.SMEM),
            *[pl.BlockSpec(piece.shape, lambda i: (0, 0)) for piece in pieces],
            *[cut(extra.shape[1]) for extra in extras],
        ],
        out_specs=[cut(width) for width in widths],
        out_shape=[jax.ShapeDtypeStruct((4 * rows, width), jnp.float32) for width in widths],
        compiler_params=pltpu.CompilerParams(vmem_limit_bytes=24 * 2**20),
        cost_estimate=SHORT,
    )(jnp.stack([x, dp]).astype(jnp.int32), *pieces, *extras)


def turn(field, cosine, sine):
    half = field.shape[1] // 2
    turned = jnp.concatenate([field[:, half:], field[:, :half]], axis=1)
    return field * cosine + turned * sine


HEADS_AT_ONCE = 2


def attend_kernel(query_in, key_in, value_in, cos_ref, sin_ref, seg_row, seg_column, *refs):
    query_ref, key_ref, value_ref, mix_ref = refs
    cosine, sine = cos_ref[...], sin_ref[...]
    key = low(turn(key_in[...], cosine, sine))
    value = low(value_in[...])
    key_ref[...], value_ref[...] = key, value
    for half in range(HEADS_AT_ONCE):
        columns = slice(half * HEAD_SIZE, (half + 1) * HEAD_SIZE)
        query = low(turn(query_in[:, columns], cosine, sine))
        query_ref[:, columns] = query
        probs = probabilities(query, key, seg_row[...], seg_column[...])
        mix_ref[:, columns] = low(matmul(low(probs), value, FIRST_WITH_FIRST))


def probabilities(query, key, seg_row, seg_column):
    scores = matmul(key, query, LAST_WITH_LAST) * HEAD_SIZE ** (-0.5)
    square = key.shape[0], key.shape[0]
    key_at = lax.broadcasted_iota(jnp.int32, square, 0)
    query_at = lax.broadcasted_iota(jnp.int32, square, 1)
    hidden = jnp.where((seg_row == seg_column) & (key_at <= query_at), 0.0, -1e30)
    hidden = jnp.concatenate([hidden] * (scores.shape[1] // key.shape[0]), axis=1)
    scores = jnp.where(hidden < 0.0, -1e30, scores)
    raised = jnp.exp(scores - jnp.max(scores, axis=0, keepdims=True))
    return raised / jnp.sum(raised, axis=0, keepdims=True)


def attend(projected, cosine, sine, segment):
    rows, width = projected.shape
    groups, heads = KEY_VALUE_HEADS, QUERY_HEADS

    steps = heads // HEADS_AT_ONCE

    def one(index):
        return pl.BlockSpec((rows, HEAD_SIZE), lambda i: (0, index(i)))

    def whole(*shape):
        return pl.BlockSpec(shape, lambda i: (0, 0))

    def shape(count):
        return jax.ShapeDtypeStruct((rows, count * HEAD_SIZE), jnp.bfloat16)

    def group(i):
        return i // (steps // groups)

    head = pl.BlockSpec((rows, HEADS_AT_ONCE * HEAD_SIZE), lambda i: (0, i))
    return pl.pallas_call(
        attend_kernel,
        grid=(steps,),
        in_specs=[
            head,
            one(lambda i: heads + group(i)),
            one(lambda i: heads + groups + group(i)),
            whole(rows, HEAD_SIZE),
            whole(rows, HEAD_SIZE),
            whole(1, rows),
            whole(rows, 1),
        ],
        out_specs=[head, one(group), one(group), head],
        out_shape=[shape(heads), shape(groups), shape(groups), shape(heads)],
        compiler_params=pltpu.CompilerParams(vmem_limit_bytes=24 * 2**20),
        cost_estimate=SHORT,
    )(projected, projected, projected, cosine, sine, segment[None, :], segment[:, None])


def attend_back_kernel(
    query_ref, key_ref, value_ref, grad_ref, cos_ref, sin_ref, seg_row, seg_column, out_ref, *sums
):
    key_sum, value_sum = sums
    step = pl.program_id(0)
    heads, groups = QUERY_HEADS, KEY_VALUE_HEADS
    steps = pl.num_programs(0) // groups
    group, place = step // steps, step % steps
    key, value = key_ref[...], value_ref[...]
    cosine, sine = cos_ref[...], -sin_ref[...]

    def put(head, field):
        at = pl.multiple_of(head * HEAD_SIZE, HEAD_SIZE)
        out_ref[:, pl.ds(at, HEAD_SIZE)] = low(field)

    def stacked(ref):
        return jnp.concatenate(
            [ref[:, at * HEAD_SIZE : (at + 1) * HEAD_SIZE] for at in range(HEADS_AT_ONCE)]
        )

    query, grad_mix = stacked(query_ref), stacked(grad_ref)
    rows = key.shape[0]
    probs = probabilities(query, key, seg_row[...], seg_column[...])
    grad_probs = matmul(value, grad_mix, LAST_WITH_LAST)
    grad_scores = low(
        probs * (grad_probs - jnp.sum(probs * grad_probs, axis=0, keepdims=True))
    )
    grad_query = matmul(grad_scores, key, FIRST_WITH_FIRST) * HEAD_SIZE ** (-0.5)
    for at in range(HEADS_AT_ONCE):
        head = grad_query[at * rows : (at + 1) * rows]
        put(step * HEADS_AT_ONCE + at, turn(head, cosine, sine))
    grad_key = matmul(grad_scores, query) * HEAD_SIZE ** (-0.5)
    grad_value = matmul(low(probs), grad_mix)

    @pl.when(place == 0)
    def _():
        key_sum[...] = grad_key
        value_sum[...] = grad_value

    @pl.when(place > 0)
    def _():
        key_sum[...] += grad_key
        value_sum[...] += grad_value

    @pl.when(place == steps - 1)
    def _():
        put(heads + group, turn(key_sum[...], cosine, sine))
        put(heads + groups + group, value_sum[...])


def attend_back(query, key, value, grad_mix, cosine, sine, segment):
    rows = query.shape[0]
    heads, groups = QUERY_HEADS, KEY_VALUE_HEADS
    steps = heads // HEADS_AT_ONCE

    def whole(*shape):
        return pl.BlockSpec(shape, lambda i: (0, 0))

    head = pl.BlockSpec((rows, HEADS_AT_ONCE * HEAD_SIZE), lambda i: (0, i))
    shared = pl.BlockSpec((rows, HEAD_SIZE), lambda i: (0, i // (steps // groups)))
    width = (heads + 2 * groups) * HEAD_SIZE
    return pl.pallas_call(
        attend_back_kernel,
        grid=(steps,),
        in_specs=[
            head,
            shared,
            shared,
            head,
            whole(rows, HEAD_SIZE),
            whole(rows, HEAD_SIZE),
            whole(1, rows),
            whole(rows, 1),
        ],
        out_specs=whole(rows, width),
        out_shape=jax.ShapeDtypeStruct((rows, width), jnp.bfloat16),
        scratch_shapes=[pltpu.VMEM((rows, HEAD_SIZE), jnp.float32)] * 2,
        compiler_params=pltpu.CompilerParams(vmem_limit_bytes=24 * 2**20),
        cost_estimate=SHORT,
    )(query, key, value, grad_mix, cosine, sine, segment[None, :], segment[:, None])


def ring_shards(
    hidden_in,
    cotangent,
    deal_order,
    lengths,
    routes,
    attention_gain,
    expert_gain,
    qkv_weight,
    out_weight,
    router_weight,
    gate_up_weight,
    down_weight,
):
    count_of_rows = hidden_in.shape[0]
    model_width = hidden_in.shape[1]
    half_rows = count_of_rows // 2
    expert_count = router_weight.shape[1]
    dp, core, at = lax.axis_index("dp"), lax.axis_index("shard"), lax.axis_index("expert")
    x, z = at % 2, at // 2
    place = (dp, x, z, core)
    row_ids = jnp.arange(count_of_rows, dtype=jnp.int32)

    def half_of(field, index):
        return lax.dynamic_slice_in_dim(field, index * half_rows, half_rows, axis=0)

    def sent_dealt(field):
        return half_of(field, dp), other_dp(half_of(field, 1 - dp)), field[count_of_rows:]

    def arrange(own_half, other_half, order):
        held_at = jnp.where(order[1, :count_of_rows] == dp, 0, half_rows)
        held_at = held_at + order[0, :count_of_rows].astype(jnp.int32)
        chosen = low(held_at[:, None] == row_ids[None, :])
        return low(matmul(chosen, jnp.concatenate([own_half, other_half], axis=0)))

    def swapped(field):
        return field, other_core(field)

    held_at = jnp.where(deal_order // half_rows == dp, 0, half_rows) + deal_order % half_rows

    def deal(field):
        field = low(matmul(low(held_at == row_ids[:, None]), field))
        return field[:half_rows], field[half_rows:]

    def to_dealt(halves):
        return halves[0], other_dp(halves[1])

    ct_0 = dealt_unit(cotangent, deal_order)
    order = ct_0[count_of_rows:]
    ct_1 = ring_z(ct_0)
    hidden_out = half_of(after(hidden_in, ct_0), 1 - dp)
    hidden_arrived = other_dp(hidden_out)
    qkv_other, out_other, up_other = (
        send(after(field, hidden_out))
        for send, field in (
            (other_core, qkv_weight),
            (other_core, out_weight),
            (from_owner, gate_up_weight[0]),
        )
    )
    small = jnp.concatenate(
        [router_weight.T, attention_gain[None], expert_gain[None], jnp.zeros_like(router_weight.T[:6])]
    )
    small = in_order(core == 0, small, other_core(small), axis=1)
    router = small[:expert_count]
    gain_first = small[expert_count : expert_count + 1].astype(jnp.float32)
    gain_second = small[expert_count + 1 : expert_count + 2].astype(jnp.float32)
    full_qkv = in_order(core == 0, qkv_weight, qkv_other)
    segment, token_position = positions_of(lengths[0], count_of_rows)
    frequency = THETA ** (-jnp.arange(HEAD_SIZE // 2, dtype=jnp.float32) / (HEAD_SIZE // 2))
    angles = token_position.astype(jnp.float32)[:, None] * frequency[None, :]
    cosine = jnp.concatenate([jnp.cos(angles)] * 2, axis=1)
    sine = jnp.concatenate([-jnp.sin(angles), jnp.sin(angles)], axis=1)
    cosine, sine, full_qkv, hidden_arrived, gain_first, gain_second, router, routes = part(
        cosine, sine, full_qkv, hidden_arrived, gain_first, gain_second, router, routes.T
    )
    tokens = arrange(half_of(hidden_in, dp), hidden_arrived, order)
    residual = tokens.astype(jnp.float32)
    inv_first = lax.rsqrt(jnp.mean(residual * residual, axis=1, keepdims=True) + EPS)
    normed_attn = low(residual * inv_first * gain_first)
    projected = matmul(normed_attn, full_qkv)
    ct_1, projected, ct_0, out_other, down_own = part(
        ct_1, projected, ct_0, out_other, down_weight[0]
    )

    ct_2 = ring_z(ct_1)
    ct_0 = sent_dealt(ct_0)
    down_other = from_owner(down_own)
    full_out = in_order(core == 0, out_weight, out_other)
    query, key, value, attn_mix = attend(projected, cosine, sine, segment)
    middle, inv_second, unit_0, gates = middle_of(
        attn_mix, full_out, tokens, gain_second, router, routes
    )
    ct_2, ct_0, ct_1, unit_0, up_other = part(ct_2, ct_0, ct_1, unit_0, up_other)

    normed_1 = ring_z(unit_0)
    normed_0 = swapped(unit_0)
    ct_1 = sent_dealt(ct_1)
    ct_0 = swapped(arrange(*ct_0))
    normed_1, normed_0, ct_0, ct_1, ct_2, down_other = part(
        normed_1, normed_0, ct_0, ct_1, ct_2, down_other
    )
    choice = jnp.stack([(core == x).astype(jnp.int32), (2 * z + core).astype(jnp.int32)])
    matrices = (gate_up_weight[0], up_other, down_weight[0], down_other)

    ct_3 = ring_z(ct_2)
    ct_2 = sent_dealt(ct_2)
    ct_1, normed_1 = swapped(arrange(*ct_1)), swapped(normed_1)
    sums_0, back_0, kept = expert_step(0, choice, normed_0, ct_0, matrices, None)
    ct_3, ct_1, normed_1, ct_2, kept = part(ct_3, ct_1, normed_1, ct_2, kept)

    normed_2 = ring_z(normed_1[0])
    ct_3 = sent_dealt(ct_3)
    ct_2 = swapped(arrange(*ct_2))
    mixes, normeds = swapped(attn_mix), swapped(normed_attn)
    sums_1, back_1, kept = expert_step(1, choice, normed_1, ct_1, matrices, kept)
    normed_2, ct_3, ct_2, back_1, kept, mixes, normeds = part(
        normed_2, ct_3, ct_2, back_1, kept, mixes, normeds
    )

    normed_3 = ring_z(normed_2)
    normed_2, back_1_other = swapped(normed_2), other_core(back_1[1])
    ct_3 = swapped(arrange(*ct_3))
    sums_2, back_2, kept = expert_step(2, choice, normed_2, ct_2, matrices, kept)
    back_1 = low(sum_blocks(back_1[0], back_1_other))
    normed_3, back_1, ct_3, back_2, kept = part(normed_3, back_1, ct_3, back_2, kept)

    back_1 = ring_z(back_1)
    normed_3, back_2_other = swapped(normed_3), other_core(back_2[1])
    sums_3, back_3, kept = expert_step(3, choice, normed_3, ct_3, matrices, kept)
    back_1, back_2_other, back_3, kept = part(back_1, back_2_other, back_3, kept)

    back_2 = ring_z(low(sum_blocks(back_2[0], back_2_other, back_1)))
    back_3_other, back_0_other = other_core(back_3[1]), other_core(back_0[1])
    sums_1_other, sums_0_other = other_core(sums_1[1]), other_core(sums_0[1])
    all_hidden, all_grad_out, all_grad_up, all_rows = kept
    half_width = model_width // 2
    down_first = low(matmul(all_hidden.T, all_grad_out[:, :half_width]))
    down_second = low(matmul(all_hidden.T, all_grad_out[:, half_width:]))
    down_second = block(down_second, dp, 2), block(down_second, 1 - dp, 2)
    (
        back_2,
        back_3_other,
        back_0_other,
        sums_1_other,
        sums_0_other,
        down_first,
        down_second,
        all_grad_up,
        all_rows,
    ) = part(
        back_2,
        back_3_other,
        back_0_other,
        sums_1_other,
        sums_0_other,
        down_first,
        down_second,
        all_grad_up,
        all_rows,
    )

    back_3 = ring_z(low(sum_blocks(back_3[0], back_3_other, back_2)))
    down_first = down_first, to_owner(down_first)
    down_second = down_second[0], other_dp(down_second[1])
    up_second = low(matmul(all_rows.T, all_grad_up[:, half_width:]))
    up_first = low(matmul(all_rows.T, all_grad_up[:, :half_width]))
    sums_1 = low(sum_blocks(sums_1[0], sums_1_other))
    sums_2_other, sums_3_other = other_core(sums_2[1]), other_core(sums_3[1])
    up_second = block(up_second, dp, 2), block(up_second, 1 - dp, 2)
    (
        back_3,
        up_first,
        up_second,
        down_first,
        down_second,
        sums_1,
        sums_2_other,
        sums_3_other,
    ) = part(
        back_3,
        up_first,
        up_second,
        down_first,
        down_second,
        sums_1,
        sums_2_other,
        sums_3_other,
    )

    sums_1 = ring_z(sums_1)
    up_first = up_first, to_owner(up_first)
    up_second = up_second[0], other_dp(up_second[1])
    grad_middle, grad_unit, grad_mix = middle_back(
        (back_0[0], back_0_other, back_3),
        gates,
        router,
        middle,
        inv_second,
        gain_second,
        ct_0[0],
        full_out,
    )
    grad_projected = attend_back(query, key, value, grad_mix, cosine, sine, segment)
    sums_1, grad_projected, grad_unit, up_first, up_second, down_first, down_second = part(
        sums_1, grad_projected, grad_unit, up_first, up_second, down_first, down_second
    )

    grads_projected, grad_units = swapped(grad_projected), swapped(grad_unit)
    up_first, up_second = add_cut(*up_first, dp), low(sum_blocks(*up_second))
    sums_2 = low(sum_blocks(sums_2[0], sums_2_other, sums_1))
    qkv = qkv_grads(normeds, grads_projected, place)
    sums_2, grad_units, qkv, down_first, down_second, up_first, up_second, grad_projected = part(
        sums_2, grad_units, qkv, down_first, down_second, up_first, up_second, grad_projected
    )

    sums_2 = ring_z(sums_2)
    qkv = slab_sum(qkv, place)
    up_first = up_first[0], owners_dp(up_first[1])
    up_second = up_second, to_owner(up_second)
    down_first, down_second, qkv = part(down_first, down_second, qkv)
    down_first, down_second = low(sum_blocks(*down_first)), low(sum_blocks(*down_second))
    down_first = block(down_first, dp, 2), block(down_first, 1 - dp, 2)
    grad_tokens = tokens_back(
        grad_projected, full_qkv, tokens, inv_first, gain_first, grad_middle
    )
    out = out_grads(mixes, normed_0, grad_units, place)
    grad_tokens = deal(grad_tokens)
    sums_3 = low(sum_blocks(sums_3[0], sums_3_other, sums_2))
    sums_3, out, qkv, up_first, up_second, down_first, down_second, grad_tokens = part(
        sums_3, out, qkv, up_first, up_second, down_first, down_second, grad_tokens
    )

    sums_3 = ring_z(sums_3)
    qkv = slab_sum_on(qkv, place)
    down_first = down_first[0], owners_dp(down_first[1])
    down_second = down_second, to_owner(down_second)
    input_gradient = to_dealt(grad_tokens)
    up_grad = low(jnp.concatenate([sum_blocks(*up_first), sum_blocks(*up_second)], axis=1))
    up_grad = block(up_grad, core, 2), block(up_grad, 1 - core, 2)
    out, qkv, up_grad, down_first, down_second, sums_3, input_gradient = part(
        out, qkv, up_grad, down_first, down_second, sums_3, input_gradient
    )

    qkv, out = line_sum(qkv), slab_sum(out, place)
    down_grad = low(jnp.concatenate([sum_blocks(*down_first), sum_blocks(*down_second)], axis=1))
    down_grad = block(down_grad, core, 2), block(down_grad, 1 - core, 2)
    layer_out = settle(held_at, middle, sums_0[0], sums_0_other, sums_3)
    out, qkv, up_grad, down_grad, layer_out = part(out, qkv, up_grad, down_grad, layer_out)

    qkv, out = line_spread(qkv, place), slab_sum_on(out, place)
    layer_out = to_dealt(layer_out)
    out, qkv, layer_out, up_grad, down_grad = part(out, qkv, layer_out, up_grad, down_grad)

    qkv, out = slab_spread(qkv, place), line_sum(out)
    out, qkv, up_grad, down_grad = part(out, qkv, up_grad, down_grad)

    qkv, out = slab_spread_on(qkv), line_spread(out, place)
    out, qkv, up_grad, down_grad = part(out, qkv, up_grad, down_grad)

    out = slab_spread(out, place)
    up_grad, down_grad = (
        jnp.where(core == x, field[0], other_core(field[1])) for field in (up_grad, down_grad)
    )
    gain = attention_gain.astype(jnp.float32)[:, None]
    qkv_grad, gain_first_grad = finish(
        finish_qkv_kernel, qkv, place, [qkv_weight, gain], [qkv_weight.shape[1], 1]
    )
    out, qkv_grad, gain_first_grad, up_grad, down_grad, layer_out, input_gradient = part(
        out, qkv_grad, gain_first_grad, up_grad, down_grad, layer_out, input_gradient
    )

    layer_out, input_gradient = (
        in_order(dp == 0, *field) for field in (layer_out, input_gradient)
    )
    out_grad, small_grad = finish_out(out, place, True, [])
    (_, first), (_, second) = slab_spread_on(out)
    out_grad, small_grad = finish_out([first, second], place, False, [out_grad, small_grad])
    gate_up_grad, down_grad = (field[None].astype(jnp.float32) for field in (up_grad, down_grad))
    return (
        layer_out,
        input_gradient,
        gain_first_grad[:, 0],
        small_grad[:, expert_count],
        qkv_grad,
        out_grad,
        small_grad[:, :expert_count],
        gate_up_grad,
        down_grad,
    )


def solution(mesh):
    ringed = (mesh.shape["dp"], mesh.shape["expert"], mesh.shape["shard"]) == (2, 8, 2)
    shards = ring_shards if ringed else routed_shards
    return jax.shard_map(
        shards,
        mesh=mesh,
        in_specs=(
            P(("dp", "expert", "shard"), None),
            P(("dp", "expert", "shard"), None),
            P(("dp", "expert", "shard"), None),
            P(("dp", "expert", "shard"), None),
            P(("dp", "expert", "shard"), None),
            P("shard"),
            P("shard"),
            P("shard", None),
            P("shard", None),
            P("shard", None),
            P("expert", None, None),
            P("expert", None, None),
        ),
        out_specs=(
            P(("dp", "expert", "shard"), None),
            P(("dp", "expert", "shard"), None),
            P("shard"),
            P("shard"),
            P("shard", None),
            P("shard", None),
            P("shard", None),
            P("expert", ("dp", "shard"), None),
            P("expert", ("dp", "shard"), None),
        ),
        check_vma=False,
    )
```
